32 devices in a mesh: dp: 8 (over z, y), fsdp: 4 (over x, core).
Axes of the slice: x: 2, y: 2, z: 4, core: 2. Of those that a mesh axis runs over, the one named last changes fastest.
Arguments:
- inputs: bfloat16 [32, 1024, 768], P('dp', 'fsdp'), may hold values from -6 to 6
- cotangent: bfloat16 [32, 1024, 768], P('dp', 'fsdp'), may hold values from -6 to 6
- doc_lengths: int32 [32, 4], P('dp'), may hold values from 1 to 896, as said below
- labels: int32 [32, 4], P('dp'), may hold values from 0 to 2
- w_query: float32 [768, 768], P(('dp', 'fsdp')), may hold values from -0.21875 to 0.21875
- b_query: float32 [768], P(('dp', 'fsdp')), may hold values from -1.75 to 1.75
- w_key: float32 [768, 768], P(('dp', 'fsdp')), may hold values from -0.21875 to 0.21875
- w_value: float32 [768, 768], P(('dp', 'fsdp')), may hold values from -0.21875 to 0.21875
- b_value: float32 [768], P(('dp', 'fsdp')), may hold values from -1.75 to 1.75
- w_out: float32 [768, 768], P(('dp', 'fsdp')), may hold values from -1.25 to 1.25
- b_out: float32 [768], P(('dp', 'fsdp')), may hold values from -1.75 to 1.75
- first_gain: float32 [768], P(('dp', 'fsdp')), may hold values from 0.5 to 1.5
- first_shift: float32 [768], P(('dp', 'fsdp')), may hold values from -1.75 to 1.75
- w_inner: float32 [768, 3072], P(('dp', 'fsdp')), may hold values from -0.21875 to 0.21875
- b_inner: float32 [3072], P(('dp', 'fsdp')), may hold values from -1.75 to 1.75
- w_outer: float32 [3072, 768], P(('dp', 'fsdp')), may hold values from -0.109375 to 0.109375
- b_outer: float32 [768], P(('dp', 'fsdp')), may hold values from -1.75 to 1.75
- second_gain: float32 [768], P(('dp', 'fsdp')), may hold values from 0.5 to 1.5
- second_shift: float32 [768], P(('dp', 'fsdp')), may hold values from -1.75 to 1.75
- w_pool: float32 [768, 768], P(('dp', 'fsdp')), may hold values from -0.21875 to 0.21875
- b_pool: float32 [768], P(('dp', 'fsdp')), may hold values from -1.75 to 1.75
- w_class: float32 [768, 3], P(('dp', 'fsdp')), may hold values from -0.4375 to 0.4375
- b_class: float32 [3], replicated, may hold values from -3 to 3
Outputs:
- layer_out: bfloat16 [32, 1024, 768], P('dp', 'fsdp')
- logits: float32 [32, 4, 3], P('dp')
- grad_inputs: bfloat16 [32, 1024, 768], P('dp', 'fsdp')
- grad_w_query: float32 [768, 768], P(('dp', 'fsdp'))
- grad_b_query: float32 [768], P(('dp', 'fsdp'))
- grad_w_key: float32 [768, 768], P(('dp', 'fsdp'))
- grad_w_value: float32 [768, 768], P(('dp', 'fsdp'))
- grad_b_value: float32 [768], P(('dp', 'fsdp'))
- grad_w_out: float32 [768, 768], P(('dp', 'fsdp'))
- grad_b_out: float32 [768], P(('dp', 'fsdp'))
- grad_first_gain: float32 [768], P(('dp', 'fsdp'))
- grad_first_shift: float32 [768], P(('dp', 'fsdp'))
- grad_w_inner: float32 [768, 3072], P(('dp', 'fsdp'))
- grad_b_inner: float32 [3072], P(('dp', 'fsdp'))
- grad_w_outer: float32 [3072, 768], P(('dp', 'fsdp'))
- grad_b_outer: float32 [768], P(('dp', 'fsdp'))
- grad_second_gain: float32 [768], P(('dp', 'fsdp'))
- grad_second_shift: float32 [768], P(('dp', 'fsdp'))
- grad_w_pool: float32 [768, 768], P(('dp', 'fsdp'))
- grad_b_pool: float32 [768], P(('dp', 'fsdp'))
- grad_w_class: float32 [768, 3], P(('dp', 'fsdp'))
- grad_b_class: float32 [3], replicated
The draws below stay inside these ranges and needn't reach their ends.
Inputs may be any that keep to these rules, and one draw needn't show every extreme that they name: `doc_lengths`: the 4 document lengths of a sequence sum to 1024; in each group of 4 consecutive sequences one (which one varies) begins with a document of exactly 896 tokens, and in each of the others every block of 256 positions holds exactly one document start.
All inputs are finite; a program needn't handle non-finite values.
Results may differ from the reference program's by a relative error of at most 0.015.
The reference program's roundings to bfloat16 on the way count: a program that leaves them out, or rounds other values in their place, can miss the bound.
Values may be sent and summed in bfloat16 or wider, within the bound.
A program may use at most 256 MiB of HBM per device.

```python
import jax
import jax.numpy as jnp
from jax import lax

D = 768
HEADS = 12
HEAD_DIM = 64
FF = 3072
CLASSES = 3
LEN = 1024
DOCS = 4
SEQ_DEV = 4
SEQUENCES = 32


def draw_doc_lengths(key, part):
    block = LEN // DOCS
    half = block // 2
    key_off = jax.random.fold_in(key, 11)
    key_cut = jax.random.fold_in(key, 12)
    key_pick = jax.random.fold_in(key, 13)
    offsets = jax.random.randint(key_off, (SEQUENCES, DOCS), 0, half + 1).astype(jnp.int32)
    offsets = offsets * (jnp.arange(DOCS, dtype=jnp.int32)[None, :] > 0).astype(jnp.int32)
    starts = jnp.arange(DOCS, dtype=jnp.int32)[None, :] * block + offsets
    ends = jnp.concatenate([starts[:, 1:], jnp.full((SEQUENCES, 1), LEN, jnp.int32)], axis=1)
    dense_rows = ends - starts
    extra = half - (DOCS - 1)
    cuts = jnp.sort(jax.random.randint(key_cut, (SEQUENCES, DOCS - 2), 0, extra + 1).astype(jnp.int32), axis=1)
    bounds = jnp.concatenate([jnp.zeros((SEQUENCES, 1), jnp.int32), cuts, jnp.full((SEQUENCES, 1), extra, jnp.int32)], axis=1)
    short_rows = bounds[:, 1:] - bounds[:, :-1] + 1
    long_rows = jnp.concatenate([jnp.full((SEQUENCES, 1), LEN - half, jnp.int32), short_rows], axis=1)
    picks = jax.random.randint(key_pick, (SEQUENCES // SEQ_DEV,), 0, SEQ_DEV).astype(jnp.int32)
    seq_index = jnp.arange(SEQUENCES, dtype=jnp.int32)
    is_long = seq_index % SEQ_DEV == jnp.repeat(picks, SEQ_DEV)
    return jnp.where(is_long[:, None], long_rows, dense_rows).astype(jnp.int32)


def touch_ends(entries, own_key, low, largest):
    longest = entries.shape.index(max(entries.shape))
    spots = []
    for shift in (0, 1):
        where = [jax.random.randint(jax.random.fold_in(own_key, axis), (), 0, length) for axis, length in enumerate(entries.shape)]
        where[longest] = (where[longest] + shift) % entries.shape[longest]
        spots.append(tuple(where))
    return entries.at[spots[0]].set(low).at[spots[1]].set(largest)


def steps_of(key, extent, cuts, smallest, top_value):
    level = 1.0
    for axis_at, shards_of in cuts:
        draws = jax.random.uniform(jax.random.fold_in(jax.random.fold_in(key, 6), axis_at), (shards_of,), jnp.float32, smallest / len(cuts), top_value / len(cuts))
        level = level * jnp.repeat(jnp.exp(draws), extent[axis_at] // shards_of).reshape((-1,) + (1,) * (len(extent) - 1 - axis_at))
    return level


def scatter_about(rng, shape, width, bound, shards=(), held_as=jnp.bfloat16):
    entries = jax.random.normal(rng, shape, jnp.float32) * width
    if len(shards) > 0:
        entries = steps_of(rng, shape, shards, -0.22, 0.18) * entries
    return jnp.clip(entries, min=-bound, max=bound).astype(held_as)


def setup_inputs(seed: int = 0) -> dict:
    seeds = jax.random.split(jax.random.key(seed), 24)
    inputs = scatter_about(seeds[0], (SEQUENCES, LEN, D), 1.0, 6.0, ((0, 8), (1, 4)))
    cotangent = scatter_about(seeds[1], (SEQUENCES, LEN, D), 1.0, 6.0, ((0, 8), (1, 4)))
    doc_lengths = draw_doc_lengths(jax.random.fold_in(seeds[23], 71), 0)
    labels = touch_ends(jax.random.randint(seeds[3], (SEQUENCES, DOCS), 0, CLASSES), jax.random.fold_in(seeds[3], 1), 0, CLASSES - 1).astype(jnp.int32)
    w_query = scatter_about(seeds[4], (D, D), D ** -0.5, 0.21875, ((0, 32),), jnp.float32)
    b_query = scatter_about(seeds[5], (D,), 0.3, 1.75, ((0, 32),), jnp.float32)
    w_key = scatter_about(seeds[6], (D, D), D ** -0.5, 0.21875, ((0, 32),), jnp.float32)
    w_value = scatter_about(seeds[7], (D, D), D ** -0.5, 0.21875, ((0, 32),), jnp.float32)
    b_value = scatter_about(seeds[8], (D,), 0.3, 1.75, ((0, 32),), jnp.float32)
    w_out = scatter_about(seeds[9], (D, D), (D // 32) ** -0.5, 1.25, ((0, 32),), jnp.float32)
    b_out = scatter_about(seeds[10], (D,), 0.3, 1.75, ((0, 32),), jnp.float32)
    first_gain = jnp.clip(1.0 + 0.1 * jax.random.normal(seeds[11], (D,), jnp.float32), 0.5, 1.5)
    first_shift = scatter_about(seeds[12], (D,), 0.3, 1.75, ((0, 32),), jnp.float32)
    w_inner = scatter_about(seeds[13], (D, FF), D ** -0.5, 0.21875, ((0, 32),), jnp.float32)
    b_inner = scatter_about(seeds[14], (FF,), 0.3, 1.75, ((0, 32),), jnp.float32)
    w_outer = scatter_about(seeds[15], (FF, D), FF ** -0.5, 0.109375, ((0, 32),), jnp.float32)
    b_outer = scatter_about(seeds[16], (D,), 0.3, 1.75, ((0, 32),), jnp.float32)
    second_gain = jnp.clip(1.0 + 0.1 * jax.random.normal(seeds[17], (D,), jnp.float32), 0.5, 1.5)
    second_shift = scatter_about(seeds[18], (D,), 0.3, 1.75, ((0, 32),), jnp.float32)
    w_pool = scatter_about(seeds[19], (D, D), D ** -0.5, 0.21875, ((0, 32),), jnp.float32)
    b_pool = scatter_about(seeds[20], (D,), 0.3, 1.75, ((0, 32),), jnp.float32)
    w_class = scatter_about(seeds[21], (D, CLASSES), (D // 4) ** -0.5, 0.4375, ((0, 32),), jnp.float32)
    b_class = scatter_about(seeds[22], (CLASSES,), 0.5, 3.0, (), jnp.float32)
    return {"inputs": inputs, "cotangent": cotangent, "doc_lengths": doc_lengths, "labels": labels, "w_query": w_query, "b_query": b_query, "w_key": w_key, "w_value": w_value, "b_value": b_value, "w_out": w_out, "b_out": b_out, "first_gain": first_gain, "first_shift": first_shift, "w_inner": w_inner, "b_inner": b_inner, "w_outer": w_outer, "b_outer": b_outer, "second_gain": second_gain, "second_shift": second_shift, "w_pool": w_pool, "b_pool": b_pool, "w_class": w_class, "b_class": b_class}


@jax.custom_vjp
def low(v):
    return lax.optimization_barrier(v.astype(jnp.bfloat16)).astype(jnp.float32)

@jax.custom_vjp
def low_back(v):
    return v

def low_keep(v):
    return (low(v), None)

def low_pass(kept, grad):
    return (grad,)

def back_keep(v):
    return (v, None)

def back_low(kept, grad):
    return (low(grad),)
low.defvjp(low_keep, low_pass)
low_back.defvjp(back_keep, back_low)

def matmul(left_side, right_side):
    return jnp.dot(left_side, right_side, precision=lax.Precision.HIGHEST)

def layer_norm(values, norm_gain, norm_shift):
    average = lax.optimization_barrier(jnp.mean(values, axis=-1, keepdims=True))
    centered = values - average
    variance = lax.optimization_barrier(jnp.mean(centered * centered, axis=-1, keepdims=True))
    return centered * lax.rsqrt(variance + 1e-06) * norm_gain + norm_shift

def segments_of(lengths_row):
    doc_ends = jnp.cumsum(lengths_row).astype(jnp.int32)
    places = jnp.arange(LEN, dtype=jnp.int32)
    return lax.optimization_barrier(jnp.sum((places[:, None] >= doc_ends[None, :]).astype(jnp.int32), axis=1))

def one_sequence(params, tokens, lengths_row):
    w_query, b_query, w_key, w_value, b_value, w_out, b_out, first_gain, first_shift, w_inner, b_inner, w_outer, b_outer, second_gain, second_shift, w_pool, b_pool, w_class, b_class = params
    queries = low(low_back(matmul(tokens, w_query) + b_query))
    key_rows = low(low_back(matmul(tokens, w_key)))
    value_rows = low(low_back(matmul(tokens, w_value) + b_value))
    query_heads = queries.reshape(LEN, HEADS, HEAD_DIM)
    key_heads = key_rows.reshape(LEN, HEADS, HEAD_DIM)
    value_heads = value_rows.reshape(LEN, HEADS, HEAD_DIM)
    scores = jnp.einsum('qhd,khd->hqk', query_heads, key_heads, precision=lax.Precision.HIGHEST) * HEAD_DIM ** (-0.5)
    segment = segments_of(lengths_row)
    same_doc = segment[:, None] == segment[None, :]
    scores = low_back(jnp.where(same_doc[None], scores, -1000000000.0))
    shifted = scores - lax.optimization_barrier(jnp.max(scores, axis=-1, keepdims=True))
    exps = jnp.exp(shifted)
    probs = low(exps / lax.optimization_barrier(jnp.sum(exps, axis=-1, keepdims=True)))
    attended = jnp.einsum('hqk,khd->qhd', probs, value_heads, precision=lax.Precision.HIGHEST).reshape(LEN, D)
    attended = low(low_back(attended))
    branch = low_back(matmul(attended, w_out) + b_out)
    normed = layer_norm(tokens + branch, first_gain, first_shift)
    inner_pre = low_back(matmul(low(normed), w_inner) + b_inner)
    activated = low(jax.nn.gelu(inner_pre, approximate=False))
    outer_out = low_back(matmul(activated, w_outer) + b_outer)
    result = layer_norm(normed + outer_out, second_gain, second_shift)
    starts = (jnp.cumsum(lengths_row) - lengths_row).astype(jnp.int32)
    picked = low(result)[starts]
    pooled = jnp.tanh(low_back(matmul(picked, w_pool) + b_pool))
    logits = low_back(matmul(low(pooled), w_class) + b_class)
    return (result, logits)

def loss_of(params, tokens, cot_values, doc_lengths, labels):
    rounded = tuple((low(member) for member in params[:-1])) + (params[-1],)

    def per_sequence(packed):
        return one_sequence(rounded, packed[0], packed[1])
    results, logits = lax.map(jax.checkpoint(per_sequence), (tokens, doc_lengths))
    shifted = logits - lax.optimization_barrier(jnp.max(logits, axis=-1, keepdims=True))
    log_probs = shifted - jnp.log(lax.optimization_barrier(jnp.sum(jnp.exp(shifted), axis=-1, keepdims=True)))
    chosen = jnp.take_along_axis(log_probs, labels[..., None], axis=-1)
    objective = jnp.sum(results * cot_values) - jnp.sum(chosen)
    return (objective, (results, logits))

def reference(inputs, cotangent, doc_lengths, labels, w_query, b_query, w_key, w_value, b_value, w_out, b_out, first_gain, first_shift, w_inner, b_inner, w_outer, b_outer, second_gain, second_shift, w_pool, b_pool, w_class, b_class):
    params = (w_query, b_query, w_key, w_value, b_value, w_out, b_out, first_gain, first_shift, w_inner, b_inner, w_outer, b_outer, second_gain, second_shift, w_pool, b_pool, w_class, b_class)
    tokens = inputs.astype(jnp.float32)
    cot_values = cotangent.astype(jnp.float32)

    def objective_of(params_in, tokens_in):
        return loss_of(params_in, tokens_in, cot_values, doc_lengths, labels)
    objective, pullback, extras = jax.vjp(objective_of, params, tokens, has_aux=True)
    results, logits = extras
    grad_params, grad_tokens = pullback(jnp.ones_like(objective))
    return (results.astype(jnp.bfloat16), logits, grad_tokens.astype(jnp.bfloat16), grad_params[0], grad_params[1], grad_params[2], grad_params[3], grad_params[4], grad_params[5], grad_params[6], grad_params[7], grad_params[8], grad_params[9], grad_params[10], grad_params[11], grad_params[12], grad_params[13], grad_params[14], grad_params[15], grad_params[16], grad_params[17], grad_params[18])
```

```python
import functools

import jax
import jax.numpy as jnp
from jax import lax
from jax.experimental import pallas as pl
from jax.experimental.pallas import tpu as pltpu
from jax.sharding import PartitionSpec as P

HEAD_DIM = 64
CLASSES = 3
MICRO = 4


def product(left_side, right_side):
    return jnp.dot(left_side, right_side, preferred_element_type=jnp.float32)


def contract_rows(left_side, right_side):
    return lax.dot_general(
        left_side, right_side, (((0,), (0,)), ((), ())), preferred_element_type=jnp.float32
    )


def times_transposed(left_side, right_side):
    return lax.dot_general(
        left_side, right_side, (((1,), (1,)), ((), ())), preferred_element_type=jnp.float32
    )


def layer_norm(values, norm_gain, norm_shift):
    average = jnp.mean(values, axis=-1, keepdims=True)
    centered = values - average
    variance = jnp.mean(centered * centered, axis=-1, keepdims=True)
    return centered * lax.rsqrt(variance + 1e-06) * norm_gain + norm_shift


def gelu_exact(values):
    return jax.nn.gelu(values, approximate=False)


def running_sum(lengths_rows):
    count = lengths_rows.shape[1]
    upper = jnp.arange(count)[:, None] <= jnp.arange(count)[None, :]
    return jnp.sum(jnp.where(upper[None], lengths_rows[:, :, None], 0), axis=1)


def segment_numbers(lengths_rows, places):
    doc_ends = running_sum(lengths_rows)
    above = (places[None, :, None] >= doc_ends[:, None, :]).astype(jnp.int32)
    return jnp.sum(above, axis=2)


def pair_heads(values):
    return values.reshape(values.shape[0], values.shape[1], 2, HEAD_DIM)


def pair_scores(query_pair, key_pair, same_doc):
    raw_scores = jnp.einsum(
        "bqhd,bkhd->bhqk", query_pair, key_pair, preferred_element_type=jnp.float32
    ) * HEAD_DIM ** (-0.5)
    return jnp.where(same_doc[:, None], raw_scores, -1000000000.0)


def lowered_masters(masters):
    return [member.astype(jnp.bfloat16) for member in masters]


def forward(tokens, lengths_rows, weights, bias_class):
    (
        w_query,
        b_query,
        w_key,
        w_value,
        b_value,
        w_out,
        b_out,
        first_gain,
        first_shift,
        w_inner,
        b_inner,
        w_outer,
        b_outer,
        second_gain,
        second_shift,
        w_pool,
        b_pool,
        w_class,
    ) = weights
    seq_count, local_len, model_width = tokens.shape
    doc_count = lengths_rows.shape[1]
    flat_rows = tokens.reshape(seq_count * local_len, model_width)
    queries = (
        (product(flat_rows, w_query) + b_query)
        .astype(jnp.bfloat16)
        .reshape(seq_count, local_len, model_width)
    )
    key_rows = (
        product(flat_rows, w_key).astype(jnp.bfloat16).reshape(seq_count, local_len, model_width)
    )
    value_rows = (
        (product(flat_rows, w_value) + b_value)
        .astype(jnp.bfloat16)
        .reshape(seq_count, local_len, model_width)
    )
    all_keys, all_values = (
        lax.all_gather(key_rows, "fsdp", axis=1, tiled=True),
        lax.all_gather(value_rows, "fsdp", axis=1, tiled=True),
    )
    full_len = all_keys.shape[1]
    own_places = lax.axis_index("fsdp") * local_len + jnp.arange(local_len, dtype=jnp.int32)
    key_places = jnp.arange(full_len, dtype=jnp.int32)
    same_doc = (
        segment_numbers(lengths_rows, own_places)[:, :, None]
        == segment_numbers(lengths_rows, key_places)[:, None, :]
    )
    pair_width = 2 * HEAD_DIM
    mixed_list = []
    log_totals = []
    for pair_index in range(model_width // pair_width):
        col_start = pair_index * pair_width
        query_pair = pair_heads(queries[:, :, col_start : col_start + pair_width])
        key_pair = pair_heads(all_keys[:, :, col_start : col_start + pair_width])
        value_pair = pair_heads(all_values[:, :, col_start : col_start + pair_width])
        scores = pair_scores(query_pair, key_pair, same_doc)
        row_peak = jnp.max(scores, axis=-1, keepdims=True)
        exp_total = jnp.sum(jnp.exp(scores - row_peak), axis=-1, keepdims=True)
        log_total = row_peak + jnp.log(exp_total)
        attn_probs = jnp.exp(scores - log_total).astype(jnp.bfloat16)
        mixed_pair = jnp.einsum(
            "bhqk,bkhd->bqhd", attn_probs, value_pair, preferred_element_type=jnp.float32
        )
        mixed_list.append(mixed_pair.reshape(seq_count, local_len, pair_width))
        log_totals.append(log_total)
    attended = (
        jnp.concatenate(mixed_list, axis=2)
        .astype(jnp.bfloat16)
        .reshape(seq_count * local_len, model_width)
    )
    branch = product(attended, w_out) + b_out
    pre_first = flat_rows.astype(jnp.float32) + branch
    normed = layer_norm(pre_first, first_gain.astype(jnp.float32), first_shift.astype(jnp.float32))
    normed_low = normed.astype(jnp.bfloat16)
    inner_pre = product(normed_low, w_inner) + b_inner
    activated = gelu_exact(inner_pre).astype(jnp.bfloat16)
    summed = normed + (product(activated, w_outer) + b_outer)
    result = layer_norm(summed, second_gain.astype(jnp.float32), second_shift.astype(jnp.float32))
    result_low = result.astype(jnp.bfloat16).reshape(seq_count, local_len, model_width)
    starts = running_sum(lengths_rows) - lengths_rows
    picker = (own_places[None, None, :] == starts[:, :, None]).astype(jnp.bfloat16)
    local_firsts = jnp.einsum(
        "bdl,blc->bdc", picker, result_low, preferred_element_type=jnp.float32
    )
    firsts = lax.psum(local_firsts, "fsdp")
    firsts_low = firsts.astype(jnp.bfloat16).reshape(seq_count * doc_count, model_width)
    pooled = jnp.tanh(product(firsts_low, w_pool) + b_pool)
    pooled_low = pooled.astype(jnp.bfloat16)
    logits = product(pooled_low, w_class) + bias_class
    stored = (
        flat_rows,
        queries,
        all_keys,
        all_values,
        same_doc,
        log_totals,
        attended,
        pre_first,
        summed,
        normed_low,
        inner_pre,
        activated,
        picker,
        firsts_low,
        pooled,
        pooled_low,
        logits,
    )
    return (result_low, logits.reshape(seq_count, doc_count, CLASSES), stored)


def backward(stored, weights, cot_rows, label_rows):
    (
        w_query,
        b_query,
        w_key,
        w_value,
        b_value,
        w_out,
        b_out,
        first_gain,
        first_shift,
        w_inner,
        b_inner,
        w_outer,
        b_outer,
        second_gain,
        second_shift,
        w_pool,
        b_pool,
        w_class,
    ) = weights
    (
        flat_rows,
        queries,
        all_keys,
        all_values,
        same_doc,
        log_totals,
        attended,
        pre_first,
        summed,
        normed_low,
        inner_pre,
        activated,
        picker,
        firsts_low,
        pooled,
        pooled_low,
        logits,
    ) = stored
    seq_count, local_len, model_width = queries.shape
    doc_count = picker.shape[1]
    owner_flag = (lax.axis_index("fsdp") == 0).astype(jnp.float32)
    row_peak = jnp.max(logits, axis=-1, keepdims=True)
    class_exp = jnp.exp(logits - row_peak)
    class_probs = class_exp / jnp.sum(class_exp, axis=-1, keepdims=True)
    onehot_labels = (
        label_rows.reshape(-1)[:, None] == jnp.arange(CLASSES, dtype=jnp.int32)[None, :]
    ).astype(jnp.float32)
    grad_logits = (class_probs - onehot_labels).astype(jnp.bfloat16)
    grad_b_class = owner_flag * jnp.sum(grad_logits.astype(jnp.float32), axis=0)
    grad_w_class = owner_flag * contract_rows(pooled_low, grad_logits)
    grad_pool_pre = (times_transposed(grad_logits, w_class) * (1.0 - pooled * pooled)).astype(
        jnp.bfloat16
    )
    grad_b_pool = owner_flag * jnp.sum(grad_pool_pre.astype(jnp.float32), axis=0)
    grad_w_pool = owner_flag * contract_rows(firsts_low, grad_pool_pre)
    grad_firsts = times_transposed(grad_pool_pre, w_pool).reshape(seq_count, doc_count, model_width)
    from_pool = jnp.einsum(
        "bdl,bdc->blc", picker.astype(jnp.float32), grad_firsts, precision=lax.Precision.HIGHEST
    )
    grad_result = cot_rows.astype(jnp.float32).reshape(-1, model_width) + from_pool.reshape(
        -1, model_width
    )
    second_back = jax.vjp(
        layer_norm, summed, second_gain.astype(jnp.float32), second_shift.astype(jnp.float32)
    )[1]
    grad_summed, grad_second_gain, grad_second_shift = second_back(grad_result)
    grad_outer = grad_summed.astype(jnp.bfloat16)
    grad_b_outer = jnp.sum(grad_outer.astype(jnp.float32), axis=0)
    grad_w_outer = contract_rows(activated, grad_outer)
    gelu_back = jax.vjp(gelu_exact, inner_pre)[1]
    grad_inner = gelu_back(times_transposed(grad_outer, w_outer))[0].astype(jnp.bfloat16)
    grad_b_inner = jnp.sum(grad_inner.astype(jnp.float32), axis=0)
    grad_w_inner = contract_rows(normed_low, grad_inner)
    grad_normed = grad_summed + times_transposed(grad_inner, w_inner)
    first_back = jax.vjp(
        layer_norm, pre_first, first_gain.astype(jnp.float32), first_shift.astype(jnp.float32)
    )[1]
    grad_pre_first, grad_first_gain, grad_first_shift = first_back(grad_normed)
    grad_branch = grad_pre_first.astype(jnp.bfloat16)
    grad_b_out = jnp.sum(grad_branch.astype(jnp.float32), axis=0)
    grad_w_out = contract_rows(attended, grad_branch)
    grad_attended = (
        times_transposed(grad_branch, w_out)
        .astype(jnp.bfloat16)
        .reshape(seq_count, local_len, model_width)
    )
    pair_width = 2 * HEAD_DIM
    query_list = []
    key_list = []
    value_list = []
    for pair_index in range(model_width // pair_width):
        col_start = pair_index * pair_width
        query_pair = pair_heads(queries[:, :, col_start : col_start + pair_width])
        key_pair = pair_heads(all_keys[:, :, col_start : col_start + pair_width])
        value_pair = pair_heads(all_values[:, :, col_start : col_start + pair_width])
        grad_pair = pair_heads(grad_attended[:, :, col_start : col_start + pair_width])
        scores = pair_scores(query_pair, key_pair, same_doc)
        attn_probs = jnp.exp(scores - log_totals[pair_index])
        grad_probs = jnp.einsum(
            "bqhd,bkhd->bhqk", grad_pair, value_pair, preferred_element_type=jnp.float32
        )
        row_dot = jnp.sum(attn_probs * grad_probs, axis=-1, keepdims=True)
        grad_scores = (attn_probs * (grad_probs - row_dot)).astype(jnp.bfloat16)
        query_part = jnp.einsum(
            "bhqk,bkhd->bqhd", grad_scores, key_pair, preferred_element_type=jnp.float32
        ) * HEAD_DIM ** (-0.5)
        query_list.append(query_part.reshape(seq_count, local_len, pair_width))
        probs_low = attn_probs.astype(jnp.bfloat16)
        key_part = jnp.einsum(
            "bhqk,bqhd->bkhd", grad_scores, query_pair, preferred_element_type=jnp.float32
        ) * HEAD_DIM ** (-0.5)
        value_part = jnp.einsum(
            "bhqk,bqhd->bkhd", probs_low, grad_pair, preferred_element_type=jnp.float32
        )
        key_list.append(key_part.reshape(seq_count, key_part.shape[1], pair_width))
        value_list.append(value_part.reshape(seq_count, value_part.shape[1], pair_width))
    key_partials = jnp.concatenate(key_list, axis=2)
    value_partials = jnp.concatenate(value_list, axis=2)
    own_keys, own_values = (
        lax.psum_scatter(
            key_partials.astype(jnp.bfloat16), "fsdp", scatter_dimension=1, tiled=True
        ).astype(jnp.float32),
        lax.psum_scatter(
            value_partials.astype(jnp.bfloat16), "fsdp", scatter_dimension=1, tiled=True
        ).astype(jnp.float32),
    )
    query_grad = jnp.concatenate(query_list, axis=2).astype(jnp.bfloat16).reshape(-1, model_width)
    key_grad = own_keys.astype(jnp.bfloat16).reshape(-1, model_width)
    value_grad = own_values.astype(jnp.bfloat16).reshape(-1, model_width)
    grad_w_query = contract_rows(flat_rows, query_grad)
    grad_b_query = jnp.sum(query_grad.astype(jnp.float32), axis=0)
    grad_w_key = contract_rows(flat_rows, key_grad)
    grad_w_value = contract_rows(flat_rows, value_grad)
    grad_b_value = jnp.sum(value_grad.astype(jnp.float32), axis=0)
    grad_tokens = (
        grad_pre_first
        + times_transposed(query_grad, w_query)
        + times_transposed(key_grad, w_key)
        + times_transposed(value_grad, w_value)
    )
    new_grads = (
        grad_w_query,
        grad_b_query,
        grad_w_key,
        grad_w_value,
        grad_b_value,
        grad_w_out,
        grad_b_out,
        grad_first_gain,
        grad_first_shift,
        grad_w_inner,
        grad_b_inner,
        grad_w_outer,
        grad_b_outer,
        grad_second_gain,
        grad_second_shift,
        grad_w_pool,
        grad_b_pool,
        grad_w_class,
    )
    return (
        new_grads,
        grad_b_class,
        grad_tokens.astype(jnp.bfloat16).reshape(seq_count, local_len, model_width),
    )


def general_body(
    inputs,
    cotangent,
    doc_lengths,
    labels,
    w_query,
    b_query,
    w_key,
    w_value,
    b_value,
    w_out,
    b_out,
    first_gain,
    first_shift,
    w_inner,
    b_inner,
    w_outer,
    b_outer,
    second_gain,
    second_shift,
    w_pool,
    b_pool,
    w_class,
    b_class,
):
    masters = (
        w_query,
        b_query,
        w_key,
        w_value,
        b_value,
        w_out,
        b_out,
        first_gain,
        first_shift,
        w_inner,
        b_inner,
        w_outer,
        b_outer,
        second_gain,
        second_shift,
        w_pool,
        b_pool,
        w_class,
    )
    group_size = lax.axis_size("dp") * lax.axis_size("fsdp")
    grad_sums = [
        jnp.zeros((member.shape[0] * group_size,) + member.shape[1:], jnp.float32)
        for member in masters
    ]
    class_sum = jnp.zeros((CLASSES,), jnp.float32)
    micro_seqs = inputs.shape[0] // MICRO
    out_list = []
    logit_list = []
    grad_list = []
    for micro_step in range(MICRO):
        first_seq = micro_step * micro_seqs
        after_seq = first_seq + micro_seqs
        tokens = inputs[first_seq:after_seq]
        lengths_rows = doc_lengths[first_seq:after_seq]
        pieces = lowered_masters(masters)
        front_weights = (
            lax.all_gather(pieces[0], ("dp", "fsdp"), axis=0, tiled=True),
            lax.all_gather(pieces[1], ("dp", "fsdp"), axis=0, tiled=True),
            lax.all_gather(pieces[2], ("dp", "fsdp"), axis=0, tiled=True),
            lax.all_gather(pieces[3], ("dp", "fsdp"), axis=0, tiled=True),
            lax.all_gather(pieces[4], ("dp", "fsdp"), axis=0, tiled=True),
            lax.all_gather(pieces[5], ("dp", "fsdp"), axis=0, tiled=True),
            lax.all_gather(pieces[6], ("dp", "fsdp"), axis=0, tiled=True),
            lax.all_gather(pieces[7], ("dp", "fsdp"), axis=0, tiled=True),
            lax.all_gather(pieces[8], ("dp", "fsdp"), axis=0, tiled=True),
            lax.all_gather(pieces[9], ("dp", "fsdp"), axis=0, tiled=True),
            lax.all_gather(pieces[10], ("dp", "fsdp"), axis=0, tiled=True),
            lax.all_gather(pieces[11], ("dp", "fsdp"), axis=0, tiled=True),
            lax.all_gather(pieces[12], ("dp", "fsdp"), axis=0, tiled=True),
            lax.all_gather(pieces[13], ("dp", "fsdp"), axis=0, tiled=True),
            lax.all_gather(pieces[14], ("dp", "fsdp"), axis=0, tiled=True),
            lax.all_gather(pieces[15], ("dp", "fsdp"), axis=0, tiled=True),
            lax.all_gather(pieces[16], ("dp", "fsdp"), axis=0, tiled=True),
            lax.all_gather(pieces[17], ("dp", "fsdp"), axis=0, tiled=True),
        )
        result_low, logits, stored = forward(tokens, lengths_rows, front_weights, b_class)
        out_list.append(result_low)
        logit_list.append(logits)
        back_weights = (
            lax.all_gather(pieces[0], ("dp", "fsdp"), axis=0, tiled=True),
            lax.all_gather(pieces[1], ("dp", "fsdp"), axis=0, tiled=True),
            lax.all_gather(pieces[2], ("dp", "fsdp"), axis=0, tiled=True),
            lax.all_gather(pieces[3], ("dp", "fsdp"), axis=0, tiled=True),
            lax.all_gather(pieces[4], ("dp", "fsdp"), axis=0, tiled=True),
            lax.all_gather(pieces[5], ("dp", "fsdp"), axis=0, tiled=True),
            lax.all_gather(pieces[6], ("dp", "fsdp"), axis=0, tiled=True),
            lax.all_gather(pieces[7], ("dp", "fsdp"), axis=0, tiled=True),
            lax.all_gather(pieces[8], ("dp", "fsdp"), axis=0, tiled=True),
            lax.all_gather(pieces[9], ("dp", "fsdp"), axis=0, tiled=True),
            lax.all_gather(pieces[10], ("dp", "fsdp"), axis=0, tiled=True),
            lax.all_gather(pieces[11], ("dp", "fsdp"), axis=0, tiled=True),
            lax.all_gather(pieces[12], ("dp", "fsdp"), axis=0, tiled=True),
            lax.all_gather(pieces[13], ("dp", "fsdp"), axis=0, tiled=True),
            lax.all_gather(pieces[14], ("dp", "fsdp"), axis=0, tiled=True),
            lax.all_gather(pieces[15], ("dp", "fsdp"), axis=0, tiled=True),
            lax.all_gather(pieces[16], ("dp", "fsdp"), axis=0, tiled=True),
            lax.all_gather(pieces[17], ("dp", "fsdp"), axis=0, tiled=True),
        )
        stored = forward(tokens, lengths_rows, back_weights, b_class)[2]
        new_grads, class_grad, grad_tokens = backward(
            stored, back_weights, cotangent[first_seq:after_seq], labels[first_seq:after_seq]
        )
        grad_sums = [running + fresh_grad for running, fresh_grad in zip(grad_sums, new_grads)]
        class_sum = class_sum + class_grad
        grad_list.append(grad_tokens)
    owned = (
        lax.psum_scatter(grad_sums[0], ("dp", "fsdp"), scatter_dimension=0, tiled=True),
        lax.psum_scatter(grad_sums[1], ("dp", "fsdp"), scatter_dimension=0, tiled=True),
        lax.psum_scatter(grad_sums[2], ("dp", "fsdp"), scatter_dimension=0, tiled=True),
        lax.psum_scatter(grad_sums[3], ("dp", "fsdp"), scatter_dimension=0, tiled=True),
        lax.psum_scatter(grad_sums[4], ("dp", "fsdp"), scatter_dimension=0, tiled=True),
        lax.psum_scatter(grad_sums[5], ("dp", "fsdp"), scatter_dimension=0, tiled=True),
        lax.psum_scatter(grad_sums[6], ("dp", "fsdp"), scatter_dimension=0, tiled=True),
        lax.psum_scatter(grad_sums[7], ("dp", "fsdp"), scatter_dimension=0, tiled=True),
        lax.psum_scatter(grad_sums[8], ("dp", "fsdp"), scatter_dimension=0, tiled=True),
        lax.psum_scatter(grad_sums[9], ("dp", "fsdp"), scatter_dimension=0, tiled=True),
        lax.psum_scatter(grad_sums[10], ("dp", "fsdp"), scatter_dimension=0, tiled=True),
        lax.psum_scatter(grad_sums[11], ("dp", "fsdp"), scatter_dimension=0, tiled=True),
        lax.psum_scatter(grad_sums[12], ("dp", "fsdp"), scatter_dimension=0, tiled=True),
        lax.psum_scatter(grad_sums[13], ("dp", "fsdp"), scatter_dimension=0, tiled=True),
        lax.psum_scatter(grad_sums[14], ("dp", "fsdp"), scatter_dimension=0, tiled=True),
        lax.psum_scatter(grad_sums[15], ("dp", "fsdp"), scatter_dimension=0, tiled=True),
        lax.psum_scatter(grad_sums[16], ("dp", "fsdp"), scatter_dimension=0, tiled=True),
        lax.psum_scatter(grad_sums[17], ("dp", "fsdp"), scatter_dimension=0, tiled=True),
    )
    class_total = lax.psum(class_sum, ("dp", "fsdp"))
    return (
        jnp.concatenate(out_list, axis=0),
        jnp.concatenate(logit_list, axis=0),
        jnp.concatenate(grad_list, axis=0),
        owned[0],
        owned[1],
        owned[2],
        owned[3],
        owned[4],
        owned[5],
        owned[6],
        owned[7],
        owned[8],
        owned[9],
        owned[10],
        owned[11],
        owned[12],
        owned[13],
        owned[14],
        owned[15],
        owned[16],
        owned[17],
        class_total,
    )


BF = jnp.bfloat16
F32 = jnp.float32
MESH = pl.DeviceIdType.MESH
ANY = pl.BlockSpec(memory_space=pl.ANY)
SMEM = pl.BlockSpec(memory_space=pltpu.SMEM)
ZS = 4
CLASS_ROWS, B_QUERY, B_VALUE, B_OUT, GAIN1, SHIFT1, B_OUTER, GAIN2, SHIFT2, B_POOL = (0, 3, 4, 5, 6, 7, 8, 9, 10, 11)
VEC_ROWS = 16


def nn(a, b):
    return lax.dot_general(a, b, (((1,), (0,)), ((), ())), preferred_element_type=F32)


def nt(a, b):
    return lax.dot_general(a, b, (((1,), (1,)), ((), ())), preferred_element_type=F32)


def tn(a, b):
    return lax.dot_general(a, b, (((0,), (0,)), ((), ())), preferred_element_type=F32)


def my_place():
    dp, fs = lax.axis_index("dp"), lax.axis_index("fsdp")
    return dp // 2, lax.rem(dp, 2), fs // 2, lax.rem(fs, 2)


def device_at(z, y, x, c):
    return (z * 2 + y, x * 2 + c)


def meet(partners):
    barrier = pltpu.get_barrier_semaphore()
    for partner in partners:
        pl.semaphore_signal(barrier, inc=1, device_id=partner, device_id_type=MESH)
    pl.semaphore_wait(barrier, len(partners))


def all_partners(z, y, x, c):
    found = [device_at(lax.rem(z + k, ZS), y, x, c) for k in range(1, ZS)]
    found.append(device_at(z, 1 - y, x, c))
    found.append(device_at(z, y, 1 - x, c))
    found.append(device_at(z, y, x, 1 - c))
    found.append(device_at(z, y, 1 - x, 1 - c))
    return found


def group_partner(k, x, c):
    return (1 - x if k >= 2 else x, 1 - c if k % 2 == 1 else c)


def gather_kernel(orders, *refs):
    count = len(orders)
    rows_ref, shards = refs[0], refs[1 : 1 + count]
    seq_ref, wholes = refs[1 + count], refs[2 + count : 2 + 2 * count]
    local_sem, row_send, row_recv, send_sem, recv_sem = refs[2 + 2 * count :]
    z, y, x, c = my_place()
    meet(all_partners(z, y, x, c))
    mine = x * 2 + c
    sent = []
    got_rows = []
    for k in range(1, 4):
        px, pc = group_partner(k, x, c)
        copy = pltpu.make_async_remote_copy(
            src_ref=rows_ref.at[px * 2 + pc],
            dst_ref=seq_ref.at[mine],
            send_sem=row_send.at[k - 1],
            recv_sem=row_recv.at[k - 1],
            device_id=device_at(z, y, px, pc),
            device_id_type=MESH,
        )
        copy.start()
        sent.append(copy)
        got_rows.append(copy)
    own = pltpu.make_async_copy(rows_ref.at[mine], seq_ref.at[mine], local_sem.at[count])
    own.start()
    local = [own]

    def place(rel):
        dz, fy, fx, fc = rel
        zz = lax.rem(z + dz, ZS)
        yy = 1 - y if fy else y
        xx = 1 - x if fx else x
        cc = 1 - c if fc else c
        return ((zz * 2 + yy) * 2 + xx) * 2 + cc

    def slot(rel):
        dz, fy, fx, fc = rel
        return ((dz * 2 + fy) * 2 + fx) * 2 + fc

    def send(a, rel, there, device, number):
        source = shards[a] if slot(rel) == 0 else wholes[a].at[place(rel)]
        copy = pltpu.make_async_remote_copy(
            src_ref=source,
            dst_ref=wholes[a].at[place(rel)],
            send_sem=send_sem.at[a, number],
            recv_sem=recv_sem.at[a, slot(there)],
            device_id=device,
            device_id_type=MESH,
        )
        copy.start()
        sent.append(copy)

    def arrive(a, rel):
        block = wholes[a].at[place(rel)]
        pltpu.make_async_remote_copy(
            src_ref=block,
            dst_ref=block,
            send_sem=send_sem.at[a, 0],
            recv_sem=recv_sem.at[a, slot(rel)],
            device_id=device_at(z, y, x, 1 - c),
            device_id_type=MESH,
        ).wait_recv()

    numbers = [0] * count

    def forward_to(a, rel, axis):
        numbers[a] += 1
        dz, fy, fx, fc = rel
        if axis == "y":
            send(a, rel, (dz, 1 - fy, fx, fc), device_at(z, 1 - y, x, c), numbers[a] - 1)
        elif axis == "x":
            send(a, rel, (dz, fy, 1 - fx, fc), device_at(z, y, 1 - x, c), numbers[a] - 1)
        else:
            send(a, rel, (dz, fy, fx, 1 - fc), device_at(z, y, x, 1 - c), numbers[a] - 1)

    for a in range(count):
        keep = pltpu.make_async_copy(
            shards[a], wholes[a].at[place((0, 0, 0, 0))], local_sem.at[a]
        )
        keep.start()
        local.append(keep)
        for k in (2, 1, 3):
            numbers[a] += 1
            send(
                a, (0, 0, 0, 0), ((ZS - k) % ZS, 0, 0, 0),
                device_at(lax.rem(z + k, ZS), y, x, c), numbers[a] - 1,
            )
        for axis in (*orders[a], "c"):
            forward_to(a, (0, 0, 0, 0), axis)
    for a in range(count):
        for dz in (1, 3, 2):
            arrive(a, (dz, 0, 0, 0))
            for axis in (*orders[a], "c"):
                forward_to(a, (dz, 0, 0, 0), axis)
    for a in range(count):
        first, second = orders[a]
        for dz in (0, 1, 3, 2):
            rel = (dz, int(first == "y"), int(first == "x"), 0)
            arrive(a, rel)
            forward_to(a, rel, second)
            forward_to(a, rel, "c")
    for a in range(count):
        first, second = orders[a]
        for dz in (0, 1, 3, 2):
            for turn in (0, 1):
                fy = 1 if second == "y" else turn
                fx = 1 if second == "x" else turn
                arrive(a, (dz, fy, fx, 0))
                forward_to(a, (dz, fy, fx, 0), "c")
    for a in range(count):
        for dz in range(ZS):
            for fy in (0, 1):
                for fx in (0, 1):
                    arrive(a, (dz, fy, fx, 1))
    for copy in got_rows:
        copy.wait_recv()
    for copy in sent:
        copy.wait_send()
    for copy in local:
        copy.wait()


def gather_all(rows, shards, orders, collective_id):
    count = len(shards)
    whole = 8 * ZS
    return pl.pallas_call(
        functools.partial(gather_kernel, orders),
        out_shape=[jax.ShapeDtypeStruct(rows.shape, rows.dtype)]
        + [jax.ShapeDtypeStruct((whole,) + s.shape, s.dtype) for s in shards],
        in_specs=[ANY] * (1 + count),
        out_specs=[ANY] * (1 + count),
        scratch_shapes=[
            pltpu.SemaphoreType.DMA((count + 1,)),
            pltpu.SemaphoreType.DMA((3,)),
            pltpu.SemaphoreType.DMA((3,)),
            pltpu.SemaphoreType.DMA((count, whole)),
            pltpu.SemaphoreType.DMA((count, whole)),
        ],
        compiler_params=pltpu.CompilerParams(collective_id=collective_id, has_side_effects=True),
        name="gather_weights",
    )(rows, *shards)


def scatter_kernel(orders, *refs):
    count = len(orders)
    rows_ref, logit_ref, parts = refs[0], refs[1], refs[2 : 2 + count]
    back_ref, logits_ref, outs = refs[2 + count], refs[3 + count], refs[4 + count : 4 + 2 * count]
    rest = refs[4 + 2 * count :]
    local_sem, row_send, row_recv, send_sem, recv_sem = rest[:5]
    keeps, firsts, seconds, thirds, fourths = (
        rest[5 + i * count : 5 + (i + 1) * count] for i in range(5)
    )
    z, y, x, c = my_place()
    mine = x * 2 + c
    local = []
    sent = []

    def half(a, ref, at_first):
        return ref.at[:, at_first] if orders[a][0] == "y" else ref.at[:, :, at_first]

    own_loads = []
    for a in range(count):
        at = y if orders[a][0] == "y" else x
        loads = []
        for turn in (0, 1):
            place = 1 - at if turn == 0 else at
            if orders[a][0] == "y":
                source = parts[a].at[:, place, :, c]
            else:
                source = parts[a].at[:, :, place, c]
            copy = pltpu.make_async_copy(source, half(a, keeps[a], place), local_sem.at[a, turn])
            copy.start()
            loads.append(copy)
        own_loads.append(loads)
    meet(all_partners(z, y, x, c))

    def push(source, target, a, number, device):
        copy = pltpu.make_async_remote_copy(
            src_ref=source,
            dst_ref=target,
            send_sem=send_sem.at[a, number],
            recv_sem=recv_sem.at[a, number],
            device_id=device,
            device_id_type=MESH,
        )
        copy.start()
        sent.append(copy)
        return copy

    sibling = []
    for a in range(count):
        at = y if orders[a][0] == "y" else x
        copies = []
        for turn in (0, 1):
            place = 1 - at if turn == 0 else at
            if orders[a][0] == "y":
                source = parts[a].at[:, place, :, 1 - c]
            else:
                source = parts[a].at[:, :, place, 1 - c]
            copies.append(
                push(source, half(a, firsts[a], place), a, turn, device_at(z, y, x, 1 - c))
            )
        sibling.append(copies)
    got_rows = []
    for k in range(1, 4):
        px, pc = group_partner(k, x, c)
        for which, (source, target) in enumerate(
            ((rows_ref.at[px * 2 + pc], back_ref.at[mine]), (logit_ref, logits_ref.at[mine]))
        ):
            copy = pltpu.make_async_remote_copy(
                src_ref=source,
                dst_ref=target,
                send_sem=row_send.at[which, k - 1],
                recv_sem=row_recv.at[which, k - 1],
                device_id=device_at(z, y, px, pc),
                device_id_type=MESH,
            )
            copy.start()
            sent.append(copy)
            got_rows.append(copy)
    for which, (source, target) in enumerate(
        ((rows_ref.at[mine], back_ref.at[mine]), (logit_ref, logits_ref.at[mine]))
    ):
        copy = pltpu.make_async_copy(source, target, local_sem.at[count, which])
        copy.start()
        local.append(copy)

    def add_into(target, source):
        total = functools.reduce(lambda p, q: p * q, target.shape[:-2], 1)
        lead = target.shape[:-2]

        def step(i, carry):
            where = []
            for size in reversed(lead):
                where.append(lax.rem(i, size))
                i = i // size
            where = tuple(reversed(where))
            target[where] = (target[where].astype(F32) + source[where].astype(F32)).astype(target.dtype)
            return carry

        lax.fori_loop(0, total, step, 0)

    waits2 = []
    for a in range(count):
        first = orders[a][0]
        at = y if first == "y" else x
        own_loads[a][0].wait()
        sibling[a][0].wait_recv()
        add_into(half(a, keeps[a], 1 - at), half(a, firsts[a], 1 - at))
        device = device_at(z, 1 - y, x, c) if first == "y" else device_at(z, y, 1 - x, c)
        waits2.append(push(half(a, keeps[a], 1 - at), seconds[a], a, 2, device))
    for a in range(count):
        at = y if orders[a][0] == "y" else x
        own_loads[a][1].wait()
        sibling[a][1].wait_recv()
        add_into(half(a, keeps[a], at), half(a, firsts[a], at))
    waits3 = []
    for a in range(count):
        first = orders[a][0]
        at, other = (y, x) if first == "y" else (x, y)
        kept = half(a, keeps[a], at)
        waits2[a].wait_recv()
        add_into(kept.at[:, 1 - other], seconds[a].at[:, 1 - other])
        device = device_at(z, y, 1 - x, c) if first == "y" else device_at(z, 1 - y, x, c)
        waits3.append(push(kept.at[:, 1 - other], thirds[a], a, 3, device))
        add_into(kept.at[:, other], seconds[a].at[:, other])
    waits4 = []
    for a in range(count):
        first = orders[a][0]
        at, other = (y, x) if first == "y" else (x, y)
        kept = half(a, keeps[a], at).at[:, other]
        waits3[a].wait_recv()
        add_into(kept, thirds[a])
        copies = []
        for k in (2, 1, 3):
            there = lax.rem(z + k, ZS)
            copies.append(
                push(kept.at[there], fourths[a].at[k - 1], a, 3 + k, device_at(there, y, x, c))
            )
        waits4.append(copies)
    for a in range(count):
        first = orders[a][0]
        at, other = (y, x) if first == "y" else (x, y)
        kept = half(a, keeps[a], at).at[:, other]
        for copy in waits4[a]:
            copy.wait_recv()
        outs[a][...] = (
            kept[z].astype(F32)
            + fourths[a][0].astype(F32)
            + fourths[a][1].astype(F32)
            + fourths[a][2].astype(F32)
        )
    for copy in got_rows:
        copy.wait_recv()
    for copy in sent:
        copy.wait_send()
    for copy in local:
        copy.wait()


def scatter_all(rows, logit_block, parts, orders, collective_id):
    count = len(parts)
    blocks = [part.shape[1:] for part in parts]
    kinds = [part.dtype for part in parts]
    split = [part.reshape((ZS, 2, 2, 2) + block) for part, block in zip(parts, blocks)]
    scratch = []
    for lead in ((ZS, 2, 2), (ZS, 2, 2), (ZS, 2), (ZS,), (ZS - 1,)):
        scratch += [pltpu.VMEM(lead + block, kind) for block, kind in zip(blocks, kinds)]
    return pl.pallas_call(
        functools.partial(scatter_kernel, orders),
        out_shape=[
            jax.ShapeDtypeStruct(rows.shape, rows.dtype),
            jax.ShapeDtypeStruct((4,) + logit_block.shape, logit_block.dtype),
        ]
        + [jax.ShapeDtypeStruct(block, F32) for block in blocks],
        in_specs=[ANY] * (2 + count),
        out_specs=[ANY] * 2 + [pl.BlockSpec(memory_space=pltpu.VMEM)] * count,
        scratch_shapes=[
            pltpu.SemaphoreType.DMA((count + 1, 2)),
            pltpu.SemaphoreType.DMA((2, 3)),
            pltpu.SemaphoreType.DMA((2, 3)),
            pltpu.SemaphoreType.DMA((count, 7)),
            pltpu.SemaphoreType.DMA((count, 7)),
        ]
        + scratch,
        compiler_params=pltpu.CompilerParams(
            collective_id=collective_id, has_side_effects=True, vmem_limit_bytes=48 * 2**20
        ),
        name="scatter_gradients",
    )(rows, logit_block, *split)


def doc_ends(lens_ref):
    ends = []
    total = 0
    for d in range(lens_ref.shape[0]):
        total = total + lens_ref[d]
        ends.append(total)
    return ends


def doc_numbers(places, ends):
    number = jnp.zeros(places.shape, jnp.int32)
    for end in ends:
        number = number + (places >= end).astype(jnp.int32)
    return number


def attend_kernel(
    lens_ref, x_ref, wq_ref, wk_ref, wv_ref, vec_ref, q_ref, k_ref, v_ref, att_ref, lse_ref, vt_ref
):
    x = x_ref[...]
    length, width = q_ref.shape
    chunk = 256
    heads = width // HEAD_DIM
    queries = (nn(x, wq_ref[...]) + vec_ref[B_QUERY : B_QUERY + 1, :]).astype(BF)
    q_ref[...] = queries
    k_ref[...] = nn(x, wk_ref[...]).astype(BF)
    values = (nn(x, wv_ref[...]) + vec_ref[B_VALUE : B_VALUE + 1, :]).astype(BF)
    v_ref[...] = values
    vt_ref[...] = values.astype(F32).T.astype(BF)
    ends = doc_ends(lens_ref)
    key_doc = doc_numbers(lax.broadcasted_iota(jnp.int32, (length, 1), 0), ends)
    lane_head = lax.broadcasted_iota(jnp.int32, (1, width), 1) // HEAD_DIM

    def step(i, carry):
        at = pl.multiple_of(i * chunk, chunk)
        query_doc = doc_numbers(lax.broadcasted_iota(jnp.int32, (1, chunk), 1) + at, ends)
        scaled = q_ref[pl.ds(at, chunk), :] * jnp.asarray(0.125, BF)
        mixed = []
        for h in range(heads):
            own = jnp.where(lane_head == h, scaled, jnp.zeros_like(scaled))
            blocks = []
            for s in range(0, length, chunk):
                scores = nt(k_ref[s : s + chunk, :], own)
                blocks.append(jnp.where(key_doc[s : s + chunk] == query_doc, scores, -1000000000.0))
            peak = functools.reduce(jnp.maximum, [jnp.max(b, axis=0, keepdims=True) for b in blocks])
            exps = [jnp.exp(b - peak) for b in blocks]
            total = functools.reduce(jnp.add, [jnp.sum(e, axis=0, keepdims=True) for e in exps])
            scale = 1.0 / total
            probs = jnp.concatenate([(e * scale).astype(BF) for e in exps], axis=0)
            mixed.append(nn(vt_ref[h * HEAD_DIM : (h + 1) * HEAD_DIM, :], probs))
            lse_ref[0, h : h + 1, pl.ds(at, chunk)] = peak + jnp.log(total)
        att_ref[pl.ds(at, chunk), :] = jnp.concatenate(mixed, axis=0).T.astype(BF)
        return carry

    lax.fori_loop(0, length // chunk, step, 0)


def attend(lens, rows, w_qkv, vectors):
    length, width = rows.shape
    group = 256
    groups = width // group
    whole = pl.BlockSpec((length, width), lambda g: (0, 0))
    part = pl.BlockSpec((length, group), lambda g: (0, g))
    return pl.pallas_call(
        attend_kernel,
        grid=(groups,),
        out_shape=[jax.ShapeDtypeStruct((length, width), BF)] * 4
        + [jax.ShapeDtypeStruct((groups, 8, length), F32)],
        in_specs=[
            SMEM,
            whole,
            pl.BlockSpec((width, group), lambda g: (0, g)),
            pl.BlockSpec((width, group), lambda g: (0, g + groups)),
            pl.BlockSpec((width, group), lambda g: (0, g + 2 * groups)),
            pl.BlockSpec((VEC_ROWS, group), lambda g: (0, g)),
        ],
        out_specs=[part] * 4 + [pl.BlockSpec((1, 8, length), lambda g: (g, 0, 0))],
        scratch_shapes=[pltpu.VMEM((group, length), BF)],
        compiler_params=pltpu.CompilerParams(vmem_limit_bytes=48 * 2**20),
        cost_estimate=pl.CostEstimate(flops=10 * 10**9, bytes_accessed=16 * 10**6, transcendentals=12 * 2**20),
        name="attend",
    )(lens, rows, w_qkv, w_qkv, w_qkv, vectors)


def attend_back_kernel(
    lens_ref, x_ref, wq_ref, wk_ref, wv_ref, q_ref, k_ref, v_ref, att_ref, datt_ref, lse_ref, start_ref,
    dwq_ref, dwk_ref, dwv_ref, bias_ref, dx_ref, xt_ref, kt_ref, dot_ref, dq_ref, dk_ref, dv_ref, acc_ref,
):
    length, width = q_ref.shape
    chunk = 256
    heads = width // HEAD_DIM
    group = pl.program_id(0)

    @pl.when(group == 0)
    def _():
        xt_ref[...] = x_ref[...].astype(F32).T.astype(BF)
        acc_ref[...] = start_ref[...]

    kt_ref[...] = k_ref[...].astype(F32).T.astype(BF)
    dot_ref[...] = (datt_ref[...].astype(F32) * att_ref[...].astype(F32)).T
    dk_ref[...] = jnp.zeros_like(dk_ref)
    dv_ref[...] = jnp.zeros_like(dv_ref)
    ends = doc_ends(lens_ref)
    key_doc = doc_numbers(lax.broadcasted_iota(jnp.int32, (length, 1), 0), ends)
    lane_head = lax.broadcasted_iota(jnp.int32, (1, width), 1) // HEAD_DIM

    def step(i, carry):
        at = pl.multiple_of(i * chunk, chunk)
        query_doc = doc_numbers(lax.broadcasted_iota(jnp.int32, (1, chunk), 1) + at, ends)
        scaled = q_ref[pl.ds(at, chunk), :] * jnp.asarray(0.125, BF)
        given = datt_ref[pl.ds(at, chunk), :]
        own_q = [jnp.where(lane_head == h, scaled, jnp.zeros_like(scaled)) for h in range(heads)]
        own_d = [jnp.where(lane_head == h, given, jnp.zeros_like(given)) for h in range(heads)]
        all_probs = [[] for _ in range(length // chunk)]
        all_grads = [[] for _ in range(length // chunk)]
        for h in range(heads):
            lse = lse_ref[0, h : h + 1, pl.ds(at, chunk)]
            dots = jnp.sum(
                dot_ref[h * HEAD_DIM : (h + 1) * HEAD_DIM, pl.ds(at, chunk)], axis=0, keepdims=True
            )
            for j in range(length // chunk):
                s = j * chunk
                scores = nt(k_ref[s : s + chunk, :], own_q[h])
                scores = jnp.where(key_doc[s : s + chunk] == query_doc, scores, -1000000000.0)
                probs = jnp.exp(scores - lse)
                grad_probs = nt(v_ref[s : s + chunk, :], own_d[h])
                all_grads[j].append((probs * (grad_probs - dots)).astype(BF))
                all_probs[j].append(probs.astype(BF))
        stacked_q = jnp.concatenate(own_q, axis=0)
        stacked_d = jnp.concatenate(own_d, axis=0)
        for j in range(length // chunk):
            s = j * chunk
            dk_ref[s : s + chunk, :] += nn(jnp.concatenate(all_grads[j], axis=1), stacked_q)
            dv_ref[s : s + chunk, :] += nn(jnp.concatenate(all_probs[j], axis=1), stacked_d)
        mixed = []
        for h in range(heads):
            column = jnp.concatenate([all_grads[j][h] for j in range(length // chunk)], axis=0)
            mixed.append(nn(kt_ref[h * HEAD_DIM : (h + 1) * HEAD_DIM, :], column))
        dq_ref[pl.ds(at, chunk), :] = (jnp.concatenate(mixed, axis=0).T * 0.125).astype(BF)
        return carry

    lax.fori_loop(0, length // chunk, step, 0)
    grad_q = dq_ref[...]
    grad_k = dk_ref[...].astype(BF)
    grad_v = dv_ref[...].astype(BF)
    xt = xt_ref[...]
    dwq_ref[...] = nn(xt, grad_q).astype(BF)
    dwk_ref[...] = nn(xt, grad_k).astype(BF)
    dwv_ref[...] = nn(xt, grad_v).astype(BF)
    bias_ref[0:1, :] = jnp.sum(grad_q.astype(F32), axis=0, keepdims=True)
    bias_ref[1:2, :] = jnp.sum(grad_v.astype(F32), axis=0, keepdims=True)
    acc_ref[...] += nt(grad_q, wq_ref[...]) + nt(grad_k, wk_ref[...]) + nt(grad_v, wv_ref[...])

    @pl.when(group == pl.num_programs(0) - 1)
    def _():
        dx_ref[...] = acc_ref[...].astype(BF)


def attend_back(lens, rows, w_qkv, q, k, v, att, datt, lse, grad_pre):
    length, width = rows.shape
    group = 256
    groups = width // group
    whole = pl.BlockSpec((length, width), lambda g: (0, 0))
    part = pl.BlockSpec((length, group), lambda g: (0, g))
    return pl.pallas_call(
        attend_back_kernel,
        grid=(groups,),
        out_shape=[jax.ShapeDtypeStruct((width, width), BF)] * 3
        + [jax.ShapeDtypeStruct((8, width), F32), jax.ShapeDtypeStruct((length, width), BF)],
        in_specs=[
            SMEM,
            whole,
            pl.BlockSpec((width, group), lambda g: (0, g)),
            pl.BlockSpec((width, group), lambda g: (0, g + groups)),
            pl.BlockSpec((width, group), lambda g: (0, g + 2 * groups)),
            part, part, part, part, part,
            pl.BlockSpec((1, 8, length), lambda g: (g, 0, 0)),
            whole,
        ],
        out_specs=[pl.BlockSpec((width, group), lambda g: (0, g))] * 3
        + [pl.BlockSpec((8, group), lambda g: (0, g)), whole],
        scratch_shapes=[
            pltpu.VMEM((width, length), BF),
            pltpu.VMEM((group, length), BF),
            pltpu.VMEM((group, length), F32),
            pltpu.VMEM((length, group), BF),
            pltpu.VMEM((length, group), F32),
            pltpu.VMEM((length, group), F32),
            pltpu.VMEM((length, width), F32),
        ],
        compiler_params=pltpu.CompilerParams(vmem_limit_bytes=56 * 2**20),
        cost_estimate=pl.CostEstimate(flops=20 * 10**9, bytes_accessed=24 * 10**6, transcendentals=12 * 2**20),
        name="attend_back",
    )(lens, rows, w_qkv, w_qkv, w_qkv, q, k, v, att, datt, lse, grad_pre)


def normal_parts(v):
    bell = jnp.exp(v * v * -0.5)
    t = 1.0 / (1.0 + jnp.abs(v) * 0.23164189)
    tail = t * (0.127414796 + t * (-0.142248368 + t * (0.710706870 + t * (-0.726576013 + t * 0.530702714)))) * bell
    return jnp.where(v >= 0.0, 1.0 - tail, tail), bell


def centered_parts(values):
    average = jnp.mean(values, axis=-1, keepdims=True)
    centered = values - average
    variance = jnp.mean(centered * centered, axis=-1, keepdims=True)
    inverse = lax.rsqrt(variance + 1e-06)
    return centered * inverse, inverse


def dense_kernel(
    lens_ref, labels_ref, x_ref, att_ref, w_inner_ref, w_out_ref, w_pool_ref, w_outer_ref, vec_ref, b_inner_ref, b_class_ref,
    pre_ref, summed_ref, low_ref, act_ref, dact_ref, lo_ref, dpool_ref, first_ref, small_ref, logits_ref, picked_ref,
):
    step = pl.program_id(0)
    rows = x_ref.shape[0]
    hidden = w_inner_ref.shape[1]
    chunk = 512

    def vec(row):
        return vec_ref[row : row + 1, :]

    pre = x_ref[...].astype(F32) + (nn(att_ref[...], w_out_ref[...]) + vec(B_OUT))
    pre_ref[...] = pre
    normed = centered_parts(pre)[0] * vec(GAIN1) + vec(SHIFT1)
    low = normed.astype(BF)
    low_ref[...] = low
    total = normed + vec(B_OUTER)
    for s in range(0, hidden, chunk):
        inner = nn(low, w_inner_ref[:, s : s + chunk]) + b_inner_ref[:, s : s + chunk]
        phi, bell = normal_parts(inner)
        activated = (inner * phi).astype(BF)
        act_ref[:, s : s + chunk] = activated
        dact_ref[:, s : s + chunk] = (phi + inner * bell * 0.3989422804014327).astype(BF)
        total = total + nn(activated, w_outer_ref[s : s + chunk, :])
    summed_ref[...] = total
    result = (centered_parts(total)[0] * vec(GAIN2) + vec(SHIFT2)).astype(BF)
    lo_ref[...] = result
    ends = doc_ends(lens_ref)
    docs = len(ends)
    places = lax.broadcasted_iota(jnp.int32, (VEC_ROWS, rows), 1) + step * rows
    row_doc = lax.broadcasted_iota(jnp.int32, (VEC_ROWS, rows), 0)
    hit = jnp.zeros((VEC_ROWS, rows), jnp.bool_)
    for d in range(docs):
        hit = hit | ((row_doc == d) & (places == ends[d] - lens_ref[d]))
    found = nn(jnp.where(hit, 1.0, 0.0).astype(BF), result)

    @pl.when(step == 0)
    def _():
        picked_ref[...] = found

    @pl.when(step > 0)
    def _():
        picked_ref[...] += found

    @pl.when(step == pl.num_programs(0) - 1)
    def _():
        picked = picked_ref[...].astype(BF)
        pooled = jnp.tanh(nn(picked, w_pool_ref[...]) + vec(B_POOL))
        pooled_low = pooled.astype(BF)
        table = vec_ref[...].astype(BF)
        logits = nt(pooled_low, table) + b_class_ref[...]
        column = lax.broadcasted_iota(jnp.int32, (VEC_ROWS, VEC_ROWS), 1)
        row = lax.broadcasted_iota(jnp.int32, (VEC_ROWS, VEC_ROWS), 0)
        logits_ref[...] = logits
        live = column < CLASSES
        shown = jnp.where(live, logits, -jnp.inf)
        exps = jnp.where(live, jnp.exp(shown - jnp.max(shown, axis=-1, keepdims=True)), 0.0)
        probs = exps / jnp.sum(exps, axis=-1, keepdims=True)
        label = jnp.zeros((VEC_ROWS, VEC_ROWS), jnp.int32)
        for d in range(docs):
            label = jnp.where(row == d, labels_ref[d], label)
        grad = jnp.where(live & (row < docs), probs - jnp.where(label == column, 1.0, 0.0), 0.0)
        grad_low = grad.astype(BF)
        grad_pool = (nn(grad_low, table) * (1.0 - pooled * pooled)).astype(BF)
        dpool_ref[...] = tn(picked, grad_pool).astype(BF)
        first_ref[...] = nt(grad_pool, w_pool_ref[...])
        small_ref[0:16, :] = tn(grad_low, pooled_low)
        small_ref[16:17, :] = jnp.sum(grad_pool.astype(F32), axis=0, keepdims=True)
        width = small_ref.shape[1]
        class_sum = jnp.sum(grad_low.astype(F32), axis=0, keepdims=True)
        small_ref[17:18, :] = jnp.concatenate(
            [class_sum, jnp.zeros((1, width - VEC_ROWS), F32)], axis=1
        )


def dense(lens, labels, rows, att, w_mid, w_outer, vectors, b_inner, b_class_row):
    length, width = rows.shape
    hidden = w_outer.shape[0]
    tile = 256
    steps = length // tile
    part = pl.BlockSpec((tile, width), lambda i: (i, 0))
    wide = pl.BlockSpec((tile, hidden), lambda i: (i, 0))

    def fixed(shape, column=0):
        return pl.BlockSpec(shape, lambda i: (0, column))

    spots = hidden // width
    return pl.pallas_call(
        dense_kernel,
        grid=(steps,),
        out_shape=[
            jax.ShapeDtypeStruct((length, width), F32),
            jax.ShapeDtypeStruct((length, width), F32),
            jax.ShapeDtypeStruct((length, width), BF),
            jax.ShapeDtypeStruct((length, hidden), BF),
            jax.ShapeDtypeStruct((length, hidden), BF),
            jax.ShapeDtypeStruct((length, width), BF),
            jax.ShapeDtypeStruct((width, width), BF),
            jax.ShapeDtypeStruct((VEC_ROWS, width), F32),
            jax.ShapeDtypeStruct((24, width), F32),
            jax.ShapeDtypeStruct((VEC_ROWS, VEC_ROWS), F32),
        ],
        in_specs=[
            SMEM, SMEM, part, part,
            fixed((width, hidden)), fixed((width, width), spots), fixed((width, width), spots + 1),
            fixed((hidden, width)), fixed((VEC_ROWS, width)), fixed((1, hidden)), fixed((1, VEC_ROWS)),
        ],
        out_specs=[
            part, part, part, wide, wide, part,
            fixed((width, width)), fixed((VEC_ROWS, width)), fixed((24, width)), fixed((VEC_ROWS, VEC_ROWS)),
        ],
        scratch_shapes=[pltpu.VMEM((VEC_ROWS, width), F32)],
        compiler_params=pltpu.CompilerParams(vmem_limit_bytes=60 * 2**20),
        cost_estimate=pl.CostEstimate(flops=11 * 10**9, bytes_accessed=40 * 10**6, transcendentals=3 * 2**20),
        name="dense",
    )(lens, labels, rows, att, w_mid, w_mid, w_mid, w_outer, vectors, b_inner, b_class_row)


def norm_back(grad, values, gain):
    hat, inverse = centered_parts(values)
    scaled = grad * gain
    mean_scaled = jnp.mean(scaled, axis=-1, keepdims=True)
    mean_cross = jnp.mean(scaled * hat, axis=-1, keepdims=True)
    back = (scaled - mean_scaled - hat * mean_cross) * inverse
    return back, jnp.sum(grad * hat, axis=0, keepdims=True), jnp.sum(grad, axis=0, keepdims=True)


def dense_back_kernel(
    lens_ref, cot_ref, summed_ref, pre_ref, dact_ref, w_inner_ref, w_out_ref, w_outer_ref, vec_ref, first_ref,
    outer_ref, inner_ref, branch_ref, datt_ref, gpre_ref, small_ref, bi_ref,
):
    step = pl.program_id(0)
    rows = cot_ref.shape[0]
    hidden = dact_ref.shape[1]
    chunk = 512

    def vec(row):
        return vec_ref[row : row + 1, :]

    @pl.when(step == 0)
    def _():
        small_ref[...] = jnp.zeros_like(small_ref)
        bi_ref[...] = jnp.zeros_like(bi_ref)

    grad = cot_ref[...].astype(F32)
    places = lax.broadcasted_iota(jnp.int32, (rows, 1), 0) + step * rows
    ends = doc_ends(lens_ref)
    placed = jnp.zeros(grad.shape, F32)
    for d in range(len(ends)):
        placed = jnp.where(places == ends[d] - lens_ref[d], first_ref[d : d + 1, :], placed)
    grad = grad + placed
    grad_summed, gain2, shift2 = norm_back(grad, summed_ref[...], vec(GAIN2))
    outer = grad_summed.astype(BF)
    outer_ref[...] = outer
    grad_normed = grad_summed
    for s in range(0, hidden, chunk):
        back = nt(outer, w_outer_ref[s : s + chunk, :])
        inner = (back * dact_ref[:, s : s + chunk].astype(F32)).astype(BF)
        inner_ref[:, s : s + chunk] = inner
        bi_ref[:, s : s + chunk] += jnp.sum(inner.astype(F32), axis=0, keepdims=True)
        grad_normed = grad_normed + nt(inner, w_inner_ref[:, s : s + chunk])
    grad_pre, gain1, shift1 = norm_back(grad_normed, pre_ref[...], vec(GAIN1))
    gpre_ref[...] = grad_pre
    branch = grad_pre.astype(BF)
    branch_ref[...] = branch
    datt_ref[...] = nt(branch, w_out_ref[...]).astype(BF)
    small_ref[0:1, :] += jnp.sum(outer.astype(F32), axis=0, keepdims=True)
    small_ref[1:2, :] += gain2
    small_ref[2:3, :] += shift2
    small_ref[3:4, :] += jnp.sum(branch.astype(F32), axis=0, keepdims=True)
    small_ref[4:5, :] += gain1
    small_ref[5:6, :] += shift1


def dense_back(lens, cot, summed, pre, dact, w_mid, w_outer, vectors, first):
    length, width = cot.shape
    hidden = w_outer.shape[0]
    tile = 256
    part = pl.BlockSpec((tile, width), lambda i: (i, 0))
    wide = pl.BlockSpec((tile, hidden), lambda i: (i, 0))

    def fixed(shape, column=0):
        return pl.BlockSpec(shape, lambda i: (0, column))

    spots = hidden // width
    return pl.pallas_call(
        dense_back_kernel,
        grid=(length // tile,),
        out_shape=[
            jax.ShapeDtypeStruct((length, width), BF),
            jax.ShapeDtypeStruct((length, hidden), BF),
            jax.ShapeDtypeStruct((length, width), BF),
            jax.ShapeDtypeStruct((length, width), BF),
            jax.ShapeDtypeStruct((length, width), F32),
            jax.ShapeDtypeStruct((8, width), F32),
            jax.ShapeDtypeStruct((1, hidden), F32),
        ],
        in_specs=[
            SMEM, part, part, part, wide,
            fixed((width, hidden)), fixed((width, width), spots), fixed((hidden, width)),
            fixed((VEC_ROWS, width)), fixed((VEC_ROWS, width)),
        ],
        out_specs=[part, wide, part, part, part, fixed((8, width)), fixed((1, hidden))],
        compiler_params=pltpu.CompilerParams(vmem_limit_bytes=60 * 2**20),
        cost_estimate=pl.CostEstimate(flops=11 * 10**9, bytes_accessed=40 * 10**6, transcendentals=0),
        name="dense_back",
    )(lens, cot, summed, pre, dact, w_mid, w_mid, w_outer, vectors, first)


def exchange(blocks):
    count = blocks.shape[0]
    mine = lax.axis_index("fsdp")
    held = jnp.zeros_like(blocks)
    own = lax.dynamic_index_in_dim(blocks, mine, 0, keepdims=True)
    held = lax.dynamic_update_slice_in_dim(held, own, mine, 0)
    for k in range(1, count):
        leaving = lax.dynamic_index_in_dim(blocks, lax.rem(mine + k, count), 0, keepdims=True)
        came = lax.ppermute(leaving, "fsdp", [(i, (i + k) % count) for i in range(count)])
        held = lax.dynamic_update_slice_in_dim(held, came, lax.rem(mine - k + count, count), 0)
    return held


def fast_body(
    inputs, cotangent, doc_lengths, labels, w_query, b_query, w_key, w_value, b_value, w_out, b_out, first_gain, first_shift,
    w_inner, b_inner, w_outer, b_outer, second_gain, second_shift, w_pool, b_pool, w_class, b_class,
):
    seqs, local_len, width = inputs.shape
    length = seqs * local_len
    devices = 8 * ZS
    mine = lax.axis_index("fsdp")
    docs = doc_lengths.shape[1]
    own_lens = lax.dynamic_index_in_dim(doc_lengths, mine, 0, keepdims=False)
    own_labels = lax.dynamic_index_in_dim(labels, mine, 0, keepdims=False)

    share = width // devices
    hidden_share = b_inner.shape[0]
    hidden = hidden_share * devices
    qkv_shard = jnp.concatenate([w_query, w_key, w_value], axis=1).astype(BF)
    mid_shard = jnp.concatenate([w_inner, w_out, w_pool], axis=1).astype(BF)
    outer_shard = w_outer.astype(BF)
    vec_shard = jnp.concatenate(
        [
            w_class.T.reshape(-1), b_query, b_value, b_out, first_gain, first_shift, b_outer, second_gain, second_shift,
            b_pool, b_inner,
        ]
    )
    vec_len = vec_shard.shape[0]
    vec_shard = jnp.pad(vec_shard, (0, 1024 - vec_len)).reshape(8, 128).astype(BF).astype(F32)

    rows, w_qkv, vec_all, w_mid, w_outer_all = gather_all(
        inputs, [qkv_shard, vec_shard, mid_shard, outer_shard], ["xy", "xy", "xy", "yx"], 1
    )
    rows = rows.reshape(length, width)
    w_qkv = w_qkv.reshape(width, 3 * width)
    w_mid = w_mid.reshape(width, hidden + 2 * width)
    w_outer_all = w_outer_all.reshape(hidden, width)
    flat_vec = vec_all.reshape(devices, 1024)
    rows_used = B_POOL + 1
    vectors = flat_vec[:, : rows_used * share].reshape(devices, rows_used, share).transpose(1, 0, 2).reshape(rows_used, width)
    vectors = jnp.pad(vectors, ((0, VEC_ROWS - rows_used), (0, 0)))
    b_inner_row = flat_vec[:, rows_used * share : vec_len].reshape(1, hidden)
    b_class_row = jnp.pad(b_class, (0, VEC_ROWS - CLASSES)).reshape(1, VEC_ROWS)

    cot = exchange(cotangent).reshape(length, width)
    q, k, v, att, lse = attend(own_lens, rows, w_qkv, vectors)
    pre, summed, low, act, dact, result, grad_pool, first, small_a, logits = dense(
        own_lens, own_labels, rows, att, w_mid, w_outer_all, vectors, b_inner_row, b_class_row
    )
    layer_out = exchange(result.reshape(seqs, local_len, width))
    outer, inner, branch, datt, grad_pre, small_b, grad_b_inner = dense_back(
        own_lens, cot, summed, pre, dact, w_mid, w_outer_all, vectors, first
    )
    grad_outer_w = tn(act, outer).astype(BF)
    grad_inner_w = tn(low, inner).astype(BF)
    grad_out_w = tn(att, branch).astype(BF)
    gwq, gwk, gwv, small_c, grad_rows = attend_back(own_lens, rows, w_qkv, q, k, v, att, datt, lse, grad_pre)

    grad_vec = jnp.concatenate(
        [
            small_a[0:CLASSES], small_c[0:2], small_b[3:4], small_b[4:6], small_b[0:1], small_b[1:3], small_a[16:17],
        ],
        axis=0,
    )
    grad_vec = grad_vec.reshape(rows_used, devices, share).transpose(1, 0, 2).reshape(devices, rows_used * share)
    grad_vec = jnp.concatenate(
        [
            grad_vec,
            grad_b_inner.reshape(devices, hidden_share),
            jnp.broadcast_to(small_a[17:18, :CLASSES], (devices, CLASSES)),
        ],
        axis=1,
    )
    grad_vec = jnp.pad(grad_vec, ((0, 0), (0, 1024 - grad_vec.shape[1]))).reshape(devices, 8, 128)
    logit_block = jnp.pad(logits[:docs, :CLASSES], ((0, 8 - docs), (0, 128 - CLASSES)))
    scattered = scatter_all(
        grad_rows.reshape(seqs, local_len, width),
        logit_block,
        [
            grad_inner_w.reshape(devices, share, hidden),
            grad_outer_w.reshape(devices, hidden_share, width),
            grad_out_w.reshape(devices, share, width),
            grad_pool.reshape(devices, share, width),
            gwq.reshape(devices, share, width),
            gwk.reshape(devices, share, width),
            gwv.reshape(devices, share, width),
            grad_vec,
        ],
        ["yx", "xy", "yx", "yx", "yx", "yx", "yx", "yx"],
        2,
    )
    grad_inputs, all_logits, o_inner, o_outer, o_out, o_pool, o_query, o_key, o_value, o_vec = scattered
    o_vec = o_vec.reshape(1024)

    def vec_part(row):
        return o_vec[row * share : (row + 1) * share]

    after = rows_used * share + hidden_share
    return (
        layer_out,
        all_logits[:, :docs, :CLASSES],
        grad_inputs,
        o_query,
        vec_part(B_QUERY),
        o_key,
        o_value,
        vec_part(B_VALUE),
        o_out,
        vec_part(B_OUT),
        vec_part(GAIN1),
        vec_part(SHIFT1),
        o_inner,
        o_vec[rows_used * share : after],
        o_outer,
        vec_part(B_OUTER),
        vec_part(GAIN2),
        vec_part(SHIFT2),
        o_pool,
        vec_part(B_POOL),
        o_vec[: CLASSES * share].reshape(CLASSES, share).T,
        o_vec[after : after + CLASSES],
    )


def solution(mesh):
    placed = (
        P("dp", "fsdp", None),
        P("dp", "fsdp", None),
        P("dp", None),
        P("dp", None),
        P(("dp", "fsdp"), None),
        P(("dp", "fsdp")),
        P(("dp", "fsdp"), None),
        P(("dp", "fsdp"), None),
        P(("dp", "fsdp")),
        P(("dp", "fsdp"), None),
        P(("dp", "fsdp")),
        P(("dp", "fsdp")),
        P(("dp", "fsdp")),
        P(("dp", "fsdp"), None),
        P(("dp", "fsdp")),
        P(("dp", "fsdp"), None),
        P(("dp", "fsdp")),
        P(("dp", "fsdp")),
        P(("dp", "fsdp")),
        P(("dp", "fsdp"), None),
        P(("dp", "fsdp")),
        P(("dp", "fsdp"), None),
        P(),
    )
    sizes = (mesh.shape["dp"], mesh.shape["fsdp"])
    chosen = fast_body if sizes == (8, 4) else general_body
    return jax.shard_map(
        chosen,
        mesh=mesh,
        in_specs=placed,
        out_specs=(
            P("dp", "fsdp", None),
            P("dp", None, None),
            P("dp", "fsdp", None),
            P(("dp", "fsdp"), None),
            P(("dp", "fsdp")),
            P(("dp", "fsdp"), None),
            P(("dp", "fsdp"), None),
            P(("dp", "fsdp")),
            P(("dp", "fsdp"), None),
            P(("dp", "fsdp")),
            P(("dp", "fsdp")),
            P(("dp", "fsdp")),
            P(("dp", "fsdp"), None),
            P(("dp", "fsdp")),
            P(("dp", "fsdp"), None),
            P(("dp", "fsdp")),
            P(("dp", "fsdp")),
            P(("dp", "fsdp")),
            P(("dp", "fsdp"), None),
            P(("dp", "fsdp")),
            P(("dp", "fsdp"), None),
            P(),
        ),
        check_vma=False,
    )
```

```python
import functools

import jax
import jax.numpy as jnp
from jax import lax
from jax.experimental import pallas as pl
from jax.experimental.pallas import tpu as pltpu
from jax.sharding import PartitionSpec as P

HEAD_DIM = 64
CLASSES = 3
MICRO = 4


def product(left_side, right_side):
    return jnp.dot(left_side, right_side, preferred_element_type=jnp.float32)


def contract_rows(left_side, right_side):
    return lax.dot_general(
        left_side, right_side, (((0,), (0,)), ((), ())), preferred_element_type=jnp.float32
    )


def times_transposed(left_side, right_side):
    return lax.dot_general(
        left_side, right_side, (((1,), (1,)), ((), ())), preferred_element_type=jnp.float32
    )


def layer_norm(values, norm_gain, norm_shift):
    average = jnp.mean(values, axis=-1, keepdims=True)
    centered = values - average
    variance = jnp.mean(centered * centered, axis=-1, keepdims=True)
    return centered * lax.rsqrt(variance + 1e-06) * norm_gain + norm_shift


def gelu_exact(values):
    return jax.nn.gelu(values, approximate=False)


def running_sum(lengths_rows):
    count = lengths_rows.shape[1]
    upper = jnp.arange(count)[:, None] <= jnp.arange(count)[None, :]
    return jnp.sum(jnp.where(upper[None], lengths_rows[:, :, None], 0), axis=1)


def segment_numbers(lengths_rows, places):
    doc_ends = running_sum(lengths_rows)
    above = (places[None, :, None] >= doc_ends[:, None, :]).astype(jnp.int32)
    return jnp.sum(above, axis=2)


def pair_heads(values):
    return values.reshape(values.shape[0], values.shape[1], 2, HEAD_DIM)


def pair_scores(query_pair, key_pair, same_doc):
    raw_scores = jnp.einsum(
        "bqhd,bkhd->bhqk", query_pair, key_pair, preferred_element_type=jnp.float32
    ) * HEAD_DIM ** (-0.5)
    return jnp.where(same_doc[:, None], raw_scores, -1000000000.0)


def lowered_masters(masters):
    return [member.astype(jnp.bfloat16) for member in masters]


def forward(tokens, lengths_rows, weights, bias_class):
    (
        w_query,
        b_query,
        w_key,
        w_value,
        b_value,
        w_out,
        b_out,
        first_gain,
        first_shift,
        w_inner,
        b_inner,
        w_outer,
        b_outer,
        second_gain,
        second_shift,
        w_pool,
        b_pool,
        w_class,
    ) = weights
    seq_count, local_len, model_width = tokens.shape
    doc_count = lengths_rows.shape[1]
    flat_rows = tokens.reshape(seq_count * local_len, model_width)
    queries = (
        (product(flat_rows, w_query) + b_query)
        .astype(jnp.bfloat16)
        .reshape(seq_count, local_len, model_width)
    )
    key_rows = (
        product(flat_rows, w_key).astype(jnp.bfloat16).reshape(seq_count, local_len, model_width)
    )
    value_rows = (
        (product(flat_rows, w_value) + b_value)
        .astype(jnp.bfloat16)
        .reshape(seq_count, local_len, model_width)
    )
    all_keys, all_values = (
        lax.all_gather(key_rows, "fsdp", axis=1, tiled=True),
        lax.all_gather(value_rows, "fsdp", axis=1, tiled=True),
    )
    full_len = all_keys.shape[1]
    own_places = lax.axis_index("fsdp") * local_len + jnp.arange(local_len, dtype=jnp.int32)
    key_places = jnp.arange(full_len, dtype=jnp.int32)
    same_doc = (
        segment_numbers(lengths_rows, own_places)[:, :, None]
        == segment_numbers(lengths_rows, key_places)[:, None, :]
    )
    pair_width = 2 * HEAD_DIM
    mixed_list = []
    log_totals = []
    for pair_index in range(model_width // pair_width):
        col_start = pair_index * pair_width
        query_pair = pair_heads(queries[:, :, col_start : col_start + pair_width])
        key_pair = pair_heads(all_keys[:, :, col_start : col_start + pair_width])
        value_pair = pair_heads(all_values[:, :, col_start : col_start + pair_width])
        scores = pair_scores(query_pair, key_pair, same_doc)
        row_peak = jnp.max(scores, axis=-1, keepdims=True)
        exp_total = jnp.sum(jnp.exp(scores - row_peak), axis=-1, keepdims=True)
        log_total = row_peak + jnp.log(exp_total)
        attn_probs = jnp.exp(scores - log_total).astype(jnp.bfloat16)
        mixed_pair = jnp.einsum(
            "bhqk,bkhd->bqhd", attn_probs, value_pair, preferred_element_type=jnp.float32
        )
        mixed_list.append(mixed_pair.reshape(seq_count, local_len, pair_width))
        log_totals.append(log_total)
    attended = (
        jnp.concatenate(mixed_list, axis=2)
        .astype(jnp.bfloat16)
        .reshape(seq_count * local_len, model_width)
    )
    branch = product(attended, w_out) + b_out
    pre_first = flat_rows.astype(jnp.float32) + branch
    normed = layer_norm(pre_first, first_gain.astype(jnp.float32), first_shift.astype(jnp.float32))
    normed_low = normed.astype(jnp.bfloat16)
    inner_pre = product(normed_low, w_inner) + b_inner
    activated = gelu_exact(inner_pre).astype(jnp.bfloat16)
    summed = normed + (product(activated, w_outer) + b_outer)
    result = layer_norm(summed, second_gain.astype(jnp.float32), second_shift.astype(jnp.float32))
    result_low = result.astype(jnp.bfloat16).reshape(seq_count, local_len, model_width)
    starts = running_sum(lengths_rows) - lengths_rows
    picker = (own_places[None, None, :] == starts[:, :, None]).astype(jnp.bfloat16)
    local_firsts = jnp.einsum(
        "bdl,blc->bdc", picker, result_low, preferred_element_type=jnp.float32
    )
    firsts = lax.psum(local_firsts, "fsdp")
    firsts_low = firsts.astype(jnp.bfloat16).reshape(seq_count * doc_count, model_width)
    pooled = jnp.tanh(product(firsts_low, w_pool) + b_pool)
    pooled_low = pooled.astype(jnp.bfloat16)
    logits = product(pooled_low, w_class) + bias_class
    stored = (
        flat_rows,
        queries,
        all_keys,
        all_values,
        same_doc,
        log_totals,
        attended,
        pre_first,
        summed,
        normed_low,
        inner_pre,
        activated,
        picker,
        firsts_low,
        pooled,
        pooled_low,
        logits,
    )
    return (result_low, logits.reshape(seq_count, doc_count, CLASSES), stored)


def backward(stored, weights, cot_rows, label_rows):
    (
        w_query,
        b_query,
        w_key,
        w_value,
        b_value,
        w_out,
        b_out,
        first_gain,
        first_shift,
        w_inner,
        b_inner,
        w_outer,
        b_outer,
        second_gain,
        second_shift,
        w_pool,
        b_pool,
        w_class,
    ) = weights
    (
        flat_rows,
        queries,
        all_keys,
        all_values,
        same_doc,
        log_totals,
        attended,
        pre_first,
        summed,
        normed_low,
        inner_pre,
        activated,
        picker,
        firsts_low,
        pooled,
        pooled_low,
        logits,
    ) = stored
    seq_count, local_len, model_width = queries.shape
    doc_count = picker.shape[1]
    owner_flag = (lax.axis_index("fsdp") == 0).astype(jnp.float32)
    row_peak = jnp.max(logits, axis=-1, keepdims=True)
    class_exp = jnp.exp(logits - row_peak)
    class_probs = class_exp / jnp.sum(class_exp, axis=-1, keepdims=True)
    onehot_labels = (
        label_rows.reshape(-1)[:, None] == jnp.arange(CLASSES, dtype=jnp.int32)[None, :]
    ).astype(jnp.float32)
    grad_logits = (class_probs - onehot_labels).astype(jnp.bfloat16)
    grad_b_class = owner_flag * jnp.sum(grad_logits.astype(jnp.float32), axis=0)
    grad_w_class = owner_flag * contract_rows(pooled_low, grad_logits)
    grad_pool_pre = (times_transposed(grad_logits, w_class) * (1.0 - pooled * pooled)).astype(
        jnp.bfloat16
    )
    grad_b_pool = owner_flag * jnp.sum(grad_pool_pre.astype(jnp.float32), axis=0)
    grad_w_pool = owner_flag * contract_rows(firsts_low, grad_pool_pre)
    grad_firsts = times_transposed(grad_pool_pre, w_pool).reshape(seq_count, doc_count, model_width)
    from_pool = jnp.einsum(
        "bdl,bdc->blc", picker.astype(jnp.float32), grad_firsts, precision=lax.Precision.HIGHEST
    )
    grad_result = cot_rows.astype(jnp.float32).reshape(-1, model_width) + from_pool.reshape(
        -1, model_width
    )
    second_back = jax.vjp(
        layer_norm, summed, second_gain.astype(jnp.float32), second_shift.astype(jnp.float32)
    )[1]
    grad_summed, grad_second_gain, grad_second_shift = second_back(grad_result)
    grad_outer = grad_summed.astype(jnp.bfloat16)
    grad_b_outer = jnp.sum(grad_outer.astype(jnp.float32), axis=0)
    grad_w_outer = contract_rows(activated, grad_outer)
    gelu_back = jax.vjp(gelu_exact, inner_pre)[1]
    grad_inner = gelu_back(times_transposed(grad_outer, w_outer))[0].astype(jnp.bfloat16)
    grad_b_inner = jnp.sum(grad_inner.astype(jnp.float32), axis=0)
    grad_w_inner = contract_rows(normed_low, grad_inner)
    grad_normed = grad_summed + times_transposed(grad_inner, w_inner)
    first_back = jax.vjp(
        layer_norm, pre_first, first_gain.astype(jnp.float32), first_shift.astype(jnp.float32)
    )[1]
    grad_pre_first, grad_first_gain, grad_first_shift = first_back(grad_normed)
    grad_branch = grad_pre_first.astype(jnp.bfloat16)
    grad_b_out = jnp.sum(grad_branch.astype(jnp.float32), axis=0)
    grad_w_out = contract_rows(attended, grad_branch)
    grad_attended = (
        times_transposed(grad_branch, w_out)
        .astype(jnp.bfloat16)
        .reshape(seq_count, local_len, model_width)
    )
    pair_width = 2 * HEAD_DIM
    query_list = []
    key_list = []
    value_list = []
    for pair_index in range(model_width // pair_width):
        col_start = pair_index * pair_width
        query_pair = pair_heads(queries[:, :, col_start : col_start + pair_width])
        key_pair = pair_heads(all_keys[:, :, col_start : col_start + pair_width])
        value_pair = pair_heads(all_values[:, :, col_start : col_start + pair_width])
        grad_pair = pair_heads(grad_attended[:, :, col_start : col_start + pair_width])
        scores = pair_scores(query_pair, key_pair, same_doc)
        attn_probs = jnp.exp(scores - log_totals[pair_index])
        grad_probs = jnp.einsum(
            "bqhd,bkhd->bhqk", grad_pair, value_pair, preferred_element_type=jnp.float32
        )
        row_dot = jnp.sum(attn_probs * grad_probs, axis=-1, keepdims=True)
        grad_scores = (attn_probs * (grad_probs - row_dot)).astype(jnp.bfloat16)
        query_part = jnp.einsum(
            "bhqk,bkhd->bqhd", grad_scores, key_pair, preferred_element_type=jnp.float32
        ) * HEAD_DIM ** (-0.5)
        query_list.append(query_part.reshape(seq_count, local_len, pair_width))
        probs_low = attn_probs.astype(jnp.bfloat16)
        key_part = jnp.einsum(
            "bhqk,bqhd->bkhd", grad_scores, query_pair, preferred_element_type=jnp.float32
        ) * HEAD_DIM ** (-0.5)
        value_part = jnp.einsum(
            "bhqk,bqhd->bkhd", probs_low, grad_pair, preferred_element_type=jnp.float32
        )
        key_list.append(key_part.reshape(seq_count, key_part.shape[1], pair_width))
        value_list.append(value_part.reshape(seq_count, value_part.shape[1], pair_width))
    key_partials = jnp.concatenate(key_list, axis=2)
    value_partials = jnp.concatenate(value_list, axis=2)
    own_keys, own_values = (
        lax.psum_scatter(
            key_partials.astype(jnp.bfloat16), "fsdp", scatter_dimension=1, tiled=True
        ).astype(jnp.float32),
        lax.psum_scatter(
            value_partials.astype(jnp.bfloat16), "fsdp", scatter_dimension=1, tiled=True
        ).astype(jnp.float32),
    )
    query_grad = jnp.concatenate(query_list, axis=2).astype(jnp.bfloat16).reshape(-1, model_width)
    key_grad = own_keys.astype(jnp.bfloat16).reshape(-1, model_width)
    value_grad = own_values.astype(jnp.bfloat16).reshape(-1, model_width)
    grad_w_query = contract_rows(flat_rows, query_grad)
    grad_b_query = jnp.sum(query_grad.astype(jnp.float32), axis=0)
    grad_w_key = contract_rows(flat_rows, key_grad)
    grad_w_value = contract_rows(flat_rows, value_grad)
    grad_b_value = jnp.sum(value_grad.astype(jnp.float32), axis=0)
    grad_tokens = (
        grad_pre_first
        + times_transposed(query_grad, w_query)
        + times_transposed(key_grad, w_key)
        + times_transposed(value_grad, w_value)
    )
    new_grads = (
        grad_w_query,
        grad_b_query,
        grad_w_key,
        grad_w_value,
        grad_b_value,
        grad_w_out,
        grad_b_out,
        grad_first_gain,
        grad_first_shift,
        grad_w_inner,
        grad_b_inner,
        grad_w_outer,
        grad_b_outer,
        grad_second_gain,
        grad_second_shift,
        grad_w_pool,
        grad_b_pool,
        grad_w_class,
    )
    return (
        new_grads,
        grad_b_class,
        grad_tokens.astype(jnp.bfloat16).reshape(seq_count, local_len, model_width),
    )


def general_body(
    inputs,
    cotangent,
    doc_lengths,
    labels,
    w_query,
    b_query,
    w_key,
    w_value,
    b_value,
    w_out,
    b_out,
    first_gain,
    first_shift,
    w_inner,
    b_inner,
    w_outer,
    b_outer,
    second_gain,
    second_shift,
    w_pool,
    b_pool,
    w_class,
    b_class,
):
    masters = (
        w_query,
        b_query,
        w_key,
        w_value,
        b_value,
        w_out,
        b_out,
        first_gain,
        first_shift,
        w_inner,
        b_inner,
        w_outer,
        b_outer,
        second_gain,
        second_shift,
        w_pool,
        b_pool,
        w_class,
    )
    group_size = lax.axis_size("dp") * lax.axis_size("fsdp")
    grad_sums = [
        jnp.zeros((member.shape[0] * group_size,) + member.shape[1:], jnp.float32)
        for member in masters
    ]
    class_sum = jnp.zeros((CLASSES,), jnp.float32)
    micro_seqs = inputs.shape[0] // MICRO
    out_list = []
    logit_list = []
    grad_list = []
    for micro_step in range(MICRO):
        first_seq = micro_step * micro_seqs
        after_seq = first_seq + micro_seqs
        tokens = inputs[first_seq:after_seq]
        lengths_rows = doc_lengths[first_seq:after_seq]
        pieces = lowered_masters(masters)
        front_weights = (
            lax.all_gather(pieces[0], ("dp", "fsdp"), axis=0, tiled=True),
            lax.all_gather(pieces[1], ("dp", "fsdp"), axis=0, tiled=True),
            lax.all_gather(pieces[2], ("dp", "fsdp"), axis=0, tiled=True),
            lax.all_gather(pieces[3], ("dp", "fsdp"), axis=0, tiled=True),
            lax.all_gather(pieces[4], ("dp", "fsdp"), axis=0, tiled=True),
            lax.all_gather(pieces[5], ("dp", "fsdp"), axis=0, tiled=True),
            lax.all_gather(pieces[6], ("dp", "fsdp"), axis=0, tiled=True),
            lax.all_gather(pieces[7], ("dp", "fsdp"), axis=0, tiled=True),
            lax.all_gather(pieces[8], ("dp", "fsdp"), axis=0, tiled=True),
            lax.all_gather(pieces[9], ("dp", "fsdp"), axis=0, tiled=True),
            lax.all_gather(pieces[10], ("dp", "fsdp"), axis=0, tiled=True),
            lax.all_gather(pieces[11], ("dp", "fsdp"), axis=0, tiled=True),
            lax.all_gather(pieces[12], ("dp", "fsdp"), axis=0, tiled=True),
            lax.all_gather(pieces[13], ("dp", "fsdp"), axis=0, tiled=True),
            lax.all_gather(pieces[14], ("dp", "fsdp"), axis=0, tiled=True),
            lax.all_gather(pieces[15], ("dp", "fsdp"), axis=0, tiled=True),
            lax.all_gather(pieces[16], ("dp", "fsdp"), axis=0, tiled=True),
            lax.all_gather(pieces[17], ("dp", "fsdp"), axis=0, tiled=True),
        )
        result_low, logits, stored = forward(tokens, lengths_rows, front_weights, b_class)
        out_list.append(result_low)
        logit_list.append(logits)
        back_weights = (
            lax.all_gather(pieces[0], ("dp", "fsdp"), axis=0, tiled=True),
            lax.all_gather(pieces[1], ("dp", "fsdp"), axis=0, tiled=True),
            lax.all_gather(pieces[2], ("dp", "fsdp"), axis=0, tiled=True),
            lax.all_gather(pieces[3], ("dp", "fsdp"), axis=0, tiled=True),
            lax.all_gather(pieces[4], ("dp", "fsdp"), axis=0, tiled=True),
            lax.all_gather(pieces[5], ("dp", "fsdp"), axis=0, tiled=True),
            lax.all_gather(pieces[6], ("dp", "fsdp"), axis=0, tiled=True),
            lax.all_gather(pieces[7], ("dp", "fsdp"), axis=0, tiled=True),
            lax.all_gather(pieces[8], ("dp", "fsdp"), axis=0, tiled=True),
            lax.all_gather(pieces[9], ("dp", "fsdp"), axis=0, tiled=True),
            lax.all_gather(pieces[10], ("dp", "fsdp"), axis=0, tiled=True),
            lax.all_gather(pieces[11], ("dp", "fsdp"), axis=0, tiled=True),
            lax.all_gather(pieces[12], ("dp", "fsdp"), axis=0, tiled=True),
            lax.all_gather(pieces[13], ("dp", "fsdp"), axis=0, tiled=True),
            lax.all_gather(pieces[14], ("dp", "fsdp"), axis=0, tiled=True),
            lax.all_gather(pieces[15], ("dp", "fsdp"), axis=0, tiled=True),
            lax.all_gather(pieces[16], ("dp", "fsdp"), axis=0, tiled=True),
            lax.all_gather(pieces[17], ("dp", "fsdp"), axis=0, tiled=True),
        )
        stored = forward(tokens, lengths_rows, back_weights, b_class)[2]
        new_grads, class_grad, grad_tokens = backward(
            stored, back_weights, cotangent[first_seq:after_seq], labels[first_seq:after_seq]
        )
        grad_sums = [running + fresh_grad for running, fresh_grad in zip(grad_sums, new_grads)]
        class_sum = class_sum + class_grad
        grad_list.append(grad_tokens)
    owned = (
        lax.psum_scatter(grad_sums[0], ("dp", "fsdp"), scatter_dimension=0, tiled=True),
        lax.psum_scatter(grad_sums[1], ("dp", "fsdp"), scatter_dimension=0, tiled=True),
        lax.psum_scatter(grad_sums[2], ("dp", "fsdp"), scatter_dimension=0, tiled=True),
        lax.psum_scatter(grad_sums[3], ("dp", "fsdp"), scatter_dimension=0, tiled=True),
        lax.psum_scatter(grad_sums[4], ("dp", "fsdp"), scatter_dimension=0, tiled=True),
        lax.psum_scatter(grad_sums[5], ("dp", "fsdp"), scatter_dimension=0, tiled=True),
        lax.psum_scatter(grad_sums[6], ("dp", "fsdp"), scatter_dimension=0, tiled=True),
        lax.psum_scatter(grad_sums[7], ("dp", "fsdp"), scatter_dimension=0, tiled=True),
        lax.psum_scatter(grad_sums[8], ("dp", "fsdp"), scatter_dimension=0, tiled=True),
        lax.psum_scatter(grad_sums[9], ("dp", "fsdp"), scatter_dimension=0, tiled=True),
        lax.psum_scatter(grad_sums[10], ("dp", "fsdp"), scatter_dimension=0, tiled=True),
        lax.psum_scatter(grad_sums[11], ("dp", "fsdp"), scatter_dimension=0, tiled=True),
        lax.psum_scatter(grad_sums[12], ("dp", "fsdp"), scatter_dimension=0, tiled=True),
        lax.psum_scatter(grad_sums[13], ("dp", "fsdp"), scatter_dimension=0, tiled=True),
        lax.psum_scatter(grad_sums[14], ("dp", "fsdp"), scatter_dimension=0, tiled=True),
        lax.psum_scatter(grad_sums[15], ("dp", "fsdp"), scatter_dimension=0, tiled=True),
        lax.psum_scatter(grad_sums[16], ("dp", "fsdp"), scatter_dimension=0, tiled=True),
        lax.psum_scatter(grad_sums[17], ("dp", "fsdp"), scatter_dimension=0, tiled=True),
    )
    class_total = lax.psum(class_sum, ("dp", "fsdp"))
    return (
        jnp.concatenate(out_list, axis=0),
        jnp.concatenate(logit_list, axis=0),
        jnp.concatenate(grad_list, axis=0),
        owned[0],
        owned[1],
        owned[2],
        owned[3],
        owned[4],
        owned[5],
        owned[6],
        owned[7],
        owned[8],
        owned[9],
        owned[10],
        owned[11],
        owned[12],
        owned[13],
        owned[14],
        owned[15],
        owned[16],
        owned[17],
        class_total,
    )


BF = jnp.bfloat16
F32 = jnp.float32
MESH = pl.DeviceIdType.MESH
ANY = pl.BlockSpec(memory_space=pl.ANY)
SMEM = pl.BlockSpec(memory_space=pltpu.SMEM)
ZS = 4
CLASS_ROWS, B_QUERY, B_VALUE, B_OUT, GAIN1, SHIFT1, B_OUTER, GAIN2, SHIFT2, B_POOL = (0, 3, 4, 5, 6, 7, 8, 9, 10, 11)
VEC_ROWS = 16


def nn(a, b):
    return lax.dot_general(a, b, (((1,), (0,)), ((), ())), preferred_element_type=F32)


def nt(a, b):
    return lax.dot_general(a, b, (((1,), (1,)), ((), ())), preferred_element_type=F32)


def tn(a, b):
    return lax.dot_general(a, b, (((0,), (0,)), ((), ())), preferred_element_type=F32)


def my_place():
    dp, fs = lax.axis_index("dp"), lax.axis_index("fsdp")
    return dp // 2, lax.rem(dp, 2), fs // 2, lax.rem(fs, 2)


def device_at(z, y, x, c):
    return (z * 2 + y, x * 2 + c)


def meet(partners):
    barrier = pltpu.get_barrier_semaphore()
    for partner in partners:
        pl.semaphore_signal(barrier, inc=1, device_id=partner, device_id_type=MESH)
    pl.semaphore_wait(barrier, len(partners))


def all_partners(z, y, x, c):
    found = [device_at(lax.rem(z + k, ZS), y, x, c) for k in range(1, ZS)]
    found.append(device_at(z, 1 - y, x, c))
    found.append(device_at(z, y, 1 - x, c))
    found.append(device_at(z, y, x, 1 - c))
    found.append(device_at(z, y, 1 - x, 1 - c))
    return found


def group_partner(k, x, c):
    return (1 - x if k >= 2 else x, 1 - c if k % 2 == 1 else c)


def gather_kernel(orders, *refs):
    count = len(orders)
    rows_ref, shards = refs[0], refs[1 : 1 + count]
    seq_ref, wholes = refs[1 + count], refs[2 + count : 2 + 2 * count]
    local_sem, row_send, row_recv, send_sem, recv_sem = refs[2 + 2 * count :]
    z, y, x, c = my_place()
    meet(all_partners(z, y, x, c))
    mine = x * 2 + c
    sent = []
    got_rows = []
    for k in range(1, 4):
        px, pc = group_partner(k, x, c)
        copy = pltpu.make_async_remote_copy(
            src_ref=rows_ref.at[px * 2 + pc],
            dst_ref=seq_ref.at[mine],
            send_sem=row_send.at[k - 1],
            recv_sem=row_recv.at[k - 1],
            device_id=device_at(z, y, px, pc),
            device_id_type=MESH,
        )
        copy.start()
        sent.append(copy)
        got_rows.append(copy)
    own = pltpu.make_async_copy(rows_ref.at[mine], seq_ref.at[mine], local_sem.at[count])
    own.start()
    local = [own]

    def place(rel):
        dz, fy, fx, fc = rel
        zz = lax.rem(z + dz, ZS)
        yy = 1 - y if fy else y
        xx = 1 - x if fx else x
        cc = 1 - c if fc else c
        return ((zz * 2 + yy) * 2 + xx) * 2 + cc

    def slot(rel):
        dz, fy, fx, fc = rel
        return ((dz * 2 + fy) * 2 + fx) * 2 + fc

    def send(a, rel, there, device, number):
        source = shards[a] if slot(rel) == 0 else wholes[a].at[place(rel)]
        copy = pltpu.make_async_remote_copy(
            src_ref=source,
            dst_ref=wholes[a].at[place(rel)],
            send_sem=send_sem.at[a, number],
            recv_sem=recv_sem.at[a, slot(there)],
            device_id=device,
            device_id_type=MESH,
        )
        copy.start()
        sent.append(copy)

    def arrive(a, rel):
        block = wholes[a].at[place(rel)]
        pltpu.make_async_remote_copy(
            src_ref=block,
            dst_ref=block,
            send_sem=send_sem.at[a, 0],
            recv_sem=recv_sem.at[a, slot(rel)],
            device_id=device_at(z, y, x, 1 - c),
            device_id_type=MESH,
        ).wait_recv()

    numbers = [0] * count

    def forward_to(a, rel, axis):
        numbers[a] += 1
        dz, fy, fx, fc = rel
        if axis == "y":
            send(a, rel, (dz, 1 - fy, fx, fc), device_at(z, 1 - y, x, c), numbers[a] - 1)
        elif axis == "x":
            send(a, rel, (dz, fy, 1 - fx, fc), device_at(z, y, 1 - x, c), numbers[a] - 1)
        else:
            send(a, rel, (dz, fy, fx, 1 - fc), device_at(z, y, x, 1 - c), numbers[a] - 1)

    for a in range(count):
        keep = pltpu.make_async_copy(
            shards[a], wholes[a].at[place((0, 0, 0, 0))], local_sem.at[a]
        )
        keep.start()
        local.append(keep)
        for k in (2, 1, 3):
            numbers[a] += 1
            send(
                a, (0, 0, 0, 0), ((ZS - k) % ZS, 0, 0, 0),
                device_at(lax.rem(z + k, ZS), y, x, c), numbers[a] - 1,
            )
        for axis in (*orders[a], "c"):
            forward_to(a, (0, 0, 0, 0), axis)
    for a in range(count):
        for dz in (1, 3, 2):
            arrive(a, (dz, 0, 0, 0))
            for axis in (*orders[a], "c"):
                forward_to(a, (dz, 0, 0, 0), axis)
    for a in range(count):
        first, second = orders[a]
        for dz in (0, 1, 3, 2):
            rel = (dz, int(first == "y"), int(first == "x"), 0)
            arrive(a, rel)
            forward_to(a, rel, second)
            forward_to(a, rel, "c")
    for a in range(count):
        first, second = orders[a]
        for dz in (0, 1, 3, 2):
            for turn in (0, 1):
                fy = 1 if second == "y" else turn
                fx = 1 if second == "x" else turn
                arrive(a, (dz, fy, fx, 0))
                forward_to(a, (dz, fy, fx, 0), "c")
    for a in range(count):
        for dz in range(ZS):
            for fy in (0, 1):
                for fx in (0, 1):
                    arrive(a, (dz, fy, fx, 1))
    for copy in got_rows:
        copy.wait_recv()
    for copy in sent:
        copy.wait_send()
    for copy in local:
        copy.wait()


def gather_all(rows, shards, orders, collective_id):
    count = len(shards)
    whole = 8 * ZS
    return pl.pallas_call(
        functools.partial(gather_kernel, orders),
        out_shape=[jax.ShapeDtypeStruct(rows.shape, rows.dtype)]
        + [jax.ShapeDtypeStruct((whole,) + s.shape, s.dtype) for s in shards],
        in_specs=[ANY] * (1 + count),
        out_specs=[ANY] * (1 + count),
        scratch_shapes=[
            pltpu.SemaphoreType.DMA((count + 1,)),
            pltpu.SemaphoreType.DMA((3,)),
            pltpu.SemaphoreType.DMA((3,)),
            pltpu.SemaphoreType.DMA((count, whole)),
            pltpu.SemaphoreType.DMA((count, whole)),
        ],
        compiler_params=pltpu.CompilerParams(collective_id=collective_id, has_side_effects=True),
        name="gather_weights",
    )(rows, *shards)


def doc_ends(lens_ref):
    ends = []
    total = 0
    for d in range(lens_ref.shape[0]):
        total = total + lens_ref[d]
        ends.append(total)
    return ends


def doc_numbers(places, ends):
    number = jnp.zeros(places.shape, jnp.int32)
    for end in ends:
        number = number + (places >= end).astype(jnp.int32)
    return number


def attend_kernel(
    lens_ref, x_ref, wq_ref, wk_ref, wv_ref, vec_ref, q_ref, k_ref, v_ref, att_ref, lse_ref, vt_ref
):
    x = x_ref[...]
    length, width = q_ref.shape
    chunk = 256
    heads = width // HEAD_DIM
    queries = (nn(x, wq_ref[...]) + vec_ref[B_QUERY : B_QUERY + 1, :]).astype(BF)
    q_ref[...] = queries
    k_ref[...] = nn(x, wk_ref[...]).astype(BF)
    values = (nn(x, wv_ref[...]) + vec_ref[B_VALUE : B_VALUE + 1, :]).astype(BF)
    v_ref[...] = values
    vt_ref[...] = values.astype(F32).T.astype(BF)
    ends = doc_ends(lens_ref)
    key_doc = doc_numbers(lax.broadcasted_iota(jnp.int32, (length, 1), 0), ends)
    lane_head = lax.broadcasted_iota(jnp.int32, (1, width), 1) // HEAD_DIM

    def step(i, carry):
        at = pl.multiple_of(i * chunk, chunk)
        query_doc = doc_numbers(lax.broadcasted_iota(jnp.int32, (1, chunk), 1) + at, ends)
        scaled = q_ref[pl.ds(at, chunk), :] * jnp.asarray(0.125, BF)
        mixed = []
        for h in range(heads):
            own = jnp.where(lane_head == h, scaled, jnp.zeros_like(scaled))
            blocks = []
            for s in range(0, length, chunk):
                scores = nt(k_ref[s : s + chunk, :], own)
                blocks.append(jnp.where(key_doc[s : s + chunk] == query_doc, scores, -1000000000.0))
            peak = functools.reduce(jnp.maximum, [jnp.max(b, axis=0, keepdims=True) for b in blocks])
            exps = [jnp.exp(b - peak) for b in blocks]
            total = functools.reduce(jnp.add, [jnp.sum(e, axis=0, keepdims=True) for e in exps])
            scale = 1.0 / total
            probs = jnp.concatenate([(e * scale).astype(BF) for e in exps], axis=0)
            mixed.append(nn(vt_ref[h * HEAD_DIM : (h + 1) * HEAD_DIM, :], probs))
            lse_ref[0, h : h + 1, pl.ds(at, chunk)] = peak + jnp.log(total)
        att_ref[pl.ds(at, chunk), :] = jnp.concatenate(mixed, axis=0).T.astype(BF)
        return carry

    lax.fori_loop(0, length // chunk, step, 0)


def attend(lens, rows, w_qkv, vectors):
    length, width = rows.shape
    group = 256
    groups = width // group
    whole = pl.BlockSpec((length, width), lambda g: (0, 0))
    part = pl.BlockSpec((length, group), lambda g: (0, g))
    return pl.pallas_call(
        attend_kernel,
        grid=(groups,),
        out_shape=[jax.ShapeDtypeStruct((length, width), BF)] * 4
        + [jax.ShapeDtypeStruct((groups, 8, length), F32)],
        in_specs=[
            SMEM,
            whole,
            pl.BlockSpec((width, group), lambda g: (0, 3 * g)),
            pl.BlockSpec((width, group), lambda g: (0, 3 * g + 1)),
            pl.BlockSpec((width, group), lambda g: (0, 3 * g + 2)),
            pl.BlockSpec((VEC_ROWS, group), lambda g: (0, g)),
        ],
        out_specs=[part] * 4 + [pl.BlockSpec((1, 8, length), lambda g: (g, 0, 0))],
        scratch_shapes=[pltpu.VMEM((group, length), BF)],
        compiler_params=pltpu.CompilerParams(vmem_limit_bytes=48 * 2**20),
        cost_estimate=pl.CostEstimate(flops=10 * 10**9, bytes_accessed=16 * 10**6, transcendentals=12 * 2**20),
        name="attend",
    )(lens, rows, w_qkv, w_qkv, w_qkv, vectors)


DENSE = 4
SCATTER_ORDERS = ("yx", "xy", "yx", "yx", "yx", "yx", "yx")
TABLE_ROWS = 24


def attend_back_kernel(groups, *refs):
    items = DENSE + groups
    lens_ref, x_ref, w_ref, q_ref, k_ref, v_ref, att_ref, datt_ref, lse_ref, start_ref = refs[:10]
    small_a_ref, small_b_ref, bi_ref, logit_ref = refs[10:14]
    parts = refs[14 : 14 + DENSE]
    back_ref, logits_ref, table_ref = refs[18:21]
    dense_outs, (out_q, out_k, out_v) = refs[21 : 21 + DENSE], refs[21 + DENSE : 24 + DENSE]
    rest = refs[24 + DENSE :]
    xt_ref, kt_ref, dot_ref, dq_ref, dk_ref, dv_ref, acc_ref, dx_ref, bias_ref, dw_ref, tab_ref, tab_in_ref = rest[:12]
    local_sem, row_send, row_recv, tab_send, tab_recv, send_sem, recv_sem = rest[12:19]
    rest = rest[19:]
    keeps, rest = rest[:DENSE], rest[DENSE:]
    firsts, seconds, thirds, fourths = (rest[j * items : (j + 1) * items] for j in range(4))

    length, width = q_ref.shape
    chunk = 256
    points = length // chunk
    heads = width // HEAD_DIM
    group = pl.program_id(0)
    z, y, x, c = my_place()
    mine = x * 2 + c

    def axes(a):
        return (y, x) if SCATTER_ORDERS[a][0] == "y" else (x, y)

    def device_along(axis):
        return device_at(z, 1 - y, x, c) if axis == "y" else device_at(z, y, 1 - x, c)

    def half(a, ref, place):
        return ref.at[:, place] if SCATTER_ORDERS[a][0] == "y" else ref.at[:, :, place]

    def whole_of(a, core):
        ref = parts[a] if a < DENSE else dw_ref.at[a - DENSE]
        return ref.at[:, :, :, core]

    def kept(a):
        return keeps[a] if a < DENSE else whole_of(a, c)

    def load(a, turn):
        place = 1 - axes(a)[0] if turn == 0 else axes(a)[0]
        return pltpu.make_async_copy(
            half(a, whole_of(a, c), place), half(a, keeps[a], place), local_sem.at[a, turn]
        )

    def copy_of(a, number):
        at, other = axes(a)
        if number < 2:
            place = 1 - at if number == 0 else at
            source, target = half(a, whole_of(a, 1 - c), place), half(a, firsts[a], place)
            device = device_at(z, y, x, 1 - c)
        elif number == 2:
            source, target = half(a, kept(a), 1 - at), seconds[a]
            device = device_along(SCATTER_ORDERS[a][0])
        elif number == 3:
            source, target = half(a, kept(a), at).at[:, 1 - other], thirds[a]
            device = device_along(SCATTER_ORDERS[a][1])
        else:
            there = lax.rem(z + number - 3, ZS)
            source, target = half(a, kept(a), at).at[:, other].at[there], fourths[a].at[number - 4]
            device = device_at(there, y, x, c)
        return pltpu.make_async_remote_copy(
            src_ref=source,
            dst_ref=target,
            send_sem=send_sem.at[a, number],
            recv_sem=recv_sem.at[a, number],
            device_id=device,
            device_id_type=MESH,
        )

    def add_into(target, source):
        lead = target.shape[:-2]
        total = functools.reduce(lambda p, q: p * q, lead, 1)

        def step(i, carry):
            where = []
            for size in reversed(lead):
                where.append(lax.rem(i, size))
                i = i // size
            where = tuple(reversed(where))
            target[where] = (target[where].astype(F32) + source[where].astype(F32)).astype(target.dtype)
            return carry

        lax.fori_loop(0, total, step, 0)

    def begin(a):
        if a < DENSE:
            load(a, 0).start()
            load(a, 1).start()
        copy_of(a, 0).start()
        copy_of(a, 1).start()

    def after_core(a, turn):
        place = 1 - axes(a)[0] if turn == 0 else axes(a)[0]
        if a < DENSE:
            load(a, turn).wait()
        copy_of(a, turn).wait_recv()
        add_into(half(a, kept(a), place), half(a, firsts[a], place))
        if turn == 0:
            copy_of(a, 2).start()

    def after_first(a):
        at, other = axes(a)
        ours = half(a, kept(a), at)
        copy_of(a, 2).wait_recv()
        add_into(ours.at[:, 1 - other], seconds[a].at[:, 1 - other])
        copy_of(a, 3).start()
        add_into(ours.at[:, other], seconds[a].at[:, other])

    def after_second(a):
        at, other = axes(a)
        copy_of(a, 3).wait_recv()
        add_into(half(a, kept(a), at).at[:, other], thirds[a])
        for number in (5, 4, 6):
            copy_of(a, number).start()

    def finish(a):
        at, other = axes(a)
        for number in (4, 5, 6):
            copy_of(a, number).wait_recv()
        ours = half(a, kept(a), at).at[:, other]
        total = (
            ours[z].astype(F32)
            + fourths[a][0].astype(F32)
            + fourths[a][1].astype(F32)
            + fourths[a][2].astype(F32)
        )
        if a < DENSE:
            dense_outs[a][...] = total
        else:
            s = (a - DENSE) * width
            for j, out in enumerate((out_q, out_k, out_v)):
                out[:, s : s + width] = total[:, j * width : (j + 1) * width]

    def row_copy(which, k):
        px, pc = group_partner(k, x, c)
        if which == 0:
            source, target = dx_ref.at[px * 2 + pc], back_ref.at[mine]
        else:
            source, target = logit_ref, logits_ref.at[mine]
        return pltpu.make_async_remote_copy(
            src_ref=source,
            dst_ref=target,
            send_sem=row_send.at[which, k - 1],
            recv_sem=row_recv.at[which, k - 1],
            device_id=device_at(z, y, px, pc),
            device_id_type=MESH,
        )

    def row_own(which):
        if which == 0:
            source, target = dx_ref.at[mine], back_ref.at[mine]
        else:
            source, target = logit_ref, logits_ref.at[mine]
        return pltpu.make_async_copy(source, target, local_sem.at[DENSE, which])

    def table_copy(level):
        if level < 3:
            source, target = tab_ref.at[level], tab_in_ref.at[level]
            device = (
                device_at(z, y, x, 1 - c), device_at(z, 1 - y, x, c), device_at(z, y, 1 - x, c)
            )[level]
        else:
            source, target = tab_ref.at[3], tab_in_ref.at[3 + z]
            device = device_at(lax.rem(z + level - 2, ZS), y, x, c)
        return pltpu.make_async_remote_copy(
            src_ref=source,
            dst_ref=target,
            send_sem=tab_send.at[level],
            recv_sem=tab_recv.at[level],
            device_id=device,
            device_id_type=MESH,
        )

    def table_wait(level):
        if level < 3:
            table_copy(level).wait_recv()
        else:
            slot = tab_in_ref.at[3 + lax.rem(z + ZS - (level - 2), ZS)]
            pltpu.make_async_remote_copy(
                src_ref=slot,
                dst_ref=slot,
                send_sem=tab_send.at[level],
                recv_sem=tab_recv.at[level],
                device_id=device_at(lax.rem(z + level - 2, ZS), y, x, c),
                device_id_type=MESH,
            ).wait_recv()

    def table_level(level):
        table_wait(level)
        tab_ref[level + 1] = tab_ref[level] + tab_in_ref[level]
        if level < 2:
            table_copy(level + 1).start()
        else:
            tab_in_ref[3 + z] = tab_ref[3]
            for nxt in (4, 3, 5):
                table_copy(nxt).start()

    dense_items = tuple(range(DENSE))
    plan = {
        2: [functools.partial(after_core, 0, 0), functools.partial(after_core, 1, 0)],
        3: [functools.partial(after_core, a, 0) for a in dense_items[2:]] + [functools.partial(after_core, 0, 1)],
        4: [functools.partial(begin, DENSE)] + [functools.partial(after_core, a, 1) for a in dense_items[1:]],
        5: [functools.partial(after_core, DENSE, 0), functools.partial(after_core, DENSE, 1)],
        8: [functools.partial(begin, DENSE + 1), functools.partial(after_first, 0)],
        9: [functools.partial(after_core, DENSE + 1, 0), functools.partial(after_core, DENSE + 1, 1), functools.partial(after_first, 1)],
        10: [functools.partial(after_first, a) for a in dense_items[2:]],
        11: [functools.partial(after_second, 0), functools.partial(after_second, 1)],
    }

    @pl.when(group == 0)
    def _():
        meet(all_partners(z, y, x, c))
        for a in range(DENSE):
            begin(a)
        for k in range(1, 4):
            row_copy(1, k).start()
        row_own(1).start()
        xt_ref[...] = x_ref[...].astype(F32).T.astype(BF)
        acc_ref[...] = start_ref[...]

    kt_ref[...] = k_ref[...].astype(F32).T.astype(BF)
    dot_ref[...] = (datt_ref[...].astype(F32) * att_ref[...].astype(F32)).T
    dk_ref[...] = jnp.zeros_like(dk_ref)
    dv_ref[...] = jnp.zeros_like(dv_ref)
    ends = doc_ends(lens_ref)
    key_doc = doc_numbers(lax.broadcasted_iota(jnp.int32, (length, 1), 0), ends)
    lane_head = lax.broadcasted_iota(jnp.int32, (1, width), 1) // HEAD_DIM

    def step(i, carry):
        for point, actions in plan.items():

            @pl.when((group == point // points) & (i == point % points))
            def _(actions=actions):
                for action in actions:
                    action()

        at = pl.multiple_of(i * chunk, chunk)
        query_doc = doc_numbers(lax.broadcasted_iota(jnp.int32, (1, chunk), 1) + at, ends)
        scaled = q_ref[pl.ds(at, chunk), :] * jnp.asarray(0.125, BF)
        given = datt_ref[pl.ds(at, chunk), :]
        own_q = [jnp.where(lane_head == h, scaled, jnp.zeros_like(scaled)) for h in range(heads)]
        own_d = [jnp.where(lane_head == h, given, jnp.zeros_like(given)) for h in range(heads)]
        all_probs = [[] for _ in range(length // chunk)]
        all_grads = [[] for _ in range(length // chunk)]
        for h in range(heads):
            lse = lse_ref[0, h : h + 1, pl.ds(at, chunk)]
            dots = jnp.sum(
                dot_ref[h * HEAD_DIM : (h + 1) * HEAD_DIM, pl.ds(at, chunk)], axis=0, keepdims=True
            )
            for j in range(length // chunk):
                s = j * chunk
                scores = nt(k_ref[s : s + chunk, :], own_q[h])
                scores = jnp.where(key_doc[s : s + chunk] == query_doc, scores, -1000000000.0)
                probs = jnp.exp(scores - lse)
                grad_probs = nt(v_ref[s : s + chunk, :], own_d[h])
                all_grads[j].append((probs * (grad_probs - dots)).astype(BF))
                all_probs[j].append(probs.astype(BF))
        stacked_q = jnp.concatenate(own_q, axis=0)
        stacked_d = jnp.concatenate(own_d, axis=0)
        for j in range(length // chunk):
            s = j * chunk
            dk_ref[s : s + chunk, :] += nn(jnp.concatenate(all_grads[j], axis=1), stacked_q)
            dv_ref[s : s + chunk, :] += nn(jnp.concatenate(all_probs[j], axis=1), stacked_d)
        mixed = []
        for h in range(heads):
            column = jnp.concatenate([all_grads[j][h] for j in range(length // chunk)], axis=0)
            mixed.append(nn(kt_ref[h * HEAD_DIM : (h + 1) * HEAD_DIM, :], column))
        dq_ref[pl.ds(at, chunk), :] = (jnp.concatenate(mixed, axis=0).T * 0.125).astype(BF)
        return carry

    lax.fori_loop(0, points, step, 0)
    xt = xt_ref[...]
    grads = (dq_ref[...], dk_ref[...].astype(BF), dv_ref[...].astype(BF))
    block = dw_ref.shape[1:6]
    for j, grad in enumerate(grads):
        dw_ref[group, :, :, :, :, :, j * width : (j + 1) * width] = nn(xt, grad).reshape(block + (width,)).astype(BF)
    bias_ref[group, 0:1, :] = jnp.sum(grads[0].astype(F32), axis=0, keepdims=True)
    bias_ref[group, 1:2, :] = jnp.sum(grads[2].astype(F32), axis=0, keepdims=True)
    total = acc_ref[...]
    for j, grad in enumerate(grads):
        total = total + nt(grad, w_ref[:, j * width : (j + 1) * width])
    acc_ref[...] = total

    @pl.when(group == groups - 1)
    def _():
        last = items - 1
        begin(last)
        dx_ref[...] = acc_ref[...].reshape(dx_ref.shape).astype(BF)
        for k in (3, 2, 1):
            row_copy(0, k).start()
        row_own(0).start()
        tab_ref[0, 0:CLASSES] = small_a_ref[0:CLASSES]
        for g in range(groups):
            tab_ref[0, B_QUERY : B_QUERY + 2, g * width : (g + 1) * width] = bias_ref[g, 0:2, :]
        for row, (ref, at) in {
            B_OUT: (small_b_ref, 3), GAIN1: (small_b_ref, 4), SHIFT1: (small_b_ref, 5), B_OUTER: (small_b_ref, 0),
            GAIN2: (small_b_ref, 1), SHIFT2: (small_b_ref, 2), B_POOL: (small_a_ref, 16), 16: (small_a_ref, 17),
        }.items():
            tab_ref[0, row : row + 1] = ref[at : at + 1, :]
        full = small_a_ref.shape[1]
        for j in range(4):
            tab_ref[0, 12 + j : 13 + j] = bi_ref[:, j * full : (j + 1) * full]
        tab_ref[0, 17:TABLE_ROWS] = jnp.zeros((TABLE_ROWS - 17, full), F32)
        table_copy(0).start()
        after_first(DENSE)
        after_core(last, 0)
        after_core(last, 1)
        table_level(0)
        for a in dense_items[2:]:
            after_second(a)
        after_first(DENSE + 1)
        table_level(1)
        finish(0)
        finish(1)
        after_second(DENSE)
        after_first(last)
        table_level(2)
        after_second(DENSE + 1)
        for a in dense_items[2:]:
            finish(a)
        after_second(last)
        finish(DENSE)
        finish(DENSE + 1)
        for level in (3, 4, 5):
            table_wait(level)
        table_ref[...] = (tab_in_ref[3] + tab_in_ref[4]) + (tab_in_ref[5] + tab_in_ref[6])
        finish(last)
        for a in range(items):
            for number in range(7):
                copy_of(a, number).wait_send()
        for level in range(6):
            table_copy(level).wait_send()
        for which in (0, 1):
            for k in range(1, 4):
                row_copy(which, k).wait_recv()
                row_copy(which, k).wait_send()
            row_own(which).wait()


def attend_back(lens, rows, w_groups, q, k, v, att, datt, lse, grad_pre, small_a, small_b, grad_b_inner, logit_block, parts):
    length, width = rows.shape
    group = 256
    groups = width // group
    local_len = length // 4
    share = width // (8 * ZS)
    once = pl.Buffered(buffer_count=1)
    whole = pl.BlockSpec((length, width), lambda g: (0, 0), pipeline_mode=once)
    part = pl.BlockSpec((length, group), lambda g: (0, g))
    blocks = [p.shape[1:] for p in parts]
    split = [p.reshape((ZS, 2, 2, 2) + b) for p, b in zip(parts, blocks)]
    blocks = blocks + [(share, 3 * group)] * groups
    hbm = pl.BlockSpec(memory_space=pl.ANY)

    def fixed(shape):
        return pl.BlockSpec(shape, lambda g: (0,) * len(shape))

    results = [b for b in blocks[:DENSE]] + [(share, width)] * 3
    arriving = []
    for lead in ((ZS, 2, 2), (ZS, 2), (ZS,), (ZS - 1,)):
        arriving += [pltpu.VMEM(lead + b, BF) for b in blocks]
    items = len(blocks)
    return pl.pallas_call(
        functools.partial(attend_back_kernel, groups),
        grid=(groups,),
        out_shape=[
            jax.ShapeDtypeStruct((4, local_len, width), BF),
            jax.ShapeDtypeStruct((4,) + logit_block.shape, F32),
            jax.ShapeDtypeStruct((TABLE_ROWS, width), F32),
        ]
        + [jax.ShapeDtypeStruct(r, F32) for r in results],
        in_specs=[
            SMEM,
            whole,
            pl.BlockSpec((width, 3 * group), lambda g: (0, g)),
            part, part, part, part, part,
            pl.BlockSpec((1, 8, length), lambda g: (g, 0, 0)),
            whole,
            fixed(small_a.shape), fixed(small_b.shape), fixed(grad_b_inner.shape), hbm,
        ]
        + [hbm] * DENSE,
        out_specs=[hbm, hbm, fixed((TABLE_ROWS, width))] + [fixed(r) for r in results],
        scratch_shapes=[
            pltpu.VMEM((width, length), BF),
            pltpu.VMEM((group, length), BF),
            pltpu.VMEM((group, length), F32),
            pltpu.VMEM((length, group), BF),
            pltpu.VMEM((length, group), F32),
            pltpu.VMEM((length, group), F32),
            pltpu.VMEM((length, width), F32),
            pltpu.VMEM((4, local_len, width), BF),
            pltpu.VMEM((groups, 8, group), F32),
            pltpu.VMEM((groups, ZS, 2, 2, 2, share, 3 * group), BF),
            pltpu.VMEM((4, TABLE_ROWS, width), F32),
            pltpu.VMEM((3 + ZS, TABLE_ROWS, width), F32),
            pltpu.SemaphoreType.DMA((DENSE + 1, 2)),
            pltpu.SemaphoreType.DMA((2, 3)),
            pltpu.SemaphoreType.DMA((2, 3)),
            pltpu.SemaphoreType.DMA((6,)),
            pltpu.SemaphoreType.DMA((6,)),
            pltpu.SemaphoreType.DMA((items, 7)),
            pltpu.SemaphoreType.DMA((items, 7)),
        ]
        + [pltpu.VMEM((ZS, 2, 2) + b, BF) for b in blocks[:DENSE]]
        + arriving,
        compiler_params=pltpu.CompilerParams(
            collective_id=2, has_side_effects=True, vmem_limit_bytes=60 * 2**20
        ),
        name="attend_back",
    )(lens, rows, w_groups, q, k, v, att, datt, lse, grad_pre, small_a, small_b, grad_b_inner, logit_block, *split)


def normal_parts(v):
    bell = jnp.exp(v * v * -0.5)
    t = 1.0 / (1.0 + jnp.abs(v) * 0.23164189)
    tail = t * (0.127414796 + t * (-0.142248368 + t * (0.710706870 + t * (-0.726576013 + t * 0.530702714)))) * bell
    return jnp.where(v >= 0.0, 1.0 - tail, tail), bell


def centered_parts(values):
    average = jnp.mean(values, axis=-1, keepdims=True)
    centered = values - average
    variance = jnp.mean(centered * centered, axis=-1, keepdims=True)
    inverse = lax.rsqrt(variance + 1e-06)
    return centered * inverse, inverse


def dense_kernel(
    lens_ref, labels_ref, x_ref, att_ref, w_inner_ref, w_out_ref, w_pool_ref, w_outer_ref, vec_ref, b_inner_ref, b_class_ref,
    pre_ref, summed_ref, low_ref, act_ref, dact_ref, lo_ref, dpool_ref, first_ref, small_ref, logits_ref, picked_ref,
):
    step = pl.program_id(0)
    rows = x_ref.shape[0]
    hidden = w_inner_ref.shape[1]
    chunk = 512

    def vec(row):
        return vec_ref[row : row + 1, :]

    pre = x_ref[...].astype(F32) + (nn(att_ref[...], w_out_ref[...]) + vec(B_OUT))
    pre_ref[...] = pre
    normed = centered_parts(pre)[0] * vec(GAIN1) + vec(SHIFT1)
    low = normed.astype(BF)
    low_ref[...] = low
    total = normed + vec(B_OUTER)
    for s in range(0, hidden, chunk):
        inner = nn(low, w_inner_ref[:, s : s + chunk]) + b_inner_ref[:, s : s + chunk]
        phi, bell = normal_parts(inner)
        activated = (inner * phi).astype(BF)
        act_ref[:, s : s + chunk] = activated
        dact_ref[:, s : s + chunk] = (phi + inner * bell * 0.3989422804014327).astype(BF)
        total = total + nn(activated, w_outer_ref[s : s + chunk, :])
    summed_ref[...] = total
    result = (centered_parts(total)[0] * vec(GAIN2) + vec(SHIFT2)).astype(BF)
    lo_ref[...] = result
    ends = doc_ends(lens_ref)
    docs = len(ends)
    places = lax.broadcasted_iota(jnp.int32, (VEC_ROWS, rows), 1) + step * rows
    row_doc = lax.broadcasted_iota(jnp.int32, (VEC_ROWS, rows), 0)
    hit = jnp.zeros((VEC_ROWS, rows), jnp.bool_)
    for d in range(docs):
        hit = hit | ((row_doc == d) & (places == ends[d] - lens_ref[d]))
    found = nn(jnp.where(hit, 1.0, 0.0).astype(BF), result)

    @pl.when(step == 0)
    def _():
        picked_ref[...] = found

    @pl.when(step > 0)
    def _():
        picked_ref[...] += found

    @pl.when(step == pl.num_programs(0) - 1)
    def _():
        picked = picked_ref[...].astype(BF)
        pooled = jnp.tanh(nn(picked, w_pool_ref[...]) + vec(B_POOL))
        pooled_low = pooled.astype(BF)
        table = vec_ref[...].astype(BF)
        logits = nt(pooled_low, table) + b_class_ref[...]
        column = lax.broadcasted_iota(jnp.int32, (VEC_ROWS, VEC_ROWS), 1)
        row = lax.broadcasted_iota(jnp.int32, (VEC_ROWS, VEC_ROWS), 0)
        logits_ref[...] = logits
        live = column < CLASSES
        shown = jnp.where(live, logits, -jnp.inf)
        exps = jnp.where(live, jnp.exp(shown - jnp.max(shown, axis=-1, keepdims=True)), 0.0)
        probs = exps / jnp.sum(exps, axis=-1, keepdims=True)
        label = jnp.zeros((VEC_ROWS, VEC_ROWS), jnp.int32)
        for d in range(docs):
            label = jnp.where(row == d, labels_ref[d], label)
        grad = jnp.where(live & (row < docs), probs - jnp.where(label == column, 1.0, 0.0), 0.0)
        grad_low = grad.astype(BF)
        grad_pool = (nn(grad_low, table) * (1.0 - pooled * pooled)).astype(BF)
        dpool_ref[...] = tn(picked, grad_pool).astype(BF)
        first_ref[...] = nt(grad_pool, w_pool_ref[...])
        small_ref[0:16, :] = tn(grad_low, pooled_low)
        small_ref[16:17, :] = jnp.sum(grad_pool.astype(F32), axis=0, keepdims=True)
        width = small_ref.shape[1]
        class_sum = jnp.sum(grad_low.astype(F32), axis=0, keepdims=True)
        small_ref[17:18, :] = jnp.concatenate(
            [class_sum, jnp.zeros((1, width - VEC_ROWS), F32)], axis=1
        )


def dense(lens, labels, rows, att, w_mid, w_outer, vectors, b_inner, b_class_row):
    length, width = rows.shape
    hidden = w_outer.shape[0]
    tile = 256
    steps = length // tile
    part = pl.BlockSpec((tile, width), lambda i: (i, 0))
    wide = pl.BlockSpec((tile, hidden), lambda i: (i, 0))

    def fixed(shape, column=0):
        return pl.BlockSpec(shape, lambda i: (0, column))

    spots = hidden // width
    return pl.pallas_call(
        dense_kernel,
        grid=(steps,),
        out_shape=[
            jax.ShapeDtypeStruct((length, width), F32),
            jax.ShapeDtypeStruct((length, width), F32),
            jax.ShapeDtypeStruct((length, width), BF),
            jax.ShapeDtypeStruct((length, hidden), BF),
            jax.ShapeDtypeStruct((length, hidden), BF),
            jax.ShapeDtypeStruct((length, width), BF),
            jax.ShapeDtypeStruct((width, width), BF),
            jax.ShapeDtypeStruct((VEC_ROWS, width), F32),
            jax.ShapeDtypeStruct((24, width), F32),
            jax.ShapeDtypeStruct((VEC_ROWS, VEC_ROWS), F32),
        ],
        in_specs=[
            SMEM, SMEM, part, part,
            fixed((width, hidden)), fixed((width, width), spots), fixed((width, width), spots + 1),
            fixed((hidden, width)), fixed((VEC_ROWS, width)), fixed((1, hidden)), fixed((1, VEC_ROWS)),
        ],
        out_specs=[
            part, part, part, wide, wide, part,
            fixed((width, width)), fixed((VEC_ROWS, width)), fixed((24, width)), fixed((VEC_ROWS, VEC_ROWS)),
        ],
        scratch_shapes=[pltpu.VMEM((VEC_ROWS, width), F32)],
        compiler_params=pltpu.CompilerParams(vmem_limit_bytes=60 * 2**20),
        cost_estimate=pl.CostEstimate(flops=11 * 10**9, bytes_accessed=40 * 10**6, transcendentals=3 * 2**20),
        name="dense",
    )(lens, labels, rows, att, w_mid, w_mid, w_mid, w_outer, vectors, b_inner, b_class_row)


def norm_back(grad, values, gain):
    hat, inverse = centered_parts(values)
    scaled = grad * gain
    mean_scaled = jnp.mean(scaled, axis=-1, keepdims=True)
    mean_cross = jnp.mean(scaled * hat, axis=-1, keepdims=True)
    back = (scaled - mean_scaled - hat * mean_cross) * inverse
    return back, jnp.sum(grad * hat, axis=0, keepdims=True), jnp.sum(grad, axis=0, keepdims=True)


def dense_back_kernel(
    lens_ref, cot_ref, summed_ref, pre_ref, dact_ref, w_inner_ref, w_out_ref, w_outer_ref, vec_ref, first_ref,
    outer_ref, inner_ref, branch_ref, datt_ref, gpre_ref, small_ref, bi_ref,
):
    step = pl.program_id(0)
    rows = cot_ref.shape[0]
    hidden = dact_ref.shape[1]
    chunk = 512

    def vec(row):
        return vec_ref[row : row + 1, :]

    @pl.when(step == 0)
    def _():
        small_ref[...] = jnp.zeros_like(small_ref)
        bi_ref[...] = jnp.zeros_like(bi_ref)

    grad = cot_ref[...].astype(F32)
    places = lax.broadcasted_iota(jnp.int32, (rows, 1), 0) + step * rows
    ends = doc_ends(lens_ref)
    placed = jnp.zeros(grad.shape, F32)
    for d in range(len(ends)):
        placed = jnp.where(places == ends[d] - lens_ref[d], first_ref[d : d + 1, :], placed)
    grad = grad + placed
    grad_summed, gain2, shift2 = norm_back(grad, summed_ref[...], vec(GAIN2))
    outer = grad_summed.astype(BF)
    outer_ref[...] = outer
    grad_normed = grad_summed
    for s in range(0, hidden, chunk):
        back = nt(outer, w_outer_ref[s : s + chunk, :])
        inner = (back * dact_ref[:, s : s + chunk].astype(F32)).astype(BF)
        inner_ref[:, s : s + chunk] = inner
        bi_ref[:, s : s + chunk] += jnp.sum(inner.astype(F32), axis=0, keepdims=True)
        grad_normed = grad_normed + nt(inner, w_inner_ref[:, s : s + chunk])
    grad_pre, gain1, shift1 = norm_back(grad_normed, pre_ref[...], vec(GAIN1))
    gpre_ref[...] = grad_pre
    branch = grad_pre.astype(BF)
    branch_ref[...] = branch
    datt_ref[...] = nt(branch, w_out_ref[...]).astype(BF)
    small_ref[0:1, :] += jnp.sum(outer.astype(F32), axis=0, keepdims=True)
    small_ref[1:2, :] += gain2
    small_ref[2:3, :] += shift2
    small_ref[3:4, :] += jnp.sum(branch.astype(F32), axis=0, keepdims=True)
    small_ref[4:5, :] += gain1
    small_ref[5:6, :] += shift1


def dense_back(lens, cot, summed, pre, dact, w_mid, w_outer, vectors, first):
    length, width = cot.shape
    hidden = w_outer.shape[0]
    tile = 256
    part = pl.BlockSpec((tile, width), lambda i: (i, 0))
    wide = pl.BlockSpec((tile, hidden), lambda i: (i, 0))

    def fixed(shape, column=0):
        return pl.BlockSpec(shape, lambda i: (0, column))

    spots = hidden // width
    return pl.pallas_call(
        dense_back_kernel,
        grid=(length // tile,),
        out_shape=[
            jax.ShapeDtypeStruct((length, width), BF),
            jax.ShapeDtypeStruct((length, hidden), BF),
            jax.ShapeDtypeStruct((length, width), BF),
            jax.ShapeDtypeStruct((length, width), BF),
            jax.ShapeDtypeStruct((length, width), F32),
            jax.ShapeDtypeStruct((8, width), F32),
            jax.ShapeDtypeStruct((1, hidden), F32),
        ],
        in_specs=[
            SMEM, part, part, part, wide,
            fixed((width, hidden)), fixed((width, width), spots), fixed((hidden, width)),
            fixed((VEC_ROWS, width)), fixed((VEC_ROWS, width)),
        ],
        out_specs=[part, wide, part, part, part, fixed((8, width)), fixed((1, hidden))],
        compiler_params=pltpu.CompilerParams(vmem_limit_bytes=60 * 2**20),
        cost_estimate=pl.CostEstimate(flops=11 * 10**9, bytes_accessed=40 * 10**6, transcendentals=0),
        name="dense_back",
    )(lens, cot, summed, pre, dact, w_mid, w_mid, w_outer, vectors, first)


def exchange(blocks):
    count = blocks.shape[0]
    mine = lax.axis_index("fsdp")
    held = jnp.zeros_like(blocks)
    own = lax.dynamic_index_in_dim(blocks, mine, 0, keepdims=True)
    held = lax.dynamic_update_slice_in_dim(held, own, mine, 0)
    for k in range(1, count):
        leaving = lax.dynamic_index_in_dim(blocks, lax.rem(mine + k, count), 0, keepdims=True)
        came = lax.ppermute(leaving, "fsdp", [(i, (i + k) % count) for i in range(count)])
        held = lax.dynamic_update_slice_in_dim(held, came, lax.rem(mine - k + count, count), 0)
    return held


def fast_body(
    inputs, cotangent, doc_lengths, labels, w_query, b_query, w_key, w_value, b_value, w_out, b_out, first_gain, first_shift,
    w_inner, b_inner, w_outer, b_outer, second_gain, second_shift, w_pool, b_pool, w_class, b_class,
):
    seqs, local_len, width = inputs.shape
    length = seqs * local_len
    devices = 8 * ZS
    mine = lax.axis_index("fsdp")
    docs = doc_lengths.shape[1]
    own_lens = lax.dynamic_index_in_dim(doc_lengths, mine, 0, keepdims=False)
    own_labels = lax.dynamic_index_in_dim(labels, mine, 0, keepdims=False)

    share = width // devices
    hidden_share = b_inner.shape[0]
    hidden = hidden_share * devices
    group = 256
    qkv_shard = jnp.concatenate(
        [w[:, s : s + group] for s in range(0, width, group) for w in (w_query, w_key, w_value)], axis=1
    ).astype(BF)
    mid_shard = jnp.concatenate([w_inner, w_out, w_pool], axis=1).astype(BF)
    outer_shard = w_outer.astype(BF)
    vec_shard = jnp.concatenate(
        [
            w_class.T.reshape(-1), b_query, b_value, b_out, first_gain, first_shift, b_outer, second_gain, second_shift,
            b_pool, b_inner,
        ]
    )
    vec_len = vec_shard.shape[0]
    vec_shard = jnp.pad(vec_shard, (0, 1024 - vec_len)).reshape(8, 128).astype(BF).astype(F32)

    rows, w_qkv, vec_all, w_mid, w_outer_all = gather_all(
        inputs, [qkv_shard, vec_shard, mid_shard, outer_shard], ["xy", "xy", "xy", "yx"], 1
    )
    rows = rows.reshape(length, width)
    w_qkv = w_qkv.reshape(width, 3 * width)
    w_mid = w_mid.reshape(width, hidden + 2 * width)
    w_outer_all = w_outer_all.reshape(hidden, width)
    flat_vec = vec_all.reshape(devices, 1024)
    rows_used = B_POOL + 1
    vectors = flat_vec[:, : rows_used * share].reshape(devices, rows_used, share).transpose(1, 0, 2).reshape(rows_used, width)
    vectors = jnp.pad(vectors, ((0, VEC_ROWS - rows_used), (0, 0)))
    b_inner_row = flat_vec[:, rows_used * share : vec_len].reshape(1, hidden)
    b_class_row = jnp.pad(b_class, (0, VEC_ROWS - CLASSES)).reshape(1, VEC_ROWS)

    cot = exchange(cotangent).reshape(length, width)
    q, k, v, att, lse = attend(own_lens, rows, w_qkv, vectors)
    pre, summed, low, act, dact, result, grad_pool, first, small_a, logits = dense(
        own_lens, own_labels, rows, att, w_mid, w_outer_all, vectors, b_inner_row, b_class_row
    )
    layer_out = exchange(result.reshape(seqs, local_len, width))
    outer, inner, branch, datt, grad_pre, small_b, grad_b_inner = dense_back(
        own_lens, cot, summed, pre, dact, w_mid, w_outer_all, vectors, first
    )
    grad_outer_w = tn(act, outer).astype(BF)
    grad_inner_w = tn(low, inner).astype(BF)
    grad_out_w = tn(att, branch).astype(BF)
    logit_block = jnp.pad(logits[:docs, :CLASSES], ((0, 8 - docs), (0, 128 - CLASSES)))
    grad_inputs, all_logits, table, o_inner, o_outer, o_out, o_pool, o_query, o_key, o_value = attend_back(
        own_lens, rows, w_qkv, q, k, v, att, datt, lse, grad_pre, small_a, small_b, grad_b_inner, logit_block,
        [
            grad_inner_w.reshape(devices, share, hidden),
            grad_outer_w.reshape(devices, hidden_share, width),
            grad_out_w.reshape(devices, share, width),
            grad_pool.reshape(devices, share, width),
        ],
    )
    device = lax.axis_index("dp") * 4 + mine
    columns = lax.dynamic_slice_in_dim(table[:12], device * share, share, 1)
    own_b_inner = lax.dynamic_slice_in_dim(table[12:16].reshape(hidden), device * hidden_share, hidden_share, 0)
    return (
        layer_out,
        all_logits[:, :docs, :CLASSES],
        grad_inputs,
        o_query,
        columns[B_QUERY],
        o_key,
        o_value,
        columns[B_VALUE],
        o_out,
        columns[B_OUT],
        columns[GAIN1],
        columns[SHIFT1],
        o_inner,
        own_b_inner,
        o_outer,
        columns[B_OUTER],
        columns[GAIN2],
        columns[SHIFT2],
        o_pool,
        columns[B_POOL],
        columns[:CLASSES].T,
        table[16, :CLASSES],
    )


def solution(mesh):
    placed = (
        P("dp", "fsdp", None),
        P("dp", "fsdp", None),
        P("dp", None),
        P("dp", None),
        P(("dp", "fsdp"), None),
        P(("dp", "fsdp")),
        P(("dp", "fsdp"), None),
        P(("dp", "fsdp"), None),
        P(("dp", "fsdp")),
        P(("dp", "fsdp"), None),
        P(("dp", "fsdp")),
        P(("dp", "fsdp")),
        P(("dp", "fsdp")),
        P(("dp", "fsdp"), None),
        P(("dp", "fsdp")),
        P(("dp", "fsdp"), None),
        P(("dp", "fsdp")),
        P(("dp", "fsdp")),
        P(("dp", "fsdp")),
        P(("dp", "fsdp"), None),
        P(("dp", "fsdp")),
        P(("dp", "fsdp"), None),
        P(),
    )
    sizes = (mesh.shape["dp"], mesh.shape["fsdp"])
    chosen = fast_body if sizes == (8, 4) else general_body
    return jax.shard_map(
        chosen,
        mesh=mesh,
        in_specs=placed,
        out_specs=(
            P("dp", "fsdp", None),
            P("dp", None, None),
            P("dp", "fsdp", None),
            P(("dp", "fsdp"), None),
            P(("dp", "fsdp")),
            P(("dp", "fsdp"), None),
            P(("dp", "fsdp"), None),
            P(("dp", "fsdp")),
            P(("dp", "fsdp"), None),
            P(("dp", "fsdp")),
            P(("dp", "fsdp")),
            P(("dp", "fsdp")),
            P(("dp", "fsdp"), None),
            P(("dp", "fsdp")),
            P(("dp", "fsdp"), None),
            P(("dp", "fsdp")),
            P(("dp", "fsdp")),
            P(("dp", "fsdp")),
            P(("dp", "fsdp"), None),
            P(("dp", "fsdp")),
            P(("dp", "fsdp"), None),
            P(),
        ),
        check_vma=False,
    )
```

```python
import functools

import jax
import jax.numpy as jnp
from jax import lax
from jax.experimental import pallas as pl
from jax.experimental.pallas import tpu as pltpu
from jax.sharding import PartitionSpec as P

HEAD_DIM = 64
CLASSES = 3
MICRO = 4


def product(left_side, right_side):
    return jnp.dot(left_side, right_side, preferred_element_type=jnp.float32)


def contract_rows(left_side, right_side):
    return lax.dot_general(
        left_side, right_side, (((0,), (0,)), ((), ())), preferred_element_type=jnp.float32
    )


def times_transposed(left_side, right_side):
    return lax.dot_general(
        left_side, right_side, (((1,), (1,)), ((), ())), preferred_element_type=jnp.float32
    )


def layer_norm(values, norm_gain, norm_shift):
    average = jnp.mean(values, axis=-1, keepdims=True)
    centered = values - average
    variance = jnp.mean(centered * centered, axis=-1, keepdims=True)
    return centered * lax.rsqrt(variance + 1e-06) * norm_gain + norm_shift


def gelu_exact(values):
    return jax.nn.gelu(values, approximate=False)


def running_sum(lengths_rows):
    count = lengths_rows.shape[1]
    upper = jnp.arange(count)[:, None] <= jnp.arange(count)[None, :]
    return jnp.sum(jnp.where(upper[None], lengths_rows[:, :, None], 0), axis=1)


def segment_numbers(lengths_rows, places):
    doc_ends = running_sum(lengths_rows)
    above = (places[None, :, None] >= doc_ends[:, None, :]).astype(jnp.int32)
    return jnp.sum(above, axis=2)


def pair_heads(values):
    return values.reshape(values.shape[0], values.shape[1], 2, HEAD_DIM)


def pair_scores(query_pair, key_pair, same_doc):
    raw_scores = jnp.einsum(
        "bqhd,bkhd->bhqk", query_pair, key_pair, preferred_element_type=jnp.float32
    ) * HEAD_DIM ** (-0.5)
    return jnp.where(same_doc[:, None], raw_scores, -1000000000.0)


def lowered_masters(masters):
    return [member.astype(jnp.bfloat16) for member in masters]


def forward(tokens, lengths_rows, weights, bias_class):
    (
        w_query,
        b_query,
        w_key,
        w_value,
        b_value,
        w_out,
        b_out,
        first_gain,
        first_shift,
        w_inner,
        b_inner,
        w_outer,
        b_outer,
        second_gain,
        second_shift,
        w_pool,
        b_pool,
        w_class,
    ) = weights
    seq_count, local_len, model_width = tokens.shape
    doc_count = lengths_rows.shape[1]
    flat_rows = tokens.reshape(seq_count * local_len, model_width)
    queries = (
        (product(flat_rows, w_query) + b_query)
        .astype(jnp.bfloat16)
        .reshape(seq_count, local_len, model_width)
    )
    key_rows = (
        product(flat_rows, w_key).astype(jnp.bfloat16).reshape(seq_count, local_len, model_width)
    )
    value_rows = (
        (product(flat_rows, w_value) + b_value)
        .astype(jnp.bfloat16)
        .reshape(seq_count, local_len, model_width)
    )
    all_keys, all_values = (
        lax.all_gather(key_rows, "fsdp", axis=1, tiled=True),
        lax.all_gather(value_rows, "fsdp", axis=1, tiled=True),
    )
    full_len = all_keys.shape[1]
    own_places = lax.axis_index("fsdp") * local_len + jnp.arange(local_len, dtype=jnp.int32)
    key_places = jnp.arange(full_len, dtype=jnp.int32)
    same_doc = (
        segment_numbers(lengths_rows, own_places)[:, :, None]
        == segment_numbers(lengths_rows, key_places)[:, None, :]
    )
    pair_width = 2 * HEAD_DIM
    mixed_list = []
    log_totals = []
    for pair_index in range(model_width // pair_width):
        col_start = pair_index * pair_width
        query_pair = pair_heads(queries[:, :, col_start : col_start + pair_width])
        key_pair = pair_heads(all_keys[:, :, col_start : col_start + pair_width])
        value_pair = pair_heads(all_values[:, :, col_start : col_start + pair_width])
        scores = pair_scores(query_pair, key_pair, same_doc)
        row_peak = jnp.max(scores, axis=-1, keepdims=True)
        exp_total = jnp.sum(jnp.exp(scores - row_peak), axis=-1, keepdims=True)
        log_total = row_peak + jnp.log(exp_total)
        attn_probs = jnp.exp(scores - log_total).astype(jnp.bfloat16)
        mixed_pair = jnp.einsum(
            "bhqk,bkhd->bqhd", attn_probs, value_pair, preferred_element_type=jnp.float32
        )
        mixed_list.append(mixed_pair.reshape(seq_count, local_len, pair_width))
        log_totals.append(log_total)
    attended = (
        jnp.concatenate(mixed_list, axis=2)
        .astype(jnp.bfloat16)
        .reshape(seq_count * local_len, model_width)
    )
    branch = product(attended, w_out) + b_out
    pre_first = flat_rows.astype(jnp.float32) + branch
    normed = layer_norm(pre_first, first_gain.astype(jnp.float32), first_shift.astype(jnp.float32))
    normed_low = normed.astype(jnp.bfloat16)
    inner_pre = product(normed_low, w_inner) + b_inner
    activated = gelu_exact(inner_pre).astype(jnp.bfloat16)
    summed = normed + (product(activated, w_outer) + b_outer)
    result = layer_norm(summed, second_gain.astype(jnp.float32), second_shift.astype(jnp.float32))
    result_low = result.astype(jnp.bfloat16).reshape(seq_count, local_len, model_width)
    starts = running_sum(lengths_rows) - lengths_rows
    picker = (own_places[None, None, :] == starts[:, :, None]).astype(jnp.bfloat16)
    local_firsts = jnp.einsum(
        "bdl,blc->bdc", picker, result_low, preferred_element_type=jnp.float32
    )
    firsts = lax.psum(local_firsts, "fsdp")
    firsts_low = firsts.astype(jnp.bfloat16).reshape(seq_count * doc_count, model_width)
    pooled = jnp.tanh(product(firsts_low, w_pool) + b_pool)
    pooled_low = pooled.astype(jnp.bfloat16)
    logits = product(pooled_low, w_class) + bias_class
    stored = (
        flat_rows,
        queries,
        all_keys,
        all_values,
        same_doc,
        log_totals,
        attended,
        pre_first,
        summed,
        normed_low,
        inner_pre,
        activated,
        picker,
        firsts_low,
        pooled,
        pooled_low,
        logits,
    )
    return (result_low, logits.reshape(seq_count, doc_count, CLASSES), stored)


def backward(stored, weights, cot_rows, label_rows):
    (
        w_query,
        b_query,
        w_key,
        w_value,
        b_value,
        w_out,
        b_out,
        first_gain,
        first_shift,
        w_inner,
        b_inner,
        w_outer,
        b_outer,
        second_gain,
        second_shift,
        w_pool,
        b_pool,
        w_class,
    ) = weights
    (
        flat_rows,
        queries,
        all_keys,
        all_values,
        same_doc,
        log_totals,
        attended,
        pre_first,
        summed,
        normed_low,
        inner_pre,
        activated,
        picker,
        firsts_low,
        pooled,
        pooled_low,
        logits,
    ) = stored
    seq_count, local_len, model_width = queries.shape
    doc_count = picker.shape[1]
    owner_flag = (lax.axis_index("fsdp") == 0).astype(jnp.float32)
    row_peak = jnp.max(logits, axis=-1, keepdims=True)
    class_exp = jnp.exp(logits - row_peak)
    class_probs = class_exp / jnp.sum(class_exp, axis=-1, keepdims=True)
    onehot_labels = (
        label_rows.reshape(-1)[:, None] == jnp.arange(CLASSES, dtype=jnp.int32)[None, :]
    ).astype(jnp.float32)
    grad_logits = (class_probs - onehot_labels).astype(jnp.bfloat16)
    grad_b_class = owner_flag * jnp.sum(grad_logits.astype(jnp.float32), axis=0)
    grad_w_class = owner_flag * contract_rows(pooled_low, grad_logits)
    grad_pool_pre = (times_transposed(grad_logits, w_class) * (1.0 - pooled * pooled)).astype(
        jnp.bfloat16
    )
    grad_b_pool = owner_flag * jnp.sum(grad_pool_pre.astype(jnp.float32), axis=0)
    grad_w_pool = owner_flag * contract_rows(firsts_low, grad_pool_pre)
    grad_firsts = times_transposed(grad_pool_pre, w_pool).reshape(seq_count, doc_count, model_width)
    from_pool = jnp.einsum(
        "bdl,bdc->blc", picker.astype(jnp.float32), grad_firsts, precision=lax.Precision.HIGHEST
    )
    grad_result = cot_rows.astype(jnp.float32).reshape(-1, model_width) + from_pool.reshape(
        -1, model_width
    )
    second_back = jax.vjp(
        layer_norm, summed, second_gain.astype(jnp.float32), second_shift.astype(jnp.float32)
    )[1]
    grad_summed, grad_second_gain, grad_second_shift = second_back(grad_result)
    grad_outer = grad_summed.astype(jnp.bfloat16)
    grad_b_outer = jnp.sum(grad_outer.astype(jnp.float32), axis=0)
    grad_w_outer = contract_rows(activated, grad_outer)
    gelu_back = jax.vjp(gelu_exact, inner_pre)[1]
    grad_inner = gelu_back(times_transposed(grad_outer, w_outer))[0].astype(jnp.bfloat16)
    grad_b_inner = jnp.sum(grad_inner.astype(jnp.float32), axis=0)
    grad_w_inner = contract_rows(normed_low, grad_inner)
    grad_normed = grad_summed + times_transposed(grad_inner, w_inner)
    first_back = jax.vjp(
        layer_norm, pre_first, first_gain.astype(jnp.float32), first_shift.astype(jnp.float32)
    )[1]
    grad_pre_first, grad_first_gain, grad_first_shift = first_back(grad_normed)
    grad_branch = grad_pre_first.astype(jnp.bfloat16)
    grad_b_out = jnp.sum(grad_branch.astype(jnp.float32), axis=0)
    grad_w_out = contract_rows(attended, grad_branch)
    grad_attended = (
        times_transposed(grad_branch, w_out)
        .astype(jnp.bfloat16)
        .reshape(seq_count, local_len, model_width)
    )
    pair_width = 2 * HEAD_DIM
    query_list = []
    key_list = []
    value_list = []
    for pair_index in range(model_width // pair_width):
        col_start = pair_index * pair_width
        query_pair = pair_heads(queries[:, :, col_start : col_start + pair_width])
        key_pair = pair_heads(all_keys[:, :, col_start : col_start + pair_width])
        value_pair = pair_heads(all_values[:, :, col_start : col_start + pair_width])
        grad_pair = pair_heads(grad_attended[:, :, col_start : col_start + pair_width])
        scores = pair_scores(query_pair, key_pair, same_doc)
        attn_probs = jnp.exp(scores - log_totals[pair_index])
        grad_probs = jnp.einsum(
            "bqhd,bkhd->bhqk", grad_pair, value_pair, preferred_element_type=jnp.float32
        )
        row_dot = jnp.sum(attn_probs * grad_probs, axis=-1, keepdims=True)
        grad_scores = (attn_probs * (grad_probs - row_dot)).astype(jnp.bfloat16)
        query_part = jnp.einsum(
            "bhqk,bkhd->bqhd", grad_scores, key_pair, preferred_element_type=jnp.float32
        ) * HEAD_DIM ** (-0.5)
        query_list.append(query_part.reshape(seq_count, local_len, pair_width))
        probs_low = attn_probs.astype(jnp.bfloat16)
        key_part = jnp.einsum(
            "bhqk,bqhd->bkhd", grad_scores, query_pair, preferred_element_type=jnp.float32
        ) * HEAD_DIM ** (-0.5)
        value_part = jnp.einsum(
            "bhqk,bqhd->bkhd", probs_low, grad_pair, preferred_element_type=jnp.float32
        )
        key_list.append(key_part.reshape(seq_count, key_part.shape[1], pair_width))
        value_list.append(value_part.reshape(seq_count, value_part.shape[1], pair_width))
    key_partials = jnp.concatenate(key_list, axis=2)
    value_partials = jnp.concatenate(value_list, axis=2)
    own_keys, own_values = (
        lax.psum_scatter(
            key_partials.astype(jnp.bfloat16), "fsdp", scatter_dimension=1, tiled=True
        ).astype(jnp.float32),
        lax.psum_scatter(
            value_partials.astype(jnp.bfloat16), "fsdp", scatter_dimension=1, tiled=True
        ).astype(jnp.float32),
    )
    query_grad = jnp.concatenate(query_list, axis=2).astype(jnp.bfloat16).reshape(-1, model_width)
    key_grad = own_keys.astype(jnp.bfloat16).reshape(-1, model_width)
    value_grad = own_values.astype(jnp.bfloat16).reshape(-1, model_width)
    grad_w_query = contract_rows(flat_rows, query_grad)
    grad_b_query = jnp.sum(query_grad.astype(jnp.float32), axis=0)
    grad_w_key = contract_rows(flat_rows, key_grad)
    grad_w_value = contract_rows(flat_rows, value_grad)
    grad_b_value = jnp.sum(value_grad.astype(jnp.float32), axis=0)
    grad_tokens = (
        grad_pre_first
        + times_transposed(query_grad, w_query)
        + times_transposed(key_grad, w_key)
        + times_transposed(value_grad, w_value)
    )
    new_grads = (
        grad_w_query,
        grad_b_query,
        grad_w_key,
        grad_w_value,
        grad_b_value,
        grad_w_out,
        grad_b_out,
        grad_first_gain,
        grad_first_shift,
        grad_w_inner,
        grad_b_inner,
        grad_w_outer,
        grad_b_outer,
        grad_second_gain,
        grad_second_shift,
        grad_w_pool,
        grad_b_pool,
        grad_w_class,
    )
    return (
        new_grads,
        grad_b_class,
        grad_tokens.astype(jnp.bfloat16).reshape(seq_count, local_len, model_width),
    )


def general_body(
    inputs,
    cotangent,
    doc_lengths,
    labels,
    w_query,
    b_query,
    w_key,
    w_value,
    b_value,
    w_out,
    b_out,
    first_gain,
    first_shift,
    w_inner,
    b_inner,
    w_outer,
    b_outer,
    second_gain,
    second_shift,
    w_pool,
    b_pool,
    w_class,
    b_class,
):
    masters = (
        w_query,
        b_query,
        w_key,
        w_value,
        b_value,
        w_out,
        b_out,
        first_gain,
        first_shift,
        w_inner,
        b_inner,
        w_outer,
        b_outer,
        second_gain,
        second_shift,
        w_pool,
        b_pool,
        w_class,
    )
    group_size = lax.axis_size("dp") * lax.axis_size("fsdp")
    grad_sums = [
        jnp.zeros((member.shape[0] * group_size,) + member.shape[1:], jnp.float32)
        for member in masters
    ]
    class_sum = jnp.zeros((CLASSES,), jnp.float32)
    micro_seqs = inputs.shape[0] // MICRO
    out_list = []
    logit_list = []
    grad_list = []
    for micro_step in range(MICRO):
        first_seq = micro_step * micro_seqs
        after_seq = first_seq + micro_seqs
        tokens = inputs[first_seq:after_seq]
        lengths_rows = doc_lengths[first_seq:after_seq]
        pieces = lowered_masters(masters)
        front_weights = (
            lax.all_gather(pieces[0], ("dp", "fsdp"), axis=0, tiled=True),
            lax.all_gather(pieces[1], ("dp", "fsdp"), axis=0, tiled=True),
            lax.all_gather(pieces[2], ("dp", "fsdp"), axis=0, tiled=True),
            lax.all_gather(pieces[3], ("dp", "fsdp"), axis=0, tiled=True),
            lax.all_gather(pieces[4], ("dp", "fsdp"), axis=0, tiled=True),
            lax.all_gather(pieces[5], ("dp", "fsdp"), axis=0, tiled=True),
            lax.all_gather(pieces[6], ("dp", "fsdp"), axis=0, tiled=True),
            lax.all_gather(pieces[7], ("dp", "fsdp"), axis=0, tiled=True),
            lax.all_gather(pieces[8], ("dp", "fsdp"), axis=0, tiled=True),
            lax.all_gather(pieces[9], ("dp", "fsdp"), axis=0, tiled=True),
            lax.all_gather(pieces[10], ("dp", "fsdp"), axis=0, tiled=True),
            lax.all_gather(pieces[11], ("dp", "fsdp"), axis=0, tiled=True),
            lax.all_gather(pieces[12], ("dp", "fsdp"), axis=0, tiled=True),
            lax.all_gather(pieces[13], ("dp", "fsdp"), axis=0, tiled=True),
            lax.all_gather(pieces[14], ("dp", "fsdp"), axis=0, tiled=True),
            lax.all_gather(pieces[15], ("dp", "fsdp"), axis=0, tiled=True),
            lax.all_gather(pieces[16], ("dp", "fsdp"), axis=0, tiled=True),
            lax.all_gather(pieces[17], ("dp", "fsdp"), axis=0, tiled=True),
        )
        result_low, logits, stored = forward(tokens, lengths_rows, front_weights, b_class)
        out_list.append(result_low)
        logit_list.append(logits)
        back_weights = (
            lax.all_gather(pieces[0], ("dp", "fsdp"), axis=0, tiled=True),
            lax.all_gather(pieces[1], ("dp", "fsdp"), axis=0, tiled=True),
            lax.all_gather(pieces[2], ("dp", "fsdp"), axis=0, tiled=True),
            lax.all_gather(pieces[3], ("dp", "fsdp"), axis=0, tiled=True),
            lax.all_gather(pieces[4], ("dp", "fsdp"), axis=0, tiled=True),
            lax.all_gather(pieces[5], ("dp", "fsdp"), axis=0, tiled=True),
            lax.all_gather(pieces[6], ("dp", "fsdp"), axis=0, tiled=True),
            lax.all_gather(pieces[7], ("dp", "fsdp"), axis=0, tiled=True),
            lax.all_gather(pieces[8], ("dp", "fsdp"), axis=0, tiled=True),
            lax.all_gather(pieces[9], ("dp", "fsdp"), axis=0, tiled=True),
            lax.all_gather(pieces[10], ("dp", "fsdp"), axis=0, tiled=True),
            lax.all_gather(pieces[11], ("dp", "fsdp"), axis=0, tiled=True),
            lax.all_gather(pieces[12], ("dp", "fsdp"), axis=0, tiled=True),
            lax.all_gather(pieces[13], ("dp", "fsdp"), axis=0, tiled=True),
            lax.all_gather(pieces[14], ("dp", "fsdp"), axis=0, tiled=True),
            lax.all_gather(pieces[15], ("dp", "fsdp"), axis=0, tiled=True),
            lax.all_gather(pieces[16], ("dp", "fsdp"), axis=0, tiled=True),
            lax.all_gather(pieces[17], ("dp", "fsdp"), axis=0, tiled=True),
        )
        stored = forward(tokens, lengths_rows, back_weights, b_class)[2]
        new_grads, class_grad, grad_tokens = backward(
            stored, back_weights, cotangent[first_seq:after_seq], labels[first_seq:after_seq]
        )
        grad_sums = [running + fresh_grad for running, fresh_grad in zip(grad_sums, new_grads)]
        class_sum = class_sum + class_grad
        grad_list.append(grad_tokens)
    owned = (
        lax.psum_scatter(grad_sums[0], ("dp", "fsdp"), scatter_dimension=0, tiled=True),
        lax.psum_scatter(grad_sums[1], ("dp", "fsdp"), scatter_dimension=0, tiled=True),
        lax.psum_scatter(grad_sums[2], ("dp", "fsdp"), scatter_dimension=0, tiled=True),
        lax.psum_scatter(grad_sums[3], ("dp", "fsdp"), scatter_dimension=0, tiled=True),
        lax.psum_scatter(grad_sums[4], ("dp", "fsdp"), scatter_dimension=0, tiled=True),
        lax.psum_scatter(grad_sums[5], ("dp", "fsdp"), scatter_dimension=0, tiled=True),
        lax.psum_scatter(grad_sums[6], ("dp", "fsdp"), scatter_dimension=0, tiled=True),
        lax.psum_scatter(grad_sums[7], ("dp", "fsdp"), scatter_dimension=0, tiled=True),
        lax.psum_scatter(grad_sums[8], ("dp", "fsdp"), scatter_dimension=0, tiled=True),
        lax.psum_scatter(grad_sums[9], ("dp", "fsdp"), scatter_dimension=0, tiled=True),
        lax.psum_scatter(grad_sums[10], ("dp", "fsdp"), scatter_dimension=0, tiled=True),
        lax.psum_scatter(grad_sums[11], ("dp", "fsdp"), scatter_dimension=0, tiled=True),
        lax.psum_scatter(grad_sums[12], ("dp", "fsdp"), scatter_dimension=0, tiled=True),
        lax.psum_scatter(grad_sums[13], ("dp", "fsdp"), scatter_dimension=0, tiled=True),
        lax.psum_scatter(grad_sums[14], ("dp", "fsdp"), scatter_dimension=0, tiled=True),
        lax.psum_scatter(grad_sums[15], ("dp", "fsdp"), scatter_dimension=0, tiled=True),
        lax.psum_scatter(grad_sums[16], ("dp", "fsdp"), scatter_dimension=0, tiled=True),
        lax.psum_scatter(grad_sums[17], ("dp", "fsdp"), scatter_dimension=0, tiled=True),
    )
    class_total = lax.psum(class_sum, ("dp", "fsdp"))
    return (
        jnp.concatenate(out_list, axis=0),
        jnp.concatenate(logit_list, axis=0),
        jnp.concatenate(grad_list, axis=0),
        owned[0],
        owned[1],
        owned[2],
        owned[3],
        owned[4],
        owned[5],
        owned[6],
        owned[7],
        owned[8],
        owned[9],
        owned[10],
        owned[11],
        owned[12],
        owned[13],
        owned[14],
        owned[15],
        owned[16],
        owned[17],
        class_total,
    )


BF = jnp.bfloat16
F32 = jnp.float32
MESH = pl.DeviceIdType.MESH
ANY = pl.BlockSpec(memory_space=pl.ANY)
SMEM = pl.BlockSpec(memory_space=pltpu.SMEM)
ZS = 4
CLASS_ROWS, B_QUERY, B_VALUE, B_OUT, GAIN1, SHIFT1, B_OUTER, GAIN2, SHIFT2, B_POOL = (0, 3, 4, 5, 6, 7, 8, 9, 10, 11)
VEC_ROWS = 16


def nn(a, b):
    return lax.dot_general(a, b, (((1,), (0,)), ((), ())), preferred_element_type=F32)


def nt(a, b):
    return lax.dot_general(a, b, (((1,), (1,)), ((), ())), preferred_element_type=F32)


def tn(a, b):
    return lax.dot_general(a, b, (((0,), (0,)), ((), ())), preferred_element_type=F32)


def my_place():
    dp, fs = lax.axis_index("dp"), lax.axis_index("fsdp")
    return dp // 2, lax.rem(dp, 2), fs // 2, lax.rem(fs, 2)


def device_at(z, y, x, c):
    return (z * 2 + y, x * 2 + c)


def meet(partners):
    barrier = pltpu.get_barrier_semaphore()
    for partner in partners:
        pl.semaphore_signal(barrier, inc=1, device_id=partner, device_id_type=MESH)
    pl.semaphore_wait(barrier, len(partners))


def all_partners(z, y, x, c):
    found = [device_at(lax.rem(z + k, ZS), y, x, c) for k in range(1, ZS)]
    found.append(device_at(z, 1 - y, x, c))
    found.append(device_at(z, y, 1 - x, c))
    found.append(device_at(z, y, x, 1 - c))
    found.append(device_at(z, y, 1 - x, 1 - c))
    return found


def group_partner(k, x, c):
    return (1 - x if k >= 2 else x, 1 - c if k % 2 == 1 else c)


def doc_ends(lens_ref):
    ends = []
    total = 0
    for d in range(lens_ref.shape[0]):
        total = total + lens_ref[d]
        ends.append(total)
    return ends


def doc_numbers(places, ends):
    number = jnp.zeros(places.shape, jnp.int32)
    for end in ends:
        number = number + (places >= end).astype(jnp.int32)
    return number


GATHER_PIECES = (
    (1, 0, 1, "rows"), (0, 0, 2, "columns"), (0, 1, 2, "columns"), (3, 0, 2, "rows"), (3, 1, 2, "rows"), (2, 0, 1, "rows"),
)
GATHER_ORDERS = ("xy", "xy", "xy", "xy", "yx", "xy", "yx", "yx", "xy")
GATHER_PLAN = {
    -1: "b0 b1 b2 z0 b3 z1 b4 z2 z3 b5 f0 z4 b6 f1 s0 f2 e0",
    0: "s1 s2 f3 f4 z5 b7",
    1: "z6 e1 e2",
    2: "b8",
    3: "s3 z7",
    4: "z8 e3",
    6: "s4 f5 f6",
    8: "f7 s5 f8 e4",
    9: "e5",
    10: "s6 s8",
    11: "s7 e8 e6",
    12: "e7",
}
DENSE_ARRAYS = 4


def part_of(piece, block):
    _, which, count, along = piece
    rows, columns = block
    if along == "rows":
        return (which * (rows // count), rows // count), (0, columns)
    return (0, rows), (which * (columns // count), columns // count)


def attend_kernel(groups, *refs):
    lens_ref, tokens_ref, table_ref, wq_ref, wk_ref, wv_ref = refs[:6]
    shards = refs[6 : 6 + DENSE_ARRAYS]
    refs = refs[6 + DENSE_ARRAYS :]
    q_ref, k_ref, v_ref, att_ref, lse_ref, w_ref, vec_ref, rows_ref = refs[:8]
    wholes = refs[8 : 8 + DENSE_ARRAYS]
    refs = refs[8 + DENSE_ARRAYS :]
    x_ref, vt_ref, qkv_shard, qkv_ref, tab_ref, tab_in_ref = refs[:6]
    local_sem, row_send, row_recv, tab_send, tab_recv, send_sem, recv_sem = refs[6:13]
    own = refs[13 : 13 + DENSE_ARRAYS]
    length, width = q_ref.shape
    chunk = 256
    points = length // chunk
    heads = width // HEAD_DIM
    items = groups + len(GATHER_PIECES)
    group = pl.program_id(0)
    z, y, x, c = my_place()
    mine = x * 2 + c

    def row_copy(k):
        px, pc = group_partner(k, x, c)
        return pltpu.make_async_remote_copy(
            src_ref=tokens_ref.at[px * 2 + pc],
            dst_ref=x_ref.at[mine],
            send_sem=row_send.at[k - 1],
            recv_sem=row_recv.at[k - 1],
            device_id=device_at(z, y, px, pc),
            device_id_type=MESH,
        )

    def row_own():
        return pltpu.make_async_copy(tokens_ref.at[mine], x_ref.at[mine], local_sem.at[0])

    def rows_out():
        return pltpu.make_async_copy(x_ref, rows_ref, local_sem.at[1])

    def table_copy(level):
        if level < 3:
            source, device = tab_ref.at[0], device_at(lax.rem(z + level + 1, ZS), y, x, c)
        else:
            source = tab_ref.at[level - 2]
            device = (device_at(z, y, 1 - x, c), device_at(z, 1 - y, x, c), device_at(z, y, x, 1 - c))[level - 3]
        return pltpu.make_async_remote_copy(
            src_ref=source,
            dst_ref=tab_in_ref.at[level],
            send_sem=tab_send.at[level],
            recv_sem=tab_recv.at[level],
            device_id=device,
            device_id_type=MESH,
        )

    def array_of(a):
        if a < groups:
            return qkv_ref.at[a], qkv_shard.at[a], None
        piece = GATHER_PIECES[a - groups]
        return wholes[piece[0]], own[piece[0]], part_of(piece, own[piece[0]].shape)

    def view(a, where):
        ref, _, part = array_of(a)
        if part is None:
            return ref.at[where]
        (r0, rows), (c0, columns) = part
        return ref.at[where + (pl.ds(r0, rows), pl.ds(c0, columns))]

    def own_block(a):
        _, ref, part = array_of(a)
        if part is None:
            return ref
        (r0, rows), (c0, columns) = part
        return ref.at[pl.ds(r0, rows), pl.ds(c0, columns)]

    everything = slice(None)

    def along(a, axis):
        return device_at(z, 1 - y, x, c) if GATHER_ORDERS[a][axis] == "y" else device_at(z, y, 1 - x, c)

    def copy_of(a, number):
        core = device_at(z, y, x, 1 - c)
        first_other = (1 - y, x) if GATHER_ORDERS[a][0] == "y" else (y, 1 - x)
        if number < 3:
            source, target = own_block(a), view(a, (z, y, x, c))
            device = device_at(lax.rem(z + number + 1, ZS), y, x, c)
        elif number < 6:
            source = target = view(a, (everything, y, x, c))
            device = (along(a, 0), along(a, 1), core)[number - 3]
        elif number < 8:
            source = target = view(a, (everything, first_other[0], first_other[1], c))
            device = along(a, 1) if number == 6 else core
        else:
            if GATHER_ORDERS[a][1] == "y":
                source = target = view(a, (everything, 1 - y, everything, c))
            else:
                source = target = view(a, (everything, everything, 1 - x, c))
            device = core
        return pltpu.make_async_remote_copy(
            src_ref=source,
            dst_ref=target,
            send_sem=send_sem.at[a, number],
            recv_sem=recv_sem.at[a, number],
            device_id=device,
            device_id_type=MESH,
        )

    def keep(a):
        return pltpu.make_async_copy(own_block(a), view(a, (z, y, x, c)), local_sem.at[2 + a])

    def take_up(point):
        for word in GATHER_PLAN.get(point, "").split():
            kind, a = word[0], int(word[1:])
            if kind == "b":
                for number in (1, 0, 2):
                    copy_of(a, number).start()
                keep(a).start()
            elif kind == "z":
                for number in (0, 1, 2):
                    copy_of(a, number).wait_recv()
                keep(a).wait()
                for number in (3, 4, 5):
                    copy_of(a, number).start()
            elif kind == "f":
                copy_of(a, 3).wait_recv()
                for number in (6, 7):
                    copy_of(a, number).start()
            elif kind == "s":
                copy_of(a, 4).wait_recv()
                copy_of(a, 6).wait_recv()
                copy_of(a, 8).start()
            else:
                for number in (5, 7, 8):
                    copy_of(a, number).wait_recv()

    @pl.when(group == 0)
    def _():
        tab_ref[0] = table_ref[...]
        for g in range(groups):
            for j, ref in enumerate((wq_ref, wk_ref, wv_ref)):
                qkv_shard[g, :, j * width : (j + 1) * width] = ref[:, g * width : (g + 1) * width].astype(BF)
        for target, ref in zip(own, shards):
            target[...] = ref[...].astype(BF)
        meet(all_partners(z, y, x, c))
        for level in (1, 0, 2):
            table_copy(level).start()
        for k in (3, 2, 1):
            row_copy(k).start()
        row_own().start()
        take_up(-1)
        for level in (0, 1, 2):
            table_copy(level).wait_recv()
        tab_ref[1] = (tab_ref[0] + tab_in_ref[0]) + (tab_in_ref[1] + tab_in_ref[2])
        for level in (3, 4, 5):
            table_copy(level).start()
            table_copy(level).wait_recv()
            tab_ref[level - 1] = tab_ref[level - 2] + tab_in_ref[level]
        vec_ref[...] = tab_ref[4]
        row_own().wait()
        for k in (1, 2, 3):
            row_copy(k).wait_recv()
        rows_out().start()

    tokens = x_ref[...].reshape(length, x_ref.shape[2])
    weights = qkv_ref[group].astype(F32).reshape(x_ref.shape[2], 3 * width).astype(BF)
    w_ref[...] = weights
    bias = tab_ref[4, B_QUERY : B_QUERY + 2, pl.ds(pl.multiple_of(group * width, width), width)]
    q_ref[...] = (nn(tokens, weights[:, :width]) + bias[0:1]).astype(BF)
    k_ref[...] = nn(tokens, weights[:, width : 2 * width]).astype(BF)
    values = (nn(tokens, weights[:, 2 * width :]) + bias[1:2]).astype(BF)
    v_ref[...] = values
    vt_ref[...] = values.astype(F32).T.astype(BF)
    ends = doc_ends(lens_ref)
    key_doc = doc_numbers(lax.broadcasted_iota(jnp.int32, (length, 1), 0), ends)
    lane_head = lax.broadcasted_iota(jnp.int32, (1, width), 1) // HEAD_DIM

    def step(i, carry):
        for point in range(groups * points):
            if point in GATHER_PLAN:

                @pl.when((group == point // points) & (i == point % points))
                def _(point=point):
                    take_up(point)

        at = pl.multiple_of(i * chunk, chunk)
        query_doc = doc_numbers(lax.broadcasted_iota(jnp.int32, (1, chunk), 1) + at, ends)
        scaled = q_ref[pl.ds(at, chunk), :] * jnp.asarray(0.125, BF)
        mixed = []
        for h in range(heads):
            own_q = jnp.where(lane_head == h, scaled, jnp.zeros_like(scaled))
            blocks = []
            for s in range(0, length, chunk):
                scores = nt(k_ref[s : s + chunk, :], own_q)
                blocks.append(jnp.where(key_doc[s : s + chunk] == query_doc, scores, -1000000000.0))
            peak = functools.reduce(jnp.maximum, [jnp.max(b, axis=0, keepdims=True) for b in blocks])
            exps = [jnp.exp(b - peak) for b in blocks]
            total = functools.reduce(jnp.add, [jnp.sum(e, axis=0, keepdims=True) for e in exps])
            scale = 1.0 / total
            probs = jnp.concatenate([(e * scale).astype(BF) for e in exps], axis=0)
            mixed.append(nn(vt_ref[h * HEAD_DIM : (h + 1) * HEAD_DIM, :], probs))
            lse_ref[0, h : h + 1, pl.ds(at, chunk)] = peak + jnp.log(total)
        att_ref[pl.ds(at, chunk), :] = jnp.concatenate(mixed, axis=0).T.astype(BF)
        return carry

    lax.fori_loop(0, points, step, 0)

    @pl.when(group == groups - 1)
    def _():
        take_up(groups * points)
        for a in range(items):
            for number in range(9):
                copy_of(a, number).wait_send()
        for level in range(6):
            table_copy(level).wait_send()
        for k in range(1, 4):
            row_copy(k).wait_send()
        rows_out().wait()


def attend(lens, tokens, table, qkv_shards, shards):
    seqs, local_len, width = tokens.shape
    length = seqs * local_len
    group = 256
    groups = width // group
    share = qkv_shards[0].shape[0]
    hbm = pl.BlockSpec(memory_space=pl.ANY)
    part = pl.BlockSpec((length, group), lambda g: (0, g))
    once = pl.Buffered(buffer_count=1)
    items = groups + len(GATHER_PIECES)

    def fixed(shape):
        return pl.BlockSpec(shape, lambda g: (0,) * len(shape), pipeline_mode=once)

    lead = (ZS, 2, 2, 2)
    return pl.pallas_call(
        functools.partial(attend_kernel, groups),
        grid=(groups,),
        out_shape=[jax.ShapeDtypeStruct((length, width), BF)] * 4
        + [
            jax.ShapeDtypeStruct((groups, 8, length), F32),
            jax.ShapeDtypeStruct((width, 3 * width), BF),
            jax.ShapeDtypeStruct((VEC_ROWS, width), F32),
            jax.ShapeDtypeStruct(tokens.shape, BF),
        ]
        + [jax.ShapeDtypeStruct(lead + s.shape, BF) for s in shards],
        in_specs=[SMEM, hbm, fixed(table.shape)]
        + [fixed(s.shape) for s in qkv_shards]
        + [fixed(s.shape) for s in shards],
        out_specs=[part] * 4
        + [
            pl.BlockSpec((1, 8, length), lambda g: (g, 0, 0)),
            pl.BlockSpec((width, 3 * group), lambda g: (0, g)),
            pl.BlockSpec((VEC_ROWS, width), lambda g: (0, 0)),
            hbm,
        ]
        + [hbm] * DENSE_ARRAYS,
        scratch_shapes=[
            pltpu.VMEM(tokens.shape, BF),
            pltpu.VMEM((group, length), BF),
            pltpu.VMEM((groups, share, 3 * group), BF),
            pltpu.VMEM((groups,) + lead + (share, 3 * group), BF),
            pltpu.VMEM((5, VEC_ROWS, width), F32),
            pltpu.VMEM((6, VEC_ROWS, width), F32),
            pltpu.SemaphoreType.DMA((2 + items,)),
            pltpu.SemaphoreType.DMA((3,)),
            pltpu.SemaphoreType.DMA((3,)),
            pltpu.SemaphoreType.DMA((6,)),
            pltpu.SemaphoreType.DMA((6,)),
            pltpu.SemaphoreType.DMA((items, 9)),
            pltpu.SemaphoreType.DMA((items, 9)),
        ]
        + [pltpu.VMEM(s.shape, BF) for s in shards],
        compiler_params=pltpu.CompilerParams(
            collective_id=1, has_side_effects=True, vmem_limit_bytes=48 * 2**20
        ),
        name="attend",
    )(lens, tokens, table, *qkv_shards, *shards)


DENSE = 4
DENSE_ITEMS = (
    (2, 0, 1, "rows", "yx"), (3, 0, 1, "rows", "xy"),
    (0, 0, 2, "columns", "yx"), (1, 0, 2, "rows", "xy"), (0, 1, 2, "columns", "yx"), (1, 1, 2, "rows", "xy"),
)
GROUP_ORDERS = ("yx", "xy", "yx")
SCATTER_PLAN = {
    -1: "b0",
    0: "b1",
    1: "c00 c01 b2 c10 c11",
    2: "b3",
    3: "c02 b4 c12 f0 f1 c03 c13 b5",
    4: "s0 s1 b6",
    5: "c04 c05 c14 c15",
    6: "z0 z1",
    7: "f2 f3",
    8: "b7",
    9: "c06 c07 c16 c17",
    10: "f4 s2 s3",
    11: "f5",
    12: "b8 dx f6 f7 t0 s4 s5 z2 c08 c18 z3 t1 s7 s6 f8 t2 z7 s8 z4 z6 z5 t3 z8",
}
PIECES = len(DENSE_ITEMS)


def order_of(a):
    return DENSE_ITEMS[a][4] if a < PIECES else GROUP_ORDERS[a - PIECES]


def cut_of(a, block):
    _, which, count, along, _ = DENSE_ITEMS[a]
    rows, columns = block
    if along == "rows":
        return (which * (rows // count), rows // count), (0, columns)
    return (0, rows), (which * (columns // count), columns // count)


TABLE_ROWS = 24


def attend_back_kernel(groups, *refs):
    items = PIECES + groups
    lens_ref, x_ref, w_ref, q_ref, k_ref, v_ref, att_ref, datt_ref, lse_ref, start_ref = refs[:10]
    small_a_ref, small_b_ref, bi_ref, logit_ref = refs[10:14]
    parts = refs[14 : 14 + DENSE]
    back_ref, logits_ref, table_ref = refs[18:21]
    dense_outs, (out_q, out_k, out_v) = refs[21 : 21 + DENSE], refs[21 + DENSE : 24 + DENSE]
    rest = refs[24 + DENSE :]
    xt_ref, kt_ref, dot_ref, dq_ref, dk_ref, dv_ref, acc_ref, dx_ref, bias_ref, dw_ref, tab_ref, tab_in_ref = rest[:12]
    local_sem, row_send, row_recv, tab_send, tab_recv, send_sem, recv_sem = rest[12:19]
    rest = rest[19:]
    keeps, rest = rest[:PIECES], rest[PIECES:]
    firsts, seconds, thirds, fourths = (rest[j * items : (j + 1) * items] for j in range(4))

    length, width = q_ref.shape
    chunk = 256
    points = length // chunk
    heads = width // HEAD_DIM
    group = pl.program_id(0)
    z, y, x, c = my_place()
    mine = x * 2 + c

    def axes(a):
        return (y, x) if order_of(a)[0] == "y" else (x, y)

    def device_along(axis):
        return device_at(z, 1 - y, x, c) if axis == "y" else device_at(z, y, 1 - x, c)

    def half(a, ref, place):
        return ref.at[:, place] if order_of(a)[0] == "y" else ref.at[:, :, place]

    def whole_of(a, core):
        if a >= PIECES:
            return dw_ref.at[a - PIECES].at[:, :, :, core]
        array = DENSE_ITEMS[a][0]
        (r0, rows), (c0, columns) = cut_of(a, parts[array].shape[-2:])
        return parts[array].at[:, :, :, core, pl.ds(r0, rows), pl.ds(c0, columns)]

    def kept(a):
        return keeps[a] if a < PIECES else whole_of(a, c)

    def load(a, turn):
        place = 1 - axes(a)[0] if turn == 0 else axes(a)[0]
        return pltpu.make_async_copy(
            half(a, whole_of(a, c), place), half(a, keeps[a], place), local_sem.at[a, turn]
        )

    def copy_of(a, number):
        at, other = axes(a)
        if number < 2:
            place = 1 - at if number == 0 else at
            source, target = half(a, whole_of(a, 1 - c), place), half(a, firsts[a], place)
            device = device_at(z, y, x, 1 - c)
        elif number == 2:
            source, target = half(a, kept(a), 1 - at), seconds[a]
            device = device_along(order_of(a)[0])
        elif number == 3:
            source, target = half(a, kept(a), at).at[:, 1 - other], thirds[a]
            device = device_along(order_of(a)[1])
        else:
            there = lax.rem(z + number - 3, ZS)
            source, target = half(a, kept(a), at).at[:, other].at[there], fourths[a].at[number - 4]
            device = device_at(there, y, x, c)
        return pltpu.make_async_remote_copy(
            src_ref=source,
            dst_ref=target,
            send_sem=send_sem.at[a, number],
            recv_sem=recv_sem.at[a, number],
            device_id=device,
            device_id_type=MESH,
        )

    def add_into(target, source):
        lead = target.shape[:-2]
        total = functools.reduce(lambda p, q: p * q, lead, 1)

        def step(i, carry):
            where = []
            for size in reversed(lead):
                where.append(lax.rem(i, size))
                i = i // size
            where = tuple(reversed(where))
            target[where] = target[where] + source[where]
            return carry

        lax.fori_loop(0, total, step, 0)

    def begin(a):
        if a < PIECES:
            load(a, 0).start()
            load(a, 1).start()
        copy_of(a, 0).start()
        copy_of(a, 1).start()

    def after_core(a, turn):
        place = 1 - axes(a)[0] if turn == 0 else axes(a)[0]
        if a < PIECES:
            load(a, turn).wait()
        copy_of(a, turn).wait_recv()
        add_into(half(a, kept(a), place), half(a, firsts[a], place))
        if turn == 0:
            copy_of(a, 2).start()

    def after_first(a):
        at, other = axes(a)
        ours = half(a, kept(a), at)
        copy_of(a, 2).wait_recv()
        add_into(ours.at[:, 1 - other], seconds[a].at[:, 1 - other])
        copy_of(a, 3).start()
        add_into(ours.at[:, other], seconds[a].at[:, other])

    def after_second(a):
        at, other = axes(a)
        copy_of(a, 3).wait_recv()
        add_into(half(a, kept(a), at).at[:, other], thirds[a])
        for number in (5, 4, 6):
            copy_of(a, number).start()

    def finish(a):
        at, other = axes(a)
        for number in (4, 5, 6):
            copy_of(a, number).wait_recv()
        ours = half(a, kept(a), at).at[:, other]
        total = (
            ours[z].astype(F32)
            + fourths[a][0].astype(F32)
            + fourths[a][1].astype(F32)
            + fourths[a][2].astype(F32)
        )
        if a < PIECES:
            out = dense_outs[DENSE_ITEMS[a][0]]
            (r0, rows), (c0, columns) = cut_of(a, out.shape)
            out[r0 : r0 + rows, c0 : c0 + columns] = total
        else:
            s = (a - PIECES) * width
            for j, out in enumerate((out_q, out_k, out_v)):
                out[:, s : s + width] = total[:, j * width : (j + 1) * width]

    def row_copy(which, k):
        px, pc = group_partner(k, x, c)
        if which == 0:
            source, target = dx_ref.at[px * 2 + pc], back_ref.at[mine]
        else:
            source, target = logit_ref, logits_ref.at[mine]
        return pltpu.make_async_remote_copy(
            src_ref=source,
            dst_ref=target,
            send_sem=row_send.at[which, k - 1],
            recv_sem=row_recv.at[which, k - 1],
            device_id=device_at(z, y, px, pc),
            device_id_type=MESH,
        )

    def row_own(which):
        if which == 0:
            source, target = dx_ref.at[mine], back_ref.at[mine]
        else:
            source, target = logit_ref, logits_ref.at[mine]
        return pltpu.make_async_copy(source, target, local_sem.at[PIECES, which])

    def table_copy(level):
        if level < 3:
            source, target = tab_ref.at[level], tab_in_ref.at[level]
            device = (
                device_at(z, y, x, 1 - c), device_at(z, 1 - y, x, c), device_at(z, y, 1 - x, c)
            )[level]
        else:
            source, target = tab_ref.at[3], tab_in_ref.at[3 + z]
            device = device_at(lax.rem(z + level - 2, ZS), y, x, c)
        return pltpu.make_async_remote_copy(
            src_ref=source,
            dst_ref=target,
            send_sem=tab_send.at[level],
            recv_sem=tab_recv.at[level],
            device_id=device,
            device_id_type=MESH,
        )

    def table_wait(level):
        if level < 3:
            table_copy(level).wait_recv()
        else:
            slot = tab_in_ref.at[3 + lax.rem(z + ZS - (level - 2), ZS)]
            pltpu.make_async_remote_copy(
                src_ref=slot,
                dst_ref=slot,
                send_sem=tab_send.at[level],
                recv_sem=tab_recv.at[level],
                device_id=device_at(lax.rem(z + level - 2, ZS), y, x, c),
                device_id_type=MESH,
            ).wait_recv()

    def table_level(level):
        if level == 3:
            for last in (3, 4, 5):
                table_wait(last)
            table_ref[...] = (tab_in_ref[3] + tab_in_ref[4]) + (tab_in_ref[5] + tab_in_ref[6])
            return
        table_wait(level)
        tab_ref[level + 1] = tab_ref[level] + tab_in_ref[level]
        if level < 2:
            table_copy(level + 1).start()
        else:
            tab_in_ref[3 + z] = tab_ref[3]
            for nxt in (4, 3, 5):
                table_copy(nxt).start()

    def take_up(point):
        for word in SCATTER_PLAN.get(point, "").split():
            kind, a = word[:-1], int(word[-1]) if word != "dx" else 0
            if kind == "b":
                begin(a)
            elif kind == "c0" or kind == "c1":
                after_core(a, int(kind[1]))
            elif kind == "f":
                after_first(a)
            elif kind == "s":
                after_second(a)
            elif kind == "z":
                finish(a)
            elif kind == "t":
                table_level(a)
            else:
                for k in (3, 2, 1):
                    row_copy(0, k).start()
                row_own(0).start()

    @pl.when(group == 0)
    def _():
        meet(all_partners(z, y, x, c))
        take_up(-1)
        for k in range(1, 4):
            row_copy(1, k).start()
        row_own(1).start()
        xt_ref[...] = x_ref[...].astype(F32).T.astype(BF)
        acc_ref[...] = start_ref[...]

    kt_ref[...] = k_ref[...].astype(F32).T.astype(BF)
    dot_ref[...] = (datt_ref[...].astype(F32) * att_ref[...].astype(F32)).T
    dk_ref[...] = jnp.zeros_like(dk_ref)
    dv_ref[...] = jnp.zeros_like(dv_ref)
    ends = doc_ends(lens_ref)
    key_doc = doc_numbers(lax.broadcasted_iota(jnp.int32, (length, 1), 0), ends)
    lane_head = lax.broadcasted_iota(jnp.int32, (1, width), 1) // HEAD_DIM

    def step(i, carry):
        for point in range(groups * points):

            @pl.when((group == point // points) & (i == point % points))
            def _(point=point):
                take_up(point)

        at = pl.multiple_of(i * chunk, chunk)
        query_doc = doc_numbers(lax.broadcasted_iota(jnp.int32, (1, chunk), 1) + at, ends)
        scaled = q_ref[pl.ds(at, chunk), :] * jnp.asarray(0.125, BF)
        given = datt_ref[pl.ds(at, chunk), :]
        own_q = [jnp.where(lane_head == h, scaled, jnp.zeros_like(scaled)) for h in range(heads)]
        own_d = [jnp.where(lane_head == h, given, jnp.zeros_like(given)) for h in range(heads)]
        all_probs = [[] for _ in range(length // chunk)]
        all_grads = [[] for _ in range(length // chunk)]
        for h in range(heads):
            lse = lse_ref[0, h : h + 1, pl.ds(at, chunk)]
            dots = jnp.sum(
                dot_ref[h * HEAD_DIM : (h + 1) * HEAD_DIM, pl.ds(at, chunk)], axis=0, keepdims=True
            )
            for j in range(length // chunk):
                s = j * chunk
                scores = nt(k_ref[s : s + chunk, :], own_q[h])
                scores = jnp.where(key_doc[s : s + chunk] == query_doc, scores, -1000000000.0)
                probs = jnp.exp(scores - lse)
                grad_probs = nt(v_ref[s : s + chunk, :], own_d[h])
                all_grads[j].append((probs * (grad_probs - dots)).astype(BF))
                all_probs[j].append(probs.astype(BF))
        stacked_q = jnp.concatenate(own_q, axis=0)
        stacked_d = jnp.concatenate(own_d, axis=0)
        for j in range(length // chunk):
            s = j * chunk
            dk_ref[s : s + chunk, :] += nn(jnp.concatenate(all_grads[j], axis=1), stacked_q)
            dv_ref[s : s + chunk, :] += nn(jnp.concatenate(all_probs[j], axis=1), stacked_d)
        mixed = []
        for h in range(heads):
            column = jnp.concatenate([all_grads[j][h] for j in range(length // chunk)], axis=0)
            mixed.append(nn(kt_ref[h * HEAD_DIM : (h + 1) * HEAD_DIM, :], column))
        dq_ref[pl.ds(at, chunk), :] = (jnp.concatenate(mixed, axis=0).T * 0.125).astype(BF)
        return carry

    lax.fori_loop(0, points, step, 0)
    xt = xt_ref[...]
    grads = (dq_ref[...], dk_ref[...].astype(BF), dv_ref[...].astype(BF))
    block = dw_ref.shape[1:6]
    for j, grad in enumerate(grads):
        dw_ref[group, :, :, :, :, :, j * width : (j + 1) * width] = nn(xt, grad).reshape(block + (width,)).astype(BF)
    bias_ref[group, 0:1, :] = jnp.sum(grads[0].astype(F32), axis=0, keepdims=True)
    bias_ref[group, 1:2, :] = jnp.sum(grads[2].astype(F32), axis=0, keepdims=True)
    total = acc_ref[...]
    for j, grad in enumerate(grads):
        total = total + nt(grad, w_ref[:, j * width : (j + 1) * width])
    acc_ref[...] = total

    @pl.when(group == groups - 1)
    def _():
        dx_ref[...] = acc_ref[...].reshape(dx_ref.shape).astype(BF)
        tab_ref[0, 0:CLASSES] = small_a_ref[0:CLASSES]
        for g in range(groups):
            tab_ref[0, B_QUERY : B_QUERY + 2, g * width : (g + 1) * width] = bias_ref[g, 0:2, :]
        for row, (ref, at) in {
            B_OUT: (small_b_ref, 3), GAIN1: (small_b_ref, 4), SHIFT1: (small_b_ref, 5), B_OUTER: (small_b_ref, 0),
            GAIN2: (small_b_ref, 1), SHIFT2: (small_b_ref, 2), B_POOL: (small_a_ref, 16), 16: (small_a_ref, 17),
        }.items():
            tab_ref[0, row : row + 1] = ref[at : at + 1, :]
        full = small_a_ref.shape[1]
        for j in range(4):
            tab_ref[0, 12 + j : 13 + j] = bi_ref[:, j * full : (j + 1) * full]
        tab_ref[0, 17:TABLE_ROWS] = jnp.zeros((TABLE_ROWS - 17, full), F32)
        table_copy(0).start()
        take_up(groups * points)
        for a in range(items):
            for number in range(7):
                copy_of(a, number).wait_send()
        for level in range(6):
            table_copy(level).wait_send()
        for which in (0, 1):
            for k in range(1, 4):
                row_copy(which, k).wait_recv()
                row_copy(which, k).wait_send()
            row_own(which).wait()


def attend_back(lens, rows, w_groups, q, k, v, att, datt, lse, grad_pre, small_a, small_b, grad_b_inner, logit_block, parts):
    length, width = rows.shape
    group = 256
    groups = width // group
    local_len = length // 4
    share = width // (8 * ZS)
    once = pl.Buffered(buffer_count=1)
    whole = pl.BlockSpec((length, width), lambda g: (0, 0), pipeline_mode=once)
    part = pl.BlockSpec((length, group), lambda g: (0, g))
    blocks = [p.shape[1:] for p in parts]
    split = [p.reshape((ZS, 2, 2, 2) + b) for p, b in zip(parts, blocks)]
    shapes = [r for r in blocks]
    cuts = [cut_of(a, blocks[DENSE_ITEMS[a][0]]) for a in range(PIECES)]
    blocks = [(r[1], q[1]) for r, q in cuts] + [(share, 3 * group)] * groups
    hbm = pl.BlockSpec(memory_space=pl.ANY)

    def fixed(shape):
        return pl.BlockSpec(shape, lambda g: (0,) * len(shape))

    results = shapes + [(share, width)] * 3
    arriving = []
    for lead in ((ZS, 2, 2), (ZS, 2), (ZS,), (ZS - 1,)):
        arriving += [pltpu.VMEM(lead + b, BF) for b in blocks]
    items = len(blocks)
    return pl.pallas_call(
        functools.partial(attend_back_kernel, groups),
        grid=(groups,),
        out_shape=[
            jax.ShapeDtypeStruct((4, local_len, width), BF),
            jax.ShapeDtypeStruct((4,) + logit_block.shape, F32),
            jax.ShapeDtypeStruct((TABLE_ROWS, width), F32),
        ]
        + [jax.ShapeDtypeStruct(r, F32) for r in results],
        in_specs=[
            SMEM,
            whole,
            pl.BlockSpec((width, 3 * group), lambda g: (0, g)),
            part, part, part, part, part,
            pl.BlockSpec((1, 8, length), lambda g: (g, 0, 0)),
            whole,
            fixed(small_a.shape), fixed(small_b.shape), fixed(grad_b_inner.shape), hbm,
        ]
        + [hbm] * DENSE,
        out_specs=[hbm, hbm, fixed((TABLE_ROWS, width))] + [fixed(r) for r in results],
        scratch_shapes=[
            pltpu.VMEM((width, length), BF),
            pltpu.VMEM((group, length), BF),
            pltpu.VMEM((group, length), F32),
            pltpu.VMEM((length, group), BF),
            pltpu.VMEM((length, group), F32),
            pltpu.VMEM((length, group), F32),
            pltpu.VMEM((length, width), F32),
            pltpu.VMEM((4, local_len, width), BF),
            pltpu.VMEM((groups, 8, group), F32),
            pltpu.VMEM((groups, ZS, 2, 2, 2, share, 3 * group), BF),
            pltpu.VMEM((4, TABLE_ROWS, width), F32),
            pltpu.VMEM((3 + ZS, TABLE_ROWS, width), F32),
            pltpu.SemaphoreType.DMA((PIECES + 1, 2)),
            pltpu.SemaphoreType.DMA((2, 3)),
            pltpu.SemaphoreType.DMA((2, 3)),
            pltpu.SemaphoreType.DMA((6,)),
            pltpu.SemaphoreType.DMA((6,)),
            pltpu.SemaphoreType.DMA((items, 7)),
            pltpu.SemaphoreType.DMA((items, 7)),
        ]
        + [pltpu.VMEM((ZS, 2, 2) + b, BF) for b in blocks[:PIECES]]
        + arriving,
        compiler_params=pltpu.CompilerParams(
            collective_id=2, has_side_effects=True, vmem_limit_bytes=60 * 2**20
        ),
        name="attend_back",
    )(lens, rows, w_groups, q, k, v, att, datt, lse, grad_pre, small_a, small_b, grad_b_inner, logit_block, *split)


def normal_parts(v):
    bell = jnp.exp(v * v * -0.5)
    t = 1.0 / (1.0 + jnp.abs(v) * 0.23164189)
    tail = t * (0.127414796 + t * (-0.142248368 + t * (0.710706870 + t * (-0.726576013 + t * 0.530702714)))) * bell
    return jnp.where(v >= 0.0, 1.0 - tail, tail), bell


def centered_parts(values):
    average = jnp.mean(values, axis=-1, keepdims=True)
    centered = values - average
    variance = jnp.mean(centered * centered, axis=-1, keepdims=True)
    inverse = lax.rsqrt(variance + 1e-06)
    return centered * inverse, inverse


def dense_kernel(
    lens_ref, labels_ref, x_ref, att_ref, w_inner_ref, w_out_ref, w_pool_ref, w_outer_ref, vec_ref, b_inner_ref, b_class_ref,
    pre_ref, summed_ref, low_ref, act_ref, dact_ref, lo_ref, dpool_ref, first_ref, small_ref, logits_ref, picked_ref,
):
    step = pl.program_id(0)
    rows = x_ref.shape[0]
    hidden = w_inner_ref.shape[1]
    chunk = 512

    def vec(row):
        return vec_ref[row : row + 1, :]

    pre = x_ref[...].astype(F32) + (nn(att_ref[...], w_out_ref[...]) + vec(B_OUT))
    pre_ref[...] = pre
    normed = centered_parts(pre)[0] * vec(GAIN1) + vec(SHIFT1)
    low = normed.astype(BF)
    low_ref[...] = low
    total = normed + vec(B_OUTER)
    for s in range(0, hidden, chunk):
        inner = nn(low, w_inner_ref[:, s : s + chunk]) + b_inner_ref[:, s : s + chunk]
        phi, bell = normal_parts(inner)
        activated = (inner * phi).astype(BF)
        act_ref[:, s : s + chunk] = activated
        dact_ref[:, s : s + chunk] = (phi + inner * bell * 0.3989422804014327).astype(BF)
        total = total + nn(activated, w_outer_ref[s : s + chunk, :])
    summed_ref[...] = total
    result = (centered_parts(total)[0] * vec(GAIN2) + vec(SHIFT2)).astype(BF)
    lo_ref[...] = result
    ends = doc_ends(lens_ref)
    docs = len(ends)
    places = lax.broadcasted_iota(jnp.int32, (VEC_ROWS, rows), 1) + step * rows
    row_doc = lax.broadcasted_iota(jnp.int32, (VEC_ROWS, rows), 0)
    hit = jnp.zeros((VEC_ROWS, rows), jnp.bool_)
    for d in range(docs):
        hit = hit | ((row_doc == d) & (places == ends[d] - lens_ref[d]))
    found = nn(jnp.where(hit, 1.0, 0.0).astype(BF), result)

    @pl.when(step == 0)
    def _():
        picked_ref[...] = found

    @pl.when(step > 0)
    def _():
        picked_ref[...] += found

    @pl.when(step == pl.num_programs(0) - 1)
    def _():
        picked = picked_ref[...].astype(BF)
        pooled = jnp.tanh(nn(picked, w_pool_ref[...]) + vec(B_POOL))
        pooled_low = pooled.astype(BF)
        table = vec_ref[...].astype(BF)
        logits = nt(pooled_low, table) + b_class_ref[...]
        column = lax.broadcasted_iota(jnp.int32, (VEC_ROWS, VEC_ROWS), 1)
        row = lax.broadcasted_iota(jnp.int32, (VEC_ROWS, VEC_ROWS), 0)
        logits_ref[...] = logits
        live = column < CLASSES
        shown = jnp.where(live, logits, -jnp.inf)
        exps = jnp.where(live, jnp.exp(shown - jnp.max(shown, axis=-1, keepdims=True)), 0.0)
        probs = exps / jnp.sum(exps, axis=-1, keepdims=True)
        label = jnp.zeros((VEC_ROWS, VEC_ROWS), jnp.int32)
        for d in range(docs):
            label = jnp.where(row == d, labels_ref[d], label)
        grad = jnp.where(live & (row < docs), probs - jnp.where(label == column, 1.0, 0.0), 0.0)
        grad_low = grad.astype(BF)
        grad_pool = (nn(grad_low, table) * (1.0 - pooled * pooled)).astype(BF)
        dpool_ref[...] = tn(picked, grad_pool).astype(BF)
        first_ref[...] = nt(grad_pool, w_pool_ref[...])
        small_ref[0:16, :] = tn(grad_low, pooled_low)
        small_ref[16:17, :] = jnp.sum(grad_pool.astype(F32), axis=0, keepdims=True)
        width = small_ref.shape[1]
        class_sum = jnp.sum(grad_low.astype(F32), axis=0, keepdims=True)
        small_ref[17:18, :] = jnp.concatenate(
            [class_sum, jnp.zeros((1, width - VEC_ROWS), F32)], axis=1
        )


def dense(lens, labels, rows, att, w_inner, w_out, w_pool, w_outer, vectors, b_inner, b_class_row):
    length, width = rows.shape
    hidden = w_outer.shape[0]
    tile = 256
    steps = length // tile
    part = pl.BlockSpec((tile, width), lambda i: (i, 0))
    wide = pl.BlockSpec((tile, hidden), lambda i: (i, 0))

    def fixed(shape, column=0):
        return pl.BlockSpec(shape, lambda i: (0, column))

    return pl.pallas_call(
        dense_kernel,
        grid=(steps,),
        out_shape=[
            jax.ShapeDtypeStruct((length, width), F32),
            jax.ShapeDtypeStruct((length, width), F32),
            jax.ShapeDtypeStruct((length, width), BF),
            jax.ShapeDtypeStruct((length, hidden), BF),
            jax.ShapeDtypeStruct((length, hidden), BF),
            jax.ShapeDtypeStruct((length, width), BF),
            jax.ShapeDtypeStruct((width, width), BF),
            jax.ShapeDtypeStruct((VEC_ROWS, width), F32),
            jax.ShapeDtypeStruct((24, width), F32),
            jax.ShapeDtypeStruct((VEC_ROWS, VEC_ROWS), F32),
        ],
        in_specs=[
            SMEM, SMEM, part, part,
            fixed((width, hidden)), fixed((width, width)), fixed((width, width)),
            fixed((hidden, width)), fixed((VEC_ROWS, width)), fixed((1, hidden)), fixed((1, VEC_ROWS)),
        ],
        out_specs=[
            part, part, part, wide, wide, part,
            fixed((width, width)), fixed((VEC_ROWS, width)), fixed((24, width)), fixed((VEC_ROWS, VEC_ROWS)),
        ],
        scratch_shapes=[pltpu.VMEM((VEC_ROWS, width), F32)],
        compiler_params=pltpu.CompilerParams(vmem_limit_bytes=60 * 2**20),
        cost_estimate=pl.CostEstimate(flops=11 * 10**9, bytes_accessed=40 * 10**6, transcendentals=3 * 2**20),
        name="dense",
    )(lens, labels, rows, att, w_inner, w_out, w_pool, w_outer, vectors, b_inner, b_class_row)


def norm_back(grad, values, gain):
    hat, inverse = centered_parts(values)
    scaled = grad * gain
    mean_scaled = jnp.mean(scaled, axis=-1, keepdims=True)
    mean_cross = jnp.mean(scaled * hat, axis=-1, keepdims=True)
    back = (scaled - mean_scaled - hat * mean_cross) * inverse
    return back, jnp.sum(grad * hat, axis=0, keepdims=True), jnp.sum(grad, axis=0, keepdims=True)


def dense_back_kernel(
    lens_ref, cot_ref, summed_ref, pre_ref, dact_ref, w_inner_ref, w_out_ref, w_outer_ref, vec_ref, first_ref,
    outer_ref, inner_ref, branch_ref, datt_ref, gpre_ref, small_ref, bi_ref,
):
    step = pl.program_id(0)
    rows = cot_ref.shape[0]
    hidden = dact_ref.shape[1]
    chunk = 512

    def vec(row):
        return vec_ref[row : row + 1, :]

    @pl.when(step == 0)
    def _():
        small_ref[...] = jnp.zeros_like(small_ref)
        bi_ref[...] = jnp.zeros_like(bi_ref)

    grad = cot_ref[...].astype(F32)
    places = lax.broadcasted_iota(jnp.int32, (rows, 1), 0) + step * rows
    ends = doc_ends(lens_ref)
    placed = jnp.zeros(grad.shape, F32)
    for d in range(len(ends)):
        placed = jnp.where(places == ends[d] - lens_ref[d], first_ref[d : d + 1, :], placed)
    grad = grad + placed
    grad_summed, gain2, shift2 = norm_back(grad, summed_ref[...], vec(GAIN2))
    outer = grad_summed.astype(BF)
    outer_ref[...] = outer
    grad_normed = grad_summed
    for s in range(0, hidden, chunk):
        back = nt(outer, w_outer_ref[s : s + chunk, :])
        inner = (back * dact_ref[:, s : s + chunk].astype(F32)).astype(BF)
        inner_ref[:, s : s + chunk] = inner
        bi_ref[:, s : s + chunk] += jnp.sum(inner.astype(F32), axis=0, keepdims=True)
        grad_normed = grad_normed + nt(inner, w_inner_ref[:, s : s + chunk])
    grad_pre, gain1, shift1 = norm_back(grad_normed, pre_ref[...], vec(GAIN1))
    gpre_ref[...] = grad_pre
    branch = grad_pre.astype(BF)
    branch_ref[...] = branch
    datt_ref[...] = nt(branch, w_out_ref[...]).astype(BF)
    small_ref[0:1, :] += jnp.sum(outer.astype(F32), axis=0, keepdims=True)
    small_ref[1:2, :] += gain2
    small_ref[2:3, :] += shift2
    small_ref[3:4, :] += jnp.sum(branch.astype(F32), axis=0, keepdims=True)
    small_ref[4:5, :] += gain1
    small_ref[5:6, :] += shift1


def dense_back(lens, cot, summed, pre, dact, w_inner, w_out, w_outer, vectors, first):
    length, width = cot.shape
    hidden = w_outer.shape[0]
    tile = 256
    part = pl.BlockSpec((tile, width), lambda i: (i, 0))
    wide = pl.BlockSpec((tile, hidden), lambda i: (i, 0))

    def fixed(shape, column=0):
        return pl.BlockSpec(shape, lambda i: (0, column))

    return pl.pallas_call(
        dense_back_kernel,
        grid=(length // tile,),
        out_shape=[
            jax.ShapeDtypeStruct((length, width), BF),
            jax.ShapeDtypeStruct((length, hidden), BF),
            jax.ShapeDtypeStruct((length, width), BF),
            jax.ShapeDtypeStruct((length, width), BF),
            jax.ShapeDtypeStruct((length, width), F32),
            jax.ShapeDtypeStruct((8, width), F32),
            jax.ShapeDtypeStruct((1, hidden), F32),
        ],
        in_specs=[
            SMEM, part, part, part, wide,
            fixed((width, hidden)), fixed((width, width)), fixed((hidden, width)),
            fixed((VEC_ROWS, width)), fixed((VEC_ROWS, width)),
        ],
        out_specs=[part, wide, part, part, part, fixed((8, width)), fixed((1, hidden))],
        compiler_params=pltpu.CompilerParams(vmem_limit_bytes=60 * 2**20),
        cost_estimate=pl.CostEstimate(flops=11 * 10**9, bytes_accessed=40 * 10**6, transcendentals=0),
        name="dense_back",
    )(lens, cot, summed, pre, dact, w_inner, w_out, w_outer, vectors, first)


def exchange(blocks):
    count = blocks.shape[0]
    mine = lax.axis_index("fsdp")
    held = jnp.zeros_like(blocks)
    own = lax.dynamic_index_in_dim(blocks, mine, 0, keepdims=True)
    held = lax.dynamic_update_slice_in_dim(held, own, mine, 0)
    for k in range(1, count):
        leaving = lax.dynamic_index_in_dim(blocks, lax.rem(mine + k, count), 0, keepdims=True)
        came = lax.ppermute(leaving, "fsdp", [(i, (i + k) % count) for i in range(count)])
        held = lax.dynamic_update_slice_in_dim(held, came, lax.rem(mine - k + count, count), 0)
    return held


def fast_body(
    inputs, cotangent, doc_lengths, labels, w_query, b_query, w_key, w_value, b_value, w_out, b_out, first_gain, first_shift,
    w_inner, b_inner, w_outer, b_outer, second_gain, second_shift, w_pool, b_pool, w_class, b_class,
):
    seqs, local_len, width = inputs.shape
    length = seqs * local_len
    devices = 8 * ZS
    mine = lax.axis_index("fsdp")
    docs = doc_lengths.shape[1]
    own_lens = lax.dynamic_index_in_dim(doc_lengths, mine, 0, keepdims=False)
    own_labels = lax.dynamic_index_in_dim(labels, mine, 0, keepdims=False)

    share = width // devices
    hidden_share = b_inner.shape[0]
    hidden = hidden_share * devices
    device = lax.axis_index("dp") * 4 + mine
    columns = jnp.stack(
        [
            *(w_class[:, j] for j in range(CLASSES)), b_query, b_value, b_out, first_gain, first_shift, b_outer, second_gain,
            second_shift, b_pool,
        ]
    )
    table = lax.dynamic_update_slice(jnp.zeros((12, width), F32), columns, (0, device * share))
    inner_rows = lax.dynamic_update_slice(jnp.zeros((hidden,), F32), b_inner, (device * hidden_share,)).reshape(4, width)
    table = jnp.concatenate([table, inner_rows], axis=0).astype(BF).astype(F32)
    q, k, v, att, lse, w_qkv, vectors, rows, full_inner, full_out, full_pool, full_outer = attend(
        own_lens, inputs, table, [w_query, w_key, w_value], [w_inner, w_out, w_pool, w_outer]
    )
    rows = rows.reshape(length, width)
    full_inner = full_inner.reshape(width, hidden)
    full_out = full_out.reshape(width, width)
    full_pool = full_pool.reshape(width, width)
    full_outer = full_outer.reshape(hidden, width)
    b_inner_row = vectors[12:16].reshape(1, hidden)
    b_class_row = jnp.pad(b_class, (0, VEC_ROWS - CLASSES)).reshape(1, VEC_ROWS)

    cotangent, _ = lax.optimization_barrier((cotangent, att))
    cot = exchange(cotangent).reshape(length, width)
    pre, summed, low, act, dact, result, grad_pool, first, small_a, logits = dense(
        own_lens, own_labels, rows, att, full_inner, full_out, full_pool, full_outer, vectors, b_inner_row, b_class_row
    )
    layer_out = exchange(result.reshape(seqs, local_len, width))
    outer, inner, branch, datt, grad_pre, small_b, grad_b_inner = dense_back(
        own_lens, cot, summed, pre, dact, full_inner, full_out, full_outer, vectors, first
    )
    grad_outer_w = tn(act, outer).astype(BF)
    grad_inner_w = tn(low, inner).astype(BF)
    grad_out_w = tn(att, branch).astype(BF)
    logit_block = jnp.pad(logits[:docs, :CLASSES], ((0, 8 - docs), (0, 128 - CLASSES)))
    grad_inputs, all_logits, totals, o_inner, o_outer, o_out, o_pool, o_query, o_key, o_value = attend_back(
        own_lens, rows, w_qkv, q, k, v, att, datt, lse, grad_pre, small_a, small_b, grad_b_inner, logit_block,
        [
            grad_inner_w.reshape(devices, share, hidden),
            grad_outer_w.reshape(devices, hidden_share, width),
            grad_out_w.reshape(devices, share, width),
            grad_pool.reshape(devices, share, width),
        ],
    )
    columns = lax.dynamic_slice_in_dim(totals[:12], device * share, share, 1)
    own_b_inner = lax.dynamic_slice_in_dim(totals[12:16].reshape(hidden), device * hidden_share, hidden_share, 0)
    return (
        layer_out,
        all_logits[:, :docs, :CLASSES],
        grad_inputs,
        o_query,
        columns[B_QUERY],
        o_key,
        o_value,
        columns[B_VALUE],
        o_out,
        columns[B_OUT],
        columns[GAIN1],
        columns[SHIFT1],
        o_inner,
        own_b_inner,
        o_outer,
        columns[B_OUTER],
        columns[GAIN2],
        columns[SHIFT2],
        o_pool,
        columns[B_POOL],
        columns[:CLASSES].T,
        totals[16, :CLASSES],
    )


def solution(mesh):
    placed = (
        P("dp", "fsdp", None),
        P("dp", "fsdp", None),
        P("dp", None),
        P("dp", None),
        P(("dp", "fsdp"), None),
        P(("dp", "fsdp")),
        P(("dp", "fsdp"), None),
        P(("dp", "fsdp"), None),
        P(("dp", "fsdp")),
        P(("dp", "fsdp"), None),
        P(("dp", "fsdp")),
        P(("dp", "fsdp")),
        P(("dp", "fsdp")),
        P(("dp", "fsdp"), None),
        P(("dp", "fsdp")),
        P(("dp", "fsdp"), None),
        P(("dp", "fsdp")),
        P(("dp", "fsdp")),
        P(("dp", "fsdp")),
        P(("dp", "fsdp"), None),
        P(("dp", "fsdp")),
        P(("dp", "fsdp"), None),
        P(),
    )
    sizes = (mesh.shape["dp"], mesh.shape["fsdp"])
    chosen = fast_body if sizes == (8, 4) else general_body
    return jax.shard_map(
        chosen,
        mesh=mesh,
        in_specs=placed,
        out_specs=(
            P("dp", "fsdp", None),
            P("dp", None, None),
            P("dp", "fsdp", None),
            P(("dp", "fsdp"), None),
            P(("dp", "fsdp")),
            P(("dp", "fsdp"), None),
            P(("dp", "fsdp"), None),
            P(("dp", "fsdp")),
            P(("dp", "fsdp"), None),
            P(("dp", "fsdp")),
            P(("dp", "fsdp")),
            P(("dp", "fsdp")),
            P(("dp", "fsdp"), None),
            P(("dp", "fsdp")),
            P(("dp", "fsdp"), None),
            P(("dp", "fsdp")),
            P(("dp", "fsdp")),
            P(("dp", "fsdp")),
            P(("dp", "fsdp"), None),
            P(("dp", "fsdp")),
            P(("dp", "fsdp"), None),
            P(),
        ),
        check_vma=False,
    )
```

```python
import functools

import jax
import jax.numpy as jnp
from jax import lax
from jax.experimental import pallas as pl
from jax.experimental.pallas import tpu as pltpu
from jax.sharding import PartitionSpec as P

HEAD_DIM = 64
CLASSES = 3
MICRO = 4


def product(left_side, right_side):
    return jnp.dot(left_side, right_side, preferred_element_type=jnp.float32)


def contract_rows(left_side, right_side):
    return lax.dot_general(
        left_side, right_side, (((0,), (0,)), ((), ())), preferred_element_type=jnp.float32
    )


def times_transposed(left_side, right_side):
    return lax.dot_general(
        left_side, right_side, (((1,), (1,)), ((), ())), preferred_element_type=jnp.float32
    )


def layer_norm(values, norm_gain, norm_shift):
    average = jnp.mean(values, axis=-1, keepdims=True)
    centered = values - average
    variance = jnp.mean(centered * centered, axis=-1, keepdims=True)
    return centered * lax.rsqrt(variance + 1e-06) * norm_gain + norm_shift


def gelu_exact(values):
    return jax.nn.gelu(values, approximate=False)


def running_sum(lengths_rows):
    count = lengths_rows.shape[1]
    upper = jnp.arange(count)[:, None] <= jnp.arange(count)[None, :]
    return jnp.sum(jnp.where(upper[None], lengths_rows[:, :, None], 0), axis=1)


def segment_numbers(lengths_rows, places):
    doc_ends = running_sum(lengths_rows)
    above = (places[None, :, None] >= doc_ends[:, None, :]).astype(jnp.int32)
    return jnp.sum(above, axis=2)


def pair_heads(values):
    return values.reshape(values.shape[0], values.shape[1], 2, HEAD_DIM)


def pair_scores(query_pair, key_pair, same_doc):
    raw_scores = jnp.einsum(
        "bqhd,bkhd->bhqk", query_pair, key_pair, preferred_element_type=jnp.float32
    ) * HEAD_DIM ** (-0.5)
    return jnp.where(same_doc[:, None], raw_scores, -1000000000.0)


def lowered_masters(masters):
    return [member.astype(jnp.bfloat16) for member in masters]


def forward(tokens, lengths_rows, weights, bias_class):
    (
        w_query,
        b_query,
        w_key,
        w_value,
        b_value,
        w_out,
        b_out,
        first_gain,
        first_shift,
        w_inner,
        b_inner,
        w_outer,
        b_outer,
        second_gain,
        second_shift,
        w_pool,
        b_pool,
        w_class,
    ) = weights
    seq_count, local_len, model_width = tokens.shape
    doc_count = lengths_rows.shape[1]
    flat_rows = tokens.reshape(seq_count * local_len, model_width)
    queries = (
        (product(flat_rows, w_query) + b_query)
        .astype(jnp.bfloat16)
        .reshape(seq_count, local_len, model_width)
    )
    key_rows = (
        product(flat_rows, w_key).astype(jnp.bfloat16).reshape(seq_count, local_len, model_width)
    )
    value_rows = (
        (product(flat_rows, w_value) + b_value)
        .astype(jnp.bfloat16)
        .reshape(seq_count, local_len, model_width)
    )
    all_keys, all_values = (
        lax.all_gather(key_rows, "fsdp", axis=1, tiled=True),
        lax.all_gather(value_rows, "fsdp", axis=1, tiled=True),
    )
    full_len = all_keys.shape[1]
    own_places = lax.axis_index("fsdp") * local_len + jnp.arange(local_len, dtype=jnp.int32)
    key_places = jnp.arange(full_len, dtype=jnp.int32)
    same_doc = (
        segment_numbers(lengths_rows, own_places)[:, :, None]
        == segment_numbers(lengths_rows, key_places)[:, None, :]
    )
    pair_width = 2 * HEAD_DIM
    mixed_list = []
    log_totals = []
    for pair_index in range(model_width // pair_width):
        col_start = pair_index * pair_width
        query_pair = pair_heads(queries[:, :, col_start : col_start + pair_width])
        key_pair = pair_heads(all_keys[:, :, col_start : col_start + pair_width])
        value_pair = pair_heads(all_values[:, :, col_start : col_start + pair_width])
        scores = pair_scores(query_pair, key_pair, same_doc)
        row_peak = jnp.max(scores, axis=-1, keepdims=True)
        exp_total = jnp.sum(jnp.exp(scores - row_peak), axis=-1, keepdims=True)
        log_total = row_peak + jnp.log(exp_total)
        attn_probs = jnp.exp(scores - log_total).astype(jnp.bfloat16)
        mixed_pair = jnp.einsum(
            "bhqk,bkhd->bqhd", attn_probs, value_pair, preferred_element_type=jnp.float32
        )
        mixed_list.append(mixed_pair.reshape(seq_count, local_len, pair_width))
        log_totals.append(log_total)
    attended = (
        jnp.concatenate(mixed_list, axis=2)
        .astype(jnp.bfloat16)
        .reshape(seq_count * local_len, model_width)
    )
    branch = product(attended, w_out) + b_out
    pre_first = flat_rows.astype(jnp.float32) + branch
    normed = layer_norm(pre_first, first_gain.astype(jnp.float32), first_shift.astype(jnp.float32))
    normed_low = normed.astype(jnp.bfloat16)
    inner_pre = product(normed_low, w_inner) + b_inner
    activated = gelu_exact(inner_pre).astype(jnp.bfloat16)
    summed = normed + (product(activated, w_outer) + b_outer)
    result = layer_norm(summed, second_gain.astype(jnp.float32), second_shift.astype(jnp.float32))
    result_low = result.astype(jnp.bfloat16).reshape(seq_count, local_len, model_width)
    starts = running_sum(lengths_rows) - lengths_rows
    picker = (own_places[None, None, :] == starts[:, :, None]).astype(jnp.bfloat16)
    local_firsts = jnp.einsum(
        "bdl,blc->bdc", picker, result_low, preferred_element_type=jnp.float32
    )
    firsts = lax.psum(local_firsts, "fsdp")
    firsts_low = firsts.astype(jnp.bfloat16).reshape(seq_count * doc_count, model_width)
    pooled = jnp.tanh(product(firsts_low, w_pool) + b_pool)
    pooled_low = pooled.astype(jnp.bfloat16)
    logits = product(pooled_low, w_class) + bias_class
    stored = (
        flat_rows,
        queries,
        all_keys,
        all_values,
        same_doc,
        log_totals,
        attended,
        pre_first,
        summed,
        normed_low,
        inner_pre,
        activated,
        picker,
        firsts_low,
        pooled,
        pooled_low,
        logits,
    )
    return (result_low, logits.reshape(seq_count, doc_count, CLASSES), stored)


def backward(stored, weights, cot_rows, label_rows):
    (
        w_query,
        b_query,
        w_key,
        w_value,
        b_value,
        w_out,
        b_out,
        first_gain,
        first_shift,
        w_inner,
        b_inner,
        w_outer,
        b_outer,
        second_gain,
        second_shift,
        w_pool,
        b_pool,
        w_class,
    ) = weights
    (
        flat_rows,
        queries,
        all_keys,
        all_values,
        same_doc,
        log_totals,
        attended,
        pre_first,
        summed,
        normed_low,
        inner_pre,
        activated,
        picker,
        firsts_low,
        pooled,
        pooled_low,
        logits,
    ) = stored
    seq_count, local_len, model_width = queries.shape
    doc_count = picker.shape[1]
    owner_flag = (lax.axis_index("fsdp") == 0).astype(jnp.float32)
    row_peak = jnp.max(logits, axis=-1, keepdims=True)
    class_exp = jnp.exp(logits - row_peak)
    class_probs = class_exp / jnp.sum(class_exp, axis=-1, keepdims=True)
    onehot_labels = (
        label_rows.reshape(-1)[:, None] == jnp.arange(CLASSES, dtype=jnp.int32)[None, :]
    ).astype(jnp.float32)
    grad_logits = (class_probs - onehot_labels).astype(jnp.bfloat16)
    grad_b_class = owner_flag * jnp.sum(grad_logits.astype(jnp.float32), axis=0)
    grad_w_class = owner_flag * contract_rows(pooled_low, grad_logits)
    grad_pool_pre = (times_transposed(grad_logits, w_class) * (1.0 - pooled * pooled)).astype(
        jnp.bfloat16
    )
    grad_b_pool = owner_flag * jnp.sum(grad_pool_pre.astype(jnp.float32), axis=0)
    grad_w_pool = owner_flag * contract_rows(firsts_low, grad_pool_pre)
    grad_firsts = times_transposed(grad_pool_pre, w_pool).reshape(seq_count, doc_count, model_width)
    from_pool = jnp.einsum(
        "bdl,bdc->blc", picker.astype(jnp.float32), grad_firsts, precision=lax.Precision.HIGHEST
    )
    grad_result = cot_rows.astype(jnp.float32).reshape(-1, model_width) + from_pool.reshape(
        -1, model_width
    )
    second_back = jax.vjp(
        layer_norm, summed, second_gain.astype(jnp.float32), second_shift.astype(jnp.float32)
    )[1]
    grad_summed, grad_second_gain, grad_second_shift = second_back(grad_result)
    grad_outer = grad_summed.astype(jnp.bfloat16)
    grad_b_outer = jnp.sum(grad_outer.astype(jnp.float32), axis=0)
    grad_w_outer = contract_rows(activated, grad_outer)
    gelu_back = jax.vjp(gelu_exact, inner_pre)[1]
    grad_inner = gelu_back(times_transposed(grad_outer, w_outer))[0].astype(jnp.bfloat16)
    grad_b_inner = jnp.sum(grad_inner.astype(jnp.float32), axis=0)
    grad_w_inner = contract_rows(normed_low, grad_inner)
    grad_normed = grad_summed + times_transposed(grad_inner, w_inner)
    first_back = jax.vjp(
        layer_norm, pre_first, first_gain.astype(jnp.float32), first_shift.astype(jnp.float32)
    )[1]
    grad_pre_first, grad_first_gain, grad_first_shift = first_back(grad_normed)
    grad_branch = grad_pre_first.astype(jnp.bfloat16)
    grad_b_out = jnp.sum(grad_branch.astype(jnp.float32), axis=0)
    grad_w_out = contract_rows(attended, grad_branch)
    grad_attended = (
        times_transposed(grad_branch, w_out)
        .astype(jnp.bfloat16)
        .reshape(seq_count, local_len, model_width)
    )
    pair_width = 2 * HEAD_DIM
    query_list = []
    key_list = []
    value_list = []
    for pair_index in range(model_width // pair_width):
        col_start = pair_index * pair_width
        query_pair = pair_heads(queries[:, :, col_start : col_start + pair_width])
        key_pair = pair_heads(all_keys[:, :, col_start : col_start + pair_width])
        value_pair = pair_heads(all_values[:, :, col_start : col_start + pair_width])
        grad_pair = pair_heads(grad_attended[:, :, col_start : col_start + pair_width])
        scores = pair_scores(query_pair, key_pair, same_doc)
        attn_probs = jnp.exp(scores - log_totals[pair_index])
        grad_probs = jnp.einsum(
            "bqhd,bkhd->bhqk", grad_pair, value_pair, preferred_element_type=jnp.float32
        )
        row_dot = jnp.sum(attn_probs * grad_probs, axis=-1, keepdims=True)
        grad_scores = (attn_probs * (grad_probs - row_dot)).astype(jnp.bfloat16)
        query_part = jnp.einsum(
            "bhqk,bkhd->bqhd", grad_scores, key_pair, preferred_element_type=jnp.float32
        ) * HEAD_DIM ** (-0.5)
        query_list.append(query_part.reshape(seq_count, local_len, pair_width))
        probs_low = attn_probs.astype(jnp.bfloat16)
        key_part = jnp.einsum(
            "bhqk,bqhd->bkhd", grad_scores, query_pair, preferred_element_type=jnp.float32
        ) * HEAD_DIM ** (-0.5)
        value_part = jnp.einsum(
            "bhqk,bqhd->bkhd", probs_low, grad_pair, preferred_element_type=jnp.float32
        )
        key_list.append(key_part.reshape(seq_count, key_part.shape[1], pair_width))
        value_list.append(value_part.reshape(seq_count, value_part.shape[1], pair_width))
    key_partials = jnp.concatenate(key_list, axis=2)
    value_partials = jnp.concatenate(value_list, axis=2)
    own_keys, own_values = (
        lax.psum_scatter(
            key_partials.astype(jnp.bfloat16), "fsdp", scatter_dimension=1, tiled=True
        ).astype(jnp.float32),
        lax.psum_scatter(
            value_partials.astype(jnp.bfloat16), "fsdp", scatter_dimension=1, tiled=True
        ).astype(jnp.float32),
    )
    query_grad = jnp.concatenate(query_list, axis=2).astype(jnp.bfloat16).reshape(-1, model_width)
    key_grad = own_keys.astype(jnp.bfloat16).reshape(-1, model_width)
    value_grad = own_values.astype(jnp.bfloat16).reshape(-1, model_width)
    grad_w_query = contract_rows(flat_rows, query_grad)
    grad_b_query = jnp.sum(query_grad.astype(jnp.float32), axis=0)
    grad_w_key = contract_rows(flat_rows, key_grad)
    grad_w_value = contract_rows(flat_rows, value_grad)
    grad_b_value = jnp.sum(value_grad.astype(jnp.float32), axis=0)
    grad_tokens = (
        grad_pre_first
        + times_transposed(query_grad, w_query)
        + times_transposed(key_grad, w_key)
        + times_transposed(value_grad, w_value)
    )
    new_grads = (
        grad_w_query,
        grad_b_query,
        grad_w_key,
        grad_w_value,
        grad_b_value,
        grad_w_out,
        grad_b_out,
        grad_first_gain,
        grad_first_shift,
        grad_w_inner,
        grad_b_inner,
        grad_w_outer,
        grad_b_outer,
        grad_second_gain,
        grad_second_shift,
        grad_w_pool,
        grad_b_pool,
        grad_w_class,
    )
    return (
        new_grads,
        grad_b_class,
        grad_tokens.astype(jnp.bfloat16).reshape(seq_count, local_len, model_width),
    )


def general_body(
    inputs,
    cotangent,
    doc_lengths,
    labels,
    w_query,
    b_query,
    w_key,
    w_value,
    b_value,
    w_out,
    b_out,
    first_gain,
    first_shift,
    w_inner,
    b_inner,
    w_outer,
    b_outer,
    second_gain,
    second_shift,
    w_pool,
    b_pool,
    w_class,
    b_class,
):
    masters = (
        w_query,
        b_query,
        w_key,
        w_value,
        b_value,
        w_out,
        b_out,
        first_gain,
        first_shift,
        w_inner,
        b_inner,
        w_outer,
        b_outer,
        second_gain,
        second_shift,
        w_pool,
        b_pool,
        w_class,
    )
    group_size = lax.axis_size("dp") * lax.axis_size("fsdp")
    grad_sums = [
        jnp.zeros((member.shape[0] * group_size,) + member.shape[1:], jnp.float32)
        for member in masters
    ]
    class_sum = jnp.zeros((CLASSES,), jnp.float32)
    micro_seqs = inputs.shape[0] // MICRO
    out_list = []
    logit_list = []
    grad_list = []
    for micro_step in range(MICRO):
        first_seq = micro_step * micro_seqs
        after_seq = first_seq + micro_seqs
        tokens = inputs[first_seq:after_seq]
        lengths_rows = doc_lengths[first_seq:after_seq]
        pieces = lowered_masters(masters)
        front_weights = (
            lax.all_gather(pieces[0], ("dp", "fsdp"), axis=0, tiled=True),
            lax.all_gather(pieces[1], ("dp", "fsdp"), axis=0, tiled=True),
            lax.all_gather(pieces[2], ("dp", "fsdp"), axis=0, tiled=True),
            lax.all_gather(pieces[3], ("dp", "fsdp"), axis=0, tiled=True),
            lax.all_gather(pieces[4], ("dp", "fsdp"), axis=0, tiled=True),
            lax.all_gather(pieces[5], ("dp", "fsdp"), axis=0, tiled=True),
            lax.all_gather(pieces[6], ("dp", "fsdp"), axis=0, tiled=True),
            lax.all_gather(pieces[7], ("dp", "fsdp"), axis=0, tiled=True),
            lax.all_gather(pieces[8], ("dp", "fsdp"), axis=0, tiled=True),
            lax.all_gather(pieces[9], ("dp", "fsdp"), axis=0, tiled=True),
            lax.all_gather(pieces[10], ("dp", "fsdp"), axis=0, tiled=True),
            lax.all_gather(pieces[11], ("dp", "fsdp"), axis=0, tiled=True),
            lax.all_gather(pieces[12], ("dp", "fsdp"), axis=0, tiled=True),
            lax.all_gather(pieces[13], ("dp", "fsdp"), axis=0, tiled=True),
            lax.all_gather(pieces[14], ("dp", "fsdp"), axis=0, tiled=True),
            lax.all_gather(pieces[15], ("dp", "fsdp"), axis=0, tiled=True),
            lax.all_gather(pieces[16], ("dp", "fsdp"), axis=0, tiled=True),
            lax.all_gather(pieces[17], ("dp", "fsdp"), axis=0, tiled=True),
        )
        result_low, logits, stored = forward(tokens, lengths_rows, front_weights, b_class)
        out_list.append(result_low)
        logit_list.append(logits)
        back_weights = (
            lax.all_gather(pieces[0], ("dp", "fsdp"), axis=0, tiled=True),
            lax.all_gather(pieces[1], ("dp", "fsdp"), axis=0, tiled=True),
            lax.all_gather(pieces[2], ("dp", "fsdp"), axis=0, tiled=True),
            lax.all_gather(pieces[3], ("dp", "fsdp"), axis=0, tiled=True),
            lax.all_gather(pieces[4], ("dp", "fsdp"), axis=0, tiled=True),
            lax.all_gather(pieces[5], ("dp", "fsdp"), axis=0, tiled=True),
            lax.all_gather(pieces[6], ("dp", "fsdp"), axis=0, tiled=True),
            lax.all_gather(pieces[7], ("dp", "fsdp"), axis=0, tiled=True),
            lax.all_gather(pieces[8], ("dp", "fsdp"), axis=0, tiled=True),
            lax.all_gather(pieces[9], ("dp", "fsdp"), axis=0, tiled=True),
            lax.all_gather(pieces[10], ("dp", "fsdp"), axis=0, tiled=True),
            lax.all_gather(pieces[11], ("dp", "fsdp"), axis=0, tiled=True),
            lax.all_gather(pieces[12], ("dp", "fsdp"), axis=0, tiled=True),
            lax.all_gather(pieces[13], ("dp", "fsdp"), axis=0, tiled=True),
            lax.all_gather(pieces[14], ("dp", "fsdp"), axis=0, tiled=True),
            lax.all_gather(pieces[15], ("dp", "fsdp"), axis=0, tiled=True),
            lax.all_gather(pieces[16], ("dp", "fsdp"), axis=0, tiled=True),
            lax.all_gather(pieces[17], ("dp", "fsdp"), axis=0, tiled=True),
        )
        stored = forward(tokens, lengths_rows, back_weights, b_class)[2]
        new_grads, class_grad, grad_tokens = backward(
            stored, back_weights, cotangent[first_seq:after_seq], labels[first_seq:after_seq]
        )
        grad_sums = [running + fresh_grad for running, fresh_grad in zip(grad_sums, new_grads)]
        class_sum = class_sum + class_grad
        grad_list.append(grad_tokens)
    owned = (
        lax.psum_scatter(grad_sums[0], ("dp", "fsdp"), scatter_dimension=0, tiled=True),
        lax.psum_scatter(grad_sums[1], ("dp", "fsdp"), scatter_dimension=0, tiled=True),
        lax.psum_scatter(grad_sums[2], ("dp", "fsdp"), scatter_dimension=0, tiled=True),
        lax.psum_scatter(grad_sums[3], ("dp", "fsdp"), scatter_dimension=0, tiled=True),
        lax.psum_scatter(grad_sums[4], ("dp", "fsdp"), scatter_dimension=0, tiled=True),
        lax.psum_scatter(grad_sums[5], ("dp", "fsdp"), scatter_dimension=0, tiled=True),
        lax.psum_scatter(grad_sums[6], ("dp", "fsdp"), scatter_dimension=0, tiled=True),
        lax.psum_scatter(grad_sums[7], ("dp", "fsdp"), scatter_dimension=0, tiled=True),
        lax.psum_scatter(grad_sums[8], ("dp", "fsdp"), scatter_dimension=0, tiled=True),
        lax.psum_scatter(grad_sums[9], ("dp", "fsdp"), scatter_dimension=0, tiled=True),
        lax.psum_scatter(grad_sums[10], ("dp", "fsdp"), scatter_dimension=0, tiled=True),
        lax.psum_scatter(grad_sums[11], ("dp", "fsdp"), scatter_dimension=0, tiled=True),
        lax.psum_scatter(grad_sums[12], ("dp", "fsdp"), scatter_dimension=0, tiled=True),
        lax.psum_scatter(grad_sums[13], ("dp", "fsdp"), scatter_dimension=0, tiled=True),
        lax.psum_scatter(grad_sums[14], ("dp", "fsdp"), scatter_dimension=0, tiled=True),
        lax.psum_scatter(grad_sums[15], ("dp", "fsdp"), scatter_dimension=0, tiled=True),
        lax.psum_scatter(grad_sums[16], ("dp", "fsdp"), scatter_dimension=0, tiled=True),
        lax.psum_scatter(grad_sums[17], ("dp", "fsdp"), scatter_dimension=0, tiled=True),
    )
    class_total = lax.psum(class_sum, ("dp", "fsdp"))
    return (
        jnp.concatenate(out_list, axis=0),
        jnp.concatenate(logit_list, axis=0),
        jnp.concatenate(grad_list, axis=0),
        owned[0],
        owned[1],
        owned[2],
        owned[3],
        owned[4],
        owned[5],
        owned[6],
        owned[7],
        owned[8],
        owned[9],
        owned[10],
        owned[11],
        owned[12],
        owned[13],
        owned[14],
        owned[15],
        owned[16],
        owned[17],
        class_total,
    )


BF = jnp.bfloat16
F32 = jnp.float32
MESH = pl.DeviceIdType.MESH
ANY = pl.BlockSpec(memory_space=pl.ANY)
SMEM = pl.BlockSpec(memory_space=pltpu.SMEM)
ZS = 4
CLASS_ROWS, B_QUERY, B_VALUE, B_OUT, GAIN1, SHIFT1, B_OUTER, GAIN2, SHIFT2, B_POOL = (0, 3, 4, 5, 6, 7, 8, 9, 10, 11)
VEC_ROWS = 16


def nn(a, b):
    return lax.dot_general(a, b, (((1,), (0,)), ((), ())), preferred_element_type=F32)


def nt(a, b):
    return lax.dot_general(a, b, (((1,), (1,)), ((), ())), preferred_element_type=F32)


def tn(a, b):
    return lax.dot_general(a, b, (((0,), (0,)), ((), ())), preferred_element_type=F32)


def my_place():
    dp, fs = lax.axis_index("dp"), lax.axis_index("fsdp")
    return dp // 2, lax.rem(dp, 2), fs // 2, lax.rem(fs, 2)


def device_at(z, y, x, c):
    return (z * 2 + y, x * 2 + c)


def meet(partners):
    barrier = pltpu.get_barrier_semaphore()
    for partner in partners:
        pl.semaphore_signal(barrier, inc=1, device_id=partner, device_id_type=MESH)
    pl.semaphore_wait(barrier, len(partners))


def all_partners(z, y, x, c):
    found = [device_at(lax.rem(z + k, ZS), y, x, c) for k in range(1, ZS)]
    found.append(device_at(z, 1 - y, x, c))
    found.append(device_at(z, y, 1 - x, c))
    found.append(device_at(z, y, x, 1 - c))
    found.append(device_at(z, y, 1 - x, 1 - c))
    return found


def group_partner(k, x, c):
    return (1 - x if k >= 2 else x, 1 - c if k % 2 == 1 else c)


def doc_ends(lens_ref):
    ends = []
    total = 0
    for d in range(lens_ref.shape[1]):
        total = total + lens_ref[lax.axis_index("fsdp"), d]
        ends.append(total)
    return ends


def doc_starts(lens_ref):
    return [0] + doc_ends(lens_ref)[:-1]


def doc_numbers(places, ends):
    number = jnp.zeros(places.shape, jnp.int32)
    for end in ends:
        number = number + (places >= end).astype(jnp.int32)
    return number


GATHER_PIECES = (
    (1, 0, 1, "rows"), (0, 0, 2, "columns"), (0, 1, 2, "columns"), (3, 0, 2, "rows"), (3, 1, 2, "rows"), (2, 0, 1, "rows"),
)
GATHER_ORDERS = ("xy", "xy", "xy", "xy", "yx", "xy", "yx", "yx", "xy")
GATHER_PLAN = {
    -1: ("b0", "b1", "b2", "z0", "b3", "z1", "b4", "z2", "z3", "b5", "f0", "z4", "b6", "f1", "s0", "f2", "e0"),
    0: ("s1", "s2", "f3", "f4", "z5", "b7"),
    1: ("z6", "e1", "e2"),
    2: ("b8",),
    3: ("s3", "z7"),
    4: ("z8", "e3"),
    6: ("s4", "f5", "f6"),
    8: ("f7", "s5", "f8", "e4"),
    9: ("e5",),
    10: ("s6", "s8"),
    11: ("s7", "e8", "e6"),
    12: ("e7",),
}
DENSE_ARRAYS = 4
VECTORS = 9


def part_of(piece, block):
    _, which, count, along = piece
    rows, columns = block
    if along == "rows":
        return (which * (rows // count), rows // count), (0, columns)
    return (0, rows), (which * (columns // count), columns // count)


def attend_kernel(groups, *refs):
    lens_ref, tokens_ref, class_ref = refs[:3]
    vectors, b_inner_ref, (wq_ref, wk_ref, wv_ref) = refs[3 : 3 + VECTORS], refs[3 + VECTORS], refs[4 + VECTORS : 7 + VECTORS]
    refs = refs[7 + VECTORS :]
    shards, refs = refs[:DENSE_ARRAYS], refs[DENSE_ARRAYS:]
    q_ref, k_ref, v_ref, att_ref, lse_ref, w_ref, vec_ref, rows_ref = refs[:8]
    wholes = refs[8 : 8 + DENSE_ARRAYS]
    refs = refs[8 + DENSE_ARRAYS :]
    x_ref, vt_ref, qkv_shard, qkv_ref, tab_ref, tab_in_ref = refs[:6]
    local_sem, row_send, row_recv, tab_send, tab_recv, send_sem, recv_sem = refs[6:13]
    own = refs[13 : 13 + DENSE_ARRAYS]
    length, width = q_ref.shape
    chunk = 256
    points = length // chunk
    heads = width // HEAD_DIM
    items = groups + len(GATHER_PIECES)
    group = pl.program_id(0)
    z, y, x, c = my_place()
    mine = x * 2 + c

    def row_copy(k):
        px, pc = group_partner(k, x, c)
        return pltpu.make_async_remote_copy(
            src_ref=tokens_ref.at[px * 2 + pc],
            dst_ref=x_ref.at[mine],
            send_sem=row_send.at[k - 1],
            recv_sem=row_recv.at[k - 1],
            device_id=device_at(z, y, px, pc),
            device_id_type=MESH,
        )

    def row_own():
        return pltpu.make_async_copy(tokens_ref.at[mine], x_ref.at[mine], local_sem.at[0])

    def rows_out():
        return pltpu.make_async_copy(x_ref, rows_ref, local_sem.at[1])

    def table_copy(level):
        if level < 3:
            source, device = tab_ref.at[0], device_at(lax.rem(z + level + 1, ZS), y, x, c)
        else:
            source = tab_ref.at[level - 2]
            device = (device_at(z, y, 1 - x, c), device_at(z, 1 - y, x, c), device_at(z, y, x, 1 - c))[level - 3]
        return pltpu.make_async_remote_copy(
            src_ref=source,
            dst_ref=tab_in_ref.at[level],
            send_sem=tab_send.at[level],
            recv_sem=tab_recv.at[level],
            device_id=device,
            device_id_type=MESH,
        )

    def array_of(a):
        if a < groups:
            return qkv_ref.at[a], qkv_shard.at[a], None
        piece = GATHER_PIECES[a - groups]
        return wholes[piece[0]], own[piece[0]], part_of(piece, own[piece[0]].shape)

    def view(a, where):
        ref, _, part = array_of(a)
        if part is None:
            return ref.at[where]
        (r0, rows), (c0, columns) = part
        return ref.at[where + (pl.ds(r0, rows), pl.ds(c0, columns))]

    def own_block(a):
        _, ref, part = array_of(a)
        if part is None:
            return ref
        (r0, rows), (c0, columns) = part
        return ref.at[pl.ds(r0, rows), pl.ds(c0, columns)]

    everything = slice(None)

    def along(a, axis):
        return device_at(z, 1 - y, x, c) if GATHER_ORDERS[a][axis] == "y" else device_at(z, y, 1 - x, c)

    def copy_of(a, number):
        core = device_at(z, y, x, 1 - c)
        first_other = (1 - y, x) if GATHER_ORDERS[a][0] == "y" else (y, 1 - x)
        if number < 3:
            source, target = own_block(a), view(a, (z, y, x, c))
            device = device_at(lax.rem(z + number + 1, ZS), y, x, c)
        elif number < 6:
            source = target = view(a, (everything, y, x, c))
            device = (along(a, 0), along(a, 1), core)[number - 3]
        elif number < 8:
            source = target = view(a, (everything, first_other[0], first_other[1], c))
            device = along(a, 1) if number == 6 else core
        else:
            if GATHER_ORDERS[a][1] == "y":
                source = target = view(a, (everything, 1 - y, everything, c))
            else:
                source = target = view(a, (everything, everything, 1 - x, c))
            device = core
        return pltpu.make_async_remote_copy(
            src_ref=source,
            dst_ref=target,
            send_sem=send_sem.at[a, number],
            recv_sem=recv_sem.at[a, number],
            device_id=device,
            device_id_type=MESH,
        )

    def keep(a):
        return pltpu.make_async_copy(own_block(a), view(a, (z, y, x, c)), local_sem.at[2 + a])

    def take_up(point):
        for word in GATHER_PLAN.get(point, ()):
            kind, a = word[0], int(word[1:])
            if kind == "b":
                for number in (1, 0, 2):
                    copy_of(a, number).start()
                keep(a).start()
            elif kind == "z":
                for number in (0, 1, 2):
                    copy_of(a, number).wait_recv()
                keep(a).wait()
                for number in (3, 4, 5):
                    copy_of(a, number).start()
            elif kind == "f":
                copy_of(a, 3).wait_recv()
                for number in (6, 7):
                    copy_of(a, number).start()
            elif kind == "s":
                copy_of(a, 4).wait_recv()
                copy_of(a, 6).wait_recv()
                copy_of(a, 8).start()
            else:
                for number in (5, 7, 8):
                    copy_of(a, number).wait_recv()

    @pl.when(group == 0)
    def _():
        device = ((z * 2 + y) * 2 + x) * 2 + c
        full = tab_ref.shape[2]

        def spread(values, at):
            n = values.shape[1]
            here = lax.broadcasted_iota(jnp.int32, (n, full), 1) - at == lax.broadcasted_iota(jnp.int32, (n, full), 0)
            return nn(values.astype(BF), jnp.where(here, 1.0, 0.0).astype(BF))

        share = class_ref.shape[1]
        tab_ref[0, 0:CLASSES] = spread(class_ref[...], device * share)
        for j, ref in enumerate(vectors):
            tab_ref[0, CLASSES + j : CLASSES + j + 1] = spread(ref[...], device * share)
        per_row = full // b_inner_ref.shape[1]
        inner_bias = spread(b_inner_ref[...], lax.rem(device, per_row) * b_inner_ref.shape[1])
        for j in range(4):
            tab_ref[0, 12 + j : 13 + j] = jnp.where(device // per_row == j, inner_bias, 0.0)
        for g in range(groups):
            for j, ref in enumerate((wq_ref, wk_ref, wv_ref)):
                qkv_shard[g, :, j * width : (j + 1) * width] = ref[:, g * width : (g + 1) * width].astype(BF)
        for target, ref in zip(own, shards):
            target[...] = ref[...].astype(BF)
        meet(all_partners(z, y, x, c))
        for level in (1, 0, 2):
            table_copy(level).start()
        for k in (3, 2, 1):
            row_copy(k).start()
        row_own().start()
        take_up(-1)
        for level in (0, 1, 2):
            table_copy(level).wait_recv()
        tab_ref[1] = (tab_ref[0] + tab_in_ref[0]) + (tab_in_ref[1] + tab_in_ref[2])
        for level in (3, 4, 5):
            table_copy(level).start()
            table_copy(level).wait_recv()
            tab_ref[level - 1] = tab_ref[level - 2] + tab_in_ref[level]
        vec_ref[...] = tab_ref[4]
        row_own().wait()
        for k in (1, 2, 3):
            row_copy(k).wait_recv()
        rows_out().start()

    tokens = x_ref[...].reshape(length, x_ref.shape[2])
    weights = qkv_ref[group].astype(F32).reshape(x_ref.shape[2], 3 * width).astype(BF)
    w_ref[...] = weights
    bias = tab_ref[4, B_QUERY : B_QUERY + 2, pl.ds(pl.multiple_of(group * width, width), width)]
    q_ref[...] = (nn(tokens, weights[:, :width]) + bias[0:1]).astype(BF)
    k_ref[...] = nn(tokens, weights[:, width : 2 * width]).astype(BF)
    values = (nn(tokens, weights[:, 2 * width :]) + bias[1:2]).astype(BF)
    v_ref[...] = values
    vt_ref[...] = values.astype(F32).T.astype(BF)
    ends = doc_ends(lens_ref)
    key_doc = doc_numbers(lax.broadcasted_iota(jnp.int32, (length, 1), 0), ends)
    lane_head = lax.broadcasted_iota(jnp.int32, (1, width), 1) // HEAD_DIM

    def step(i, carry):
        for point in range(groups * points):
            if point in GATHER_PLAN:

                @pl.when((group == point // points) & (i == point % points))
                def _(point=point):
                    take_up(point)

        at = pl.multiple_of(i * chunk, chunk)
        query_doc = doc_numbers(lax.broadcasted_iota(jnp.int32, (1, chunk), 1) + at, ends)
        scaled = q_ref[pl.ds(at, chunk), :] * jnp.asarray(0.125, BF)
        mixed = []
        for h in range(heads):
            own_q = jnp.where(lane_head == h, scaled, jnp.zeros_like(scaled))
            blocks = []
            for s in range(0, length, chunk):
                scores = nt(k_ref[s : s + chunk, :], own_q)
                blocks.append(jnp.where(key_doc[s : s + chunk] == query_doc, scores, -1000000000.0))
            peak = functools.reduce(jnp.maximum, [jnp.max(b, axis=0, keepdims=True) for b in blocks])
            exps = [jnp.exp(b - peak) for b in blocks]
            total = functools.reduce(jnp.add, [jnp.sum(e, axis=0, keepdims=True) for e in exps])
            scale = 1.0 / total
            probs = jnp.concatenate([(e * scale).astype(BF) for e in exps], axis=0)
            mixed.append(nn(vt_ref[h * HEAD_DIM : (h + 1) * HEAD_DIM, :], probs))
            lse_ref[0, h : h + 1, pl.ds(at, chunk)] = peak + jnp.log(total)
        att_ref[pl.ds(at, chunk), :] = jnp.concatenate(mixed, axis=0).T.astype(BF)
        return carry

    lax.fori_loop(0, points, step, 0)

    @pl.when(group == groups - 1)
    def _():
        take_up(groups * points)
        for a in range(items):
            for number in range(9):
                copy_of(a, number).wait_send()
        for level in range(6):
            table_copy(level).wait_send()
        for k in range(1, 4):
            row_copy(k).wait_send()
        rows_out().wait()


def attend(lens, tokens, class_shard, vectors, b_inner, qkv_shards, shards):
    seqs, local_len, width = tokens.shape
    length = seqs * local_len
    group = 256
    groups = width // group
    share = qkv_shards[0].shape[0]
    hbm = pl.BlockSpec(memory_space=pl.ANY)
    part = pl.BlockSpec((length, group), lambda g: (0, g))
    once = pl.Buffered(buffer_count=1)
    items = groups + len(GATHER_PIECES)

    def fixed(shape):
        return pl.BlockSpec(shape, lambda g: (0,) * len(shape), pipeline_mode=once)

    lead = (ZS, 2, 2, 2)
    return pl.pallas_call(
        functools.partial(attend_kernel, groups),
        grid=(groups,),
        out_shape=[jax.ShapeDtypeStruct((length, width), BF)] * 4
        + [
            jax.ShapeDtypeStruct((groups, 8, length), F32),
            jax.ShapeDtypeStruct((width, 3 * width), BF),
            jax.ShapeDtypeStruct((VEC_ROWS, width), F32),
            jax.ShapeDtypeStruct(tokens.shape, BF),
        ]
        + [jax.ShapeDtypeStruct(lead + s.shape, BF) for s in shards],
        in_specs=[SMEM, hbm, fixed(class_shard.shape)]
        + [fixed(v.shape) for v in vectors]
        + [fixed(b_inner.shape)]
        + [fixed(s.shape) for s in qkv_shards]
        + [fixed(s.shape) for s in shards],
        out_specs=[part] * 4
        + [
            pl.BlockSpec((1, 8, length), lambda g: (g, 0, 0)),
            pl.BlockSpec((width, 3 * group), lambda g: (0, g)),
            pl.BlockSpec((VEC_ROWS, width), lambda g: (0, 0)),
            hbm,
        ]
        + [hbm] * DENSE_ARRAYS,
        scratch_shapes=[
            pltpu.VMEM(tokens.shape, BF),
            pltpu.VMEM((group, length), BF),
            pltpu.VMEM((groups, share, 3 * group), BF),
            pltpu.VMEM((groups,) + lead + (share, 3 * group), BF),
            pltpu.VMEM((5, VEC_ROWS, width), F32),
            pltpu.VMEM((6, VEC_ROWS, width), F32),
            pltpu.SemaphoreType.DMA((2 + items,)),
            pltpu.SemaphoreType.DMA((3,)),
            pltpu.SemaphoreType.DMA((3,)),
            pltpu.SemaphoreType.DMA((6,)),
            pltpu.SemaphoreType.DMA((6,)),
            pltpu.SemaphoreType.DMA((items, 9)),
            pltpu.SemaphoreType.DMA((items, 9)),
        ]
        + [pltpu.VMEM(s.shape, BF) for s in shards],
        compiler_params=pltpu.CompilerParams(
            collective_id=1, has_side_effects=True, vmem_limit_bytes=60 * 2**20
        ),
        name="attend",
    )(lens, tokens, class_shard, *vectors, b_inner, *qkv_shards, *shards)


DENSE = 4
DENSE_ITEMS = (
    (2, 0, 1, "rows", "yx"), (3, 0, 1, "rows", "xy"),
    (0, 0, 2, "columns", "yx"), (1, 0, 2, "rows", "xy"), (0, 1, 2, "columns", "yx"), (1, 1, 2, "rows", "xy"),
)
GROUP_ORDERS = ("yx", "xy", "yx")
SCATTER_PLAN = {
    -1: ("b0",),
    0: ("b1",),
    1: ("c00", "c01", "b2", "c10", "c11"),
    2: ("b3",),
    3: ("c02", "b4", "c12", "f0", "f1", "c03", "c13", "b5"),
    4: ("s0", "s1", "b6"),
    5: ("c04", "c05", "c14", "c15"),
    6: ("z0", "z1"),
    7: ("f2", "f3"),
    8: ("b7",),
    9: ("c06", "c07", "c16", "c17"),
    10: ("f4", "s2", "s3"),
    11: ("f5",),
    12: ("b8", "dx", "f6", "f7", "t0", "s4", "s5", "z2", "c08", "c18", "z3", "t1", "s7", "s6", "f8", "t2", "z7", "s8", "z4", "z6", "z5", "t3", "z8"),
}
PIECES = len(DENSE_ITEMS)


def order_of(a):
    return DENSE_ITEMS[a][4] if a < PIECES else GROUP_ORDERS[a - PIECES]


def cut_of(a, block):
    _, which, count, along, _ = DENSE_ITEMS[a]
    rows, columns = block
    if along == "rows":
        return (which * (rows // count), rows // count), (0, columns)
    return (0, rows), (which * (columns // count), columns // count)


TABLE_ROWS = 24


def attend_back_kernel(groups, *refs):
    items = PIECES + groups
    lens_ref, x_ref, w_ref, q_ref, k_ref, v_ref, att_ref, datt_ref, lse_ref, start_ref = refs[:10]
    small_a_ref, small_b_ref, bi_ref, logit_ref = refs[10:14]
    parts = refs[14 : 14 + DENSE]
    back_ref, logits_ref, small_ref = refs[18:21]
    dense_outs, group_outs = refs[21 : 21 + DENSE], refs[21 + DENSE : 24 + DENSE]
    rest = refs[24 + DENSE :]
    xt_ref, kt_ref, dot_ref, dq_ref, dk_ref, dv_ref, acc_ref, dx_ref, bias_ref, dw_ref, tab_ref, tab_in_ref = rest[:12]
    local_sem, row_send, row_recv, tab_send, tab_recv, send_sem, recv_sem = rest[12:19]
    rest = rest[19:]
    keeps, rest = rest[:PIECES], rest[PIECES:]
    firsts, seconds, thirds, fourths = (rest[j * items : (j + 1) * items] for j in range(4))

    length, width = q_ref.shape
    chunk = 256
    points = length // chunk
    heads = width // HEAD_DIM
    group = pl.program_id(0)
    z, y, x, c = my_place()
    mine = x * 2 + c

    def axes(a):
        return (y, x) if order_of(a)[0] == "y" else (x, y)

    def device_along(axis):
        return device_at(z, 1 - y, x, c) if axis == "y" else device_at(z, y, 1 - x, c)

    def half(a, ref, place):
        return ref.at[:, place] if order_of(a)[0] == "y" else ref.at[:, :, place]

    def whole_of(a, core):
        if a >= PIECES:
            return dw_ref.at[a - PIECES].at[:, :, :, core]
        array = DENSE_ITEMS[a][0]
        (r0, rows), (c0, columns) = cut_of(a, parts[array].shape[-2:])
        return parts[array].at[:, :, :, core, pl.ds(r0, rows), pl.ds(c0, columns)]

    def kept(a):
        return keeps[a] if a < PIECES else whole_of(a, c)

    def load(a, turn):
        place = 1 - axes(a)[0] if turn == 0 else axes(a)[0]
        return pltpu.make_async_copy(
            half(a, whole_of(a, c), place), half(a, keeps[a], place), local_sem.at[a, turn]
        )

    def copy_of(a, number):
        at, other = axes(a)
        if number < 2:
            place = 1 - at if number == 0 else at
            source, target = half(a, whole_of(a, 1 - c), place), half(a, firsts[a], place)
            device = device_at(z, y, x, 1 - c)
        elif number == 2:
            source, target = half(a, kept(a), 1 - at), seconds[a]
            device = device_along(order_of(a)[0])
        elif number == 3:
            source, target = half(a, kept(a), at).at[:, 1 - other], thirds[a]
            device = device_along(order_of(a)[1])
        else:
            there = lax.rem(z + number - 3, ZS)
            source, target = half(a, kept(a), at).at[:, other].at[there], fourths[a].at[number - 4]
            device = device_at(there, y, x, c)
        return pltpu.make_async_remote_copy(
            src_ref=source,
            dst_ref=target,
            send_sem=send_sem.at[a, number],
            recv_sem=recv_sem.at[a, number],
            device_id=device,
            device_id_type=MESH,
        )

    def add_into(target, source):
        lead = target.shape[:-2]
        total = functools.reduce(lambda p, q: p * q, lead, 1)

        def step(i, carry):
            where = []
            for size in reversed(lead):
                where.append(lax.rem(i, size))
                i = i // size
            where = tuple(reversed(where))
            target[where] = target[where] + source[where]
            return carry

        lax.fori_loop(0, total, step, 0)

    def begin(a):
        if a < PIECES:
            load(a, 0).start()
            load(a, 1).start()
        copy_of(a, 0).start()
        copy_of(a, 1).start()

    def after_core(a, turn):
        place = 1 - axes(a)[0] if turn == 0 else axes(a)[0]
        if a < PIECES:
            load(a, turn).wait()
        copy_of(a, turn).wait_recv()
        add_into(half(a, kept(a), place), half(a, firsts[a], place))
        if turn == 0:
            copy_of(a, 2).start()

    def after_first(a):
        at, other = axes(a)
        ours = half(a, kept(a), at)
        copy_of(a, 2).wait_recv()
        add_into(ours.at[:, 1 - other], seconds[a].at[:, 1 - other])
        copy_of(a, 3).start()
        add_into(ours.at[:, other], seconds[a].at[:, other])

    def after_second(a):
        at, other = axes(a)
        copy_of(a, 3).wait_recv()
        add_into(half(a, kept(a), at).at[:, other], thirds[a])
        for number in (5, 4, 6):
            copy_of(a, number).start()

    def finish(a):
        at, other = axes(a)
        for number in (4, 5, 6):
            copy_of(a, number).wait_recv()
        ours = half(a, kept(a), at).at[:, other]
        total = (
            ours[z].astype(F32)
            + fourths[a][0].astype(F32)
            + fourths[a][1].astype(F32)
            + fourths[a][2].astype(F32)
        )
        if a < PIECES:
            out = dense_outs[DENSE_ITEMS[a][0]]
            (r0, rows), (c0, columns) = cut_of(a, out.shape)
            out[r0 : r0 + rows, c0 : c0 + columns] = total
        else:
            s = (a - PIECES) * width
            for j, out in enumerate(group_outs):
                out[:, s : s + width] = total[:, j * width : (j + 1) * width]

    def row_copy(which, k):
        px, pc = group_partner(k, x, c)
        if which == 0:
            source, target = dx_ref.at[px * 2 + pc], back_ref.at[mine]
        else:
            source, target = logit_ref, logits_ref.at[mine]
        return pltpu.make_async_remote_copy(
            src_ref=source,
            dst_ref=target,
            send_sem=row_send.at[which, k - 1],
            recv_sem=row_recv.at[which, k - 1],
            device_id=device_at(z, y, px, pc),
            device_id_type=MESH,
        )

    def row_own(which):
        if which == 0:
            source, target = dx_ref.at[mine], back_ref.at[mine]
        else:
            source, target = logit_ref, logits_ref.at[mine]
        return pltpu.make_async_copy(source, target, local_sem.at[PIECES, which])

    def table_copy(level):
        if level < 3:
            source, target = tab_ref.at[level], tab_in_ref.at[level]
            device = (
                device_at(z, y, x, 1 - c), device_at(z, 1 - y, x, c), device_at(z, y, 1 - x, c)
            )[level]
        else:
            source, target = tab_ref.at[3], tab_in_ref.at[3 + z]
            device = device_at(lax.rem(z + level - 2, ZS), y, x, c)
        return pltpu.make_async_remote_copy(
            src_ref=source,
            dst_ref=target,
            send_sem=tab_send.at[level],
            recv_sem=tab_recv.at[level],
            device_id=device,
            device_id_type=MESH,
        )

    def table_wait(level):
        if level < 3:
            table_copy(level).wait_recv()
        else:
            slot = tab_in_ref.at[3 + lax.rem(z + ZS - (level - 2), ZS)]
            pltpu.make_async_remote_copy(
                src_ref=slot,
                dst_ref=slot,
                send_sem=tab_send.at[level],
                recv_sem=tab_recv.at[level],
                device_id=device_at(lax.rem(z + level - 2, ZS), y, x, c),
                device_id_type=MESH,
            ).wait_recv()

    def table_level(level):
        if level == 3:
            for last in (3, 4, 5):
                table_wait(last)
            table = (tab_in_ref[3] + tab_in_ref[4]) + (tab_in_ref[5] + tab_in_ref[6])
            device = ((z * 2 + y) * 2 + x) * 2 + c
            full = table.shape[1]
            row = lax.broadcasted_iota(jnp.int32, (full, 128), 0)
            lane = lax.broadcasted_iota(jnp.int32, (full, 128), 1)

            def own_lanes(values, size, at):
                chosen = jnp.where((row == at + lane) & (lane < size), 1.0, 0.0)
                return lax.dot_general(
                    values, chosen, (((1,), (0,)), ((), ())), preferred_element_type=F32, precision=lax.Precision.HIGHEST
                )

            per_row = full * 4 // (8 * ZS)
            small_ref[0:TABLE_ROWS] = own_lanes(table, full // (8 * ZS), device * (full // (8 * ZS)))
            inner_bias = own_lanes(table, per_row, lax.rem(device, full // per_row) * per_row)
            for j in range(4):

                @pl.when(device // (full // per_row) == j)
                def _(j=j):
                    small_ref[TABLE_ROWS : TABLE_ROWS + 1] = inner_bias[12 + j : 13 + j]

            small_ref[TABLE_ROWS + 1 : TABLE_ROWS + 2] = table[16:17, 0:128]
            return
        table_wait(level)
        tab_ref[level + 1] = tab_ref[level] + tab_in_ref[level]
        if level < 2:
            table_copy(level + 1).start()
        else:
            tab_in_ref[3 + z] = tab_ref[3]
            for nxt in (4, 3, 5):
                table_copy(nxt).start()

    def take_up(point):
        for word in SCATTER_PLAN.get(point, ()):
            kind, a = word[:-1], int(word[-1]) if word != "dx" else 0
            if kind == "b":
                begin(a)
            elif kind == "c0" or kind == "c1":
                after_core(a, int(kind[1]))
            elif kind == "f":
                after_first(a)
            elif kind == "s":
                after_second(a)
            elif kind == "z":
                finish(a)
            elif kind == "t":
                table_level(a)
            else:
                for k in (3, 2, 1):
                    row_copy(0, k).start()
                row_own(0).start()

    @pl.when(group == 0)
    def _():
        meet(all_partners(z, y, x, c))
        take_up(-1)
        for k in range(1, 4):
            row_copy(1, k).start()
        row_own(1).start()
        xt_ref[...] = x_ref[...].astype(F32).T.astype(BF)
        acc_ref[...] = start_ref[...]

    kt_ref[...] = k_ref[...].astype(F32).T.astype(BF)
    dot_ref[...] = (datt_ref[...].astype(F32) * att_ref[...].astype(F32)).T
    dk_ref[...] = jnp.zeros_like(dk_ref)
    dv_ref[...] = jnp.zeros_like(dv_ref)
    ends = doc_ends(lens_ref)
    key_doc = doc_numbers(lax.broadcasted_iota(jnp.int32, (length, 1), 0), ends)
    lane_head = lax.broadcasted_iota(jnp.int32, (1, width), 1) // HEAD_DIM

    def step(i, carry):
        for point in range(groups * points):

            @pl.when((group == point // points) & (i == point % points))
            def _(point=point):
                take_up(point)

        at = pl.multiple_of(i * chunk, chunk)
        query_doc = doc_numbers(lax.broadcasted_iota(jnp.int32, (1, chunk), 1) + at, ends)
        scaled = q_ref[pl.ds(at, chunk), :] * jnp.asarray(0.125, BF)
        given = datt_ref[pl.ds(at, chunk), :]
        own_q = [jnp.where(lane_head == h, scaled, jnp.zeros_like(scaled)) for h in range(heads)]
        own_d = [jnp.where(lane_head == h, given, jnp.zeros_like(given)) for h in range(heads)]
        all_probs = [[] for _ in range(length // chunk)]
        all_grads = [[] for _ in range(length // chunk)]
        for h in range(heads):
            lse = lse_ref[0, h : h + 1, pl.ds(at, chunk)]
            dots = jnp.sum(
                dot_ref[h * HEAD_DIM : (h + 1) * HEAD_DIM, pl.ds(at, chunk)], axis=0, keepdims=True
            )
            for j in range(length // chunk):
                s = j * chunk
                scores = nt(k_ref[s : s + chunk, :], own_q[h])
                scores = jnp.where(key_doc[s : s + chunk] == query_doc, scores, -1000000000.0)
                probs = jnp.exp(scores - lse)
                grad_probs = nt(v_ref[s : s + chunk, :], own_d[h])
                all_grads[j].append((probs * (grad_probs - dots)).astype(BF))
                all_probs[j].append(probs.astype(BF))
        stacked_q = jnp.concatenate(own_q, axis=0)
        stacked_d = jnp.concatenate(own_d, axis=0)
        for j in range(length // chunk):
            s = j * chunk
            dk_ref[s : s + chunk, :] += nn(jnp.concatenate(all_grads[j], axis=1), stacked_q)
            dv_ref[s : s + chunk, :] += nn(jnp.concatenate(all_probs[j], axis=1), stacked_d)
        mixed = []
        for h in range(heads):
            column = jnp.concatenate([all_grads[j][h] for j in range(length // chunk)], axis=0)
            mixed.append(nn(kt_ref[h * HEAD_DIM : (h + 1) * HEAD_DIM, :], column))
        dq_ref[pl.ds(at, chunk), :] = (jnp.concatenate(mixed, axis=0).T * 0.125).astype(BF)
        return carry

    lax.fori_loop(0, points, step, 0)
    xt = xt_ref[...]
    grads = (dq_ref[...], dk_ref[...].astype(BF), dv_ref[...].astype(BF))
    block = dw_ref.shape[1:6]
    for j, grad in enumerate(grads):
        dw_ref[group, :, :, :, :, :, j * width : (j + 1) * width] = nn(xt, grad).reshape(block + (width,)).astype(BF)
    bias_ref[group, 0:1, :] = jnp.sum(grads[0].astype(F32), axis=0, keepdims=True)
    bias_ref[group, 1:2, :] = jnp.sum(grads[2].astype(F32), axis=0, keepdims=True)
    total = acc_ref[...]
    for j, grad in enumerate(grads):
        total = total + nt(grad, w_ref[:, j * width : (j + 1) * width])
    acc_ref[...] = total

    @pl.when(group == groups - 1)
    def _():
        dx_ref[...] = acc_ref[...].reshape(dx_ref.shape).astype(BF)
        tab_ref[0, 0:CLASSES] = small_a_ref[0:CLASSES]
        for g in range(groups):
            tab_ref[0, B_QUERY : B_QUERY + 2, g * width : (g + 1) * width] = bias_ref[g, 0:2, :]
        for row, (ref, at) in {
            B_OUT: (small_b_ref, 3), GAIN1: (small_b_ref, 4), SHIFT1: (small_b_ref, 5), B_OUTER: (small_b_ref, 0),
            GAIN2: (small_b_ref, 1), SHIFT2: (small_b_ref, 2), B_POOL: (small_a_ref, 16), 16: (small_a_ref, 17),
        }.items():
            tab_ref[0, row : row + 1] = ref[at : at + 1, :]
        full = small_a_ref.shape[1]
        for j in range(4):
            tab_ref[0, 12 + j : 13 + j] = bi_ref[:, j * full : (j + 1) * full]
        tab_ref[0, 17:TABLE_ROWS] = jnp.zeros((TABLE_ROWS - 17, full), F32)
        table_copy(0).start()
        take_up(groups * points)
        for a in range(items):
            for number in range(7):
                copy_of(a, number).wait_send()
        for level in range(6):
            table_copy(level).wait_send()
        for which in (0, 1):
            for k in range(1, 4):
                row_copy(which, k).wait_recv()
                row_copy(which, k).wait_send()
            row_own(which).wait()


def attend_back(lens, rows, w_groups, q, k, v, att, datt, lse, grad_pre, small_a, small_b, grad_b_inner, logit_block, parts):
    length, width = rows.shape
    group = 256
    groups = width // group
    local_len = length // 4
    share = width // (8 * ZS)
    once = pl.Buffered(buffer_count=1)
    whole = pl.BlockSpec((length, width), lambda g: (0, 0), pipeline_mode=once)
    part = pl.BlockSpec((length, group), lambda g: (0, g))
    blocks = [p.shape[1:] for p in parts]
    split = [p.reshape((ZS, 2, 2, 2) + b) for p, b in zip(parts, blocks)]
    shapes = [r for r in blocks]
    cuts = [cut_of(a, blocks[DENSE_ITEMS[a][0]]) for a in range(PIECES)]
    blocks = [(r[1], q[1]) for r, q in cuts] + [(share, 3 * group)] * groups
    hbm = pl.BlockSpec(memory_space=pl.ANY)

    def fixed(shape):
        return pl.BlockSpec(shape, lambda g: (0,) * len(shape))

    results = [(TABLE_ROWS + 8, 128)] + shapes + [(share, width)] * 3
    arriving = []
    for lead in ((ZS, 2, 2), (ZS, 2), (ZS,), (ZS - 1,)):
        arriving += [pltpu.VMEM(lead + b, BF) for b in blocks]
    items = len(blocks)
    return pl.pallas_call(
        functools.partial(attend_back_kernel, groups),
        grid=(groups,),
        out_shape=[
            jax.ShapeDtypeStruct((4, local_len, width), BF),
            jax.ShapeDtypeStruct((4,) + logit_block.shape, F32),
        ]
        + [jax.ShapeDtypeStruct(r, F32) for r in results],
        in_specs=[
            SMEM,
            whole,
            pl.BlockSpec((width, 3 * group), lambda g: (0, g)),
            part, part, part, part, part,
            pl.BlockSpec((1, 8, length), lambda g: (g, 0, 0)),
            whole,
            fixed(small_a.shape), fixed(small_b.shape), fixed(grad_b_inner.shape), hbm,
        ]
        + [hbm] * DENSE,
        out_specs=[hbm, hbm] + [fixed(r) for r in results],
        scratch_shapes=[
            pltpu.VMEM((width, length), BF),
            pltpu.VMEM((group, length), BF),
            pltpu.VMEM((group, length), F32),
            pltpu.VMEM((length, group), BF),
            pltpu.VMEM((length, group), F32),
            pltpu.VMEM((length, group), F32),
            pltpu.VMEM((length, width), F32),
            pltpu.VMEM((4, local_len, width), BF),
            pltpu.VMEM((groups, 8, group), F32),
            pltpu.VMEM((groups, ZS, 2, 2, 2, share, 3 * group), BF),
            pltpu.VMEM((4, TABLE_ROWS, width), F32),
            pltpu.VMEM((3 + ZS, TABLE_ROWS, width), F32),
            pltpu.SemaphoreType.DMA((PIECES + 1, 2)),
            pltpu.SemaphoreType.DMA((2, 3)),
            pltpu.SemaphoreType.DMA((2, 3)),
            pltpu.SemaphoreType.DMA((6,)),
            pltpu.SemaphoreType.DMA((6,)),
            pltpu.SemaphoreType.DMA((items, 7)),
            pltpu.SemaphoreType.DMA((items, 7)),
        ]
        + [pltpu.VMEM((ZS, 2, 2) + b, BF) for b in blocks[:PIECES]]
        + arriving,
        compiler_params=pltpu.CompilerParams(
            collective_id=2, has_side_effects=True, vmem_limit_bytes=60 * 2**20
        ),
        name="attend_back",
    )(lens, rows, w_groups, q, k, v, att, datt, lse, grad_pre, small_a, small_b, grad_b_inner, logit_block, *split)


def row_copies(source_ref, target_ref, send_sem, recv_sem):
    z, y, x, c = my_place()
    copies = []
    for k in (3, 2, 1):
        px, pc = group_partner(k, x, c)
        copies.append(
            pltpu.make_async_remote_copy(
                src_ref=source_ref.at[px * 2 + pc],
                dst_ref=target_ref.at[x * 2 + c],
                send_sem=send_sem.at[k - 1],
                recv_sem=recv_sem.at[k - 1],
                device_id=device_at(z, y, px, pc),
                device_id_type=MESH,
            )
        )
    return copies, pltpu.make_async_copy(source_ref.at[x * 2 + c], target_ref.at[x * 2 + c], send_sem.at[3])


def begin_rows(*refs):
    z, y, x, c = my_place()
    meet([device_at(z, y, *group_partner(k, x, c)) for k in range(1, 4)])
    copies, own = row_copies(*refs)
    for copy in copies:
        copy.start()
    own.start()


def end_rows(*refs):
    copies, own = row_copies(*refs)
    for copy in copies:
        copy.wait()
    own.wait()


ROW_SEMAPHORES = [pltpu.SemaphoreType.DMA((4,)), pltpu.SemaphoreType.DMA((3,))]


def normal_parts(v):
    bell = jnp.exp(v * v * -0.5)
    t = 1.0 / (1.0 + jnp.abs(v) * 0.23164189)
    tail = t * (0.127414796 + t * (-0.142248368 + t * (0.710706870 + t * (-0.726576013 + t * 0.530702714)))) * bell
    return jnp.where(v >= 0.0, 1.0 - tail, tail), bell


def centered_parts(values):
    average = jnp.mean(values, axis=-1, keepdims=True)
    centered = values - average
    variance = jnp.mean(centered * centered, axis=-1, keepdims=True)
    inverse = lax.rsqrt(variance + 1e-06)
    return centered * inverse, inverse


def dense_kernel(
    lens_ref, labels_ref, b_class_ref, cot_ref, x_ref, att_ref, w_inner_ref, w_out_ref, w_pool_ref, w_outer_ref, vec_ref,
    pre_ref, summed_ref, low_ref, act_ref, dact_ref, lo_ref, dpool_ref, first_ref, small_ref, logits_ref, cot_rows_ref,
    picked_ref, row_send, row_recv,
):
    step = pl.program_id(0)

    @pl.when(step == 0)
    def _():
        begin_rows(cot_ref, cot_rows_ref, row_send, row_recv)

    rows = x_ref.shape[0]
    hidden = w_inner_ref.shape[1]
    chunk = 512

    def vec(row):
        return vec_ref[row : row + 1, :]

    full = vec_ref.shape[1]

    def bias_at(s):
        pieces, stop = [], s + chunk
        while s < stop:
            row, at = s // full, s % full
            size = min(stop - s, full - at)
            pieces.append(vec_ref[12 + row : 13 + row, at : at + size])
            s += size
        return pieces[0] if len(pieces) == 1 else jnp.concatenate(pieces, axis=1)

    pre = x_ref[...].astype(F32) + (nn(att_ref[...], w_out_ref[...]) + vec(B_OUT))
    pre_ref[...] = pre
    normed = centered_parts(pre)[0] * vec(GAIN1) + vec(SHIFT1)
    low = normed.astype(BF)
    low_ref[...] = low
    total = normed + vec(B_OUTER)
    for s in range(0, hidden, chunk):
        inner = nn(low, w_inner_ref[:, s : s + chunk]) + bias_at(s)
        phi, bell = normal_parts(inner)
        activated = (inner * phi).astype(BF)
        act_ref[:, s : s + chunk] = activated
        dact_ref[:, s : s + chunk] = (phi + inner * bell * 0.3989422804014327).astype(BF)
        total = total + nn(activated, w_outer_ref[s : s + chunk, :])
    summed_ref[...] = total
    result = (centered_parts(total)[0] * vec(GAIN2) + vec(SHIFT2)).astype(BF)
    lo_ref[...] = result
    starts = doc_starts(lens_ref)
    docs = len(starts)
    places = lax.broadcasted_iota(jnp.int32, (VEC_ROWS, rows), 1) + step * rows
    row_doc = lax.broadcasted_iota(jnp.int32, (VEC_ROWS, rows), 0)
    hit = jnp.zeros((VEC_ROWS, rows), jnp.bool_)
    for d in range(docs):
        hit = hit | ((row_doc == d) & (places == starts[d]))
    found = nn(jnp.where(hit, 1.0, 0.0).astype(BF), result)

    @pl.when(step == 0)
    def _():
        picked_ref[...] = found

    @pl.when(step > 0)
    def _():
        picked_ref[...] += found

    @pl.when(step == pl.num_programs(0) - 1)
    def _():
        picked = picked_ref[...].astype(BF)
        pooled = jnp.tanh(nn(picked, w_pool_ref[...]) + vec(B_POOL))
        pooled_low = pooled.astype(BF)
        table = vec_ref[...].astype(BF)
        column = lax.broadcasted_iota(jnp.int32, (VEC_ROWS, VEC_ROWS), 1)
        row = lax.broadcasted_iota(jnp.int32, (VEC_ROWS, VEC_ROWS), 0)
        class_bias = jnp.zeros((VEC_ROWS, VEC_ROWS), F32)
        for j in range(CLASSES):
            class_bias = jnp.where(column == j, b_class_ref[j], class_bias)
        logits = nt(pooled_low, table) + class_bias
        logits_ref[...] = jnp.concatenate([logits[0:8], jnp.zeros((8, 128 - VEC_ROWS), F32)], axis=1)
        live = column < CLASSES
        shown = jnp.where(live, logits, -jnp.inf)
        exps = jnp.where(live, jnp.exp(shown - jnp.max(shown, axis=-1, keepdims=True)), 0.0)
        probs = exps / jnp.sum(exps, axis=-1, keepdims=True)
        label = jnp.zeros((VEC_ROWS, VEC_ROWS), jnp.int32)
        for d in range(docs):
            label = jnp.where(row == d, labels_ref[lax.axis_index("fsdp"), d], label)
        grad = jnp.where(live & (row < docs), probs - jnp.where(label == column, 1.0, 0.0), 0.0)
        grad_low = grad.astype(BF)
        grad_pool = (nn(grad_low, table) * (1.0 - pooled * pooled)).astype(BF)
        dpool_ref[...] = tn(picked, grad_pool).astype(BF)
        first_ref[...] = nt(grad_pool, w_pool_ref[...])
        small_ref[0:16, :] = tn(grad_low, pooled_low)
        small_ref[16:17, :] = jnp.sum(grad_pool.astype(F32), axis=0, keepdims=True)
        width = small_ref.shape[1]
        class_sum = jnp.sum(grad_low.astype(F32), axis=0, keepdims=True)
        small_ref[17:18, :] = jnp.concatenate(
            [class_sum, jnp.zeros((1, width - VEC_ROWS), F32)], axis=1
        )
        end_rows(cot_ref, cot_rows_ref, row_send, row_recv)


def dense(lens, labels, b_class, cot, rows, att, w_inner, w_out, w_pool, w_outer, vectors):
    length, width = rows.shape
    hidden = w_outer.shape[0]
    tile = 256
    steps = length // tile
    part = pl.BlockSpec((tile, width), lambda i: (i, 0))
    wide = pl.BlockSpec((tile, hidden), lambda i: (i, 0))

    def fixed(shape, column=0):
        return pl.BlockSpec(shape, lambda i: (0, column))

    return pl.pallas_call(
        dense_kernel,
        grid=(steps,),
        out_shape=[
            jax.ShapeDtypeStruct((length, width), F32),
            jax.ShapeDtypeStruct((length, width), F32),
            jax.ShapeDtypeStruct((length, width), BF),
            jax.ShapeDtypeStruct((length, hidden), BF),
            jax.ShapeDtypeStruct((length, hidden), BF),
            jax.ShapeDtypeStruct((length, width), BF),
            jax.ShapeDtypeStruct((width, width), BF),
            jax.ShapeDtypeStruct((VEC_ROWS, width), F32),
            jax.ShapeDtypeStruct((24, width), F32),
            jax.ShapeDtypeStruct((8, 128), F32),
            jax.ShapeDtypeStruct(cot.shape, BF),
        ],
        in_specs=[
            SMEM, SMEM, SMEM, ANY, part, part,
            fixed((width, hidden)), fixed((width, width)), fixed((width, width)),
            fixed((hidden, width)), fixed((VEC_ROWS, width)),
        ],
        out_specs=[
            part, part, part, wide, wide, part,
            fixed((width, width)), fixed((VEC_ROWS, width)), fixed((24, width)), fixed((8, 128)), ANY,
        ],
        scratch_shapes=[pltpu.VMEM((VEC_ROWS, width), F32)] + ROW_SEMAPHORES,
        compiler_params=pltpu.CompilerParams(
            collective_id=3, has_side_effects=True, vmem_limit_bytes=60 * 2**20
        ),
        cost_estimate=pl.CostEstimate(flops=11 * 10**9, bytes_accessed=40 * 10**6, transcendentals=3 * 2**20),
        name="dense",
    )(lens, labels, b_class, cot, rows, att, w_inner, w_out, w_pool, w_outer, vectors)


def norm_back(grad, values, gain):
    hat, inverse = centered_parts(values)
    scaled = grad * gain
    mean_scaled = jnp.mean(scaled, axis=-1, keepdims=True)
    mean_cross = jnp.mean(scaled * hat, axis=-1, keepdims=True)
    back = (scaled - mean_scaled - hat * mean_cross) * inverse
    return back, jnp.sum(grad * hat, axis=0, keepdims=True), jnp.sum(grad, axis=0, keepdims=True)


def dense_back_kernel(
    lens_ref, result_ref, cot_ref, summed_ref, pre_ref, dact_ref, w_inner_ref, w_out_ref, w_outer_ref, vec_ref, first_ref,
    outer_ref, inner_ref, branch_ref, datt_ref, gpre_ref, small_ref, bi_ref, back_ref, row_send, row_recv,
):
    step = pl.program_id(0)
    rows = cot_ref.shape[0]
    hidden = dact_ref.shape[1]
    chunk = 512

    def vec(row):
        return vec_ref[row : row + 1, :]

    @pl.when(step == 0)
    def _():
        begin_rows(result_ref, back_ref, row_send, row_recv)
        small_ref[...] = jnp.zeros_like(small_ref)
        bi_ref[...] = jnp.zeros_like(bi_ref)

    grad = cot_ref[...].astype(F32)
    places = lax.broadcasted_iota(jnp.int32, (rows, 1), 0) + step * rows
    placed = jnp.zeros(grad.shape, F32)
    for d, start in enumerate(doc_starts(lens_ref)):
        placed = jnp.where(places == start, first_ref[d : d + 1, :], placed)
    grad = grad + placed
    grad_summed, gain2, shift2 = norm_back(grad, summed_ref[...], vec(GAIN2))
    outer = grad_summed.astype(BF)
    outer_ref[...] = outer
    grad_normed = grad_summed
    for s in range(0, hidden, chunk):
        back = nt(outer, w_outer_ref[s : s + chunk, :])
        inner = (back * dact_ref[:, s : s + chunk].astype(F32)).astype(BF)
        inner_ref[:, s : s + chunk] = inner
        bi_ref[:, s : s + chunk] += jnp.sum(inner.astype(F32), axis=0, keepdims=True)
        grad_normed = grad_normed + nt(inner, w_inner_ref[:, s : s + chunk])
    grad_pre, gain1, shift1 = norm_back(grad_normed, pre_ref[...], vec(GAIN1))
    gpre_ref[...] = grad_pre
    branch = grad_pre.astype(BF)
    branch_ref[...] = branch
    datt_ref[...] = nt(branch, w_out_ref[...]).astype(BF)
    small_ref[0:1, :] += jnp.sum(outer.astype(F32), axis=0, keepdims=True)
    small_ref[1:2, :] += gain2
    small_ref[2:3, :] += shift2
    small_ref[3:4, :] += jnp.sum(branch.astype(F32), axis=0, keepdims=True)
    small_ref[4:5, :] += gain1
    small_ref[5:6, :] += shift1

    @pl.when(step == pl.num_programs(0) - 1)
    def _():
        end_rows(result_ref, back_ref, row_send, row_recv)


def dense_back(lens, result, cot, summed, pre, dact, w_inner, w_out, w_outer, vectors, first):
    length, width = cot.shape
    hidden = w_outer.shape[0]
    tile = 256
    part = pl.BlockSpec((tile, width), lambda i: (i, 0))
    wide = pl.BlockSpec((tile, hidden), lambda i: (i, 0))

    def fixed(shape, column=0):
        return pl.BlockSpec(shape, lambda i: (0, column))

    return pl.pallas_call(
        dense_back_kernel,
        grid=(length // tile,),
        out_shape=[
            jax.ShapeDtypeStruct((length, width), BF),
            jax.ShapeDtypeStruct((length, hidden), BF),
            jax.ShapeDtypeStruct((length, width), BF),
            jax.ShapeDtypeStruct((length, width), BF),
            jax.ShapeDtypeStruct((length, width), F32),
            jax.ShapeDtypeStruct((8, width), F32),
            jax.ShapeDtypeStruct((1, hidden), F32),
            jax.ShapeDtypeStruct(result.shape, BF),
        ],
        in_specs=[
            SMEM, ANY, part, part, part, wide,
            fixed((width, hidden)), fixed((width, width)), fixed((hidden, width)),
            fixed((VEC_ROWS, width)), fixed((VEC_ROWS, width)),
        ],
        out_specs=[part, wide, part, part, part, fixed((8, width)), fixed((1, hidden)), ANY],
        scratch_shapes=ROW_SEMAPHORES,
        compiler_params=pltpu.CompilerParams(
            collective_id=4, has_side_effects=True, vmem_limit_bytes=60 * 2**20
        ),
        cost_estimate=pl.CostEstimate(flops=11 * 10**9, bytes_accessed=40 * 10**6, transcendentals=0),
        name="dense_back",
    )(lens, result, cot, summed, pre, dact, w_inner, w_out, w_outer, vectors, first)


def results_kernel(large, small_ref, *refs):
    sources, refs = refs[:large], refs[large:]
    targets, columns, inner_ref, class_ref, sem, *held = refs[:large], refs[large : large + VECTORS], *refs[large + VECTORS :]
    arriving = [pltpu.make_async_copy(s, h, sem.at[0, j]) for j, (s, h) in enumerate(zip(sources, held))]
    leaving = [pltpu.make_async_copy(h, t, sem.at[1, j]) for j, (h, t) in enumerate(zip(held, targets))]
    for copy in arriving:
        copy.start()
    for j, ref in enumerate(columns):
        ref[...] = small_ref[B_QUERY + j : B_QUERY + j + 1, 0 : ref.shape[1]]
    inner_ref[...] = small_ref[TABLE_ROWS : TABLE_ROWS + 1, 0 : inner_ref.shape[1]]
    class_ref[...] = small_ref[TABLE_ROWS + 1 : TABLE_ROWS + 2, 0 : class_ref.shape[1]]
    for came, goes in zip(arriving, leaving):
        came.wait()
        goes.start()
    for goes in leaving:
        goes.wait()


def write_results(small, arrays, share, hidden_share):
    shapes = [jax.ShapeDtypeStruct(a.shape, a.dtype) for a in arrays]
    vectors = [(1, share)] * VECTORS + [(1, hidden_share), (1, CLASSES)]
    inside = pl.BlockSpec(memory_space=pltpu.VMEM)
    return pl.pallas_call(
        functools.partial(results_kernel, len(arrays)),
        out_shape=shapes + [jax.ShapeDtypeStruct(v, F32) for v in vectors],
        in_specs=[inside] + [ANY] * len(arrays),
        out_specs=[ANY] * len(arrays) + [inside] * len(vectors),
        scratch_shapes=[pltpu.SemaphoreType.DMA((2, len(arrays)))] + [pltpu.VMEM(a.shape, a.dtype) for a in arrays],
        compiler_params=pltpu.CompilerParams(vmem_limit_bytes=60 * 2**20),
        name="results",
    )(small, *arrays)


def fast_body(
    inputs, cotangent, doc_lengths, labels, w_query, b_query, w_key, w_value, b_value, w_out, b_out, first_gain, first_shift,
    w_inner, b_inner, w_outer, b_outer, second_gain, second_shift, w_pool, b_pool, w_class, b_class,
):
    seqs, local_len, width = inputs.shape
    length = seqs * local_len
    devices = 8 * ZS
    docs = doc_lengths.shape[1]
    share = width // devices
    hidden_share = b_inner.shape[0]
    hidden = hidden_share * devices
    vector_shards = [b_query, b_value, b_out, first_gain, first_shift, b_outer, second_gain, second_shift, b_pool]
    q, k, v, att, lse, w_qkv, vectors, rows, full_inner, full_out, full_pool, full_outer = attend(
        doc_lengths, inputs, w_class.T, [member.reshape(1, share) for member in vector_shards], b_inner.reshape(1, hidden_share),
        [w_query, w_key, w_value], [w_inner, w_out, w_pool, w_outer],
    )
    rows = rows.reshape(length, width)
    full_inner = full_inner.reshape(width, hidden)
    full_out = full_out.reshape(width, width)
    full_pool = full_pool.reshape(width, width)
    full_outer = full_outer.reshape(hidden, width)
    pre, summed, low, act, dact, result, grad_pool, first, small_a, logit_block, cot = dense(
        doc_lengths, labels, b_class, cotangent, rows, att, full_inner, full_out, full_pool, full_outer, vectors
    )
    outer, inner, branch, datt, grad_pre, small_b, grad_b_inner, layer_out = dense_back(
        doc_lengths, result.reshape(seqs, local_len, width), cot.reshape(length, width), summed, pre, dact, full_inner, full_out,
        full_outer, vectors, first,
    )
    grad_outer_w = tn(act, outer).astype(BF)
    grad_inner_w = tn(low, inner).astype(BF)
    grad_out_w = tn(att, branch).astype(BF)
    grad_inputs, all_logits, small, *sums = attend_back(
        doc_lengths, rows, w_qkv, q, k, v, att, datt, lse, grad_pre, small_a, small_b, grad_b_inner, logit_block,
        [
            grad_inner_w.reshape(devices, share, hidden),
            grad_outer_w.reshape(devices, hidden_share, width),
            grad_out_w.reshape(devices, share, width),
            grad_pool.reshape(devices, share, width),
        ],
    )

    done = write_results(small, [grad_inputs, layer_out, *sums], share, hidden_share)
    grad_inputs, layer_out, o_inner, o_outer, o_out, o_pool, o_query, o_key, o_value = done[:9]
    (
        o_b_query, o_b_value, o_b_out, o_gain1, o_shift1, o_b_outer, o_gain2, o_shift2, o_b_pool, o_b_inner, o_b_class,
    ) = (vector.reshape(-1) for vector in done[9:])
    return (
        layer_out,
        all_logits[:, :docs, :CLASSES],
        grad_inputs,
        o_query,
        o_b_query,
        o_key,
        o_value,
        o_b_value,
        o_out,
        o_b_out,
        o_gain1,
        o_shift1,
        o_inner,
        o_b_inner,
        o_outer,
        o_b_outer,
        o_gain2,
        o_shift2,
        o_pool,
        o_b_pool,
        small[:CLASSES, :share].T,
        o_b_class,
    )


def solution(mesh):
    placed = (
        P("dp", "fsdp", None),
        P("dp", "fsdp", None),
        P("dp", None),
        P("dp", None),
        P(("dp", "fsdp"), None),
        P(("dp", "fsdp")),
        P(("dp", "fsdp"), None),
        P(("dp", "fsdp"), None),
        P(("dp", "fsdp")),
        P(("dp", "fsdp"), None),
        P(("dp", "fsdp")),
        P(("dp", "fsdp")),
        P(("dp", "fsdp")),
        P(("dp", "fsdp"), None),
        P(("dp", "fsdp")),
        P(("dp", "fsdp"), None),
        P(("dp", "fsdp")),
        P(("dp", "fsdp")),
        P(("dp", "fsdp")),
        P(("dp", "fsdp"), None),
        P(("dp", "fsdp")),
        P(("dp", "fsdp"), None),
        P(),
    )
    sizes = (mesh.shape["dp"], mesh.shape["fsdp"])
    chosen = fast_body if sizes == (8, 4) else general_body
    return jax.shard_map(
        chosen,
        mesh=mesh,
        in_specs=placed,
        out_specs=(
            P("dp", "fsdp", None),
            P("dp", None, None),
            P("dp", "fsdp", None),
            P(("dp", "fsdp"), None),
            P(("dp", "fsdp")),
            P(("dp", "fsdp"), None),
            P(("dp", "fsdp"), None),
            P(("dp", "fsdp")),
            P(("dp", "fsdp"), None),
            P(("dp", "fsdp")),
            P(("dp", "fsdp")),
            P(("dp", "fsdp")),
            P(("dp", "fsdp"), None),
            P(("dp", "fsdp")),
            P(("dp", "fsdp"), None),
            P(("dp", "fsdp")),
            P(("dp", "fsdp")),
            P(("dp", "fsdp")),
            P(("dp", "fsdp"), None),
            P(("dp", "fsdp")),
            P(("dp", "fsdp"), None),
            P(),
        ),
        check_vma=False,
    )
```

```python
import functools

import jax
import jax.numpy as jnp
from jax import lax
from jax.experimental import pallas as pl
from jax.experimental.pallas import tpu as pltpu
from jax.sharding import PartitionSpec as P

HEAD_DIM = 64
CLASSES = 3
MICRO = 4


def product(left_side, right_side):
    return jnp.dot(left_side, right_side, preferred_element_type=jnp.float32)


def contract_rows(left_side, right_side):
    return lax.dot_general(
        left_side, right_side, (((0,), (0,)), ((), ())), preferred_element_type=jnp.float32
    )


def times_transposed(left_side, right_side):
    return lax.dot_general(
        left_side, right_side, (((1,), (1,)), ((), ())), preferred_element_type=jnp.float32
    )


def layer_norm(values, norm_gain, norm_shift):
    average = jnp.mean(values, axis=-1, keepdims=True)
    centered = values - average
    variance = jnp.mean(centered * centered, axis=-1, keepdims=True)
    return centered * lax.rsqrt(variance + 1e-06) * norm_gain + norm_shift


def gelu_exact(values):
    return jax.nn.gelu(values, approximate=False)


def running_sum(lengths_rows):
    count = lengths_rows.shape[1]
    upper = jnp.arange(count)[:, None] <= jnp.arange(count)[None, :]
    return jnp.sum(jnp.where(upper[None], lengths_rows[:, :, None], 0), axis=1)


def segment_numbers(lengths_rows, places):
    doc_ends = running_sum(lengths_rows)
    above = (places[None, :, None] >= doc_ends[:, None, :]).astype(jnp.int32)
    return jnp.sum(above, axis=2)


def pair_heads(values):
    return values.reshape(values.shape[0], values.shape[1], 2, HEAD_DIM)


def pair_scores(query_pair, key_pair, same_doc):
    raw_scores = jnp.einsum(
        "bqhd,bkhd->bhqk", query_pair, key_pair, preferred_element_type=jnp.float32
    ) * HEAD_DIM ** (-0.5)
    return jnp.where(same_doc[:, None], raw_scores, -1000000000.0)


def lowered_masters(masters):
    return [member.astype(jnp.bfloat16) for member in masters]


def forward(tokens, lengths_rows, weights, bias_class):
    (
        w_query,
        b_query,
        w_key,
        w_value,
        b_value,
        w_out,
        b_out,
        first_gain,
        first_shift,
        w_inner,
        b_inner,
        w_outer,
        b_outer,
        second_gain,
        second_shift,
        w_pool,
        b_pool,
        w_class,
    ) = weights
    seq_count, local_len, model_width = tokens.shape
    doc_count = lengths_rows.shape[1]
    flat_rows = tokens.reshape(seq_count * local_len, model_width)
    queries = (
        (product(flat_rows, w_query) + b_query)
        .astype(jnp.bfloat16)
        .reshape(seq_count, local_len, model_width)
    )
    key_rows = (
        product(flat_rows, w_key).astype(jnp.bfloat16).reshape(seq_count, local_len, model_width)
    )
    value_rows = (
        (product(flat_rows, w_value) + b_value)
        .astype(jnp.bfloat16)
        .reshape(seq_count, local_len, model_width)
    )
    all_keys, all_values = (
        lax.all_gather(key_rows, "fsdp", axis=1, tiled=True),
        lax.all_gather(value_rows, "fsdp", axis=1, tiled=True),
    )
    full_len = all_keys.shape[1]
    own_places = lax.axis_index("fsdp") * local_len + jnp.arange(local_len, dtype=jnp.int32)
    key_places = jnp.arange(full_len, dtype=jnp.int32)
    same_doc = (
        segment_numbers(lengths_rows, own_places)[:, :, None]
        == segment_numbers(lengths_rows, key_places)[:, None, :]
    )
    pair_width = 2 * HEAD_DIM
    mixed_list = []
    log_totals = []
    for pair_index in range(model_width // pair_width):
        col_start = pair_index * pair_width
        query_pair = pair_heads(queries[:, :, col_start : col_start + pair_width])
        key_pair = pair_heads(all_keys[:, :, col_start : col_start + pair_width])
        value_pair = pair_heads(all_values[:, :, col_start : col_start + pair_width])
        scores = pair_scores(query_pair, key_pair, same_doc)
        row_peak = jnp.max(scores, axis=-1, keepdims=True)
        exp_total = jnp.sum(jnp.exp(scores - row_peak), axis=-1, keepdims=True)
        log_total = row_peak + jnp.log(exp_total)
        attn_probs = jnp.exp(scores - log_total).astype(jnp.bfloat16)
        mixed_pair = jnp.einsum(
            "bhqk,bkhd->bqhd", attn_probs, value_pair, preferred_element_type=jnp.float32
        )
        mixed_list.append(mixed_pair.reshape(seq_count, local_len, pair_width))
        log_totals.append(log_total)
    attended = (
        jnp.concatenate(mixed_list, axis=2)
        .astype(jnp.bfloat16)
        .reshape(seq_count * local_len, model_width)
    )
    branch = product(attended, w_out) + b_out
    pre_first = flat_rows.astype(jnp.float32) + branch
    normed = layer_norm(pre_first, first_gain.astype(jnp.float32), first_shift.astype(jnp.float32))
    normed_low = normed.astype(jnp.bfloat16)
    inner_pre = product(normed_low, w_inner) + b_inner
    activated = gelu_exact(inner_pre).astype(jnp.bfloat16)
    summed = normed + (product(activated, w_outer) + b_outer)
    result = layer_norm(summed, second_gain.astype(jnp.float32), second_shift.astype(jnp.float32))
    result_low = result.astype(jnp.bfloat16).reshape(seq_count, local_len, model_width)
    starts = running_sum(lengths_rows) - lengths_rows
    picker = (own_places[None, None, :] == starts[:, :, None]).astype(jnp.bfloat16)
    local_firsts = jnp.einsum(
        "bdl,blc->bdc", picker, result_low, preferred_element_type=jnp.float32
    )
    firsts = lax.psum(local_firsts, "fsdp")
    firsts_low = firsts.astype(jnp.bfloat16).reshape(seq_count * doc_count, model_width)
    pooled = jnp.tanh(product(firsts_low, w_pool) + b_pool)
    pooled_low = pooled.astype(jnp.bfloat16)
    logits = product(pooled_low, w_class) + bias_class
    stored = (
        flat_rows,
        queries,
        all_keys,
        all_values,
        same_doc,
        log_totals,
        attended,
        pre_first,
        summed,
        normed_low,
        inner_pre,
        activated,
        picker,
        firsts_low,
        pooled,
        pooled_low,
        logits,
    )
    return (result_low, logits.reshape(seq_count, doc_count, CLASSES), stored)


def backward(stored, weights, cot_rows, label_rows):
    (
        w_query,
        b_query,
        w_key,
        w_value,
        b_value,
        w_out,
        b_out,
        first_gain,
        first_shift,
        w_inner,
        b_inner,
        w_outer,
        b_outer,
        second_gain,
        second_shift,
        w_pool,
        b_pool,
        w_class,
    ) = weights
    (
        flat_rows,
        queries,
        all_keys,
        all_values,
        same_doc,
        log_totals,
        attended,
        pre_first,
        summed,
        normed_low,
        inner_pre,
        activated,
        picker,
        firsts_low,
        pooled,
        pooled_low,
        logits,
    ) = stored
    seq_count, local_len, model_width = queries.shape
    doc_count = picker.shape[1]
    owner_flag = (lax.axis_index("fsdp") == 0).astype(jnp.float32)
    row_peak = jnp.max(logits, axis=-1, keepdims=True)
    class_exp = jnp.exp(logits - row_peak)
    class_probs = class_exp / jnp.sum(class_exp, axis=-1, keepdims=True)
    onehot_labels = (
        label_rows.reshape(-1)[:, None] == jnp.arange(CLASSES, dtype=jnp.int32)[None, :]
    ).astype(jnp.float32)
    grad_logits = (class_probs - onehot_labels).astype(jnp.bfloat16)
    grad_b_class = owner_flag * jnp.sum(grad_logits.astype(jnp.float32), axis=0)
    grad_w_class = owner_flag * contract_rows(pooled_low, grad_logits)
    grad_pool_pre = (times_transposed(grad_logits, w_class) * (1.0 - pooled * pooled)).astype(
        jnp.bfloat16
    )
    grad_b_pool = owner_flag * jnp.sum(grad_pool_pre.astype(jnp.float32), axis=0)
    grad_w_pool = owner_flag * contract_rows(firsts_low, grad_pool_pre)
    grad_firsts = times_transposed(grad_pool_pre, w_pool).reshape(seq_count, doc_count, model_width)
    from_pool = jnp.einsum(
        "bdl,bdc->blc", picker.astype(jnp.float32), grad_firsts, precision=lax.Precision.HIGHEST
    )
    grad_result = cot_rows.astype(jnp.float32).reshape(-1, model_width) + from_pool.reshape(
        -1, model_width
    )
    second_back = jax.vjp(
        layer_norm, summed, second_gain.astype(jnp.float32), second_shift.astype(jnp.float32)
    )[1]
    grad_summed, grad_second_gain, grad_second_shift = second_back(grad_result)
    grad_outer = grad_summed.astype(jnp.bfloat16)
    grad_b_outer = jnp.sum(grad_outer.astype(jnp.float32), axis=0)
    grad_w_outer = contract_rows(activated, grad_outer)
    gelu_back = jax.vjp(gelu_exact, inner_pre)[1]
    grad_inner = gelu_back(times_transposed(grad_outer, w_outer))[0].astype(jnp.bfloat16)
    grad_b_inner = jnp.sum(grad_inner.astype(jnp.float32), axis=0)
    grad_w_inner = contract_rows(normed_low, grad_inner)
    grad_normed = grad_summed + times_transposed(grad_inner, w_inner)
    first_back = jax.vjp(
        layer_norm, pre_first, first_gain.astype(jnp.float32), first_shift.astype(jnp.float32)
    )[1]
    grad_pre_first, grad_first_gain, grad_first_shift = first_back(grad_normed)
    grad_branch = grad_pre_first.astype(jnp.bfloat16)
    grad_b_out = jnp.sum(grad_branch.astype(jnp.float32), axis=0)
    grad_w_out = contract_rows(attended, grad_branch)
    grad_attended = (
        times_transposed(grad_branch, w_out)
        .astype(jnp.bfloat16)
        .reshape(seq_count, local_len, model_width)
    )
    pair_width = 2 * HEAD_DIM
    query_list = []
    key_list = []
    value_list = []
    for pair_index in range(model_width // pair_width):
        col_start = pair_index * pair_width
        query_pair = pair_heads(queries[:, :, col_start : col_start + pair_width])
        key_pair = pair_heads(all_keys[:, :, col_start : col_start + pair_width])
        value_pair = pair_heads(all_values[:, :, col_start : col_start + pair_width])
        grad_pair = pair_heads(grad_attended[:, :, col_start : col_start + pair_width])
        scores = pair_scores(query_pair, key_pair, same_doc)
        attn_probs = jnp.exp(scores - log_totals[pair_index])
        grad_probs = jnp.einsum(
            "bqhd,bkhd->bhqk", grad_pair, value_pair, preferred_element_type=jnp.float32
        )
        row_dot = jnp.sum(attn_probs * grad_probs, axis=-1, keepdims=True)
        grad_scores = (attn_probs * (grad_probs - row_dot)).astype(jnp.bfloat16)
        query_part = jnp.einsum(
            "bhqk,bkhd->bqhd", grad_scores, key_pair, preferred_element_type=jnp.float32
        ) * HEAD_DIM ** (-0.5)
        query_list.append(query_part.reshape(seq_count, local_len, pair_width))
        probs_low = attn_probs.astype(jnp.bfloat16)
        key_part = jnp.einsum(
            "bhqk,bqhd->bkhd", grad_scores, query_pair, preferred_element_type=jnp.float32
        ) * HEAD_DIM ** (-0.5)
        value_part = jnp.einsum(
            "bhqk,bqhd->bkhd", probs_low, grad_pair, preferred_element_type=jnp.float32
        )
        key_list.append(key_part.reshape(seq_count, key_part.shape[1], pair_width))
        value_list.append(value_part.reshape(seq_count, value_part.shape[1], pair_width))
    key_partials = jnp.concatenate(key_list, axis=2)
    value_partials = jnp.concatenate(value_list, axis=2)
    own_keys, own_values = (
        lax.psum_scatter(
            key_partials.astype(jnp.bfloat16), "fsdp", scatter_dimension=1, tiled=True
        ).astype(jnp.float32),
        lax.psum_scatter(
            value_partials.astype(jnp.bfloat16), "fsdp", scatter_dimension=1, tiled=True
        ).astype(jnp.float32),
    )
    query_grad = jnp.concatenate(query_list, axis=2).astype(jnp.bfloat16).reshape(-1, model_width)
    key_grad = own_keys.astype(jnp.bfloat16).reshape(-1, model_width)
    value_grad = own_values.astype(jnp.bfloat16).reshape(-1, model_width)
    grad_w_query = contract_rows(flat_rows, query_grad)
    grad_b_query = jnp.sum(query_grad.astype(jnp.float32), axis=0)
    grad_w_key = contract_rows(flat_rows, key_grad)
    grad_w_value = contract_rows(flat_rows, value_grad)
    grad_b_value = jnp.sum(value_grad.astype(jnp.float32), axis=0)
    grad_tokens = (
        grad_pre_first
        + times_transposed(query_grad, w_query)
        + times_transposed(key_grad, w_key)
        + times_transposed(value_grad, w_value)
    )
    new_grads = (
        grad_w_query,
        grad_b_query,
        grad_w_key,
        grad_w_value,
        grad_b_value,
        grad_w_out,
        grad_b_out,
        grad_first_gain,
        grad_first_shift,
        grad_w_inner,
        grad_b_inner,
        grad_w_outer,
        grad_b_outer,
        grad_second_gain,
        grad_second_shift,
        grad_w_pool,
        grad_b_pool,
        grad_w_class,
    )
    return (
        new_grads,
        grad_b_class,
        grad_tokens.astype(jnp.bfloat16).reshape(seq_count, local_len, model_width),
    )


def general_body(
    inputs,
    cotangent,
    doc_lengths,
    labels,
    w_query,
    b_query,
    w_key,
    w_value,
    b_value,
    w_out,
    b_out,
    first_gain,
    first_shift,
    w_inner,
    b_inner,
    w_outer,
    b_outer,
    second_gain,
    second_shift,
    w_pool,
    b_pool,
    w_class,
    b_class,
):
    masters = (
        w_query,
        b_query,
        w_key,
        w_value,
        b_value,
        w_out,
        b_out,
        first_gain,
        first_shift,
        w_inner,
        b_inner,
        w_outer,
        b_outer,
        second_gain,
        second_shift,
        w_pool,
        b_pool,
        w_class,
    )
    group_size = lax.axis_size("dp") * lax.axis_size("fsdp")
    grad_sums = [
        jnp.zeros((member.shape[0] * group_size,) + member.shape[1:], jnp.float32)
        for member in masters
    ]
    class_sum = jnp.zeros((CLASSES,), jnp.float32)
    micro_seqs = inputs.shape[0] // MICRO
    out_list = []
    logit_list = []
    grad_list = []
    for micro_step in range(MICRO):
        first_seq = micro_step * micro_seqs
        after_seq = first_seq + micro_seqs
        tokens = inputs[first_seq:after_seq]
        lengths_rows = doc_lengths[first_seq:after_seq]
        pieces = lowered_masters(masters)
        front_weights = (
            lax.all_gather(pieces[0], ("dp", "fsdp"), axis=0, tiled=True),
            lax.all_gather(pieces[1], ("dp", "fsdp"), axis=0, tiled=True),
            lax.all_gather(pieces[2], ("dp", "fsdp"), axis=0, tiled=True),
            lax.all_gather(pieces[3], ("dp", "fsdp"), axis=0, tiled=True),
            lax.all_gather(pieces[4], ("dp", "fsdp"), axis=0, tiled=True),
            lax.all_gather(pieces[5], ("dp", "fsdp"), axis=0, tiled=True),
            lax.all_gather(pieces[6], ("dp", "fsdp"), axis=0, tiled=True),
            lax.all_gather(pieces[7], ("dp", "fsdp"), axis=0, tiled=True),
            lax.all_gather(pieces[8], ("dp", "fsdp"), axis=0, tiled=True),
            lax.all_gather(pieces[9], ("dp", "fsdp"), axis=0, tiled=True),
            lax.all_gather(pieces[10], ("dp", "fsdp"), axis=0, tiled=True),
            lax.all_gather(pieces[11], ("dp", "fsdp"), axis=0, tiled=True),
            lax.all_gather(pieces[12], ("dp", "fsdp"), axis=0, tiled=True),
            lax.all_gather(pieces[13], ("dp", "fsdp"), axis=0, tiled=True),
            lax.all_gather(pieces[14], ("dp", "fsdp"), axis=0, tiled=True),
            lax.all_gather(pieces[15], ("dp", "fsdp"), axis=0, tiled=True),
            lax.all_gather(pieces[16], ("dp", "fsdp"), axis=0, tiled=True),
            lax.all_gather(pieces[17], ("dp", "fsdp"), axis=0, tiled=True),
        )
        result_low, logits, stored = forward(tokens, lengths_rows, front_weights, b_class)
        out_list.append(result_low)
        logit_list.append(logits)
        back_weights = (
            lax.all_gather(pieces[0], ("dp", "fsdp"), axis=0, tiled=True),
            lax.all_gather(pieces[1], ("dp", "fsdp"), axis=0, tiled=True),
            lax.all_gather(pieces[2], ("dp", "fsdp"), axis=0, tiled=True),
            lax.all_gather(pieces[3], ("dp", "fsdp"), axis=0, tiled=True),
            lax.all_gather(pieces[4], ("dp", "fsdp"), axis=0, tiled=True),
            lax.all_gather(pieces[5], ("dp", "fsdp"), axis=0, tiled=True),
            lax.all_gather(pieces[6], ("dp", "fsdp"), axis=0, tiled=True),
            lax.all_gather(pieces[7], ("dp", "fsdp"), axis=0, tiled=True),
            lax.all_gather(pieces[8], ("dp", "fsdp"), axis=0, tiled=True),
            lax.all_gather(pieces[9], ("dp", "fsdp"), axis=0, tiled=True),
            lax.all_gather(pieces[10], ("dp", "fsdp"), axis=0, tiled=True),
            lax.all_gather(pieces[11], ("dp", "fsdp"), axis=0, tiled=True),
            lax.all_gather(pieces[12], ("dp", "fsdp"), axis=0, tiled=True),
            lax.all_gather(pieces[13], ("dp", "fsdp"), axis=0, tiled=True),
            lax.all_gather(pieces[14], ("dp", "fsdp"), axis=0, tiled=True),
            lax.all_gather(pieces[15], ("dp", "fsdp"), axis=0, tiled=True),
            lax.all_gather(pieces[16], ("dp", "fsdp"), axis=0, tiled=True),
            lax.all_gather(pieces[17], ("dp", "fsdp"), axis=0, tiled=True),
        )
        stored = forward(tokens, lengths_rows, back_weights, b_class)[2]
        new_grads, class_grad, grad_tokens = backward(
            stored, back_weights, cotangent[first_seq:after_seq], labels[first_seq:after_seq]
        )
        grad_sums = [running + fresh_grad for running, fresh_grad in zip(grad_sums, new_grads)]
        class_sum = class_sum + class_grad
        grad_list.append(grad_tokens)
    owned = (
        lax.psum_scatter(grad_sums[0], ("dp", "fsdp"), scatter_dimension=0, tiled=True),
        lax.psum_scatter(grad_sums[1], ("dp", "fsdp"), scatter_dimension=0, tiled=True),
        lax.psum_scatter(grad_sums[2], ("dp", "fsdp"), scatter_dimension=0, tiled=True),
        lax.psum_scatter(grad_sums[3], ("dp", "fsdp"), scatter_dimension=0, tiled=True),
        lax.psum_scatter(grad_sums[4], ("dp", "fsdp"), scatter_dimension=0, tiled=True),
        lax.psum_scatter(grad_sums[5], ("dp", "fsdp"), scatter_dimension=0, tiled=True),
        lax.psum_scatter(grad_sums[6], ("dp", "fsdp"), scatter_dimension=0, tiled=True),
        lax.psum_scatter(grad_sums[7], ("dp", "fsdp"), scatter_dimension=0, tiled=True),
        lax.psum_scatter(grad_sums[8], ("dp", "fsdp"), scatter_dimension=0, tiled=True),
        lax.psum_scatter(grad_sums[9], ("dp", "fsdp"), scatter_dimension=0, tiled=True),
        lax.psum_scatter(grad_sums[10], ("dp", "fsdp"), scatter_dimension=0, tiled=True),
        lax.psum_scatter(grad_sums[11], ("dp", "fsdp"), scatter_dimension=0, tiled=True),
        lax.psum_scatter(grad_sums[12], ("dp", "fsdp"), scatter_dimension=0, tiled=True),
        lax.psum_scatter(grad_sums[13], ("dp", "fsdp"), scatter_dimension=0, tiled=True),
        lax.psum_scatter(grad_sums[14], ("dp", "fsdp"), scatter_dimension=0, tiled=True),
        lax.psum_scatter(grad_sums[15], ("dp", "fsdp"), scatter_dimension=0, tiled=True),
        lax.psum_scatter(grad_sums[16], ("dp", "fsdp"), scatter_dimension=0, tiled=True),
        lax.psum_scatter(grad_sums[17], ("dp", "fsdp"), scatter_dimension=0, tiled=True),
    )
    class_total = lax.psum(class_sum, ("dp", "fsdp"))
    return (
        jnp.concatenate(out_list, axis=0),
        jnp.concatenate(logit_list, axis=0),
        jnp.concatenate(grad_list, axis=0),
        owned[0],
        owned[1],
        owned[2],
        owned[3],
        owned[4],
        owned[5],
        owned[6],
        owned[7],
        owned[8],
        owned[9],
        owned[10],
        owned[11],
        owned[12],
        owned[13],
        owned[14],
        owned[15],
        owned[16],
        owned[17],
        class_total,
    )


BF = jnp.bfloat16
F32 = jnp.float32
MESH = pl.DeviceIdType.MESH
ANY = pl.BlockSpec(memory_space=pl.ANY)
SMEM = pl.BlockSpec(memory_space=pltpu.SMEM)
ZS = 4
CLASS_ROWS, B_QUERY, B_VALUE, B_OUT, GAIN1, SHIFT1, B_OUTER, GAIN2, SHIFT2, B_POOL = (0, 3, 4, 5, 6, 7, 8, 9, 10, 11)
VEC_ROWS = 16
KB, K0, K1, KF, KS, KZ, KE, KT, KX = range(9)


def nn(a, b):
    return lax.dot_general(a, b, (((1,), (0,)), ((), ())), preferred_element_type=F32)


def nt(a, b):
    return lax.dot_general(a, b, (((1,), (1,)), ((), ())), preferred_element_type=F32)


def tn(a, b):
    return lax.dot_general(a, b, (((0,), (0,)), ((), ())), preferred_element_type=F32)


def my_place():
    dp, fs = lax.axis_index("dp"), lax.axis_index("fsdp")
    return dp // 2, lax.rem(dp, 2), fs // 2, lax.rem(fs, 2)


def device_at(z, y, x, c):
    return (z * 2 + y, x * 2 + c)


def meet(partners):
    barrier = pltpu.get_barrier_semaphore()
    for partner in partners:
        pl.semaphore_signal(barrier, inc=1, device_id=partner, device_id_type=MESH)
    pl.semaphore_wait(barrier, len(partners))


def all_partners(z, y, x, c):
    found = [device_at(lax.rem(z + k, ZS), y, x, c) for k in range(1, ZS)]
    found.append(device_at(z, 1 - y, x, c))
    found.append(device_at(z, y, 1 - x, c))
    found.append(device_at(z, y, x, 1 - c))
    found.append(device_at(z, y, 1 - x, 1 - c))
    return found


def group_partner(k, x, c):
    return (1 - x if k >= 2 else x, 1 - c if k % 2 == 1 else c)


def doc_ends(lens_ref):
    ends = []
    total = 0
    for d in range(lens_ref.shape[1]):
        total = total + lens_ref[lax.axis_index("fsdp"), d]
        ends.append(total)
    return ends


def doc_starts(lens_ref):
    return [0] + doc_ends(lens_ref)[:-1]


def doc_numbers(places, ends):
    number = jnp.zeros(places.shape, jnp.int32)
    for end in ends:
        number = number + (places >= end).astype(jnp.int32)
    return number


def gather_tools(plan, orders, view, own_block, keep_sem, send_sem, recv_sem, other=None):
    z, y, x, c = my_place()
    everything = slice(None)

    def along(a, axis):
        return device_at(z, 1 - y, x, c) if orders[a][axis] == "y" else device_at(z, y, 1 - x, c)

    def copy_of(a, number):
        core = device_at(z, y, x, 1 - c)
        first_other = (1 - y, x) if orders[a][0] == "y" else (y, 1 - x)
        if number < 3:
            source, target = own_block(a), view(a, (z, y, x, c))
            device = device_at(lax.rem(z + number + 1, ZS), y, x, c)
        elif number < 6:
            source = target = view(a, (everything, y, x, c))
            device = (along(a, 0), along(a, 1), core)[number - 3]
        elif number < 8:
            source = target = view(a, (everything, first_other[0], first_other[1], c))
            device = along(a, 1) if number == 6 else core
        else:
            if orders[a][1] == "y":
                source = target = view(a, (everything, 1 - y, everything, c))
            else:
                source = target = view(a, (everything, everything, 1 - x, c))
            device = core
        return pltpu.make_async_remote_copy(
            src_ref=source,
            dst_ref=target,
            send_sem=send_sem.at[a, number],
            recv_sem=recv_sem.at[a, number],
            device_id=device,
            device_id_type=MESH,
        )

    def keep(a):
        return pltpu.make_async_copy(own_block(a), view(a, (z, y, x, c)), keep_sem.at[a])

    def take_up(point):
        for kind, a in plan.get(point, ()):
            if kind == KB:
                for number in (1, 0, 2):
                    copy_of(a, number).start()
                keep(a).start()
            elif kind == KZ:
                for number in (0, 1, 2):
                    copy_of(a, number).wait_recv()
                keep(a).wait()
                for number in (3, 4, 5):
                    copy_of(a, number).start()
            elif kind == KF:
                copy_of(a, 3).wait_recv()
                for number in (6, 7):
                    copy_of(a, number).start()
            elif kind == KS:
                copy_of(a, 4).wait_recv()
                copy_of(a, 6).wait_recv()
                copy_of(a, 8).start()
            elif kind == KT:
                other(a)
            else:
                for number in (5, 7, 8):
                    copy_of(a, number).wait_recv()

    def all_sent():
        for a in range(len(orders)):
            for number in range(9):
                copy_of(a, number).wait_send()

    return take_up, all_sent


GATHER_PIECES = ((1, 0, 1, "rows"), (0, 0, 2, "columns"), (0, 1, 2, "columns"), (2, 0, 2, "rows"), (2, 1, 2, "rows"))
GATHER_ORDERS = ("xy", "xy", "yx", "xy", "yx", "xy", "yx", "xy")
GATHER_PLAN = {
    -1: (
        (KB, 0), (KT, 0), (KZ, 0), (KB, 1), (KB, 2), (KT, 1), (KB, 3), (KB, 4), (KB, 5), (KF, 0), (KT, 2), (KS, 0), (KB, 6), (KZ, 1),
        (KT, 3), (KZ, 2), (KZ, 3), (KE, 0),
    ),
    0: ((KB, 7),),
    1: ((KF, 1), (KF, 2), (KF, 3), (KZ, 4)),
    3: ((KS, 1), (KS, 2), (KZ, 5), (KS, 3), (KE, 1)),
    4: ((KZ, 6), (KE, 2), (KE, 3), (KF, 4)),
    5: ((KF, 5),),
    7: ((KZ, 7),),
    8: ((KS, 4), (KF, 6)),
    9: ((KS, 5), (KE, 4), (KF, 7), (KE, 5)),
    10: ((KS, 6),),
    11: ((KS, 7), (KE, 6)),
    12: ((KE, 7),),
}
DENSE_ARRAYS = 3
VECTORS = 9


def part_of(piece, block):
    _, which, count, along = piece
    rows, columns = block
    if along == "rows":
        return (which * (rows // count), rows // count), (0, columns)
    return (0, rows), (which * (columns // count), columns // count)


def attend_kernel(groups, *refs):
    lens_ref, tokens_ref, class_ref = refs[:3]
    vectors, b_inner_ref, (wq_ref, wk_ref, wv_ref) = refs[3 : 3 + VECTORS], refs[3 + VECTORS], refs[4 + VECTORS : 7 + VECTORS]
    refs = refs[7 + VECTORS :]
    shards, refs = refs[:DENSE_ARRAYS], refs[DENSE_ARRAYS:]
    q_ref, k_ref, v_ref, att_ref, lse_ref, w_ref, vec_ref, rows_ref = refs[:8]
    wholes = refs[8 : 8 + DENSE_ARRAYS]
    refs = refs[8 + DENSE_ARRAYS :]
    x_ref, vt_ref, qkv_shard, qkv_ref, tab_ref, tab_in_ref = refs[:6]
    local_sem, row_send, row_recv, tab_send, tab_recv, send_sem, recv_sem = refs[6:13]
    own = refs[13 : 13 + DENSE_ARRAYS]
    length, width = q_ref.shape
    chunk = 256
    points = length // chunk
    heads = width // HEAD_DIM
    items = groups + len(GATHER_PIECES)
    group = pl.program_id(0)
    z, y, x, c = my_place()
    mine = x * 2 + c

    def row_copy(k):
        px, pc = group_partner(k, x, c)
        return pltpu.make_async_remote_copy(
            src_ref=tokens_ref.at[px * 2 + pc],
            dst_ref=x_ref.at[mine],
            send_sem=row_send.at[k - 1],
            recv_sem=row_recv.at[k - 1],
            device_id=device_at(z, y, px, pc),
            device_id_type=MESH,
        )

    def row_own():
        return pltpu.make_async_copy(tokens_ref.at[mine], x_ref.at[mine], local_sem.at[0])

    def rows_out():
        return pltpu.make_async_copy(x_ref, rows_ref, local_sem.at[1])

    def table_copy(level):
        if level < 3:
            source, device = tab_ref.at[0], device_at(lax.rem(z + level + 1, ZS), y, x, c)
        else:
            source = tab_ref.at[level - 2]
            device = (device_at(z, y, 1 - x, c), device_at(z, 1 - y, x, c), device_at(z, y, x, 1 - c))[level - 3]
        return pltpu.make_async_remote_copy(
            src_ref=source,
            dst_ref=tab_in_ref.at[level],
            send_sem=tab_send.at[level],
            recv_sem=tab_recv.at[level],
            device_id=device,
            device_id_type=MESH,
        )

    def array_of(a):
        if a < groups:
            return qkv_ref.at[a], qkv_shard.at[a], None
        piece = GATHER_PIECES[a - groups]
        return wholes[piece[0]], own[piece[0]], part_of(piece, own[piece[0]].shape)

    def view(a, where):
        ref, _, part = array_of(a)
        if part is None:
            return ref.at[where]
        (r0, rows), (c0, columns) = part
        return ref.at[where + (pl.ds(r0, rows), pl.ds(c0, columns))]

    def own_block(a):
        _, ref, part = array_of(a)
        if part is None:
            return ref
        (r0, rows), (c0, columns) = part
        return ref.at[pl.ds(r0, rows), pl.ds(c0, columns)]

    def table_level(level):
        if level == 0:
            for k in (0, 1, 2):
                table_copy(k).wait_recv()
            tab_ref[1] = (tab_ref[0] + tab_in_ref[0]) + (tab_in_ref[1] + tab_in_ref[2])
        else:
            table_copy(level + 2).wait_recv()
            tab_ref[level + 1] = tab_ref[level] + tab_in_ref[level + 2]
        if level < 3:
            table_copy(level + 3).start()
        else:
            vec_ref[...] = tab_ref[4]

    take_up, all_sent = gather_tools(
        GATHER_PLAN, GATHER_ORDERS, view, own_block, local_sem.at[pl.ds(2, items)], send_sem, recv_sem, table_level
    )

    @pl.when(group == 0)
    def _():
        device = ((z * 2 + y) * 2 + x) * 2 + c
        full = tab_ref.shape[2]

        def spread(values, at):
            n = values.shape[1]
            here = lax.broadcasted_iota(jnp.int32, (n, full), 1) - at == lax.broadcasted_iota(jnp.int32, (n, full), 0)
            return nn(values.astype(BF), jnp.where(here, 1.0, 0.0).astype(BF))

        share = class_ref.shape[1]
        tab_ref[0, 0:CLASSES] = spread(class_ref[...], device * share)
        for j, ref in enumerate(vectors):
            tab_ref[0, CLASSES + j : CLASSES + j + 1] = spread(ref[...], device * share)
        per_row = full // b_inner_ref.shape[1]
        inner_bias = spread(b_inner_ref[...], lax.rem(device, per_row) * b_inner_ref.shape[1])
        for j in range(4):
            tab_ref[0, 12 + j : 13 + j] = jnp.where(device // per_row == j, inner_bias, 0.0)
        for g in range(groups):
            for j, ref in enumerate((wq_ref, wk_ref, wv_ref)):
                qkv_shard[g, :, j * width : (j + 1) * width] = ref[:, g * width : (g + 1) * width].astype(BF)
        for target, ref in zip(own, shards):
            target[...] = ref[...].astype(BF)
        meet(all_partners(z, y, x, c))
        for level in (1, 0, 2):
            table_copy(level).start()
        for k in (3, 2, 1):
            row_copy(k).start()
        row_own().start()
        take_up(-1)
        row_own().wait()
        for k in (1, 2, 3):
            row_copy(k).wait_recv()
        rows_out().start()

    tokens = x_ref[...].reshape(length, x_ref.shape[2])
    weights = qkv_ref[group].astype(F32).reshape(x_ref.shape[2], 3 * width).astype(BF)
    w_ref[...] = weights
    bias = tab_ref[4, B_QUERY : B_QUERY + 2, pl.ds(pl.multiple_of(group * width, width), width)]
    q_ref[...] = (nn(tokens, weights[:, :width]) + bias[0:1]).astype(BF)
    k_ref[...] = nn(tokens, weights[:, width : 2 * width]).astype(BF)
    values = (nn(tokens, weights[:, 2 * width :]) + bias[1:2]).astype(BF)
    v_ref[...] = values
    vt_ref[...] = values.astype(F32).T.astype(BF)
    ends = doc_ends(lens_ref)
    key_doc = doc_numbers(lax.broadcasted_iota(jnp.int32, (length, 1), 0), ends)
    lane_head = lax.broadcasted_iota(jnp.int32, (1, width), 1) // HEAD_DIM

    def step(i, carry):
        for point in range(groups * points):
            if point in GATHER_PLAN:

                @pl.when((group == point // points) & (i == point % points))
                def _(point=point):
                    take_up(point)

        at = pl.multiple_of(i * chunk, chunk)
        query_doc = doc_numbers(lax.broadcasted_iota(jnp.int32, (1, chunk), 1) + at, ends)
        scaled = q_ref[pl.ds(at, chunk), :] * jnp.asarray(0.125, BF)
        mixed = []
        for h in range(heads):
            own_q = jnp.where(lane_head == h, scaled, jnp.zeros_like(scaled))
            blocks = []
            for s in range(0, length, chunk):
                scores = nt(k_ref[s : s + chunk, :], own_q)
                blocks.append(jnp.where(key_doc[s : s + chunk] == query_doc, scores, -1000000000.0))
            peak = functools.reduce(jnp.maximum, [jnp.max(b, axis=0, keepdims=True) for b in blocks])
            exps = [jnp.exp(b - peak) for b in blocks]
            total = functools.reduce(jnp.add, [jnp.sum(e, axis=0, keepdims=True) for e in exps])
            scale = 1.0 / total
            probs = jnp.concatenate([(e * scale).astype(BF) for e in exps], axis=0)
            mixed.append(nn(vt_ref[h * HEAD_DIM : (h + 1) * HEAD_DIM, :], probs))
            lse_ref[0, h : h + 1, pl.ds(at, chunk)] = peak + jnp.log(total)
        att_ref[pl.ds(at, chunk), :] = jnp.concatenate(mixed, axis=0).T.astype(BF)
        return carry

    lax.fori_loop(0, points, step, 0)

    @pl.when(group == groups - 1)
    def _():
        take_up(groups * points)
        all_sent()
        for level in range(6):
            table_copy(level).wait_send()
        for k in range(1, 4):
            row_copy(k).wait_send()
        rows_out().wait()


def attend(lens, tokens, class_shard, vectors, b_inner, qkv_shards, shards):
    seqs, local_len, width = tokens.shape
    length = seqs * local_len
    group = 256
    groups = width // group
    share = qkv_shards[0].shape[0]
    hbm = pl.BlockSpec(memory_space=pl.ANY)
    part = pl.BlockSpec((length, group), lambda g: (0, g))
    once = pl.Buffered(buffer_count=1)
    items = groups + len(GATHER_PIECES)

    def fixed(shape):
        return pl.BlockSpec(shape, lambda g: (0,) * len(shape), pipeline_mode=once)

    lead = (ZS, 2, 2, 2)
    return pl.pallas_call(
        functools.partial(attend_kernel, groups),
        grid=(groups,),
        out_shape=[jax.ShapeDtypeStruct((length, width), BF)] * 4
        + [
            jax.ShapeDtypeStruct((groups, 8, length), F32),
            jax.ShapeDtypeStruct((width, 3 * width), BF),
            jax.ShapeDtypeStruct((VEC_ROWS, width), F32),
            jax.ShapeDtypeStruct(tokens.shape, BF),
        ]
        + [jax.ShapeDtypeStruct(lead + s.shape, BF) for s in shards],
        in_specs=[SMEM, hbm, fixed(class_shard.shape)]
        + [fixed(v.shape) for v in vectors]
        + [fixed(b_inner.shape)]
        + [fixed(s.shape) for s in qkv_shards]
        + [fixed(s.shape) for s in shards],
        out_specs=[part] * 4
        + [
            pl.BlockSpec((1, 8, length), lambda g: (g, 0, 0)),
            pl.BlockSpec((width, 3 * group), lambda g: (0, g)),
            pl.BlockSpec((VEC_ROWS, width), lambda g: (0, 0)),
            hbm,
        ]
        + [hbm] * DENSE_ARRAYS,
        scratch_shapes=[
            pltpu.VMEM(tokens.shape, BF),
            pltpu.VMEM((group, length), BF),
            pltpu.VMEM((groups, share, 3 * group), BF),
            pltpu.VMEM((groups,) + lead + (share, 3 * group), BF),
            pltpu.VMEM((5, VEC_ROWS, width), F32),
            pltpu.VMEM((6, VEC_ROWS, width), F32),
            pltpu.SemaphoreType.DMA((2 + items,)),
            pltpu.SemaphoreType.DMA((3,)),
            pltpu.SemaphoreType.DMA((3,)),
            pltpu.SemaphoreType.DMA((6,)),
            pltpu.SemaphoreType.DMA((6,)),
            pltpu.SemaphoreType.DMA((items, 9)),
            pltpu.SemaphoreType.DMA((items, 9)),
        ]
        + [pltpu.VMEM(s.shape, BF) for s in shards],
        compiler_params=pltpu.CompilerParams(
            collective_id=1, has_side_effects=True, vmem_limit_bytes=60 * 2**20
        ),
        name="attend",
    )(lens, tokens, class_shard, *vectors, b_inner, *qkv_shards, *shards)


DENSE = 4
DENSE_ITEMS = (
    (2, 0, 1, "rows", "yx"), (3, 0, 1, "rows", "xy"),
    (0, 0, 2, "columns", "yx"), (1, 0, 2, "rows", "xy"), (0, 1, 2, "columns", "yx"), (1, 1, 2, "rows", "xy"),
)
GROUP_ORDERS = ("yx", "xy", "yx")
SCATTER_PLAN = {
    -1: ((KB, 0),),
    0: ((KB, 1),),
    1: ((K0, 0), (K0, 1), (KB, 2), (K1, 0), (K1, 1)),
    2: ((KB, 3),),
    3: ((K0, 2), (KB, 4), (K1, 2), (KF, 0), (KF, 1), (K0, 3), (K1, 3), (KB, 5)),
    4: ((KS, 0), (KS, 1), (KB, 6)),
    5: ((K0, 4), (K0, 5), (K1, 4), (K1, 5)),
    6: ((KZ, 0), (KZ, 1)),
    7: ((KF, 2), (KF, 3)),
    8: ((KB, 7),),
    9: ((K0, 6), (K0, 7), (K1, 6), (K1, 7)),
    10: ((KF, 4), (KS, 2), (KS, 3)),
    11: ((KF, 5),),
    12: ((KB, 8), (KX, 0), (KF, 6), (KF, 7), (KT, 0), (KS, 4), (KS, 5), (KZ, 2), (K0, 8), (K1, 8), (KZ, 3), (KT, 1), (KS, 7), (KS, 6), (KF, 8), (KT, 2), (KZ, 7), (KS, 8), (KZ, 4), (KZ, 6), (KZ, 5), (KT, 3), (KZ, 8)),
}
PIECES = len(DENSE_ITEMS)


def order_of(a):
    return DENSE_ITEMS[a][4] if a < PIECES else GROUP_ORDERS[a - PIECES]


def cut_of(a, block):
    _, which, count, along, _ = DENSE_ITEMS[a]
    rows, columns = block
    if along == "rows":
        return (which * (rows // count), rows // count), (0, columns)
    return (0, rows), (which * (columns // count), columns // count)


TABLE_ROWS = 24


def attend_back_kernel(groups, *refs):
    items = PIECES + groups
    lens_ref, x_ref, w_ref, q_ref, k_ref, v_ref, att_ref, datt_ref, lse_ref, start_ref = refs[:10]
    small_a_ref, small_b_ref, bi_ref, logit_ref = refs[10:14]
    parts = refs[14 : 14 + DENSE]
    back_ref, logits_ref, small_ref = refs[18:21]
    dense_outs, group_outs = refs[21 : 21 + DENSE], refs[21 + DENSE : 24 + DENSE]
    rest = refs[24 + DENSE :]
    xt_ref, kt_ref, dot_ref, dq_ref, dk_ref, dv_ref, acc_ref, dx_ref, bias_ref, dw_ref, tab_ref, tab_in_ref = rest[:12]
    local_sem, row_send, row_recv, tab_send, tab_recv, send_sem, recv_sem = rest[12:19]
    rest = rest[19:]
    keeps, rest = rest[:PIECES], rest[PIECES:]
    firsts, seconds, thirds, fourths = (rest[j * items : (j + 1) * items] for j in range(4))

    length, width = q_ref.shape
    chunk = 256
    points = length // chunk
    heads = width // HEAD_DIM
    group = pl.program_id(0)
    z, y, x, c = my_place()
    mine = x * 2 + c

    def axes(a):
        return (y, x) if order_of(a)[0] == "y" else (x, y)

    def device_along(axis):
        return device_at(z, 1 - y, x, c) if axis == "y" else device_at(z, y, 1 - x, c)

    def half(a, ref, place):
        return ref.at[:, place] if order_of(a)[0] == "y" else ref.at[:, :, place]

    def whole_of(a, core):
        if a >= PIECES:
            return dw_ref.at[a - PIECES].at[:, :, :, core]
        array = DENSE_ITEMS[a][0]
        (r0, rows), (c0, columns) = cut_of(a, parts[array].shape[-2:])
        return parts[array].at[:, :, :, core, pl.ds(r0, rows), pl.ds(c0, columns)]

    def kept(a):
        return keeps[a] if a < PIECES else whole_of(a, c)

    def load(a, turn):
        place = 1 - axes(a)[0] if turn == 0 else axes(a)[0]
        return pltpu.make_async_copy(
            half(a, whole_of(a, c), place), half(a, keeps[a], place), local_sem.at[a, turn]
        )

    def copy_of(a, number):
        at, other = axes(a)
        if number < 2:
            place = 1 - at if number == 0 else at
            source, target = half(a, whole_of(a, 1 - c), place), half(a, firsts[a], place)
            device = device_at(z, y, x, 1 - c)
        elif number == 2:
            source, target = half(a, kept(a), 1 - at), seconds[a]
            device = device_along(order_of(a)[0])
        elif number == 3:
            source, target = half(a, kept(a), at).at[:, 1 - other], thirds[a]
            device = device_along(order_of(a)[1])
        else:
            there = lax.rem(z + number - 3, ZS)
            source, target = half(a, kept(a), at).at[:, other].at[there], fourths[a].at[number - 4]
            device = device_at(there, y, x, c)
        return pltpu.make_async_remote_copy(
            src_ref=source,
            dst_ref=target,
            send_sem=send_sem.at[a, number],
            recv_sem=recv_sem.at[a, number],
            device_id=device,
            device_id_type=MESH,
        )

    def add_into(target, source):
        lead = target.shape[:-2]
        total = functools.reduce(lambda p, q: p * q, lead, 1)

        def step(i, carry):
            where = []
            for size in reversed(lead):
                where.append(lax.rem(i, size))
                i = i // size
            where = tuple(reversed(where))
            target[where] = target[where] + source[where]
            return carry

        lax.fori_loop(0, total, step, 0)

    def begin(a):
        if a < PIECES:
            load(a, 0).start()
            load(a, 1).start()
        copy_of(a, 0).start()
        copy_of(a, 1).start()

    def after_core(a, turn):
        place = 1 - axes(a)[0] if turn == 0 else axes(a)[0]
        if a < PIECES:
            load(a, turn).wait()
        copy_of(a, turn).wait_recv()
        add_into(half(a, kept(a), place), half(a, firsts[a], place))
        if turn == 0:
            copy_of(a, 2).start()

    def after_first(a):
        at, other = axes(a)
        ours = half(a, kept(a), at)
        copy_of(a, 2).wait_recv()
        add_into(ours.at[:, 1 - other], seconds[a].at[:, 1 - other])
        copy_of(a, 3).start()
        add_into(ours.at[:, other], seconds[a].at[:, other])

    def after_second(a):
        at, other = axes(a)
        copy_of(a, 3).wait_recv()
        add_into(half(a, kept(a), at).at[:, other], thirds[a])
        for number in (5, 4, 6):
            copy_of(a, number).start()

    def finish(a):
        at, other = axes(a)
        for number in (4, 5, 6):
            copy_of(a, number).wait_recv()
        ours = half(a, kept(a), at).at[:, other]
        total = (
            ours[z].astype(F32)
            + fourths[a][0].astype(F32)
            + fourths[a][1].astype(F32)
            + fourths[a][2].astype(F32)
        )
        if a < PIECES:
            out = dense_outs[DENSE_ITEMS[a][0]]
            (r0, rows), (c0, columns) = cut_of(a, out.shape)
            out[r0 : r0 + rows, c0 : c0 + columns] = total
        else:
            s = (a - PIECES) * width
            for j, out in enumerate(group_outs):
                out[:, s : s + width] = total[:, j * width : (j + 1) * width]

    def row_copy(which, k):
        px, pc = group_partner(k, x, c)
        if which == 0:
            source, target = dx_ref.at[px * 2 + pc], back_ref.at[mine]
        else:
            source, target = logit_ref, logits_ref.at[mine]
        return pltpu.make_async_remote_copy(
            src_ref=source,
            dst_ref=target,
            send_sem=row_send.at[which, k - 1],
            recv_sem=row_recv.at[which, k - 1],
            device_id=device_at(z, y, px, pc),
            device_id_type=MESH,
        )

    def row_own(which):
        if which == 0:
            source, target = dx_ref.at[mine], back_ref.at[mine]
        else:
            source, target = logit_ref, logits_ref.at[mine]
        return pltpu.make_async_copy(source, target, local_sem.at[PIECES, which])

    def table_copy(level):
        if level < 3:
            source, target = tab_ref.at[level], tab_in_ref.at[level]
            device = (
                device_at(z, y, x, 1 - c), device_at(z, 1 - y, x, c), device_at(z, y, 1 - x, c)
            )[level]
        else:
            source, target = tab_ref.at[3], tab_in_ref.at[3 + z]
            device = device_at(lax.rem(z + level - 2, ZS), y, x, c)
        return pltpu.make_async_remote_copy(
            src_ref=source,
            dst_ref=target,
            send_sem=tab_send.at[level],
            recv_sem=tab_recv.at[level],
            device_id=device,
            device_id_type=MESH,
        )

    def table_wait(level):
        if level < 3:
            table_copy(level).wait_recv()
        else:
            slot = tab_in_ref.at[3 + lax.rem(z + ZS - (level - 2), ZS)]
            pltpu.make_async_remote_copy(
                src_ref=slot,
                dst_ref=slot,
                send_sem=tab_send.at[level],
                recv_sem=tab_recv.at[level],
                device_id=device_at(lax.rem(z + level - 2, ZS), y, x, c),
                device_id_type=MESH,
            ).wait_recv()

    def table_level(level):
        if level == 3:
            for last in (3, 4, 5):
                table_wait(last)
            table = (tab_in_ref[3] + tab_in_ref[4]) + (tab_in_ref[5] + tab_in_ref[6])
            device = ((z * 2 + y) * 2 + x) * 2 + c
            full = table.shape[1]
            row = lax.broadcasted_iota(jnp.int32, (full, 128), 0)
            lane = lax.broadcasted_iota(jnp.int32, (full, 128), 1)

            def own_lanes(values, size, at):
                chosen = jnp.where((row == at + lane) & (lane < size), 1.0, 0.0)
                return lax.dot_general(
                    values, chosen, (((1,), (0,)), ((), ())), preferred_element_type=F32, precision=lax.Precision.HIGHEST
                )

            per_row = full * 4 // (8 * ZS)
            small_ref[0:TABLE_ROWS] = own_lanes(table, full // (8 * ZS), device * (full // (8 * ZS)))
            inner_bias = own_lanes(table, per_row, lax.rem(device, full // per_row) * per_row)
            for j in range(4):

                @pl.when(device // (full // per_row) == j)
                def _(j=j):
                    small_ref[TABLE_ROWS : TABLE_ROWS + 1] = inner_bias[12 + j : 13 + j]

            small_ref[TABLE_ROWS + 1 : TABLE_ROWS + 2] = table[16:17, 0:128]
            return
        table_wait(level)
        tab_ref[level + 1] = tab_ref[level] + tab_in_ref[level]
        if level < 2:
            table_copy(level + 1).start()
        else:
            tab_in_ref[3 + z] = tab_ref[3]
            for nxt in (4, 3, 5):
                table_copy(nxt).start()

    def take_up(point):
        for kind, a in SCATTER_PLAN.get(point, ()):
            if kind == KB:
                begin(a)
            elif kind == K0 or kind == K1:
                after_core(a, 0 if kind == K0 else 1)
            elif kind == KF:
                after_first(a)
            elif kind == KS:
                after_second(a)
            elif kind == KZ:
                finish(a)
            elif kind == KT:
                table_level(a)
            else:
                for k in (3, 2, 1):
                    row_copy(0, k).start()
                row_own(0).start()

    @pl.when(group == 0)
    def _():
        meet(all_partners(z, y, x, c))
        take_up(-1)
        for k in range(1, 4):
            row_copy(1, k).start()
        row_own(1).start()
        xt_ref[...] = x_ref[...].astype(F32).T.astype(BF)
        acc_ref[...] = start_ref[...]

    kt_ref[...] = k_ref[...].astype(F32).T.astype(BF)
    dot_ref[...] = (datt_ref[...].astype(F32) * att_ref[...].astype(F32)).T
    dk_ref[...] = jnp.zeros_like(dk_ref)
    dv_ref[...] = jnp.zeros_like(dv_ref)
    ends = doc_ends(lens_ref)
    key_doc = doc_numbers(lax.broadcasted_iota(jnp.int32, (length, 1), 0), ends)
    lane_head = lax.broadcasted_iota(jnp.int32, (1, width), 1) // HEAD_DIM

    def step(i, carry):
        for point in range(groups * points):

            @pl.when((group == point // points) & (i == point % points))
            def _(point=point):
                take_up(point)

        at = pl.multiple_of(i * chunk, chunk)
        query_doc = doc_numbers(lax.broadcasted_iota(jnp.int32, (1, chunk), 1) + at, ends)
        scaled = q_ref[pl.ds(at, chunk), :] * jnp.asarray(0.125, BF)
        given = datt_ref[pl.ds(at, chunk), :]
        own_q = [jnp.where(lane_head == h, scaled, jnp.zeros_like(scaled)) for h in range(heads)]
        own_d = [jnp.where(lane_head == h, given, jnp.zeros_like(given)) for h in range(heads)]
        all_probs = [[] for _ in range(length // chunk)]
        all_grads = [[] for _ in range(length // chunk)]
        for h in range(heads):
            lse = lse_ref[0, h : h + 1, pl.ds(at, chunk)]
            dots = jnp.sum(
                dot_ref[h * HEAD_DIM : (h + 1) * HEAD_DIM, pl.ds(at, chunk)], axis=0, keepdims=True
            )
            for j in range(length // chunk):
                s = j * chunk
                scores = nt(k_ref[s : s + chunk, :], own_q[h])
                scores = jnp.where(key_doc[s : s + chunk] == query_doc, scores, -1000000000.0)
                probs = jnp.exp(scores - lse)
                grad_probs = nt(v_ref[s : s + chunk, :], own_d[h])
                all_grads[j].append((probs * (grad_probs - dots)).astype(BF))
                all_probs[j].append(probs.astype(BF))
        stacked_q = jnp.concatenate(own_q, axis=0)
        stacked_d = jnp.concatenate(own_d, axis=0)
        for j in range(length // chunk):
            s = j * chunk
            dk_ref[s : s + chunk, :] += nn(jnp.concatenate(all_grads[j], axis=1), stacked_q)
            dv_ref[s : s + chunk, :] += nn(jnp.concatenate(all_probs[j], axis=1), stacked_d)
        mixed = []
        for h in range(heads):
            column = jnp.concatenate([all_grads[j][h] for j in range(length // chunk)], axis=0)
            mixed.append(nn(kt_ref[h * HEAD_DIM : (h + 1) * HEAD_DIM, :], column))
        dq_ref[pl.ds(at, chunk), :] = (jnp.concatenate(mixed, axis=0).T * 0.125).astype(BF)
        return carry

    lax.fori_loop(0, points, step, 0)
    xt = xt_ref[...]
    grads = (dq_ref[...], dk_ref[...].astype(BF), dv_ref[...].astype(BF))
    block = dw_ref.shape[1:6]
    for j, grad in enumerate(grads):
        dw_ref[group, :, :, :, :, :, j * width : (j + 1) * width] = nn(xt, grad).reshape(block + (width,)).astype(BF)
    bias_ref[group, 0:1, :] = jnp.sum(grads[0].astype(F32), axis=0, keepdims=True)
    bias_ref[group, 1:2, :] = jnp.sum(grads[2].astype(F32), axis=0, keepdims=True)
    total = acc_ref[...]
    for j, grad in enumerate(grads):
        total = total + nt(grad, w_ref[:, j * width : (j + 1) * width])
    acc_ref[...] = total

    @pl.when(group == groups - 1)
    def _():
        dx_ref[...] = acc_ref[...].reshape(dx_ref.shape).astype(BF)
        tab_ref[0, 0:CLASSES] = small_a_ref[0:CLASSES]
        for g in range(groups):
            tab_ref[0, B_QUERY : B_QUERY + 2, g * width : (g + 1) * width] = bias_ref[g, 0:2, :]
        for row, (ref, at) in {
            B_OUT: (small_b_ref, 3), GAIN1: (small_b_ref, 4), SHIFT1: (small_b_ref, 5), B_OUTER: (small_b_ref, 0),
            GAIN2: (small_b_ref, 1), SHIFT2: (small_b_ref, 2), B_POOL: (small_a_ref, 16), 16: (small_a_ref, 17),
        }.items():
            tab_ref[0, row : row + 1] = ref[at : at + 1, :]
        full = small_a_ref.shape[1]
        for j in range(4):
            tab_ref[0, 12 + j : 13 + j] = bi_ref[:, j * full : (j + 1) * full]
        tab_ref[0, 17:TABLE_ROWS] = jnp.zeros((TABLE_ROWS - 17, full), F32)
        table_copy(0).start()
        take_up(groups * points)
        for a in range(items):
            for number in range(7):
                copy_of(a, number).wait_send()
        for level in range(6):
            table_copy(level).wait_send()
        for which in (0, 1):
            for k in range(1, 4):
                row_copy(which, k).wait_recv()
                row_copy(which, k).wait_send()
            row_own(which).wait()


def attend_back(lens, rows, w_groups, q, k, v, att, datt, lse, grad_pre, small_a, small_b, grad_b_inner, logit_block, parts):
    length, width = rows.shape
    group = 256
    groups = width // group
    local_len = length // 4
    share = width // (8 * ZS)
    once = pl.Buffered(buffer_count=1)
    whole = pl.BlockSpec((length, width), lambda g: (0, 0), pipeline_mode=once)
    part = pl.BlockSpec((length, group), lambda g: (0, g))
    blocks = [p.shape[1:] for p in parts]
    split = [p.reshape((ZS, 2, 2, 2) + b) for p, b in zip(parts, blocks)]
    shapes = [r for r in blocks]
    cuts = [cut_of(a, blocks[DENSE_ITEMS[a][0]]) for a in range(PIECES)]
    blocks = [(r[1], q[1]) for r, q in cuts] + [(share, 3 * group)] * groups
    hbm = pl.BlockSpec(memory_space=pl.ANY)

    def fixed(shape):
        return pl.BlockSpec(shape, lambda g: (0,) * len(shape))

    results = [(TABLE_ROWS + 8, 128)] + shapes + [(share, width)] * 3
    arriving = []
    for lead in ((ZS, 2, 2), (ZS, 2), (ZS,), (ZS - 1,)):
        arriving += [pltpu.VMEM(lead + b, BF) for b in blocks]
    items = len(blocks)
    return pl.pallas_call(
        functools.partial(attend_back_kernel, groups),
        grid=(groups,),
        out_shape=[
            jax.ShapeDtypeStruct((4, local_len, width), BF),
            jax.ShapeDtypeStruct((4,) + logit_block.shape, F32),
        ]
        + [jax.ShapeDtypeStruct(r, F32) for r in results],
        in_specs=[
            SMEM,
            whole,
            pl.BlockSpec((width, 3 * group), lambda g: (0, g)),
            part, part, part, part, part,
            pl.BlockSpec((1, 8, length), lambda g: (g, 0, 0)),
            whole,
            fixed(small_a.shape), fixed(small_b.shape), fixed(grad_b_inner.shape), hbm,
        ]
        + [hbm] * DENSE,
        out_specs=[hbm, hbm] + [fixed(r) for r in results],
        scratch_shapes=[
            pltpu.VMEM((width, length), BF),
            pltpu.VMEM((group, length), BF),
            pltpu.VMEM((group, length), F32),
            pltpu.VMEM((length, group), BF),
            pltpu.VMEM((length, group), F32),
            pltpu.VMEM((length, group), F32),
            pltpu.VMEM((length, width), F32),
            pltpu.VMEM((4, local_len, width), BF),
            pltpu.VMEM((groups, 8, group), F32),
            pltpu.VMEM((groups, ZS, 2, 2, 2, share, 3 * group), BF),
            pltpu.VMEM((4, TABLE_ROWS, width), F32),
            pltpu.VMEM((3 + ZS, TABLE_ROWS, width), F32),
            pltpu.SemaphoreType.DMA((PIECES + 1, 2)),
            pltpu.SemaphoreType.DMA((2, 3)),
            pltpu.SemaphoreType.DMA((2, 3)),
            pltpu.SemaphoreType.DMA((6,)),
            pltpu.SemaphoreType.DMA((6,)),
            pltpu.SemaphoreType.DMA((items, 7)),
            pltpu.SemaphoreType.DMA((items, 7)),
        ]
        + [pltpu.VMEM((ZS, 2, 2) + b, BF) for b in blocks[:PIECES]]
        + arriving,
        compiler_params=pltpu.CompilerParams(
            collective_id=2, has_side_effects=True, vmem_limit_bytes=60 * 2**20
        ),
        name="attend_back",
    )(lens, rows, w_groups, q, k, v, att, datt, lse, grad_pre, small_a, small_b, grad_b_inner, logit_block, *split)


def row_copies(source_ref, target_ref, send_sem, recv_sem):
    z, y, x, c = my_place()
    copies = []
    for k in (3, 2, 1):
        px, pc = group_partner(k, x, c)
        copies.append(
            pltpu.make_async_remote_copy(
                src_ref=source_ref.at[px * 2 + pc],
                dst_ref=target_ref.at[x * 2 + c],
                send_sem=send_sem.at[k - 1],
                recv_sem=recv_sem.at[k - 1],
                device_id=device_at(z, y, px, pc),
                device_id_type=MESH,
            )
        )
    return copies, pltpu.make_async_copy(source_ref.at[x * 2 + c], target_ref.at[x * 2 + c], send_sem.at[3])


ROW_SEMAPHORES = [pltpu.SemaphoreType.DMA((4,)), pltpu.SemaphoreType.DMA((3,))]


def normal_parts(v):
    bell = jnp.exp(v * v * -0.5)
    t = 1.0 / (1.0 + jnp.abs(v) * 0.23164189)
    tail = t * (0.127414796 + t * (-0.142248368 + t * (0.710706870 + t * (-0.726576013 + t * 0.530702714)))) * bell
    return jnp.where(v >= 0.0, 1.0 - tail, tail), bell


def centered_parts(values):
    average = jnp.mean(values, axis=-1, keepdims=True)
    centered = values - average
    variance = jnp.mean(centered * centered, axis=-1, keepdims=True)
    inverse = lax.rsqrt(variance + 1e-06)
    return centered * inverse, inverse


def norm_back(grad, values, gain):
    hat, inverse = centered_parts(values)
    scaled = grad * gain
    mean_scaled = jnp.mean(scaled, axis=-1, keepdims=True)
    mean_cross = jnp.mean(scaled * hat, axis=-1, keepdims=True)
    back = (scaled - mean_scaled - hat * mean_cross) * inverse
    return back, jnp.sum(grad * hat, axis=0, keepdims=True), jnp.sum(grad, axis=0, keepdims=True)


MIDDLE_ORDERS = ("xy",)
MIDDLE_PLAN = {
    0: ((KB, 0),),
    2: ((KZ, 0),),
    5: ((KF, 0),),
    8: ((KS, 0),),
    14: ((KE, 0),),
}
COTANGENT_POINT = 3


def middle_kernel(tiles, *refs):
    (
        lens_ref, labels_ref, b_class_ref, cot_ref, x_ref, att_ref, w_inner_ref, w_out_ref, outer_hbm_ref, pool_shard_ref,
        vec_ref,
    ) = refs[:11]
    (
        low_ref, act_out_ref, outer_ref, inner_ref, branch_ref, datt_ref, gpre_ref, dpool_ref, small_a_ref, small_b_ref, bi_ref,
        logits_ref, layer_out_ref,
    ) = refs[11:24]
    (
        act_ref, dact_ref, pre_ref, summed_ref, result_ref, cot_rows_ref, first_ref, picked_ref, own_pool, w_outer_ref, pool_ref,
        outer_sem, act_sem, keep_sem, send_sem, recv_sem, cot_send, cot_recv, lo_send, lo_recv,
    ) = refs[24:]
    step = pl.program_id(0)
    rows, full = x_ref.shape
    chunks = act_ref.shape[1] // full

    def view(a, where):
        return pool_ref.at[where]

    def own_block(a):
        return own_pool

    gather_up, all_sent = gather_tools(MIDDLE_PLAN, MIDDLE_ORDERS, view, own_block, keep_sem, send_sem, recv_sem)

    def take_up(point):
        if point in MIDDLE_PLAN or point == COTANGENT_POINT:

            @pl.when(step == point // 2)
            def _():
                gather_up(point)
                if point == COTANGENT_POINT:
                    copies, own = row_copies(cot_ref, cot_rows_ref, cot_send, cot_recv)
                    for copy in copies:
                        copy.start()
                    own.start()

    def outer_copy():
        return pltpu.make_async_copy(outer_hbm_ref, w_outer_ref, outer_sem.at[0])

    def act_copy(tile):
        where = pl.ds(tile * rows, rows)
        return pltpu.make_async_copy(act_ref.at[where], act_out_ref.at[where], act_sem.at[tile])

    def vec(row):
        return vec_ref[row : row + 1, :]

    @pl.when(step == 0)
    def _():
        outer_copy().start()
        own_pool[...] = pool_shard_ref[...].astype(BF)
        z, y, x, c = my_place()
        meet(all_partners(z, y, x, c))

    tile = lax.rem(step, tiles)
    here = pl.ds(pl.multiple_of(tile * rows, rows), rows)
    for point in range(0, 2 * tiles, 2):
        take_up(point)

    @pl.when(step < tiles)
    def _():
        pre = x_ref[...].astype(F32) + (nn(att_ref[...], w_out_ref[...]) + vec(B_OUT))
        pre_ref[here, :] = pre
        low = (centered_parts(pre)[0] * vec(GAIN1) + vec(SHIFT1)).astype(BF)
        low_ref[...] = low
        for j in range(chunks):
            if j == chunks // 2:
                for point in range(1, 2 * tiles, 2):
                    take_up(point)
            s = j * full
            hidden = nn(low, w_inner_ref[:, s : s + full]) + vec(12 + j)
            phi, bell = normal_parts(hidden)
            act_ref[here, s : s + full] = (hidden * phi).astype(BF)
            dact_ref[here, s : s + full] = (phi + hidden * bell * 0.3989422804014327).astype(BF)
        for t in range(tiles):

            @pl.when(step == t)
            def _(t=t):
                act_copy(t).start()

    for point in range(2 * tiles, 4 * tiles, 2):
        take_up(point)

    def outer_part(j):
        return w_outer_ref[j].reshape(full, full)

    @pl.when(step == tiles)
    def _():
        outer_copy().wait()

    @pl.when((step >= tiles) & (step < 2 * tiles))
    def _():
        total = centered_parts(pre_ref[here, :])[0] * vec(GAIN1) + vec(SHIFT1) + vec(B_OUTER)
        for j in range(chunks):
            total = total + nn(act_ref[here, j * full : (j + 1) * full], outer_part(j))
        summed_ref[here, :] = total
        result = (centered_parts(total)[0] * vec(GAIN2) + vec(SHIFT2)).astype(BF)
        result_ref[tile] = result
        starts = doc_starts(lens_ref)
        places = lax.broadcasted_iota(jnp.int32, (VEC_ROWS, rows), 1) + tile * rows
        row_doc = lax.broadcasted_iota(jnp.int32, (VEC_ROWS, rows), 0)
        hit = jnp.zeros((VEC_ROWS, rows), jnp.bool_)
        for d, start in enumerate(starts):
            hit = hit | ((row_doc == d) & (places == start))
        found = nn(jnp.where(hit, 1.0, 0.0).astype(BF), result)

        @pl.when(tile == 0)
        def _():
            picked_ref[...] = found

        @pl.when(tile > 0)
        def _():
            picked_ref[...] += found

    @pl.when(step == 2 * tiles - 1)
    def _():
        copies, own = row_copies(result_ref, layer_out_ref, lo_send, lo_recv)
        for copy in copies:
            copy.start()
        own.start()
        w_pool = pool_ref[...].astype(F32).reshape(full, full).astype(BF)
        docs = lens_ref.shape[1]
        picked = picked_ref[...].astype(BF)
        pooled = jnp.tanh(nn(picked, w_pool) + vec(B_POOL))
        pooled_low = pooled.astype(BF)
        table = vec_ref[...].astype(BF)
        column = lax.broadcasted_iota(jnp.int32, (VEC_ROWS, VEC_ROWS), 1)
        row = lax.broadcasted_iota(jnp.int32, (VEC_ROWS, VEC_ROWS), 0)
        class_bias = jnp.zeros((VEC_ROWS, VEC_ROWS), F32)
        for j in range(CLASSES):
            class_bias = jnp.where(column == j, b_class_ref[j], class_bias)
        logits = nt(pooled_low, table) + class_bias
        logits_ref[...] = jnp.concatenate([logits[0:8], jnp.zeros((8, 128 - VEC_ROWS), F32)], axis=1)
        live = column < CLASSES
        shown = jnp.where(live, logits, -jnp.inf)
        exps = jnp.where(live, jnp.exp(shown - jnp.max(shown, axis=-1, keepdims=True)), 0.0)
        probs = exps / jnp.sum(exps, axis=-1, keepdims=True)
        label = jnp.zeros((VEC_ROWS, VEC_ROWS), jnp.int32)
        for d in range(docs):
            label = jnp.where(row == d, labels_ref[lax.axis_index("fsdp"), d], label)
        grad = jnp.where(live & (row < docs), probs - jnp.where(label == column, 1.0, 0.0), 0.0)
        grad_low = grad.astype(BF)
        grad_pool = (nn(grad_low, table) * (1.0 - pooled * pooled)).astype(BF)
        dpool_ref[...] = tn(picked, grad_pool).astype(BF)
        first_ref[...] = nt(grad_pool, w_pool)
        small_a_ref[0:16, :] = tn(grad_low, pooled_low)
        small_a_ref[16:17, :] = jnp.sum(grad_pool.astype(F32), axis=0, keepdims=True)
        class_sum = jnp.sum(grad_low.astype(F32), axis=0, keepdims=True)
        small_a_ref[17:18, :] = jnp.concatenate([class_sum, jnp.zeros((1, full - VEC_ROWS), F32)], axis=1)
        small_b_ref[...] = jnp.zeros_like(small_b_ref)
        bi_ref[...] = jnp.zeros_like(bi_ref)
        copies, own = row_copies(cot_ref, cot_rows_ref, cot_send, cot_recv)
        for copy in copies:
            copy.wait()
        own.wait()

    @pl.when(step >= 2 * tiles)
    def _():
        grad = cot_rows_ref[tile].astype(F32)
        places = lax.broadcasted_iota(jnp.int32, (rows, 1), 0) + tile * rows
        placed = jnp.zeros(grad.shape, F32)
        for d, start in enumerate(doc_starts(lens_ref)):
            placed = jnp.where(places == start, first_ref[d : d + 1, :], placed)
        grad = grad + placed
        grad_summed, gain2, shift2 = norm_back(grad, summed_ref[here, :], vec(GAIN2))
        outer = grad_summed.astype(BF)
        outer_ref[...] = outer
        grad_normed = grad_summed
        for j in range(chunks):
            s = j * full
            back = nt(outer, outer_part(j))
            inner = (back * dact_ref[here, s : s + full].astype(F32)).astype(BF)
            inner_ref[:, s : s + full] = inner
            bi_ref[:, s : s + full] += jnp.sum(inner.astype(F32), axis=0, keepdims=True)
            grad_normed = grad_normed + nt(inner, w_inner_ref[:, s : s + full])
        grad_pre, gain1, shift1 = norm_back(grad_normed, pre_ref[here, :], vec(GAIN1))
        gpre_ref[...] = grad_pre
        branch = grad_pre.astype(BF)
        branch_ref[...] = branch
        datt_ref[...] = nt(branch, w_out_ref[...]).astype(BF)
        small_b_ref[0:1, :] += jnp.sum(outer.astype(F32), axis=0, keepdims=True)
        small_b_ref[1:2, :] += gain2
        small_b_ref[2:3, :] += shift2
        small_b_ref[3:4, :] += jnp.sum(branch.astype(F32), axis=0, keepdims=True)
        small_b_ref[4:5, :] += gain1
        small_b_ref[5:6, :] += shift1

    @pl.when(step == 3 * tiles - 1)
    def _():
        all_sent()
        for t in range(tiles):
            act_copy(t).wait()
        copies, own = row_copies(result_ref, layer_out_ref, lo_send, lo_recv)
        for copy in copies:
            copy.wait()
        own.wait()


def middle(lens, labels, b_class, cot, rows, att, w_inner, w_out, w_outer, pool_shard, vectors):
    length, width = rows.shape
    hidden = w_inner.shape[1]
    tile = 256
    tiles = length // tile
    items = len(MIDDLE_ORDERS)
    once = pl.Buffered(buffer_count=1)
    early = pl.BlockSpec((tile, width), lambda i: (jnp.minimum(i, tiles - 1), 0))

    def late(size):
        return pl.BlockSpec((tile, size), lambda i: (jnp.maximum(i - 2 * tiles, 0), 0))

    def fixed(shape):
        return pl.BlockSpec(shape, lambda i: (0,) * len(shape), pipeline_mode=once)

    lead = (ZS, 2, 2, 2)
    return pl.pallas_call(
        functools.partial(middle_kernel, tiles),
        grid=(3 * tiles,),
        out_shape=[
            jax.ShapeDtypeStruct((length, width), BF),
            jax.ShapeDtypeStruct((length, hidden), BF),
            jax.ShapeDtypeStruct((length, width), BF),
            jax.ShapeDtypeStruct((length, hidden), BF),
            jax.ShapeDtypeStruct((length, width), BF),
            jax.ShapeDtypeStruct((length, width), BF),
            jax.ShapeDtypeStruct((length, width), F32),
            jax.ShapeDtypeStruct((width, width), BF),
            jax.ShapeDtypeStruct((24, width), F32),
            jax.ShapeDtypeStruct((8, width), F32),
            jax.ShapeDtypeStruct((1, hidden), F32),
            jax.ShapeDtypeStruct((8, 128), F32),
            jax.ShapeDtypeStruct(cot.shape, BF),
        ],
        in_specs=[
            SMEM, SMEM, SMEM, ANY, early, early, fixed((width, hidden)), fixed((width, width)), ANY,
            fixed(pool_shard.shape), fixed((VEC_ROWS, width)),
        ],
        out_specs=[
            early, ANY, late(width), late(hidden), late(width), late(width), late(width), fixed((width, width)),
            fixed((24, width)), fixed((8, width)), fixed((1, hidden)), fixed((8, 128)), ANY,
        ],
        scratch_shapes=[
            pltpu.VMEM((length, hidden), BF),
            pltpu.VMEM((length, hidden), BF),
            pltpu.VMEM((length, width), F32),
            pltpu.VMEM((length, width), F32),
            pltpu.VMEM(cot.shape, BF),
            pltpu.VMEM(cot.shape, BF),
            pltpu.VMEM((VEC_ROWS, width), F32),
            pltpu.VMEM((VEC_ROWS, width), F32),
            pltpu.VMEM(pool_shard.shape, BF),
            pltpu.VMEM(w_outer.shape, BF),
            pltpu.VMEM(lead + pool_shard.shape, BF),
            pltpu.SemaphoreType.DMA((1,)),
            pltpu.SemaphoreType.DMA((tiles,)),
            pltpu.SemaphoreType.DMA((items,)),
            pltpu.SemaphoreType.DMA((items, 9)),
            pltpu.SemaphoreType.DMA((items, 9)),
        ]
        + ROW_SEMAPHORES * 2,
        compiler_params=pltpu.CompilerParams(collective_id=3, has_side_effects=True, vmem_limit_bytes=60 * 2**20),
        name="middle",
    )(lens, labels, b_class, cot, rows, att, w_inner, w_out, w_outer, pool_shard, vectors)


def results_kernel(large, small_ref, *refs):
    sources, refs = refs[:large], refs[large:]
    targets, columns, inner_ref, class_ref, sem, *held = refs[:large], refs[large : large + VECTORS], *refs[large + VECTORS :]
    arriving = [pltpu.make_async_copy(s, h, sem.at[0, j]) for j, (s, h) in enumerate(zip(sources, held))]
    leaving = [pltpu.make_async_copy(h, t, sem.at[1, j]) for j, (h, t) in enumerate(zip(held, targets))]
    for copy in arriving:
        copy.start()
    for j, ref in enumerate(columns):
        ref[...] = small_ref[B_QUERY + j : B_QUERY + j + 1, 0 : ref.shape[1]]
    inner_ref[...] = small_ref[TABLE_ROWS : TABLE_ROWS + 1, 0 : inner_ref.shape[1]]
    class_ref[...] = small_ref[TABLE_ROWS + 1 : TABLE_ROWS + 2, 0 : class_ref.shape[1]]
    for came, goes in zip(arriving, leaving):
        came.wait()
        goes.start()
    for goes in leaving:
        goes.wait()


def write_results(small, arrays, share, hidden_share):
    shapes = [jax.ShapeDtypeStruct(a.shape, a.dtype) for a in arrays]
    vectors = [(1, share)] * VECTORS + [(1, hidden_share), (1, CLASSES)]
    inside = pl.BlockSpec(memory_space=pltpu.VMEM)
    return pl.pallas_call(
        functools.partial(results_kernel, len(arrays)),
        out_shape=shapes + [jax.ShapeDtypeStruct(v, F32) for v in vectors],
        in_specs=[inside] + [ANY] * len(arrays),
        out_specs=[ANY] * len(arrays) + [inside] * len(vectors),
        scratch_shapes=[pltpu.SemaphoreType.DMA((2, len(arrays)))] + [pltpu.VMEM(a.shape, a.dtype) for a in arrays],
        compiler_params=pltpu.CompilerParams(vmem_limit_bytes=60 * 2**20),
        name="results",
    )(small, *arrays)


def fast_body(
    inputs, cotangent, doc_lengths, labels, w_query, b_query, w_key, w_value, b_value, w_out, b_out, first_gain, first_shift,
    w_inner, b_inner, w_outer, b_outer, second_gain, second_shift, w_pool, b_pool, w_class, b_class,
):
    seqs, local_len, width = inputs.shape
    length = seqs * local_len
    devices = 8 * ZS
    docs = doc_lengths.shape[1]
    share = width // devices
    hidden_share = b_inner.shape[0]
    hidden = hidden_share * devices
    vector_shards = [b_query, b_value, b_out, first_gain, first_shift, b_outer, second_gain, second_shift, b_pool]
    q, k, v, att, lse, w_qkv, vectors, rows, full_inner, full_out, full_outer = attend(
        doc_lengths, inputs, w_class.T, [member.reshape(1, share) for member in vector_shards], b_inner.reshape(1, hidden_share),
        [w_query, w_key, w_value], [w_inner, w_out, w_outer],
    )
    rows = rows.reshape(length, width)
    full_inner = full_inner.reshape(width, hidden)
    full_out = full_out.reshape(width, width)
    low, act, outer, inner, branch, datt, grad_pre, grad_pool, small_a, small_b, grad_b_inner, logit_block, layer_out = middle(
        doc_lengths, labels, b_class, cotangent, rows, att, full_inner, full_out, full_outer, w_pool, vectors
    )
    grad_outer_w = tn(act, outer).astype(BF)
    grad_inner_w = tn(low, inner).astype(BF)
    grad_out_w = tn(att, branch).astype(BF)
    grad_inputs, all_logits, small, *sums = attend_back(
        doc_lengths, rows, w_qkv, q, k, v, att, datt, lse, grad_pre, small_a, small_b, grad_b_inner, logit_block,
        [
            grad_inner_w.reshape(devices, share, hidden),
            grad_outer_w.reshape(devices, hidden_share, width),
            grad_out_w.reshape(devices, share, width),
            grad_pool.reshape(devices, share, width),
        ],
    )

    done = write_results(small, [grad_inputs, layer_out, *sums], share, hidden_share)
    grad_inputs, layer_out, o_inner, o_outer, o_out, o_pool, o_query, o_key, o_value = done[:9]
    (
        o_b_query, o_b_value, o_b_out, o_gain1, o_shift1, o_b_outer, o_gain2, o_shift2, o_b_pool, o_b_inner, o_b_class,
    ) = (vector.reshape(-1) for vector in done[9:])
    return (
        layer_out,
        all_logits[:, :docs, :CLASSES],
        grad_inputs,
        o_query,
        o_b_query,
        o_key,
        o_value,
        o_b_value,
        o_out,
        o_b_out,
        o_gain1,
        o_shift1,
        o_inner,
        o_b_inner,
        o_outer,
        o_b_outer,
        o_gain2,
        o_shift2,
        o_pool,
        o_b_pool,
        small[:CLASSES, :share].T,
        o_b_class,
    )


def solution(mesh):
    placed = (
        P("dp", "fsdp", None),
        P("dp", "fsdp", None),
        P("dp", None),
        P("dp", None),
        P(("dp", "fsdp"), None),
        P(("dp", "fsdp")),
        P(("dp", "fsdp"), None),
        P(("dp", "fsdp"), None),
        P(("dp", "fsdp")),
        P(("dp", "fsdp"), None),
        P(("dp", "fsdp")),
        P(("dp", "fsdp")),
        P(("dp", "fsdp")),
        P(("dp", "fsdp"), None),
        P(("dp", "fsdp")),
        P(("dp", "fsdp"), None),
        P(("dp", "fsdp")),
        P(("dp", "fsdp")),
        P(("dp", "fsdp")),
        P(("dp", "fsdp"), None),
        P(("dp", "fsdp")),
        P(("dp", "fsdp"), None),
        P(),
    )
    sizes = (mesh.shape["dp"], mesh.shape["fsdp"])
    chosen = fast_body if sizes == (8, 4) else general_body
    return jax.shard_map(
        chosen,
        mesh=mesh,
        in_specs=placed,
        out_specs=(
            P("dp", "fsdp", None),
            P("dp", None, None),
            P("dp", "fsdp", None),
            P(("dp", "fsdp"), None),
            P(("dp", "fsdp")),
            P(("dp", "fsdp"), None),
            P(("dp", "fsdp"), None),
            P(("dp", "fsdp")),
            P(("dp", "fsdp"), None),
            P(("dp", "fsdp")),
            P(("dp", "fsdp")),
            P(("dp", "fsdp")),
            P(("dp", "fsdp"), None),
            P(("dp", "fsdp")),
            P(("dp", "fsdp"), None),
            P(("dp", "fsdp")),
            P(("dp", "fsdp")),
            P(("dp", "fsdp")),
            P(("dp", "fsdp"), None),
            P(("dp", "fsdp")),
            P(("dp", "fsdp"), None),
            P(),
        ),
        check_vma=False,
    )
```

```python
import functools

import jax
import jax.numpy as jnp
from jax import lax
from jax.experimental import pallas as pl
from jax.experimental.pallas import tpu as pltpu
from jax.sharding import PartitionSpec as P

HEAD_DIM = 64
CLASSES = 3
MICRO = 4


def product(left_side, right_side):
    return jnp.dot(left_side, right_side, preferred_element_type=jnp.float32)


def contract_rows(left_side, right_side):
    return lax.dot_general(
        left_side, right_side, (((0,), (0,)), ((), ())), preferred_element_type=jnp.float32
    )


def times_transposed(left_side, right_side):
    return lax.dot_general(
        left_side, right_side, (((1,), (1,)), ((), ())), preferred_element_type=jnp.float32
    )


def layer_norm(values, norm_gain, norm_shift):
    average = jnp.mean(values, axis=-1, keepdims=True)
    centered = values - average
    variance = jnp.mean(centered * centered, axis=-1, keepdims=True)
    return centered * lax.rsqrt(variance + 1e-06) * norm_gain + norm_shift


def gelu_exact(values):
    return jax.nn.gelu(values, approximate=False)


def running_sum(lengths_rows):
    count = lengths_rows.shape[1]
    upper = jnp.arange(count)[:, None] <= jnp.arange(count)[None, :]
    return jnp.sum(jnp.where(upper[None], lengths_rows[:, :, None], 0), axis=1)


def segment_numbers(lengths_rows, places):
    doc_ends = running_sum(lengths_rows)
    above = (places[None, :, None] >= doc_ends[:, None, :]).astype(jnp.int32)
    return jnp.sum(above, axis=2)


def pair_heads(values):
    return values.reshape(values.shape[0], values.shape[1], 2, HEAD_DIM)


def pair_scores(query_pair, key_pair, same_doc):
    raw_scores = jnp.einsum(
        "bqhd,bkhd->bhqk", query_pair, key_pair, preferred_element_type=jnp.float32
    ) * HEAD_DIM ** (-0.5)
    return jnp.where(same_doc[:, None], raw_scores, -1000000000.0)


def lowered_masters(masters):
    return [member.astype(jnp.bfloat16) for member in masters]


def forward(tokens, lengths_rows, weights, bias_class):
    (
        w_query,
        b_query,
        w_key,
        w_value,
        b_value,
        w_out,
        b_out,
        first_gain,
        first_shift,
        w_inner,
        b_inner,
        w_outer,
        b_outer,
        second_gain,
        second_shift,
        w_pool,
        b_pool,
        w_class,
    ) = weights
    seq_count, local_len, model_width = tokens.shape
    doc_count = lengths_rows.shape[1]
    flat_rows = tokens.reshape(seq_count * local_len, model_width)
    queries = (
        (product(flat_rows, w_query) + b_query)
        .astype(jnp.bfloat16)
        .reshape(seq_count, local_len, model_width)
    )
    key_rows = (
        product(flat_rows, w_key).astype(jnp.bfloat16).reshape(seq_count, local_len, model_width)
    )
    value_rows = (
        (product(flat_rows, w_value) + b_value)
        .astype(jnp.bfloat16)
        .reshape(seq_count, local_len, model_width)
    )
    all_keys, all_values = (
        lax.all_gather(key_rows, "fsdp", axis=1, tiled=True),
        lax.all_gather(value_rows, "fsdp", axis=1, tiled=True),
    )
    full_len = all_keys.shape[1]
    own_places = lax.axis_index("fsdp") * local_len + jnp.arange(local_len, dtype=jnp.int32)
    key_places = jnp.arange(full_len, dtype=jnp.int32)
    same_doc = (
        segment_numbers(lengths_rows, own_places)[:, :, None]
        == segment_numbers(lengths_rows, key_places)[:, None, :]
    )
    pair_width = 2 * HEAD_DIM
    mixed_list = []
    log_totals = []
    for pair_index in range(model_width // pair_width):
        col_start = pair_index * pair_width
        query_pair = pair_heads(queries[:, :, col_start : col_start + pair_width])
        key_pair = pair_heads(all_keys[:, :, col_start : col_start + pair_width])
        value_pair = pair_heads(all_values[:, :, col_start : col_start + pair_width])
        scores = pair_scores(query_pair, key_pair, same_doc)
        row_peak = jnp.max(scores, axis=-1, keepdims=True)
        exp_total = jnp.sum(jnp.exp(scores - row_peak), axis=-1, keepdims=True)
        log_total = row_peak + jnp.log(exp_total)
        attn_probs = jnp.exp(scores - log_total).astype(jnp.bfloat16)
        mixed_pair = jnp.einsum(
            "bhqk,bkhd->bqhd", attn_probs, value_pair, preferred_element_type=jnp.float32
        )
        mixed_list.append(mixed_pair.reshape(seq_count, local_len, pair_width))
        log_totals.append(log_total)
    attended = (
        jnp.concatenate(mixed_list, axis=2)
        .astype(jnp.bfloat16)
        .reshape(seq_count * local_len, model_width)
    )
    branch = product(attended, w_out) + b_out
    pre_first = flat_rows.astype(jnp.float32) + branch
    normed = layer_norm(pre_first, first_gain.astype(jnp.float32), first_shift.astype(jnp.float32))
    normed_low = normed.astype(jnp.bfloat16)
    inner_pre = product(normed_low, w_inner) + b_inner
    activated = gelu_exact(inner_pre).astype(jnp.bfloat16)
    summed = normed + (product(activated, w_outer) + b_outer)
    result = layer_norm(summed, second_gain.astype(jnp.float32), second_shift.astype(jnp.float32))
    result_low = result.astype(jnp.bfloat16).reshape(seq_count, local_len, model_width)
    starts = running_sum(lengths_rows) - lengths_rows
    picker = (own_places[None, None, :] == starts[:, :, None]).astype(jnp.bfloat16)
    local_firsts = jnp.einsum(
        "bdl,blc->bdc", picker, result_low, preferred_element_type=jnp.float32
    )
    firsts = lax.psum(local_firsts, "fsdp")
    firsts_low = firsts.astype(jnp.bfloat16).reshape(seq_count * doc_count, model_width)
    pooled = jnp.tanh(product(firsts_low, w_pool) + b_pool)
    pooled_low = pooled.astype(jnp.bfloat16)
    logits = product(pooled_low, w_class) + bias_class
    stored = (
        flat_rows,
        queries,
        all_keys,
        all_values,
        same_doc,
        log_totals,
        attended,
        pre_first,
        summed,
        normed_low,
        inner_pre,
        activated,
        picker,
        firsts_low,
        pooled,
        pooled_low,
        logits,
    )
    return (result_low, logits.reshape(seq_count, doc_count, CLASSES), stored)


def backward(stored, weights, cot_rows, label_rows):
    (
        w_query,
        b_query,
        w_key,
        w_value,
        b_value,
        w_out,
        b_out,
        first_gain,
        first_shift,
        w_inner,
        b_inner,
        w_outer,
        b_outer,
        second_gain,
        second_shift,
        w_pool,
        b_pool,
        w_class,
    ) = weights
    (
        flat_rows,
        queries,
        all_keys,
        all_values,
        same_doc,
        log_totals,
        attended,
        pre_first,
        summed,
        normed_low,
        inner_pre,
        activated,
        picker,
        firsts_low,
        pooled,
        pooled_low,
        logits,
    ) = stored
    seq_count, local_len, model_width = queries.shape
    doc_count = picker.shape[1]
    owner_flag = (lax.axis_index("fsdp") == 0).astype(jnp.float32)
    row_peak = jnp.max(logits, axis=-1, keepdims=True)
    class_exp = jnp.exp(logits - row_peak)
    class_probs = class_exp / jnp.sum(class_exp, axis=-1, keepdims=True)
    onehot_labels = (
        label_rows.reshape(-1)[:, None] == jnp.arange(CLASSES, dtype=jnp.int32)[None, :]
    ).astype(jnp.float32)
    grad_logits = (class_probs - onehot_labels).astype(jnp.bfloat16)
    grad_b_class = owner_flag * jnp.sum(grad_logits.astype(jnp.float32), axis=0)
    grad_w_class = owner_flag * contract_rows(pooled_low, grad_logits)
    grad_pool_pre = (times_transposed(grad_logits, w_class) * (1.0 - pooled * pooled)).astype(
        jnp.bfloat16
    )
    grad_b_pool = owner_flag * jnp.sum(grad_pool_pre.astype(jnp.float32), axis=0)
    grad_w_pool = owner_flag * contract_rows(firsts_low, grad_pool_pre)
    grad_firsts = times_transposed(grad_pool_pre, w_pool).reshape(seq_count, doc_count, model_width)
    from_pool = jnp.einsum(
        "bdl,bdc->blc", picker.astype(jnp.float32), grad_firsts, precision=lax.Precision.HIGHEST
    )
    grad_result = cot_rows.astype(jnp.float32).reshape(-1, model_width) + from_pool.reshape(
        -1, model_width
    )
    second_back = jax.vjp(
        layer_norm, summed, second_gain.astype(jnp.float32), second_shift.astype(jnp.float32)
    )[1]
    grad_summed, grad_second_gain, grad_second_shift = second_back(grad_result)
    grad_outer = grad_summed.astype(jnp.bfloat16)
    grad_b_outer = jnp.sum(grad_outer.astype(jnp.float32), axis=0)
    grad_w_outer = contract_rows(activated, grad_outer)
    gelu_back = jax.vjp(gelu_exact, inner_pre)[1]
    grad_inner = gelu_back(times_transposed(grad_outer, w_outer))[0].astype(jnp.bfloat16)
    grad_b_inner = jnp.sum(grad_inner.astype(jnp.float32), axis=0)
    grad_w_inner = contract_rows(normed_low, grad_inner)
    grad_normed = grad_summed + times_transposed(grad_inner, w_inner)
    first_back = jax.vjp(
        layer_norm, pre_first, first_gain.astype(jnp.float32), first_shift.astype(jnp.float32)
    )[1]
    grad_pre_first, grad_first_gain, grad_first_shift = first_back(grad_normed)
    grad_branch = grad_pre_first.astype(jnp.bfloat16)
    grad_b_out = jnp.sum(grad_branch.astype(jnp.float32), axis=0)
    grad_w_out = contract_rows(attended, grad_branch)
    grad_attended = (
        times_transposed(grad_branch, w_out)
        .astype(jnp.bfloat16)
        .reshape(seq_count, local_len, model_width)
    )
    pair_width = 2 * HEAD_DIM
    query_list = []
    key_list = []
    value_list = []
    for pair_index in range(model_width // pair_width):
        col_start = pair_index * pair_width
        query_pair = pair_heads(queries[:, :, col_start : col_start + pair_width])
        key_pair = pair_heads(all_keys[:, :, col_start : col_start + pair_width])
        value_pair = pair_heads(all_values[:, :, col_start : col_start + pair_width])
        grad_pair = pair_heads(grad_attended[:, :, col_start : col_start + pair_width])
        scores = pair_scores(query_pair, key_pair, same_doc)
        attn_probs = jnp.exp(scores - log_totals[pair_index])
        grad_probs = jnp.einsum(
            "bqhd,bkhd->bhqk", grad_pair, value_pair, preferred_element_type=jnp.float32
        )
        row_dot = jnp.sum(attn_probs * grad_probs, axis=-1, keepdims=True)
        grad_scores = (attn_probs * (grad_probs - row_dot)).astype(jnp.bfloat16)
        query_part = jnp.einsum(
            "bhqk,bkhd->bqhd", grad_scores, key_pair, preferred_element_type=jnp.float32
        ) * HEAD_DIM ** (-0.5)
        query_list.append(query_part.reshape(seq_count, local_len, pair_width))
        probs_low = attn_probs.astype(jnp.bfloat16)
        key_part = jnp.einsum(
            "bhqk,bqhd->bkhd", grad_scores, query_pair, preferred_element_type=jnp.float32
        ) * HEAD_DIM ** (-0.5)
        value_part = jnp.einsum(
            "bhqk,bqhd->bkhd", probs_low, grad_pair, preferred_element_type=jnp.float32
        )
        key_list.append(key_part.reshape(seq_count, key_part.shape[1], pair_width))
        value_list.append(value_part.reshape(seq_count, value_part.shape[1], pair_width))
    key_partials = jnp.concatenate(key_list, axis=2)
    value_partials = jnp.concatenate(value_list, axis=2)
    own_keys, own_values = (
        lax.psum_scatter(
            key_partials.astype(jnp.bfloat16), "fsdp", scatter_dimension=1, tiled=True
        ).astype(jnp.float32),
        lax.psum_scatter(
            value_partials.astype(jnp.bfloat16), "fsdp", scatter_dimension=1, tiled=True
        ).astype(jnp.float32),
    )
    query_grad = jnp.concatenate(query_list, axis=2).astype(jnp.bfloat16).reshape(-1, model_width)
    key_grad = own_keys.astype(jnp.bfloat16).reshape(-1, model_width)
    value_grad = own_values.astype(jnp.bfloat16).reshape(-1, model_width)
    grad_w_query = contract_rows(flat_rows, query_grad)
    grad_b_query = jnp.sum(query_grad.astype(jnp.float32), axis=0)
    grad_w_key = contract_rows(flat_rows, key_grad)
    grad_w_value = contract_rows(flat_rows, value_grad)
    grad_b_value = jnp.sum(value_grad.astype(jnp.float32), axis=0)
    grad_tokens = (
        grad_pre_first
        + times_transposed(query_grad, w_query)
        + times_transposed(key_grad, w_key)
        + times_transposed(value_grad, w_value)
    )
    new_grads = (
        grad_w_query,
        grad_b_query,
        grad_w_key,
        grad_w_value,
        grad_b_value,
        grad_w_out,
        grad_b_out,
        grad_first_gain,
        grad_first_shift,
        grad_w_inner,
        grad_b_inner,
        grad_w_outer,
        grad_b_outer,
        grad_second_gain,
        grad_second_shift,
        grad_w_pool,
        grad_b_pool,
        grad_w_class,
    )
    return (
        new_grads,
        grad_b_class,
        grad_tokens.astype(jnp.bfloat16).reshape(seq_count, local_len, model_width),
    )


def general_body(
    inputs,
    cotangent,
    doc_lengths,
    labels,
    w_query,
    b_query,
    w_key,
    w_value,
    b_value,
    w_out,
    b_out,
    first_gain,
    first_shift,
    w_inner,
    b_inner,
    w_outer,
    b_outer,
    second_gain,
    second_shift,
    w_pool,
    b_pool,
    w_class,
    b_class,
):
    masters = (
        w_query,
        b_query,
        w_key,
        w_value,
        b_value,
        w_out,
        b_out,
        first_gain,
        first_shift,
        w_inner,
        b_inner,
        w_outer,
        b_outer,
        second_gain,
        second_shift,
        w_pool,
        b_pool,
        w_class,
    )
    group_size = lax.axis_size("dp") * lax.axis_size("fsdp")
    grad_sums = [
        jnp.zeros((member.shape[0] * group_size,) + member.shape[1:], jnp.float32)
        for member in masters
    ]
    class_sum = jnp.zeros((CLASSES,), jnp.float32)
    micro_seqs = inputs.shape[0] // MICRO
    out_list = []
    logit_list = []
    grad_list = []
    for micro_step in range(MICRO):
        first_seq = micro_step * micro_seqs
        after_seq = first_seq + micro_seqs
        tokens = inputs[first_seq:after_seq]
        lengths_rows = doc_lengths[first_seq:after_seq]
        pieces = lowered_masters(masters)
        front_weights = (
            lax.all_gather(pieces[0], ("dp", "fsdp"), axis=0, tiled=True),
            lax.all_gather(pieces[1], ("dp", "fsdp"), axis=0, tiled=True),
            lax.all_gather(pieces[2], ("dp", "fsdp"), axis=0, tiled=True),
            lax.all_gather(pieces[3], ("dp", "fsdp"), axis=0, tiled=True),
            lax.all_gather(pieces[4], ("dp", "fsdp"), axis=0, tiled=True),
            lax.all_gather(pieces[5], ("dp", "fsdp"), axis=0, tiled=True),
            lax.all_gather(pieces[6], ("dp", "fsdp"), axis=0, tiled=True),
            lax.all_gather(pieces[7], ("dp", "fsdp"), axis=0, tiled=True),
            lax.all_gather(pieces[8], ("dp", "fsdp"), axis=0, tiled=True),
            lax.all_gather(pieces[9], ("dp", "fsdp"), axis=0, tiled=True),
            lax.all_gather(pieces[10], ("dp", "fsdp"), axis=0, tiled=True),
            lax.all_gather(pieces[11], ("dp", "fsdp"), axis=0, tiled=True),
            lax.all_gather(pieces[12], ("dp", "fsdp"), axis=0, tiled=True),
            lax.all_gather(pieces[13], ("dp", "fsdp"), axis=0, tiled=True),
            lax.all_gather(pieces[14], ("dp", "fsdp"), axis=0, tiled=True),
            lax.all_gather(pieces[15], ("dp", "fsdp"), axis=0, tiled=True),
            lax.all_gather(pieces[16], ("dp", "fsdp"), axis=0, tiled=True),
            lax.all_gather(pieces[17], ("dp", "fsdp"), axis=0, tiled=True),
        )
        result_low, logits, stored = forward(tokens, lengths_rows, front_weights, b_class)
        out_list.append(result_low)
        logit_list.append(logits)
        back_weights = (
            lax.all_gather(pieces[0], ("dp", "fsdp"), axis=0, tiled=True),
            lax.all_gather(pieces[1], ("dp", "fsdp"), axis=0, tiled=True),
            lax.all_gather(pieces[2], ("dp", "fsdp"), axis=0, tiled=True),
            lax.all_gather(pieces[3], ("dp", "fsdp"), axis=0, tiled=True),
            lax.all_gather(pieces[4], ("dp", "fsdp"), axis=0, tiled=True),
            lax.all_gather(pieces[5], ("dp", "fsdp"), axis=0, tiled=True),
            lax.all_gather(pieces[6], ("dp", "fsdp"), axis=0, tiled=True),
            lax.all_gather(pieces[7], ("dp", "fsdp"), axis=0, tiled=True),
            lax.all_gather(pieces[8], ("dp", "fsdp"), axis=0, tiled=True),
            lax.all_gather(pieces[9], ("dp", "fsdp"), axis=0, tiled=True),
            lax.all_gather(pieces[10], ("dp", "fsdp"), axis=0, tiled=True),
            lax.all_gather(pieces[11], ("dp", "fsdp"), axis=0, tiled=True),
            lax.all_gather(pieces[12], ("dp", "fsdp"), axis=0, tiled=True),
            lax.all_gather(pieces[13], ("dp", "fsdp"), axis=0, tiled=True),
            lax.all_gather(pieces[14], ("dp", "fsdp"), axis=0, tiled=True),
            lax.all_gather(pieces[15], ("dp", "fsdp"), axis=0, tiled=True),
            lax.all_gather(pieces[16], ("dp", "fsdp"), axis=0, tiled=True),
            lax.all_gather(pieces[17], ("dp", "fsdp"), axis=0, tiled=True),
        )
        stored = forward(tokens, lengths_rows, back_weights, b_class)[2]
        new_grads, class_grad, grad_tokens = backward(
            stored, back_weights, cotangent[first_seq:after_seq], labels[first_seq:after_seq]
        )
        grad_sums = [running + fresh_grad for running, fresh_grad in zip(grad_sums, new_grads)]
        class_sum = class_sum + class_grad
        grad_list.append(grad_tokens)
    owned = (
        lax.psum_scatter(grad_sums[0], ("dp", "fsdp"), scatter_dimension=0, tiled=True),
        lax.psum_scatter(grad_sums[1], ("dp", "fsdp"), scatter_dimension=0, tiled=True),
        lax.psum_scatter(grad_sums[2], ("dp", "fsdp"), scatter_dimension=0, tiled=True),
        lax.psum_scatter(grad_sums[3], ("dp", "fsdp"), scatter_dimension=0, tiled=True),
        lax.psum_scatter(grad_sums[4], ("dp", "fsdp"), scatter_dimension=0, tiled=True),
        lax.psum_scatter(grad_sums[5], ("dp", "fsdp"), scatter_dimension=0, tiled=True),
        lax.psum_scatter(grad_sums[6], ("dp", "fsdp"), scatter_dimension=0, tiled=True),
        lax.psum_scatter(grad_sums[7], ("dp", "fsdp"), scatter_dimension=0, tiled=True),
        lax.psum_scatter(grad_sums[8], ("dp", "fsdp"), scatter_dimension=0, tiled=True),
        lax.psum_scatter(grad_sums[9], ("dp", "fsdp"), scatter_dimension=0, tiled=True),
        lax.psum_scatter(grad_sums[10], ("dp", "fsdp"), scatter_dimension=0, tiled=True),
        lax.psum_scatter(grad_sums[11], ("dp", "fsdp"), scatter_dimension=0, tiled=True),
        lax.psum_scatter(grad_sums[12], ("dp", "fsdp"), scatter_dimension=0, tiled=True),
        lax.psum_scatter(grad_sums[13], ("dp", "fsdp"), scatter_dimension=0, tiled=True),
        lax.psum_scatter(grad_sums[14], ("dp", "fsdp"), scatter_dimension=0, tiled=True),
        lax.psum_scatter(grad_sums[15], ("dp", "fsdp"), scatter_dimension=0, tiled=True),
        lax.psum_scatter(grad_sums[16], ("dp", "fsdp"), scatter_dimension=0, tiled=True),
        lax.psum_scatter(grad_sums[17], ("dp", "fsdp"), scatter_dimension=0, tiled=True),
    )
    class_total = lax.psum(class_sum, ("dp", "fsdp"))
    return (
        jnp.concatenate(out_list, axis=0),
        jnp.concatenate(logit_list, axis=0),
        jnp.concatenate(grad_list, axis=0),
        owned[0],
        owned[1],
        owned[2],
        owned[3],
        owned[4],
        owned[5],
        owned[6],
        owned[7],
        owned[8],
        owned[9],
        owned[10],
        owned[11],
        owned[12],
        owned[13],
        owned[14],
        owned[15],
        owned[16],
        owned[17],
        class_total,
    )


BF = jnp.bfloat16
F32 = jnp.float32
MESH = pl.DeviceIdType.MESH
ANY = pl.BlockSpec(memory_space=pl.ANY)
SMEM = pl.BlockSpec(memory_space=pltpu.SMEM)
ZS = 4
CLASS_ROWS, B_QUERY, B_VALUE, B_OUT, GAIN1, SHIFT1, B_OUTER, GAIN2, SHIFT2, B_POOL = (0, 3, 4, 5, 6, 7, 8, 9, 10, 11)
VEC_ROWS = 16
KB, K0, K1, KF, KS, KZ, KE, KT = range(8)


def nn(a, b):
    return lax.dot_general(a, b, (((1,), (0,)), ((), ())), preferred_element_type=F32)


def nt(a, b):
    return lax.dot_general(a, b, (((1,), (1,)), ((), ())), preferred_element_type=F32)


def tn(a, b):
    return lax.dot_general(a, b, (((0,), (0,)), ((), ())), preferred_element_type=F32)


def my_place():
    dp, fs = lax.axis_index("dp"), lax.axis_index("fsdp")
    return dp // 2, lax.rem(dp, 2), fs // 2, lax.rem(fs, 2)


def device_at(z, y, x, c):
    return (z * 2 + y, x * 2 + c)


def meet(partners):
    barrier = pltpu.get_barrier_semaphore()
    for partner in partners:
        pl.semaphore_signal(barrier, inc=1, device_id=partner, device_id_type=MESH)
    pl.semaphore_wait(barrier, len(partners))


def all_partners(z, y, x, c):
    found = [device_at(lax.rem(z + k, ZS), y, x, c) for k in range(1, ZS)]
    found.append(device_at(z, 1 - y, x, c))
    found.append(device_at(z, y, 1 - x, c))
    found.append(device_at(z, y, x, 1 - c))
    found.append(device_at(z, y, 1 - x, 1 - c))
    return found


def group_partner(k, x, c):
    return (1 - x if k >= 2 else x, 1 - c if k % 2 == 1 else c)


def doc_ends(lens_ref):
    ends = []
    total = 0
    for d in range(lens_ref.shape[1]):
        total = total + lens_ref[lax.axis_index("fsdp"), d]
        ends.append(total)
    return ends


def doc_starts(lens_ref):
    return [0] + doc_ends(lens_ref)[:-1]


def doc_numbers(places, ends):
    number = jnp.zeros(places.shape, jnp.int32)
    for end in ends:
        number = number + (places >= end).astype(jnp.int32)
    return number


def gather_tools(plan, orders, view, own_block, keep_sem, send_sem, recv_sem, other=None):
    z, y, x, c = my_place()
    everything = slice(None)

    def along(a, axis):
        return device_at(z, 1 - y, x, c) if orders[a][axis] == "y" else device_at(z, y, 1 - x, c)

    def copy_of(a, number):
        core = device_at(z, y, x, 1 - c)
        first_other = (1 - y, x) if orders[a][0] == "y" else (y, 1 - x)
        if number < 3:
            source, target = own_block(a), view(a, (z, y, x, c))
            device = device_at(lax.rem(z + number + 1, ZS), y, x, c)
        elif number < 6:
            source = target = view(a, (everything, y, x, c))
            device = (along(a, 0), along(a, 1), core)[number - 3]
        elif number < 8:
            source = target = view(a, (everything, first_other[0], first_other[1], c))
            device = along(a, 1) if number == 6 else core
        else:
            if orders[a][1] == "y":
                source = target = view(a, (everything, 1 - y, everything, c))
            else:
                source = target = view(a, (everything, everything, 1 - x, c))
            device = core
        return pltpu.make_async_remote_copy(
            src_ref=source,
            dst_ref=target,
            send_sem=send_sem.at[a, number],
            recv_sem=recv_sem.at[a, number],
            device_id=device,
            device_id_type=MESH,
        )

    def keep(a):
        return pltpu.make_async_copy(own_block(a), view(a, (z, y, x, c)), keep_sem.at[a])

    def take_up(point):
        for kind, a in plan.get(point, ()):
            if kind == KB:
                for number in (1, 0, 2):
                    copy_of(a, number).start()
                keep(a).start()
            elif kind == KZ:
                for number in (0, 1, 2):
                    copy_of(a, number).wait_recv()
                keep(a).wait()
                for number in (3, 4, 5):
                    copy_of(a, number).start()
            elif kind == KF:
                copy_of(a, 3).wait_recv()
                for number in (6, 7):
                    copy_of(a, number).start()
            elif kind == KS:
                copy_of(a, 4).wait_recv()
                copy_of(a, 6).wait_recv()
                copy_of(a, 8).start()
            elif kind == KT:
                other(a)
            else:
                for number in (5, 7, 8):
                    copy_of(a, number).wait_recv()

    def all_sent():
        for a in range(len(orders)):
            for number in range(9):
                copy_of(a, number).wait_send()

    return take_up, all_sent


GATHER_PIECES = ((1, 0, 1, "rows"), (0, 0, 2, "columns"), (0, 1, 2, "columns"), (2, 0, 2, "rows"), (2, 1, 2, "rows"))
GATHER_ORDERS = ("xy", "xy", "yx", "xy", "yx", "xy", "yx", "xy")
GATHER_PLAN = {
    -1: (
        (KB, 0), (KT, 0), (KZ, 0), (KB, 1), (KB, 2), (KT, 1), (KB, 3), (KB, 4), (KB, 5), (KF, 0), (KT, 2), (KS, 0), (KB, 6), (KZ, 1),
        (KT, 3), (KZ, 2), (KZ, 3), (KE, 0),
    ),
    0: ((KB, 7),),
    1: ((KF, 1), (KF, 2), (KF, 3), (KZ, 4)),
    3: ((KS, 1), (KS, 2), (KZ, 5), (KS, 3), (KE, 1)),
    4: ((KZ, 6), (KE, 2), (KE, 3), (KF, 4)),
    5: ((KF, 5),),
    7: ((KZ, 7),),
    8: ((KS, 4), (KF, 6)),
    9: ((KS, 5), (KE, 4), (KF, 7), (KE, 5)),
    10: ((KS, 6),),
    11: ((KS, 7), (KE, 6)),
    12: ((KE, 7),),
}
DENSE_ARRAYS = 3
VECTORS = 9


def part_of(piece, block):
    _, which, count, along = piece
    rows, columns = block
    if along == "rows":
        return (which * (rows // count), rows // count), (0, columns)
    return (0, rows), (which * (columns // count), columns // count)


def key_marks(length, ends):
    number = doc_numbers(lax.broadcasted_iota(jnp.int32, (length, 1), 0), ends)
    lane = lax.broadcasted_iota(jnp.int32, (length, 128), 1)
    return jnp.where(lane == number, 1.0, 0.0).astype(BF)


def query_marks(at, count, ends):
    number = doc_numbers(lax.broadcasted_iota(jnp.int32, (count, 1), 0) + at, ends)
    lane = lax.broadcasted_iota(jnp.int32, (count, 128), 1)
    return jnp.where(lane == number, 0.0, -1000000000.0).astype(BF)


def attend_kernel(groups, *refs):
    lens_ref, tokens_ref, class_ref = refs[:3]
    vectors, b_inner_ref, (wq_ref, wk_ref, wv_ref) = refs[3 : 3 + VECTORS], refs[3 + VECTORS], refs[4 + VECTORS : 7 + VECTORS]
    refs = refs[7 + VECTORS :]
    shards, refs = refs[:DENSE_ARRAYS], refs[DENSE_ARRAYS:]
    q_ref, k_ref, v_ref, att_ref, lse_ref, w_ref, vec_ref, rows_ref = refs[:8]
    wholes = refs[8 : 8 + DENSE_ARRAYS]
    refs = refs[8 + DENSE_ARRAYS :]
    x_ref, vt_ref, marked_ref, qkv_shard, qkv_ref, tab_ref, tab_in_ref = refs[:7]
    local_sem, row_send, row_recv, tab_send, tab_recv, send_sem, recv_sem = refs[7:14]
    own = refs[14 : 14 + DENSE_ARRAYS]
    length, width = q_ref.shape
    chunk = 256
    points = length // chunk
    heads = width // HEAD_DIM
    items = groups + len(GATHER_PIECES)
    group = pl.program_id(0)
    z, y, x, c = my_place()
    mine = x * 2 + c

    def row_copy(k):
        px, pc = group_partner(k, x, c)
        return pltpu.make_async_remote_copy(
            src_ref=tokens_ref.at[px * 2 + pc],
            dst_ref=x_ref.at[mine],
            send_sem=row_send.at[k - 1],
            recv_sem=row_recv.at[k - 1],
            device_id=device_at(z, y, px, pc),
            device_id_type=MESH,
        )

    def row_own():
        return pltpu.make_async_copy(tokens_ref.at[mine], x_ref.at[mine], local_sem.at[0])

    def rows_out():
        return pltpu.make_async_copy(x_ref, rows_ref, local_sem.at[1])

    def table_copy(level):
        if level < 3:
            source, device = tab_ref.at[0], device_at(lax.rem(z + level + 1, ZS), y, x, c)
        else:
            source = tab_ref.at[level - 2]
            device = (device_at(z, y, 1 - x, c), device_at(z, 1 - y, x, c), device_at(z, y, x, 1 - c))[level - 3]
        return pltpu.make_async_remote_copy(
            src_ref=source,
            dst_ref=tab_in_ref.at[level],
            send_sem=tab_send.at[level],
            recv_sem=tab_recv.at[level],
            device_id=device,
            device_id_type=MESH,
        )

    def array_of(a):
        if a < groups:
            return qkv_ref.at[a], qkv_shard.at[a], None
        piece = GATHER_PIECES[a - groups]
        return wholes[piece[0]], own[piece[0]], part_of(piece, own[piece[0]].shape)

    def view(a, where):
        ref, _, part = array_of(a)
        if part is None:
            return ref.at[where]
        (r0, rows), (c0, columns) = part
        return ref.at[where + (pl.ds(r0, rows), pl.ds(c0, columns))]

    def own_block(a):
        _, ref, part = array_of(a)
        if part is None:
            return ref
        (r0, rows), (c0, columns) = part
        return ref.at[pl.ds(r0, rows), pl.ds(c0, columns)]

    def table_level(level):
        if level == 0:
            for k in (0, 1, 2):
                table_copy(k).wait_recv()
            tab_ref[1] = (tab_ref[0] + tab_in_ref[0]) + (tab_in_ref[1] + tab_in_ref[2])
        else:
            table_copy(level + 2).wait_recv()
            tab_ref[level + 1] = tab_ref[level] + tab_in_ref[level + 2]
        if level < 3:
            table_copy(level + 3).start()
        else:
            vec_ref[...] = tab_ref[4]

    take_up, all_sent = gather_tools(
        GATHER_PLAN, GATHER_ORDERS, view, own_block, local_sem.at[pl.ds(2, items)], send_sem, recv_sem, table_level
    )

    @pl.when(group == 0)
    def _():
        device = ((z * 2 + y) * 2 + x) * 2 + c
        full = tab_ref.shape[2]

        def spread(values, at):
            n = values.shape[1]
            here = lax.broadcasted_iota(jnp.int32, (n, full), 1) - at == lax.broadcasted_iota(jnp.int32, (n, full), 0)
            return nn(values.astype(BF), jnp.where(here, 1.0, 0.0).astype(BF))

        share = class_ref.shape[1]
        tab_ref[0, 0:CLASSES] = spread(class_ref[...], device * share)
        for j, ref in enumerate(vectors):
            tab_ref[0, CLASSES + j : CLASSES + j + 1] = spread(ref[...], device * share)
        per_row = full // b_inner_ref.shape[1]
        inner_bias = spread(b_inner_ref[...], lax.rem(device, per_row) * b_inner_ref.shape[1])
        for j in range(4):
            tab_ref[0, 12 + j : 13 + j] = jnp.where(device // per_row == j, inner_bias, 0.0)
        for g in range(groups):
            for j, ref in enumerate((wq_ref, wk_ref, wv_ref)):
                qkv_shard[g, :, j * width : (j + 1) * width] = ref[:, g * width : (g + 1) * width].astype(BF)
        for target, ref in zip(own, shards):
            target[...] = ref[...].astype(BF)
        meet(all_partners(z, y, x, c))
        for level in (1, 0, 2):
            table_copy(level).start()
        for k in (3, 2, 1):
            row_copy(k).start()
        row_own().start()
        take_up(-1)
        row_own().wait()
        for k in (1, 2, 3):
            row_copy(k).wait_recv()
        rows_out().start()

    tokens = x_ref[...].reshape(length, x_ref.shape[2])
    weights = qkv_ref[group].astype(F32).reshape(x_ref.shape[2], 3 * width).astype(BF)
    w_ref[...] = weights
    bias = tab_ref[4, B_QUERY : B_QUERY + 2, pl.ds(pl.multiple_of(group * width, width), width)]
    q_ref[...] = (nn(tokens, weights[:, :width]) + bias[0:1]).astype(BF)
    keys = nn(tokens, weights[:, width : 2 * width]).astype(BF)
    k_ref[...] = keys
    values = (nn(tokens, weights[:, 2 * width :]) + bias[1:2]).astype(BF)
    v_ref[...] = values
    vt_ref[...] = values.astype(F32).T.astype(BF)
    ends = doc_ends(lens_ref)
    marks = key_marks(length, ends)
    for pair in range(width // 128):
        marked_ref[pair] = jnp.concatenate([keys[:, pair * 128 : (pair + 1) * 128], marks], axis=1)
    lane_half = lax.broadcasted_iota(jnp.int32, (1, 128), 1) // HEAD_DIM

    def step(i, carry):
        for point in range(groups * points):
            if point in GATHER_PLAN:

                @pl.when((group == point // points) & (i == point % points))
                def _(point=point):
                    take_up(point)

        at = pl.multiple_of(i * chunk, chunk)
        ours = query_marks(at, chunk, ends)
        scaled = q_ref[pl.ds(at, chunk), :] * jnp.asarray(0.125, BF)
        mixed = []
        for h in range(heads):
            two = scaled[:, h // 2 * 128 : (h // 2 + 1) * 128]
            own_q = jnp.concatenate([jnp.where(lane_half == h % 2, two, jnp.zeros_like(two)), ours], axis=1)
            blocks = [nt(marked_ref[h // 2, s : s + chunk, :], own_q) for s in range(0, length, chunk)]
            peak = functools.reduce(jnp.maximum, [jnp.max(b, axis=0, keepdims=True) for b in blocks])
            exps = [jnp.exp(b - peak) for b in blocks]
            total = functools.reduce(jnp.add, [jnp.sum(e, axis=0, keepdims=True) for e in exps])
            scale = 1.0 / total
            probs = jnp.concatenate([(e * scale).astype(BF) for e in exps], axis=0)
            mixed.append(nn(vt_ref[h * HEAD_DIM : (h + 1) * HEAD_DIM, :], probs))
            lse_ref[0, h : h + 1, pl.ds(at, chunk)] = peak + jnp.log(total)
        att_ref[pl.ds(at, chunk), :] = jnp.concatenate(mixed, axis=0).T.astype(BF)
        return carry

    lax.fori_loop(0, points, step, 0)

    @pl.when(group == groups - 1)
    def _():
        take_up(groups * points)
        all_sent()
        for level in range(6):
            table_copy(level).wait_send()
        for k in range(1, 4):
            row_copy(k).wait_send()
        rows_out().wait()


def attend(lens, tokens, class_shard, vectors, b_inner, qkv_shards, shards):
    seqs, local_len, width = tokens.shape
    length = seqs * local_len
    group = 256
    groups = width // group
    share = qkv_shards[0].shape[0]
    hbm = pl.BlockSpec(memory_space=pl.ANY)
    part = pl.BlockSpec((length, group), lambda g: (0, g))
    once = pl.Buffered(buffer_count=1)
    items = groups + len(GATHER_PIECES)

    def fixed(shape):
        return pl.BlockSpec(shape, lambda g: (0,) * len(shape), pipeline_mode=once)

    lead = (ZS, 2, 2, 2)
    return pl.pallas_call(
        functools.partial(attend_kernel, groups),
        grid=(groups,),
        out_shape=[jax.ShapeDtypeStruct((length, width), BF)] * 4
        + [
            jax.ShapeDtypeStruct((groups, 8, length), F32),
            jax.ShapeDtypeStruct((width, 3 * width), BF),
            jax.ShapeDtypeStruct((VEC_ROWS, width), F32),
            jax.ShapeDtypeStruct(tokens.shape, BF),
        ]
        + [jax.ShapeDtypeStruct(lead + s.shape, BF) for s in shards],
        in_specs=[SMEM, hbm, fixed(class_shard.shape)]
        + [fixed(v.shape) for v in vectors]
        + [fixed(b_inner.shape)]
        + [fixed(s.shape) for s in qkv_shards]
        + [fixed(s.shape) for s in shards],
        out_specs=[part] * 4
        + [
            pl.BlockSpec((1, 8, length), lambda g: (g, 0, 0)),
            pl.BlockSpec((width, 3 * group), lambda g: (0, g)),
            pl.BlockSpec((VEC_ROWS, width), lambda g: (0, 0)),
            hbm,
        ]
        + [hbm] * DENSE_ARRAYS,
        scratch_shapes=[
            pltpu.VMEM(tokens.shape, BF),
            pltpu.VMEM((group, length), BF),
            pltpu.VMEM((group // 128, length, 256), BF),
            pltpu.VMEM((groups, share, 3 * group), BF),
            pltpu.VMEM((groups,) + lead + (share, 3 * group), BF),
            pltpu.VMEM((5, VEC_ROWS, width), F32),
            pltpu.VMEM((6, VEC_ROWS, width), F32),
            pltpu.SemaphoreType.DMA((2 + items,)),
            pltpu.SemaphoreType.DMA((3,)),
            pltpu.SemaphoreType.DMA((3,)),
            pltpu.SemaphoreType.DMA((6,)),
            pltpu.SemaphoreType.DMA((6,)),
            pltpu.SemaphoreType.DMA((items, 9)),
            pltpu.SemaphoreType.DMA((items, 9)),
        ]
        + [pltpu.VMEM(s.shape, BF) for s in shards],
        compiler_params=pltpu.CompilerParams(
            collective_id=1, has_side_effects=True, vmem_limit_bytes=60 * 2**20
        ),
        name="attend",
    )(lens, tokens, class_shard, *vectors, b_inner, *qkv_shards, *shards)


DENSE = 4
DENSE_ITEMS = (
    (0, 0, 2, "columns", "yx"), (1, 0, 2, "rows", "xy"), (0, 1, 2, "columns", "yx"), (1, 1, 2, "rows", "xy"),
    (2, 0, 1, "rows", "yx"), (3, 0, 1, "rows", "yx"),
)
GROUP_ORDERS = ("yx", "xy", "yx")
SCATTER_PLAN = {
    -1: ((KB, 0),),
    0: ((KB, 1),),
    1: ((K0, 0), (K0, 1), (KB, 2), (K1, 0), (KB, 3), (K1, 1)),
    2: ((KB, 4),),
    3: ((K0, 2), (K0, 3), (KB, 5), (K1, 2), (K1, 3)),
    4: ((KF, 0), (KF, 1), (KB, 6)),
    6: ((K0, 4), (K1, 4)),
    8: ((KF, 2), (KF, 3), (KS, 0), (KS, 1), (K0, 5), (KB, 7), (K1, 5)),
    9: ((KF, 4), (K0, 7), (K1, 7)),
    10: ((K0, 6), (K1, 6)),
    11: ((KS, 2),),
    12: (
        (KS, 4), (KT, 0), (KF, 7), (KS, 3), (KZ, 0), (KZ, 1), (KF, 5), (K0, 8), (K1, 8), (KT, 1), (KF, 6), (KZ, 2), (KS, 7), (KZ, 4),
        (KS, 5), (KF, 8), (KT, 2), (KS, 6), (KZ, 3), (KZ, 7), (KZ, 5), (KS, 8), (KZ, 6), (KT, 3), (KZ, 8),
    ),
}
PIECES = len(DENSE_ITEMS)


def order_of(a):
    return DENSE_ITEMS[a][4] if a < PIECES else GROUP_ORDERS[a - PIECES]


def cut_of(a, block):
    _, which, count, along, _ = DENSE_ITEMS[a]
    rows, columns = block
    if along == "rows":
        return (which * (rows // count), rows // count), (0, columns)
    return (0, rows), (which * (columns // count), columns // count)


TABLE_ROWS = 24


def attend_back_kernel(groups, *refs):
    items = PIECES + groups
    lens_ref, x_ref, w_ref, q_ref, k_ref, v_ref, att_ref, datt_ref, lse_ref, start_ref = refs[:10]
    small_a_ref, small_b_ref, bi_ref, logit_ref = refs[10:14]
    parts = refs[14 : 14 + DENSE]
    back_ref, logits_ref, small_ref = refs[18:21]
    dense_outs, group_outs = refs[21 : 21 + DENSE], refs[21 + DENSE : 24 + DENSE]
    rest = refs[24 + DENSE :]
    xt_ref, kt_ref, marked_ref, dot_ref, dq_ref, dk_ref, dv_ref, acc_ref, dx_ref, bias_ref, dw_ref, tab_ref, tab_in_ref = rest[:13]
    local_sem, row_send, row_recv, tab_send, tab_recv, send_sem, recv_sem = rest[13:20]
    rest = rest[20:]
    keeps, rest = rest[:PIECES], rest[PIECES:]
    firsts, seconds, thirds, fourths = (rest[j * items : (j + 1) * items] for j in range(4))

    length, width = q_ref.shape
    chunk = 256
    points = length // chunk
    heads = width // HEAD_DIM
    group = pl.program_id(0)
    z, y, x, c = my_place()
    mine = x * 2 + c

    def axes(a):
        return (y, x) if order_of(a)[0] == "y" else (x, y)

    def device_along(axis):
        return device_at(z, 1 - y, x, c) if axis == "y" else device_at(z, y, 1 - x, c)

    def half(a, ref, place):
        return ref.at[:, place] if order_of(a)[0] == "y" else ref.at[:, :, place]

    def whole_of(a, core):
        if a >= PIECES:
            return dw_ref.at[a - PIECES].at[:, :, :, core]
        array = DENSE_ITEMS[a][0]
        (r0, rows), (c0, columns) = cut_of(a, parts[array].shape[-2:])
        return parts[array].at[:, :, :, core, pl.ds(r0, rows), pl.ds(c0, columns)]

    def kept(a):
        return keeps[a] if a < PIECES else whole_of(a, c)

    def load(a, turn):
        place = 1 - axes(a)[0] if turn == 0 else axes(a)[0]
        return pltpu.make_async_copy(
            half(a, whole_of(a, c), place), half(a, keeps[a], place), local_sem.at[a, turn]
        )

    def copy_of(a, number):
        at, other = axes(a)
        if number < 2:
            place = 1 - at if number == 0 else at
            source, target = half(a, whole_of(a, 1 - c), place), half(a, firsts[a], place)
            device = device_at(z, y, x, 1 - c)
        elif number == 2:
            source, target = half(a, kept(a), 1 - at), seconds[a]
            device = device_along(order_of(a)[0])
        elif number == 3:
            source, target = half(a, kept(a), at).at[:, 1 - other], thirds[a]
            device = device_along(order_of(a)[1])
        else:
            there = lax.rem(z + number - 3, ZS)
            source, target = half(a, kept(a), at).at[:, other].at[there], fourths[a].at[number - 4]
            device = device_at(there, y, x, c)
        return pltpu.make_async_remote_copy(
            src_ref=source,
            dst_ref=target,
            send_sem=send_sem.at[a, number],
            recv_sem=recv_sem.at[a, number],
            device_id=device,
            device_id_type=MESH,
        )

    def add_into(target, source):
        lead = target.shape[:-2]
        total = functools.reduce(lambda p, q: p * q, lead, 1)

        def step(i, carry):
            where = []
            for size in reversed(lead):
                where.append(lax.rem(i, size))
                i = i // size
            where = tuple(reversed(where))
            target[where] = target[where] + source[where]
            return carry

        lax.fori_loop(0, total, step, 0)

    def begin(a):
        if a < PIECES:
            load(a, 0).start()
            load(a, 1).start()
        copy_of(a, 0).start()
        copy_of(a, 1).start()

    def after_core(a, turn):
        place = 1 - axes(a)[0] if turn == 0 else axes(a)[0]
        if a < PIECES:
            load(a, turn).wait()
        copy_of(a, turn).wait_recv()
        add_into(half(a, kept(a), place), half(a, firsts[a], place))
        if turn == 0:
            copy_of(a, 2).start()

    def after_first(a):
        at, other = axes(a)
        ours = half(a, kept(a), at)
        copy_of(a, 2).wait_recv()
        add_into(ours.at[:, 1 - other], seconds[a].at[:, 1 - other])
        copy_of(a, 3).start()
        add_into(ours.at[:, other], seconds[a].at[:, other])

    def after_second(a):
        at, other = axes(a)
        copy_of(a, 3).wait_recv()
        add_into(half(a, kept(a), at).at[:, other], thirds[a])
        for number in (5, 4, 6):
            copy_of(a, number).start()

    def finish(a):
        at, other = axes(a)
        for number in (4, 5, 6):
            copy_of(a, number).wait_recv()
        ours = half(a, kept(a), at).at[:, other]
        total = (
            ours[z].astype(F32)
            + fourths[a][0].astype(F32)
            + fourths[a][1].astype(F32)
            + fourths[a][2].astype(F32)
        )
        if a < PIECES:
            out = dense_outs[DENSE_ITEMS[a][0]]
            (r0, rows), (c0, columns) = cut_of(a, out.shape)
            out[r0 : r0 + rows, c0 : c0 + columns] = total
        else:
            s = (a - PIECES) * width
            for j, out in enumerate(group_outs):
                out[:, s : s + width] = total[:, j * width : (j + 1) * width]

    def row_copy(which, k):
        px, pc = group_partner(k, x, c)
        if which == 0:
            source, target = dx_ref.at[px * 2 + pc], back_ref.at[mine]
        else:
            source, target = logit_ref, logits_ref.at[mine]
        return pltpu.make_async_remote_copy(
            src_ref=source,
            dst_ref=target,
            send_sem=row_send.at[which, k - 1],
            recv_sem=row_recv.at[which, k - 1],
            device_id=device_at(z, y, px, pc),
            device_id_type=MESH,
        )

    def row_own(which):
        if which == 0:
            source, target = dx_ref.at[mine], back_ref.at[mine]
        else:
            source, target = logit_ref, logits_ref.at[mine]
        return pltpu.make_async_copy(source, target, local_sem.at[PIECES, which])

    def table_copy(level):
        if level < 3:
            source, target = tab_ref.at[level], tab_in_ref.at[level]
            device = (
                device_at(z, y, x, 1 - c), device_at(z, 1 - y, x, c), device_at(z, y, 1 - x, c)
            )[level]
        else:
            source, target = tab_ref.at[3], tab_in_ref.at[3 + z]
            device = device_at(lax.rem(z + level - 2, ZS), y, x, c)
        return pltpu.make_async_remote_copy(
            src_ref=source,
            dst_ref=target,
            send_sem=tab_send.at[level],
            recv_sem=tab_recv.at[level],
            device_id=device,
            device_id_type=MESH,
        )

    def table_wait(level):
        if level < 3:
            table_copy(level).wait_recv()
        else:
            slot = tab_in_ref.at[3 + lax.rem(z + ZS - (level - 2), ZS)]
            pltpu.make_async_remote_copy(
                src_ref=slot,
                dst_ref=slot,
                send_sem=tab_send.at[level],
                recv_sem=tab_recv.at[level],
                device_id=device_at(lax.rem(z + level - 2, ZS), y, x, c),
                device_id_type=MESH,
            ).wait_recv()

    def table_level(level):
        if level == 3:
            for last in (3, 4, 5):
                table_wait(last)
            table = (tab_in_ref[3] + tab_in_ref[4]) + (tab_in_ref[5] + tab_in_ref[6])
            device = ((z * 2 + y) * 2 + x) * 2 + c
            full = table.shape[1]
            row = lax.broadcasted_iota(jnp.int32, (full, 128), 0)
            lane = lax.broadcasted_iota(jnp.int32, (full, 128), 1)

            def own_lanes(values, size, at):
                chosen = jnp.where((row == at + lane) & (lane < size), 1.0, 0.0)
                return lax.dot_general(
                    values, chosen, (((1,), (0,)), ((), ())), preferred_element_type=F32, precision=lax.Precision.HIGHEST
                )

            per_row = full * 4 // (8 * ZS)
            small_ref[0:TABLE_ROWS] = own_lanes(table, full // (8 * ZS), device * (full // (8 * ZS)))
            inner_bias = own_lanes(table, per_row, lax.rem(device, full // per_row) * per_row)
            for j in range(4):

                @pl.when(device // (full // per_row) == j)
                def _(j=j):
                    small_ref[TABLE_ROWS : TABLE_ROWS + 1] = inner_bias[12 + j : 13 + j]

            small_ref[TABLE_ROWS + 1 : TABLE_ROWS + 2] = table[16:17, 0:128]
            return
        table_wait(level)
        tab_ref[level + 1] = tab_ref[level] + tab_in_ref[level]
        if level < 2:
            table_copy(level + 1).start()
        else:
            tab_in_ref[3 + z] = tab_ref[3]
            for nxt in (4, 3, 5):
                table_copy(nxt).start()

    def take_up(point):
        for kind, a in SCATTER_PLAN.get(point, ()):
            if kind == KB:
                begin(a)
            elif kind == K0 or kind == K1:
                after_core(a, 0 if kind == K0 else 1)
            elif kind == KF:
                after_first(a)
            elif kind == KS:
                after_second(a)
            elif kind == KZ:
                finish(a)
            else:
                table_level(a)

    @pl.when(group == 0)
    def _():
        meet(all_partners(z, y, x, c))
        take_up(-1)
        for k in range(1, 4):
            row_copy(1, k).start()
        row_own(1).start()
        xt_ref[...] = x_ref[...].astype(F32).T.astype(BF)
        acc_ref[...] = start_ref[...]

    kt_ref[...] = k_ref[...].astype(F32).T.astype(BF)
    dot_ref[...] = (datt_ref[...].astype(F32) * att_ref[...].astype(F32)).T
    dk_ref[...] = jnp.zeros_like(dk_ref)
    dv_ref[...] = jnp.zeros_like(dv_ref)
    ends = doc_ends(lens_ref)
    marks = key_marks(length, ends)
    for pair in range(width // 128):
        marked_ref[pair] = jnp.concatenate([k_ref[:, pair * 128 : (pair + 1) * 128], marks], axis=1)
    lane_half = lax.broadcasted_iota(jnp.int32, (1, 128), 1) // HEAD_DIM
    lane_head = lax.broadcasted_iota(jnp.int32, (1, width), 1) // HEAD_DIM

    def step(i, carry):
        for point in range(groups * points):

            @pl.when((group == point // points) & (i == point % points))
            def _(point=point):
                take_up(point)

        at = pl.multiple_of(i * chunk, chunk)
        ours = query_marks(at, chunk, ends)
        scaled = q_ref[pl.ds(at, chunk), :] * jnp.asarray(0.125, BF)
        given = datt_ref[pl.ds(at, chunk), :]
        own_q = [jnp.where(lane_head == h, scaled, jnp.zeros_like(scaled)) for h in range(heads)]
        own_d = [jnp.where(lane_head == h, given, jnp.zeros_like(given)) for h in range(heads)]
        all_probs = [[] for _ in range(length // chunk)]
        all_grads = [[] for _ in range(length // chunk)]
        for h in range(heads):
            lse = lse_ref[0, h : h + 1, pl.ds(at, chunk)]
            dots = jnp.sum(
                dot_ref[h * HEAD_DIM : (h + 1) * HEAD_DIM, pl.ds(at, chunk)], axis=0, keepdims=True
            )
            two = scaled[:, h // 2 * 128 : (h // 2 + 1) * 128]
            marked_q = jnp.concatenate([jnp.where(lane_half == h % 2, two, jnp.zeros_like(two)), ours], axis=1)
            for j in range(length // chunk):
                s = j * chunk
                scores = nt(marked_ref[h // 2, s : s + chunk, :], marked_q)
                probs = jnp.exp(scores - lse)
                grad_probs = nt(v_ref[s : s + chunk, :], own_d[h])
                all_grads[j].append((probs * (grad_probs - dots)).astype(BF))
                all_probs[j].append(probs.astype(BF))
        stacked_q = jnp.concatenate(own_q, axis=0)
        stacked_d = jnp.concatenate(own_d, axis=0)
        for j in range(length // chunk):
            s = j * chunk
            dk_ref[s : s + chunk, :] += nn(jnp.concatenate(all_grads[j], axis=1), stacked_q)
            dv_ref[s : s + chunk, :] += nn(jnp.concatenate(all_probs[j], axis=1), stacked_d)
        mixed = []
        for h in range(heads):
            column = jnp.concatenate([all_grads[j][h] for j in range(length // chunk)], axis=0)
            mixed.append(nn(kt_ref[h * HEAD_DIM : (h + 1) * HEAD_DIM, :], column))
        dq_ref[pl.ds(at, chunk), :] = (jnp.concatenate(mixed, axis=0).T * 0.125).astype(BF)
        return carry

    lax.fori_loop(0, points, step, 0)
    xt = xt_ref[...]
    grads = (dq_ref[...], dk_ref[...].astype(BF), dv_ref[...].astype(BF))
    block = dw_ref.shape[1:6]
    for j, grad in enumerate(grads):
        dw_ref[group, :, :, :, :, :, j * width : (j + 1) * width] = nn(xt, grad).reshape(block + (width,)).astype(BF)
    bias_ref[group, 0:1, :] = jnp.sum(grads[0].astype(F32), axis=0, keepdims=True)
    bias_ref[group, 1:2, :] = jnp.sum(grads[2].astype(F32), axis=0, keepdims=True)

    @pl.when(group < groups - 1)
    def _():
        total = acc_ref[...]
        for j, grad in enumerate(grads):
            total = total + nt(grad, w_ref[:, j * width : (j + 1) * width])
        acc_ref[...] = total

    @pl.when(group == groups - 1)
    def _():
        begin(items - 1)
        size = dx_ref.shape[1]
        for k in (3, 2, 1, 0):
            px, pc = group_partner(k, x, c)
            block = px * 2 + pc
            here = pl.ds(pl.multiple_of(block * size, size), size)
            total = acc_ref[here, :]
            for j, ref in enumerate((dq_ref, dk_ref, dv_ref)):
                total = total + nt(ref[here, :].astype(BF), w_ref[:, j * width : (j + 1) * width])
            dx_ref[block] = total.astype(BF)
            if k == 0:
                row_own(0).start()
            else:
                row_copy(0, k).start()
        tab_ref[0, 0:CLASSES] = small_a_ref[0:CLASSES]
        for g in range(groups):
            tab_ref[0, B_QUERY : B_QUERY + 2, g * width : (g + 1) * width] = bias_ref[g, 0:2, :]
        for row, (ref, at) in {
            B_OUT: (small_b_ref, 3), GAIN1: (small_b_ref, 4), SHIFT1: (small_b_ref, 5), B_OUTER: (small_b_ref, 0),
            GAIN2: (small_b_ref, 1), SHIFT2: (small_b_ref, 2), B_POOL: (small_a_ref, 16), 16: (small_a_ref, 17),
        }.items():
            tab_ref[0, row : row + 1] = ref[at : at + 1, :]
        full = small_a_ref.shape[1]
        for j in range(4):
            tab_ref[0, 12 + j : 13 + j] = bi_ref[:, j * full : (j + 1) * full]
        tab_ref[0, 17:TABLE_ROWS] = jnp.zeros((TABLE_ROWS - 17, full), F32)
        table_copy(0).start()
        take_up(groups * points)
        for a in range(items):
            for number in range(7):
                copy_of(a, number).wait_send()
        for level in range(6):
            table_copy(level).wait_send()
        for which in (0, 1):
            for k in range(1, 4):
                row_copy(which, k).wait_recv()
                row_copy(which, k).wait_send()
            row_own(which).wait()


def attend_back(lens, rows, w_groups, q, k, v, att, datt, lse, grad_pre, small_a, small_b, grad_b_inner, logit_block, parts):
    length, width = rows.shape
    group = 256
    groups = width // group
    local_len = length // 4
    share = width // (8 * ZS)
    once = pl.Buffered(buffer_count=1)
    whole = pl.BlockSpec((length, width), lambda g: (0, 0), pipeline_mode=once)
    part = pl.BlockSpec((length, group), lambda g: (0, g))
    blocks = [p.shape[1:] for p in parts]
    split = [p.reshape((ZS, 2, 2, 2) + b) for p, b in zip(parts, blocks)]
    shapes = [r for r in blocks]
    cuts = [cut_of(a, blocks[DENSE_ITEMS[a][0]]) for a in range(PIECES)]
    blocks = [(r[1], q[1]) for r, q in cuts] + [(share, 3 * group)] * groups
    hbm = pl.BlockSpec(memory_space=pl.ANY)

    def fixed(shape):
        return pl.BlockSpec(shape, lambda g: (0,) * len(shape))

    results = [(TABLE_ROWS + 8, 128)] + shapes + [(share, width)] * 3
    arriving = []
    for lead in ((ZS, 2, 2), (ZS, 2), (ZS,), (ZS - 1,)):
        arriving += [pltpu.VMEM(lead + b, BF) for b in blocks]
    items = len(blocks)
    return pl.pallas_call(
        functools.partial(attend_back_kernel, groups),
        grid=(groups,),
        out_shape=[
            jax.ShapeDtypeStruct((4, local_len, width), BF),
            jax.ShapeDtypeStruct((4,) + logit_block.shape, F32),
        ]
        + [jax.ShapeDtypeStruct(r, F32) for r in results],
        in_specs=[
            SMEM,
            whole,
            pl.BlockSpec((width, 3 * group), lambda g: (0, g)),
            part, part, part, part, part,
            pl.BlockSpec((1, 8, length), lambda g: (g, 0, 0)),
            whole,
            fixed(small_a.shape), fixed(small_b.shape), fixed(grad_b_inner.shape), hbm,
        ]
        + [hbm] * DENSE,
        out_specs=[hbm, hbm] + [fixed(r) for r in results],
        scratch_shapes=[
            pltpu.VMEM((width, length), BF),
            pltpu.VMEM((group, length), BF),
            pltpu.VMEM((group // 128, length, 256), BF),
            pltpu.VMEM((group, length), F32),
            pltpu.VMEM((length, group), BF),
            pltpu.VMEM((length, group), F32),
            pltpu.VMEM((length, group), F32),
            pltpu.VMEM((length, width), F32),
            pltpu.VMEM((4, local_len, width), BF),
            pltpu.VMEM((groups, 8, group), F32),
            pltpu.VMEM((groups, ZS, 2, 2, 2, share, 3 * group), BF),
            pltpu.VMEM((4, TABLE_ROWS, width), F32),
            pltpu.VMEM((3 + ZS, TABLE_ROWS, width), F32),
            pltpu.SemaphoreType.DMA((PIECES + 1, 2)),
            pltpu.SemaphoreType.DMA((2, 3)),
            pltpu.SemaphoreType.DMA((2, 3)),
            pltpu.SemaphoreType.DMA((6,)),
            pltpu.SemaphoreType.DMA((6,)),
            pltpu.SemaphoreType.DMA((items, 7)),
            pltpu.SemaphoreType.DMA((items, 7)),
        ]
        + [pltpu.VMEM((ZS, 2, 2) + b, BF) for b in blocks[:PIECES]]
        + arriving,
        compiler_params=pltpu.CompilerParams(
            collective_id=2, has_side_effects=True, vmem_limit_bytes=60 * 2**20
        ),
        name="attend_back",
    )(lens, rows, w_groups, q, k, v, att, datt, lse, grad_pre, small_a, small_b, grad_b_inner, logit_block, *split)


def row_copies(source_ref, target_ref, send_sem, recv_sem):
    z, y, x, c = my_place()
    copies = []
    for k in (3, 2, 1):
        px, pc = group_partner(k, x, c)
        copies.append(
            pltpu.make_async_remote_copy(
                src_ref=source_ref.at[px * 2 + pc],
                dst_ref=target_ref.at[x * 2 + c],
                send_sem=send_sem.at[k - 1],
                recv_sem=recv_sem.at[k - 1],
                device_id=device_at(z, y, px, pc),
                device_id_type=MESH,
            )
        )
    return copies, pltpu.make_async_copy(source_ref.at[x * 2 + c], target_ref.at[x * 2 + c], send_sem.at[3])


ROW_SEMAPHORES = [pltpu.SemaphoreType.DMA((4,)), pltpu.SemaphoreType.DMA((3,))]


def normal_parts(v):
    bell = jnp.exp(v * v * -0.5)
    t = 1.0 / (1.0 + jnp.abs(v) * 0.23164189)
    tail = t * (0.127414796 + t * (-0.142248368 + t * (0.710706870 + t * (-0.726576013 + t * 0.530702714)))) * bell
    return jnp.where(v >= 0.0, 1.0 - tail, tail), bell


def centered_parts(values):
    average = jnp.mean(values, axis=-1, keepdims=True)
    centered = values - average
    variance = jnp.mean(centered * centered, axis=-1, keepdims=True)
    inverse = lax.rsqrt(variance + 1e-06)
    return centered * inverse, inverse


def norm_back(grad, values, gain):
    hat, inverse = centered_parts(values)
    scaled = grad * gain
    mean_scaled = jnp.mean(scaled, axis=-1, keepdims=True)
    mean_cross = jnp.mean(scaled * hat, axis=-1, keepdims=True)
    back = (scaled - mean_scaled - hat * mean_cross) * inverse
    return back, jnp.sum(grad * hat, axis=0, keepdims=True), jnp.sum(grad, axis=0, keepdims=True)


MIDDLE_ORDERS = ("xy",)
MIDDLE_PLAN = {
    0: ((KB, 0),),
    2: ((KZ, 0),),
    5: ((KF, 0),),
    8: ((KS, 0),),
    14: ((KE, 0),),
}
COTANGENT_POINT = 3


def middle_kernel(tiles, *refs):
    (
        lens_ref, labels_ref, b_class_ref, cot_ref, x_ref, att_ref, w_inner_ref, w_out_ref, outer_hbm_ref, pool_shard_ref,
        vec_ref,
    ) = refs[:11]
    (
        low_ref, act_out_ref, outer_ref, inner_ref, branch_ref, datt_ref, gpre_ref, dpool_ref, small_a_ref, small_b_ref, bi_ref,
        logits_ref, layer_out_ref,
    ) = refs[11:24]
    (
        act_ref, dact_ref, pre_ref, summed_ref, result_ref, cot_rows_ref, first_ref, picked_ref, own_pool, w_outer_ref, pool_ref,
        outer_sem, act_sem, keep_sem, send_sem, recv_sem, cot_send, cot_recv, lo_send, lo_recv,
    ) = refs[24:]
    step = pl.program_id(0)
    rows, full = x_ref.shape
    chunks = act_ref.shape[1] // full

    def view(a, where):
        return pool_ref.at[where]

    def own_block(a):
        return own_pool

    gather_up, all_sent = gather_tools(MIDDLE_PLAN, MIDDLE_ORDERS, view, own_block, keep_sem, send_sem, recv_sem)

    def take_up(point):
        if point in MIDDLE_PLAN or point == COTANGENT_POINT:

            @pl.when(step == point // 2)
            def _():
                gather_up(point)
                if point == COTANGENT_POINT:
                    copies, own = row_copies(cot_ref, cot_rows_ref, cot_send, cot_recv)
                    for copy in copies:
                        copy.start()
                    own.start()

    def outer_copy():
        return pltpu.make_async_copy(outer_hbm_ref, w_outer_ref, outer_sem.at[0])

    def act_copy(tile):
        where = pl.ds(tile * rows, rows)
        return pltpu.make_async_copy(act_ref.at[where], act_out_ref.at[where], act_sem.at[tile])

    def vec(row):
        return vec_ref[row : row + 1, :]

    @pl.when(step == 0)
    def _():
        outer_copy().start()
        own_pool[...] = pool_shard_ref[...].astype(BF)
        z, y, x, c = my_place()
        meet(all_partners(z, y, x, c))

    tile = lax.rem(step, tiles)
    here = pl.ds(pl.multiple_of(tile * rows, rows), rows)
    for point in range(0, 2 * tiles, 2):
        take_up(point)

    @pl.when(step < tiles)
    def _():
        pre = x_ref[...].astype(F32) + (nn(att_ref[...], w_out_ref[...]) + vec(B_OUT))
        pre_ref[here, :] = pre
        low = (centered_parts(pre)[0] * vec(GAIN1) + vec(SHIFT1)).astype(BF)
        low_ref[...] = low
        for j in range(chunks):
            if j == chunks // 2:
                for point in range(1, 2 * tiles, 2):
                    take_up(point)
            s = j * full
            hidden = nn(low, w_inner_ref[:, s : s + full]) + vec(12 + j)
            phi, bell = normal_parts(hidden)
            act_ref[here, s : s + full] = (hidden * phi).astype(BF)
            dact_ref[here, s : s + full] = (phi + hidden * bell * 0.3989422804014327).astype(BF)
        for t in range(tiles):

            @pl.when(step == t)
            def _(t=t):
                act_copy(t).start()

    for point in range(2 * tiles, 4 * tiles, 2):
        take_up(point)

    def outer_part(j):
        return w_outer_ref[j].reshape(full, full)

    @pl.when(step == tiles)
    def _():
        outer_copy().wait()

    @pl.when((step >= tiles) & (step < 2 * tiles))
    def _():
        total = centered_parts(pre_ref[here, :])[0] * vec(GAIN1) + vec(SHIFT1) + vec(B_OUTER)
        for j in range(chunks):
            total = total + nn(act_ref[here, j * full : (j + 1) * full], outer_part(j))
        summed_ref[here, :] = total
        result = (centered_parts(total)[0] * vec(GAIN2) + vec(SHIFT2)).astype(BF)
        result_ref[tile] = result
        starts = doc_starts(lens_ref)
        places = lax.broadcasted_iota(jnp.int32, (VEC_ROWS, rows), 1) + tile * rows
        row_doc = lax.broadcasted_iota(jnp.int32, (VEC_ROWS, rows), 0)
        hit = jnp.zeros((VEC_ROWS, rows), jnp.bool_)
        for d, start in enumerate(starts):
            hit = hit | ((row_doc == d) & (places == start))
        found = nn(jnp.where(hit, 1.0, 0.0).astype(BF), result)

        @pl.when(tile == 0)
        def _():
            picked_ref[...] = found

        @pl.when(tile > 0)
        def _():
            picked_ref[...] += found

    @pl.when(step == 2 * tiles - 1)
    def _():
        copies, own = row_copies(result_ref, layer_out_ref, lo_send, lo_recv)
        for copy in copies:
            copy.start()
        own.start()
        w_pool = pool_ref[...].astype(F32).reshape(full, full).astype(BF)
        docs = lens_ref.shape[1]
        picked = picked_ref[...].astype(BF)
        pooled = jnp.tanh(nn(picked, w_pool) + vec(B_POOL))
        pooled_low = pooled.astype(BF)
        table = vec_ref[...].astype(BF)
        column = lax.broadcasted_iota(jnp.int32, (VEC_ROWS, VEC_ROWS), 1)
        row = lax.broadcasted_iota(jnp.int32, (VEC_ROWS, VEC_ROWS), 0)
        class_bias = jnp.zeros((VEC_ROWS, VEC_ROWS), F32)
        for j in range(CLASSES):
            class_bias = jnp.where(column == j, b_class_ref[j], class_bias)
        logits = nt(pooled_low, table) + class_bias
        logits_ref[...] = jnp.concatenate([logits[0:8], jnp.zeros((8, 128 - VEC_ROWS), F32)], axis=1)
        live = column < CLASSES
        shown = jnp.where(live, logits, -jnp.inf)
        exps = jnp.where(live, jnp.exp(shown - jnp.max(shown, axis=-1, keepdims=True)), 0.0)
        probs = exps / jnp.sum(exps, axis=-1, keepdims=True)
        label = jnp.zeros((VEC_ROWS, VEC_ROWS), jnp.int32)
        for d in range(docs):
            label = jnp.where(row == d, labels_ref[lax.axis_index("fsdp"), d], label)
        grad = jnp.where(live & (row < docs), probs - jnp.where(label == column, 1.0, 0.0), 0.0)
        grad_low = grad.astype(BF)
        grad_pool = (nn(grad_low, table) * (1.0 - pooled * pooled)).astype(BF)
        dpool_ref[...] = tn(picked, grad_pool).astype(BF)
        first_ref[...] = nt(grad_pool, w_pool)
        small_a_ref[0:16, :] = tn(grad_low, pooled_low)
        small_a_ref[16:17, :] = jnp.sum(grad_pool.astype(F32), axis=0, keepdims=True)
        class_sum = jnp.sum(grad_low.astype(F32), axis=0, keepdims=True)
        small_a_ref[17:18, :] = jnp.concatenate([class_sum, jnp.zeros((1, full - VEC_ROWS), F32)], axis=1)
        small_b_ref[...] = jnp.zeros_like(small_b_ref)
        bi_ref[...] = jnp.zeros_like(bi_ref)
        copies, own = row_copies(cot_ref, cot_rows_ref, cot_send, cot_recv)
        for copy in copies:
            copy.wait()
        own.wait()

    @pl.when(step >= 2 * tiles)
    def _():
        grad = cot_rows_ref[tile].astype(F32)
        places = lax.broadcasted_iota(jnp.int32, (rows, 1), 0) + tile * rows
        placed = jnp.zeros(grad.shape, F32)
        for d, start in enumerate(doc_starts(lens_ref)):
            placed = jnp.where(places == start, first_ref[d : d + 1, :], placed)
        grad = grad + placed
        grad_summed, gain2, shift2 = norm_back(grad, summed_ref[here, :], vec(GAIN2))
        outer = grad_summed.astype(BF)
        outer_ref[...] = outer
        grad_normed = grad_summed
        for j in range(chunks):
            s = j * full
            back = nt(outer, outer_part(j))
            inner = (back * dact_ref[here, s : s + full].astype(F32)).astype(BF)
            inner_ref[:, s : s + full] = inner
            bi_ref[:, s : s + full] += jnp.sum(inner.astype(F32), axis=0, keepdims=True)
            grad_normed = grad_normed + nt(inner, w_inner_ref[:, s : s + full])
        grad_pre, gain1, shift1 = norm_back(grad_normed, pre_ref[here, :], vec(GAIN1))
        gpre_ref[...] = grad_pre
        branch = grad_pre.astype(BF)
        branch_ref[...] = branch
        datt_ref[...] = nt(branch, w_out_ref[...]).astype(BF)
        small_b_ref[0:1, :] += jnp.sum(outer.astype(F32), axis=0, keepdims=True)
        small_b_ref[1:2, :] += gain2
        small_b_ref[2:3, :] += shift2
        small_b_ref[3:4, :] += jnp.sum(branch.astype(F32), axis=0, keepdims=True)
        small_b_ref[4:5, :] += gain1
        small_b_ref[5:6, :] += shift1

    @pl.when(step == 3 * tiles - 1)
    def _():
        all_sent()
        for t in range(tiles):
            act_copy(t).wait()
        copies, own = row_copies(result_ref, layer_out_ref, lo_send, lo_recv)
        for copy in copies:
            copy.wait()
        own.wait()


def middle(lens, labels, b_class, cot, rows, att, w_inner, w_out, w_outer, pool_shard, vectors):
    length, width = rows.shape
    hidden = w_inner.shape[1]
    tile = 256
    tiles = length // tile
    items = len(MIDDLE_ORDERS)
    once = pl.Buffered(buffer_count=1)
    early = pl.BlockSpec((tile, width), lambda i: (jnp.minimum(i, tiles - 1), 0))

    def late(size):
        return pl.BlockSpec((tile, size), lambda i: (jnp.maximum(i - 2 * tiles, 0), 0))

    def fixed(shape):
        return pl.BlockSpec(shape, lambda i: (0,) * len(shape), pipeline_mode=once)

    lead = (ZS, 2, 2, 2)
    return pl.pallas_call(
        functools.partial(middle_kernel, tiles),
        grid=(3 * tiles,),
        out_shape=[
            jax.ShapeDtypeStruct((length, width), BF),
            jax.ShapeDtypeStruct((length, hidden), BF),
            jax.ShapeDtypeStruct((length, width), BF),
            jax.ShapeDtypeStruct((length, hidden), BF),
            jax.ShapeDtypeStruct((length, width), BF),
            jax.ShapeDtypeStruct((length, width), BF),
            jax.ShapeDtypeStruct((length, width), F32),
            jax.ShapeDtypeStruct((width, width), BF),
            jax.ShapeDtypeStruct((24, width), F32),
            jax.ShapeDtypeStruct((8, width), F32),
            jax.ShapeDtypeStruct((1, hidden), F32),
            jax.ShapeDtypeStruct((8, 128), F32),
            jax.ShapeDtypeStruct(cot.shape, BF),
        ],
        in_specs=[
            SMEM, SMEM, SMEM, ANY, early, early, fixed((width, hidden)), fixed((width, width)), ANY,
            fixed(pool_shard.shape), fixed((VEC_ROWS, width)),
        ],
        out_specs=[
            early, ANY, late(width), late(hidden), late(width), late(width), late(width), fixed((width, width)),
            fixed((24, width)), fixed((8, width)), fixed((1, hidden)), fixed((8, 128)), ANY,
        ],
        scratch_shapes=[
            pltpu.VMEM((length, hidden), BF),
            pltpu.VMEM((length, hidden), BF),
            pltpu.VMEM((length, width), F32),
            pltpu.VMEM((length, width), F32),
            pltpu.VMEM(cot.shape, BF),
            pltpu.VMEM(cot.shape, BF),
            pltpu.VMEM((VEC_ROWS, width), F32),
            pltpu.VMEM((VEC_ROWS, width), F32),
            pltpu.VMEM(pool_shard.shape, BF),
            pltpu.VMEM(w_outer.shape, BF),
            pltpu.VMEM(lead + pool_shard.shape, BF),
            pltpu.SemaphoreType.DMA((1,)),
            pltpu.SemaphoreType.DMA((tiles,)),
            pltpu.SemaphoreType.DMA((items,)),
            pltpu.SemaphoreType.DMA((items, 9)),
            pltpu.SemaphoreType.DMA((items, 9)),
        ]
        + ROW_SEMAPHORES * 2,
        compiler_params=pltpu.CompilerParams(collective_id=3, has_side_effects=True, vmem_limit_bytes=60 * 2**20),
        name="middle",
    )(lens, labels, b_class, cot, rows, att, w_inner, w_out, w_outer, pool_shard, vectors)


def results_kernel(large, small_ref, *refs):
    sources, refs = refs[:large], refs[large:]
    targets, columns, inner_ref, class_ref, sem, *held = refs[:large], refs[large : large + VECTORS], *refs[large + VECTORS :]
    arriving = [pltpu.make_async_copy(s, h, sem.at[0, j]) for j, (s, h) in enumerate(zip(sources, held))]
    leaving = [pltpu.make_async_copy(h, t, sem.at[1, j]) for j, (h, t) in enumerate(zip(held, targets))]
    for copy in arriving:
        copy.start()
    for j, ref in enumerate(columns):
        ref[...] = small_ref[B_QUERY + j : B_QUERY + j + 1, 0 : ref.shape[1]]
    inner_ref[...] = small_ref[TABLE_ROWS : TABLE_ROWS + 1, 0 : inner_ref.shape[1]]
    class_ref[...] = small_ref[TABLE_ROWS + 1 : TABLE_ROWS + 2, 0 : class_ref.shape[1]]
    for came, goes in zip(arriving, leaving):
        came.wait()
        goes.start()
    for goes in leaving:
        goes.wait()


def write_results(small, arrays, share, hidden_share):
    shapes = [jax.ShapeDtypeStruct(a.shape, a.dtype) for a in arrays]
    vectors = [(1, share)] * VECTORS + [(1, hidden_share), (1, CLASSES)]
    inside = pl.BlockSpec(memory_space=pltpu.VMEM)
    return pl.pallas_call(
        functools.partial(results_kernel, len(arrays)),
        out_shape=shapes + [jax.ShapeDtypeStruct(v, F32) for v in vectors],
        in_specs=[inside] + [ANY] * len(arrays),
        out_specs=[ANY] * len(arrays) + [inside] * len(vectors),
        scratch_shapes=[pltpu.SemaphoreType.DMA((2, len(arrays)))] + [pltpu.VMEM(a.shape, a.dtype) for a in arrays],
        compiler_params=pltpu.CompilerParams(vmem_limit_bytes=60 * 2**20),
        name="results",
    )(small, *arrays)


def fast_body(
    inputs, cotangent, doc_lengths, labels, w_query, b_query, w_key, w_value, b_value, w_out, b_out, first_gain, first_shift,
    w_inner, b_inner, w_outer, b_outer, second_gain, second_shift, w_pool, b_pool, w_class, b_class,
):
    seqs, local_len, width = inputs.shape
    length = seqs * local_len
    devices = 8 * ZS
    docs = doc_lengths.shape[1]
    share = width // devices
    hidden_share = b_inner.shape[0]
    hidden = hidden_share * devices
    vector_shards = [b_query, b_value, b_out, first_gain, first_shift, b_outer, second_gain, second_shift, b_pool]
    q, k, v, att, lse, w_qkv, vectors, rows, full_inner, full_out, full_outer = attend(
        doc_lengths, inputs, w_class.T, [member.reshape(1, share) for member in vector_shards], b_inner.reshape(1, hidden_share),
        [w_query, w_key, w_value], [w_inner, w_out, w_outer],
    )
    rows = rows.reshape(length, width)
    full_inner = full_inner.reshape(width, hidden)
    full_out = full_out.reshape(width, width)
    low, act, outer, inner, branch, datt, grad_pre, grad_pool, small_a, small_b, grad_b_inner, logit_block, layer_out = middle(
        doc_lengths, labels, b_class, cotangent, rows, att, full_inner, full_out, full_outer, w_pool, vectors
    )
    grad_outer_w = tn(act, outer).astype(BF)
    grad_inner_w = tn(low, inner).astype(BF)
    grad_out_w = tn(att, branch).astype(BF)
    grad_inputs, all_logits, small, *sums = attend_back(
        doc_lengths, rows, w_qkv, q, k, v, att, datt, lse, grad_pre, small_a, small_b, grad_b_inner, logit_block,
        [
            grad_inner_w.reshape(devices, share, hidden),
            grad_outer_w.reshape(devices, hidden_share, width),
            grad_out_w.reshape(devices, share, width),
            grad_pool.reshape(devices, share, width),
        ],
    )

    done = write_results(small, [grad_inputs, layer_out, *sums], share, hidden_share)
    grad_inputs, layer_out, o_inner, o_outer, o_out, o_pool, o_query, o_key, o_value = done[:9]
    (
        o_b_query, o_b_value, o_b_out, o_gain1, o_shift1, o_b_outer, o_gain2, o_shift2, o_b_pool, o_b_inner, o_b_class,
    ) = (vector.reshape(-1) for vector in done[9:])
    return (
        layer_out,
        all_logits[:, :docs, :CLASSES],
        grad_inputs,
        o_query,
        o_b_query,
        o_key,
        o_value,
        o_b_value,
        o_out,
        o_b_out,
        o_gain1,
        o_shift1,
        o_inner,
        o_b_inner,
        o_outer,
        o_b_outer,
        o_gain2,
        o_shift2,
        o_pool,
        o_b_pool,
        small[:CLASSES, :share].T,
        o_b_class,
    )


def solution(mesh):
    placed = (
        P("dp", "fsdp", None),
        P("dp", "fsdp", None),
        P("dp", None),
        P("dp", None),
        P(("dp", "fsdp"), None),
        P(("dp", "fsdp")),
        P(("dp", "fsdp"), None),
        P(("dp", "fsdp"), None),
        P(("dp", "fsdp")),
        P(("dp", "fsdp"), None),
        P(("dp", "fsdp")),
        P(("dp", "fsdp")),
        P(("dp", "fsdp")),
        P(("dp", "fsdp"), None),
        P(("dp", "fsdp")),
        P(("dp", "fsdp"), None),
        P(("dp", "fsdp")),
        P(("dp", "fsdp")),
        P(("dp", "fsdp")),
        P(("dp", "fsdp"), None),
        P(("dp", "fsdp")),
        P(("dp", "fsdp"), None),
        P(),
    )
    sizes = (mesh.shape["dp"], mesh.shape["fsdp"])
    chosen = fast_body if sizes == (8, 4) else general_body
    return jax.shard_map(
        chosen,
        mesh=mesh,
        in_specs=placed,
        out_specs=(
            P("dp", "fsdp", None),
            P("dp", None, None),
            P("dp", "fsdp", None),
            P(("dp", "fsdp"), None),
            P(("dp", "fsdp")),
            P(("dp", "fsdp"), None),
            P(("dp", "fsdp"), None),
            P(("dp", "fsdp")),
            P(("dp", "fsdp"), None),
            P(("dp", "fsdp")),
            P(("dp", "fsdp")),
            P(("dp", "fsdp")),
            P(("dp", "fsdp"), None),
            P(("dp", "fsdp")),
            P(("dp", "fsdp"), None),
            P(("dp", "fsdp")),
            P(("dp", "fsdp")),
            P(("dp", "fsdp")),
            P(("dp", "fsdp"), None),
            P(("dp", "fsdp")),
            P(("dp", "fsdp"), None),
            P(),
        ),
        check_vma=False,
    )
```

```python
import functools

import jax
import jax.numpy as jnp
from jax import lax
from jax.experimental import pallas as pl
from jax.experimental.pallas import tpu as pltpu
from jax.sharding import PartitionSpec as P

HEAD_DIM = 64
CLASSES = 3
MICRO = 4


def product(left_side, right_side):
    return jnp.dot(left_side, right_side, preferred_element_type=jnp.float32)


def contract_rows(left_side, right_side):
    return lax.dot_general(
        left_side, right_side, (((0,), (0,)), ((), ())), preferred_element_type=jnp.float32
    )


def times_transposed(left_side, right_side):
    return lax.dot_general(
        left_side, right_side, (((1,), (1,)), ((), ())), preferred_element_type=jnp.float32
    )


def layer_norm(values, norm_gain, norm_shift):
    average = jnp.mean(values, axis=-1, keepdims=True)
    centered = values - average
    variance = jnp.mean(centered * centered, axis=-1, keepdims=True)
    return centered * lax.rsqrt(variance + 1e-06) * norm_gain + norm_shift


def gelu_exact(values):
    return jax.nn.gelu(values, approximate=False)


def running_sum(lengths_rows):
    count = lengths_rows.shape[1]
    upper = jnp.arange(count)[:, None] <= jnp.arange(count)[None, :]
    return jnp.sum(jnp.where(upper[None], lengths_rows[:, :, None], 0), axis=1)


def segment_numbers(lengths_rows, places):
    doc_ends = running_sum(lengths_rows)
    above = (places[None, :, None] >= doc_ends[:, None, :]).astype(jnp.int32)
    return jnp.sum(above, axis=2)


def pair_heads(values):
    return values.reshape(values.shape[0], values.shape[1], 2, HEAD_DIM)


def pair_scores(query_pair, key_pair, same_doc):
    raw_scores = jnp.einsum(
        "bqhd,bkhd->bhqk", query_pair, key_pair, preferred_element_type=jnp.float32
    ) * HEAD_DIM ** (-0.5)
    return jnp.where(same_doc[:, None], raw_scores, -1000000000.0)


def lowered_masters(masters):
    return [member.astype(jnp.bfloat16) for member in masters]


def forward(tokens, lengths_rows, weights, bias_class):
    (
        w_query,
        b_query,
        w_key,
        w_value,
        b_value,
        w_out,
        b_out,
        first_gain,
        first_shift,
        w_inner,
        b_inner,
        w_outer,
        b_outer,
        second_gain,
        second_shift,
        w_pool,
        b_pool,
        w_class,
    ) = weights
    seq_count, local_len, model_width = tokens.shape
    doc_count = lengths_rows.shape[1]
    flat_rows = tokens.reshape(seq_count * local_len, model_width)
    queries = (
        (product(flat_rows, w_query) + b_query)
        .astype(jnp.bfloat16)
        .reshape(seq_count, local_len, model_width)
    )
    key_rows = (
        product(flat_rows, w_key).astype(jnp.bfloat16).reshape(seq_count, local_len, model_width)
    )
    value_rows = (
        (product(flat_rows, w_value) + b_value)
        .astype(jnp.bfloat16)
        .reshape(seq_count, local_len, model_width)
    )
    all_keys, all_values = (
        lax.all_gather(key_rows, "fsdp", axis=1, tiled=True),
        lax.all_gather(value_rows, "fsdp", axis=1, tiled=True),
    )
    full_len = all_keys.shape[1]
    own_places = lax.axis_index("fsdp") * local_len + jnp.arange(local_len, dtype=jnp.int32)
    key_places = jnp.arange(full_len, dtype=jnp.int32)
    same_doc = (
        segment_numbers(lengths_rows, own_places)[:, :, None]
        == segment_numbers(lengths_rows, key_places)[:, None, :]
    )
    pair_width = 2 * HEAD_DIM
    mixed_list = []
    log_totals = []
    for pair_index in range(model_width // pair_width):
        col_start = pair_index * pair_width
        query_pair = pair_heads(queries[:, :, col_start : col_start + pair_width])
        key_pair = pair_heads(all_keys[:, :, col_start : col_start + pair_width])
        value_pair = pair_heads(all_values[:, :, col_start : col_start + pair_width])
        scores = pair_scores(query_pair, key_pair, same_doc)
        row_peak = jnp.max(scores, axis=-1, keepdims=True)
        exp_total = jnp.sum(jnp.exp(scores - row_peak), axis=-1, keepdims=True)
        log_total = row_peak + jnp.log(exp_total)
        attn_probs = jnp.exp(scores - log_total).astype(jnp.bfloat16)
        mixed_pair = jnp.einsum(
            "bhqk,bkhd->bqhd", attn_probs, value_pair, preferred_element_type=jnp.float32
        )
        mixed_list.append(mixed_pair.reshape(seq_count, local_len, pair_width))
        log_totals.append(log_total)
    attended = (
        jnp.concatenate(mixed_list, axis=2)
        .astype(jnp.bfloat16)
        .reshape(seq_count * local_len, model_width)
    )
    branch = product(attended, w_out) + b_out
    pre_first = flat_rows.astype(jnp.float32) + branch
    normed = layer_norm(pre_first, first_gain.astype(jnp.float32), first_shift.astype(jnp.float32))
    normed_low = normed.astype(jnp.bfloat16)
    inner_pre = product(normed_low, w_inner) + b_inner
    activated = gelu_exact(inner_pre).astype(jnp.bfloat16)
    summed = normed + (product(activated, w_outer) + b_outer)
    result = layer_norm(summed, second_gain.astype(jnp.float32), second_shift.astype(jnp.float32))
    result_low = result.astype(jnp.bfloat16).reshape(seq_count, local_len, model_width)
    starts = running_sum(lengths_rows) - lengths_rows
    picker = (own_places[None, None, :] == starts[:, :, None]).astype(jnp.bfloat16)
    local_firsts = jnp.einsum(
        "bdl,blc->bdc", picker, result_low, preferred_element_type=jnp.float32
    )
    firsts = lax.psum(local_firsts, "fsdp")
    firsts_low = firsts.astype(jnp.bfloat16).reshape(seq_count * doc_count, model_width)
    pooled = jnp.tanh(product(firsts_low, w_pool) + b_pool)
    pooled_low = pooled.astype(jnp.bfloat16)
    logits = product(pooled_low, w_class) + bias_class
    stored = (
        flat_rows,
        queries,
        all_keys,
        all_values,
        same_doc,
        log_totals,
        attended,
        pre_first,
        summed,
        normed_low,
        inner_pre,
        activated,
        picker,
        firsts_low,
        pooled,
        pooled_low,
        logits,
    )
    return (result_low, logits.reshape(seq_count, doc_count, CLASSES), stored)


def backward(stored, weights, cot_rows, label_rows):
    (
        w_query,
        b_query,
        w_key,
        w_value,
        b_value,
        w_out,
        b_out,
        first_gain,
        first_shift,
        w_inner,
        b_inner,
        w_outer,
        b_outer,
        second_gain,
        second_shift,
        w_pool,
        b_pool,
        w_class,
    ) = weights
    (
        flat_rows,
        queries,
        all_keys,
        all_values,
        same_doc,
        log_totals,
        attended,
        pre_first,
        summed,
        normed_low,
        inner_pre,
        activated,
        picker,
        firsts_low,
        pooled,
        pooled_low,
        logits,
    ) = stored
    seq_count, local_len, model_width = queries.shape
    doc_count = picker.shape[1]
    owner_flag = (lax.axis_index("fsdp") == 0).astype(jnp.float32)
    row_peak = jnp.max(logits, axis=-1, keepdims=True)
    class_exp = jnp.exp(logits - row_peak)
    class_probs = class_exp / jnp.sum(class_exp, axis=-1, keepdims=True)
    onehot_labels = (
        label_rows.reshape(-1)[:, None] == jnp.arange(CLASSES, dtype=jnp.int32)[None, :]
    ).astype(jnp.float32)
    grad_logits = (class_probs - onehot_labels).astype(jnp.bfloat16)
    grad_b_class = owner_flag * jnp.sum(grad_logits.astype(jnp.float32), axis=0)
    grad_w_class = owner_flag * contract_rows(pooled_low, grad_logits)
    grad_pool_pre = (times_transposed(grad_logits, w_class) * (1.0 - pooled * pooled)).astype(
        jnp.bfloat16
    )
    grad_b_pool = owner_flag * jnp.sum(grad_pool_pre.astype(jnp.float32), axis=0)
    grad_w_pool = owner_flag * contract_rows(firsts_low, grad_pool_pre)
    grad_firsts = times_transposed(grad_pool_pre, w_pool).reshape(seq_count, doc_count, model_width)
    from_pool = jnp.einsum(
        "bdl,bdc->blc", picker.astype(jnp.float32), grad_firsts, precision=lax.Precision.HIGHEST
    )
    grad_result = cot_rows.astype(jnp.float32).reshape(-1, model_width) + from_pool.reshape(
        -1, model_width
    )
    second_back = jax.vjp(
        layer_norm, summed, second_gain.astype(jnp.float32), second_shift.astype(jnp.float32)
    )[1]
    grad_summed, grad_second_gain, grad_second_shift = second_back(grad_result)
    grad_outer = grad_summed.astype(jnp.bfloat16)
    grad_b_outer = jnp.sum(grad_outer.astype(jnp.float32), axis=0)
    grad_w_outer = contract_rows(activated, grad_outer)
    gelu_back = jax.vjp(gelu_exact, inner_pre)[1]
    grad_inner = gelu_back(times_transposed(grad_outer, w_outer))[0].astype(jnp.bfloat16)
    grad_b_inner = jnp.sum(grad_inner.astype(jnp.float32), axis=0)
    grad_w_inner = contract_rows(normed_low, grad_inner)
    grad_normed = grad_summed + times_transposed(grad_inner, w_inner)
    first_back = jax.vjp(
        layer_norm, pre_first, first_gain.astype(jnp.float32), first_shift.astype(jnp.float32)
    )[1]
    grad_pre_first, grad_first_gain, grad_first_shift = first_back(grad_normed)
    grad_branch = grad_pre_first.astype(jnp.bfloat16)
    grad_b_out = jnp.sum(grad_branch.astype(jnp.float32), axis=0)
    grad_w_out = contract_rows(attended, grad_branch)
    grad_attended = (
        times_transposed(grad_branch, w_out)
        .astype(jnp.bfloat16)
        .reshape(seq_count, local_len, model_width)
    )
    pair_width = 2 * HEAD_DIM
    query_list = []
    key_list = []
    value_list = []
    for pair_index in range(model_width // pair_width):
        col_start = pair_index * pair_width
        query_pair = pair_heads(queries[:, :, col_start : col_start + pair_width])
        key_pair = pair_heads(all_keys[:, :, col_start : col_start + pair_width])
        value_pair = pair_heads(all_values[:, :, col_start : col_start + pair_width])
        grad_pair = pair_heads(grad_attended[:, :, col_start : col_start + pair_width])
        scores = pair_scores(query_pair, key_pair, same_doc)
        attn_probs = jnp.exp(scores - log_totals[pair_index])
        grad_probs = jnp.einsum(
            "bqhd,bkhd->bhqk", grad_pair, value_pair, preferred_element_type=jnp.float32
        )
        row_dot = jnp.sum(attn_probs * grad_probs, axis=-1, keepdims=True)
        grad_scores = (attn_probs * (grad_probs - row_dot)).astype(jnp.bfloat16)
        query_part = jnp.einsum(
            "bhqk,bkhd->bqhd", grad_scores, key_pair, preferred_element_type=jnp.float32
        ) * HEAD_DIM ** (-0.5)
        query_list.append(query_part.reshape(seq_count, local_len, pair_width))
        probs_low = attn_probs.astype(jnp.bfloat16)
        key_part = jnp.einsum(
            "bhqk,bqhd->bkhd", grad_scores, query_pair, preferred_element_type=jnp.float32
        ) * HEAD_DIM ** (-0.5)
        value_part = jnp.einsum(
            "bhqk,bqhd->bkhd", probs_low, grad_pair, preferred_element_type=jnp.float32
        )
        key_list.append(key_part.reshape(seq_count, key_part.shape[1], pair_width))
        value_list.append(value_part.reshape(seq_count, value_part.shape[1], pair_width))
    key_partials = jnp.concatenate(key_list, axis=2)
    value_partials = jnp.concatenate(value_list, axis=2)
    own_keys, own_values = (
        lax.psum_scatter(
            key_partials.astype(jnp.bfloat16), "fsdp", scatter_dimension=1, tiled=True
        ).astype(jnp.float32),
        lax.psum_scatter(
            value_partials.astype(jnp.bfloat16), "fsdp", scatter_dimension=1, tiled=True
        ).astype(jnp.float32),
    )
    query_grad = jnp.concatenate(query_list, axis=2).astype(jnp.bfloat16).reshape(-1, model_width)
    key_grad = own_keys.astype(jnp.bfloat16).reshape(-1, model_width)
    value_grad = own_values.astype(jnp.bfloat16).reshape(-1, model_width)
    grad_w_query = contract_rows(flat_rows, query_grad)
    grad_b_query = jnp.sum(query_grad.astype(jnp.float32), axis=0)
    grad_w_key = contract_rows(flat_rows, key_grad)
    grad_w_value = contract_rows(flat_rows, value_grad)
    grad_b_value = jnp.sum(value_grad.astype(jnp.float32), axis=0)
    grad_tokens = (
        grad_pre_first
        + times_transposed(query_grad, w_query)
        + times_transposed(key_grad, w_key)
        + times_transposed(value_grad, w_value)
    )
    new_grads = (
        grad_w_query,
        grad_b_query,
        grad_w_key,
        grad_w_value,
        grad_b_value,
        grad_w_out,
        grad_b_out,
        grad_first_gain,
        grad_first_shift,
        grad_w_inner,
        grad_b_inner,
        grad_w_outer,
        grad_b_outer,
        grad_second_gain,
        grad_second_shift,
        grad_w_pool,
        grad_b_pool,
        grad_w_class,
    )
    return (
        new_grads,
        grad_b_class,
        grad_tokens.astype(jnp.bfloat16).reshape(seq_count, local_len, model_width),
    )


def general_body(
    inputs,
    cotangent,
    doc_lengths,
    labels,
    w_query,
    b_query,
    w_key,
    w_value,
    b_value,
    w_out,
    b_out,
    first_gain,
    first_shift,
    w_inner,
    b_inner,
    w_outer,
    b_outer,
    second_gain,
    second_shift,
    w_pool,
    b_pool,
    w_class,
    b_class,
):
    masters = (
        w_query,
        b_query,
        w_key,
        w_value,
        b_value,
        w_out,
        b_out,
        first_gain,
        first_shift,
        w_inner,
        b_inner,
        w_outer,
        b_outer,
        second_gain,
        second_shift,
        w_pool,
        b_pool,
        w_class,
    )
    group_size = lax.axis_size("dp") * lax.axis_size("fsdp")
    grad_sums = [
        jnp.zeros((member.shape[0] * group_size,) + member.shape[1:], jnp.float32)
        for member in masters
    ]
    class_sum = jnp.zeros((CLASSES,), jnp.float32)
    micro_seqs = inputs.shape[0] // MICRO
    out_list = []
    logit_list = []
    grad_list = []
    for micro_step in range(MICRO):
        first_seq = micro_step * micro_seqs
        after_seq = first_seq + micro_seqs
        tokens = inputs[first_seq:after_seq]
        lengths_rows = doc_lengths[first_seq:after_seq]
        pieces = lowered_masters(masters)
        front_weights = (
            lax.all_gather(pieces[0], ("dp", "fsdp"), axis=0, tiled=True),
            lax.all_gather(pieces[1], ("dp", "fsdp"), axis=0, tiled=True),
            lax.all_gather(pieces[2], ("dp", "fsdp"), axis=0, tiled=True),
            lax.all_gather(pieces[3], ("dp", "fsdp"), axis=0, tiled=True),
            lax.all_gather(pieces[4], ("dp", "fsdp"), axis=0, tiled=True),
            lax.all_gather(pieces[5], ("dp", "fsdp"), axis=0, tiled=True),
            lax.all_gather(pieces[6], ("dp", "fsdp"), axis=0, tiled=True),
            lax.all_gather(pieces[7], ("dp", "fsdp"), axis=0, tiled=True),
            lax.all_gather(pieces[8], ("dp", "fsdp"), axis=0, tiled=True),
            lax.all_gather(pieces[9], ("dp", "fsdp"), axis=0, tiled=True),
            lax.all_gather(pieces[10], ("dp", "fsdp"), axis=0, tiled=True),
            lax.all_gather(pieces[11], ("dp", "fsdp"), axis=0, tiled=True),
            lax.all_gather(pieces[12], ("dp", "fsdp"), axis=0, tiled=True),
            lax.all_gather(pieces[13], ("dp", "fsdp"), axis=0, tiled=True),
            lax.all_gather(pieces[14], ("dp", "fsdp"), axis=0, tiled=True),
            lax.all_gather(pieces[15], ("dp", "fsdp"), axis=0, tiled=True),
            lax.all_gather(pieces[16], ("dp", "fsdp"), axis=0, tiled=True),
            lax.all_gather(pieces[17], ("dp", "fsdp"), axis=0, tiled=True),
        )
        result_low, logits, stored = forward(tokens, lengths_rows, front_weights, b_class)
        out_list.append(result_low)
        logit_list.append(logits)
        back_weights = (
            lax.all_gather(pieces[0], ("dp", "fsdp"), axis=0, tiled=True),
            lax.all_gather(pieces[1], ("dp", "fsdp"), axis=0, tiled=True),
            lax.all_gather(pieces[2], ("dp", "fsdp"), axis=0, tiled=True),
            lax.all_gather(pieces[3], ("dp", "fsdp"), axis=0, tiled=True),
            lax.all_gather(pieces[4], ("dp", "fsdp"), axis=0, tiled=True),
            lax.all_gather(pieces[5], ("dp", "fsdp"), axis=0, tiled=True),
            lax.all_gather(pieces[6], ("dp", "fsdp"), axis=0, tiled=True),
            lax.all_gather(pieces[7], ("dp", "fsdp"), axis=0, tiled=True),
            lax.all_gather(pieces[8], ("dp", "fsdp"), axis=0, tiled=True),
            lax.all_gather(pieces[9], ("dp", "fsdp"), axis=0, tiled=True),
            lax.all_gather(pieces[10], ("dp", "fsdp"), axis=0, tiled=True),
            lax.all_gather(pieces[11], ("dp", "fsdp"), axis=0, tiled=True),
            lax.all_gather(pieces[12], ("dp", "fsdp"), axis=0, tiled=True),
            lax.all_gather(pieces[13], ("dp", "fsdp"), axis=0, tiled=True),
            lax.all_gather(pieces[14], ("dp", "fsdp"), axis=0, tiled=True),
            lax.all_gather(pieces[15], ("dp", "fsdp"), axis=0, tiled=True),
            lax.all_gather(pieces[16], ("dp", "fsdp"), axis=0, tiled=True),
            lax.all_gather(pieces[17], ("dp", "fsdp"), axis=0, tiled=True),
        )
        stored = forward(tokens, lengths_rows, back_weights, b_class)[2]
        new_grads, class_grad, grad_tokens = backward(
            stored, back_weights, cotangent[first_seq:after_seq], labels[first_seq:after_seq]
        )
        grad_sums = [running + fresh_grad for running, fresh_grad in zip(grad_sums, new_grads)]
        class_sum = class_sum + class_grad
        grad_list.append(grad_tokens)
    owned = (
        lax.psum_scatter(grad_sums[0], ("dp", "fsdp"), scatter_dimension=0, tiled=True),
        lax.psum_scatter(grad_sums[1], ("dp", "fsdp"), scatter_dimension=0, tiled=True),
        lax.psum_scatter(grad_sums[2], ("dp", "fsdp"), scatter_dimension=0, tiled=True),
        lax.psum_scatter(grad_sums[3], ("dp", "fsdp"), scatter_dimension=0, tiled=True),
        lax.psum_scatter(grad_sums[4], ("dp", "fsdp"), scatter_dimension=0, tiled=True),
        lax.psum_scatter(grad_sums[5], ("dp", "fsdp"), scatter_dimension=0, tiled=True),
        lax.psum_scatter(grad_sums[6], ("dp", "fsdp"), scatter_dimension=0, tiled=True),
        lax.psum_scatter(grad_sums[7], ("dp", "fsdp"), scatter_dimension=0, tiled=True),
        lax.psum_scatter(grad_sums[8], ("dp", "fsdp"), scatter_dimension=0, tiled=True),
        lax.psum_scatter(grad_sums[9], ("dp", "fsdp"), scatter_dimension=0, tiled=True),
        lax.psum_scatter(grad_sums[10], ("dp", "fsdp"), scatter_dimension=0, tiled=True),
        lax.psum_scatter(grad_sums[11], ("dp", "fsdp"), scatter_dimension=0, tiled=True),
        lax.psum_scatter(grad_sums[12], ("dp", "fsdp"), scatter_dimension=0, tiled=True),
        lax.psum_scatter(grad_sums[13], ("dp", "fsdp"), scatter_dimension=0, tiled=True),
        lax.psum_scatter(grad_sums[14], ("dp", "fsdp"), scatter_dimension=0, tiled=True),
        lax.psum_scatter(grad_sums[15], ("dp", "fsdp"), scatter_dimension=0, tiled=True),
        lax.psum_scatter(grad_sums[16], ("dp", "fsdp"), scatter_dimension=0, tiled=True),
        lax.psum_scatter(grad_sums[17], ("dp", "fsdp"), scatter_dimension=0, tiled=True),
    )
    class_total = lax.psum(class_sum, ("dp", "fsdp"))
    return (
        jnp.concatenate(out_list, axis=0),
        jnp.concatenate(logit_list, axis=0),
        jnp.concatenate(grad_list, axis=0),
        owned[0],
        owned[1],
        owned[2],
        owned[3],
        owned[4],
        owned[5],
        owned[6],
        owned[7],
        owned[8],
        owned[9],
        owned[10],
        owned[11],
        owned[12],
        owned[13],
        owned[14],
        owned[15],
        owned[16],
        owned[17],
        class_total,
    )


BF = jnp.bfloat16
F32 = jnp.float32
MESH = pl.DeviceIdType.MESH
ANY = pl.BlockSpec(memory_space=pl.ANY)
SMEM = pl.BlockSpec(memory_space=pltpu.SMEM)
ZS = 4
CLASS_ROWS, B_QUERY, B_VALUE, B_OUT, GAIN1, SHIFT1, B_OUTER, GAIN2, SHIFT2, B_POOL = (0, 3, 4, 5, 6, 7, 8, 9, 10, 11)
VEC_ROWS = 16
KB, K0, K1, KF, KS, KZ, KE, KT = range(8)


def nn(a, b):
    return lax.dot_general(a, b, (((1,), (0,)), ((), ())), preferred_element_type=F32)


def nt(a, b):
    return lax.dot_general(a, b, (((1,), (1,)), ((), ())), preferred_element_type=F32)


def tn(a, b):
    return lax.dot_general(a, b, (((0,), (0,)), ((), ())), preferred_element_type=F32)


def my_place():
    dp, fs = lax.axis_index("dp"), lax.axis_index("fsdp")
    return dp // 2, lax.rem(dp, 2), fs // 2, lax.rem(fs, 2)


def device_at(z, y, x, c):
    return (z * 2 + y, x * 2 + c)


def meet(partners):
    barrier = pltpu.get_barrier_semaphore()
    for partner in partners:
        pl.semaphore_signal(barrier, inc=1, device_id=partner, device_id_type=MESH)
    pl.semaphore_wait(barrier, len(partners))


def all_partners(z, y, x, c):
    found = [device_at(lax.rem(z + k, ZS), y, x, c) for k in range(1, ZS)]
    found.append(device_at(z, 1 - y, x, c))
    found.append(device_at(z, y, 1 - x, c))
    found.append(device_at(z, y, x, 1 - c))
    found.append(device_at(z, y, 1 - x, 1 - c))
    return found


def group_partner(k, x, c):
    return (1 - x if k >= 2 else x, 1 - c if k % 2 == 1 else c)


def doc_ends(lens_ref):
    ends = []
    total = 0
    for d in range(lens_ref.shape[1]):
        total = total + lens_ref[lax.axis_index("fsdp"), d]
        ends.append(total)
    return ends


def doc_starts(lens_ref):
    return [0] + doc_ends(lens_ref)[:-1]


def doc_numbers(places, ends):
    number = jnp.zeros(places.shape, jnp.int32)
    for end in ends:
        number = number + (places >= end).astype(jnp.int32)
    return number


def gather_tools(plan, orders, view, own_block, keep_sem, send_sem, recv_sem, other=None):
    z, y, x, c = my_place()
    everything = slice(None)

    def along(a, axis):
        return device_at(z, 1 - y, x, c) if orders[a][axis] == "y" else device_at(z, y, 1 - x, c)

    def copy_of(a, number):
        core = device_at(z, y, x, 1 - c)
        first_other = (1 - y, x) if orders[a][0] == "y" else (y, 1 - x)
        if number < 3:
            source, target = own_block(a), view(a, (z, y, x, c))
            device = device_at(lax.rem(z + number + 1, ZS), y, x, c)
        elif number < 6:
            source = target = view(a, (everything, y, x, c))
            device = (along(a, 0), along(a, 1), core)[number - 3]
        elif number < 8:
            source = target = view(a, (everything, first_other[0], first_other[1], c))
            device = along(a, 1) if number == 6 else core
        else:
            if orders[a][1] == "y":
                source = target = view(a, (everything, 1 - y, everything, c))
            else:
                source = target = view(a, (everything, everything, 1 - x, c))
            device = core
        return pltpu.make_async_remote_copy(
            src_ref=source,
            dst_ref=target,
            send_sem=send_sem.at[a, number],
            recv_sem=recv_sem.at[a, number],
            device_id=device,
            device_id_type=MESH,
        )

    def keep(a):
        return pltpu.make_async_copy(own_block(a), view(a, (z, y, x, c)), keep_sem.at[a])

    def take_up(point):
        for kind, a in plan.get(point, ()):
            if kind == KB:
                for number in (1, 0, 2):
                    copy_of(a, number).start()
                keep(a).start()
            elif kind == KZ:
                for number in (0, 1, 2):
                    copy_of(a, number).wait_recv()
                keep(a).wait()
                for number in (3, 4, 5):
                    copy_of(a, number).start()
            elif kind == KF:
                copy_of(a, 3).wait_recv()
                for number in (6, 7):
                    copy_of(a, number).start()
            elif kind == KS:
                copy_of(a, 4).wait_recv()
                copy_of(a, 6).wait_recv()
                copy_of(a, 8).start()
            elif kind == KT:
                other(a)
            else:
                for number in (5, 7, 8):
                    copy_of(a, number).wait_recv()

    def all_sent():
        for a in range(len(orders)):
            for number in range(9):
                copy_of(a, number).wait_send()

    return take_up, all_sent


GATHER_PIECES = ((1, 0, 1, "rows"), (0, 0, 2, "columns"), (0, 1, 2, "columns"), (2, 0, 2, "rows"), (2, 1, 2, "rows"))
GATHER_ORDERS = ("xy", "xy", "yx", "xy", "yx", "xy", "yx", "xy")
GATHER_PLAN = {
    -1: (
        (KB, 0), (KT, 0), (KZ, 0), (KB, 1), (KB, 2), (KT, 1), (KB, 3), (KB, 4), (KB, 5), (KF, 0), (KT, 2), (KS, 0), (KB, 6), (KZ, 1),
        (KT, 3), (KZ, 2), (KZ, 3), (KE, 0),
    ),
    0: ((KB, 7),),
    1: ((KF, 1), (KF, 2), (KF, 3), (KZ, 4)),
    3: ((KS, 1), (KS, 2), (KZ, 5), (KS, 3), (KE, 1)),
    4: ((KZ, 6), (KE, 2), (KE, 3), (KF, 4)),
    5: ((KF, 5),),
    7: ((KZ, 7),),
    8: ((KS, 4), (KF, 6)),
    9: ((KS, 5), (KE, 4), (KF, 7), (KE, 5)),
    10: ((KS, 6),),
    11: ((KS, 7), (KE, 6)),
    12: ((KE, 7),),
}
DENSE_ARRAYS = 3
VECTORS = 9


def part_of(piece, block):
    _, which, count, along = piece
    rows, columns = block
    if along == "rows":
        return (which * (rows // count), rows // count), (0, columns)
    return (0, rows), (which * (columns // count), columns // count)


def key_marks(length, ends):
    number = doc_numbers(lax.broadcasted_iota(jnp.int32, (length, 1), 0), ends)
    lane = lax.broadcasted_iota(jnp.int32, (length, 128), 1)
    return jnp.where(lane == number, 1.0, 0.0).astype(BF)


def query_marks(at, count, ends):
    number = doc_numbers(lax.broadcasted_iota(jnp.int32, (count, 1), 0) + at, ends)
    lane = lax.broadcasted_iota(jnp.int32, (count, 128), 1)
    return jnp.where(lane == number, 0.0, -1000000000.0).astype(BF)


def attend_kernel(groups, *refs):
    lens_ref, tokens_ref, class_ref = refs[:3]
    vectors, b_inner_ref, (wq_ref, wk_ref, wv_ref) = refs[3 : 3 + VECTORS], refs[3 + VECTORS], refs[4 + VECTORS : 7 + VECTORS]
    refs = refs[7 + VECTORS :]
    shards, refs = refs[:DENSE_ARRAYS], refs[DENSE_ARRAYS:]
    q_ref, k_ref, v_ref, att_ref, lse_ref, w_ref, vec_ref, rows_ref = refs[:8]
    wholes = refs[8 : 8 + DENSE_ARRAYS]
    refs = refs[8 + DENSE_ARRAYS :]
    x_ref, vt_ref, marked_ref, qkv_shard, qkv_ref, tab_ref, tab_in_ref = refs[:7]
    local_sem, row_send, row_recv, tab_send, tab_recv, send_sem, recv_sem = refs[7:14]
    own = refs[14 : 14 + DENSE_ARRAYS]
    length, width = q_ref.shape
    chunk = 256
    points = length // chunk
    heads = width // HEAD_DIM
    items = groups + len(GATHER_PIECES)
    group = pl.program_id(0)
    z, y, x, c = my_place()
    mine = x * 2 + c

    def row_copy(k):
        px, pc = group_partner(k, x, c)
        return pltpu.make_async_remote_copy(
            src_ref=tokens_ref.at[px * 2 + pc],
            dst_ref=x_ref.at[mine],
            send_sem=row_send.at[k - 1],
            recv_sem=row_recv.at[k - 1],
            device_id=device_at(z, y, px, pc),
            device_id_type=MESH,
        )

    def row_own():
        return pltpu.make_async_copy(tokens_ref.at[mine], x_ref.at[mine], local_sem.at[0])

    def rows_out():
        return pltpu.make_async_copy(x_ref, rows_ref, local_sem.at[1])

    def table_copy(level):
        if level < 3:
            source, device = tab_ref.at[0], device_at(lax.rem(z + level + 1, ZS), y, x, c)
        else:
            source = tab_ref.at[level - 2]
            device = (device_at(z, y, 1 - x, c), device_at(z, 1 - y, x, c), device_at(z, y, x, 1 - c))[level - 3]
        return pltpu.make_async_remote_copy(
            src_ref=source,
            dst_ref=tab_in_ref.at[level],
            send_sem=tab_send.at[level],
            recv_sem=tab_recv.at[level],
            device_id=device,
            device_id_type=MESH,
        )

    def array_of(a):
        if a < groups:
            return qkv_ref.at[a], qkv_shard.at[a], None
        piece = GATHER_PIECES[a - groups]
        return wholes[piece[0]], own[piece[0]], part_of(piece, own[piece[0]].shape)

    def view(a, where):
        ref, _, part = array_of(a)
        if part is None:
            return ref.at[where]
        (r0, rows), (c0, columns) = part
        return ref.at[where + (pl.ds(r0, rows), pl.ds(c0, columns))]

    def own_block(a):
        _, ref, part = array_of(a)
        if part is None:
            return ref
        (r0, rows), (c0, columns) = part
        return ref.at[pl.ds(r0, rows), pl.ds(c0, columns)]

    def table_level(level):
        if level == 0:
            for k in (0, 1, 2):
                table_copy(k).wait_recv()
            tab_ref[1] = (tab_ref[0] + tab_in_ref[0]) + (tab_in_ref[1] + tab_in_ref[2])
        else:
            table_copy(level + 2).wait_recv()
            tab_ref[level + 1] = tab_ref[level] + tab_in_ref[level + 2]
        if level < 3:
            table_copy(level + 3).start()
        else:
            vec_ref[...] = tab_ref[4]

    take_up, all_sent = gather_tools(
        GATHER_PLAN, GATHER_ORDERS, view, own_block, local_sem.at[pl.ds(2, items)], send_sem, recv_sem, table_level
    )

    @pl.when(group == 0)
    def _():
        device = ((z * 2 + y) * 2 + x) * 2 + c
        full = tab_ref.shape[2]

        def spread(values, at):
            n = values.shape[1]
            here = lax.broadcasted_iota(jnp.int32, (n, full), 1) - at == lax.broadcasted_iota(jnp.int32, (n, full), 0)
            return nn(values.astype(BF), jnp.where(here, 1.0, 0.0).astype(BF))

        share = class_ref.shape[1]
        tab_ref[0, 0:CLASSES] = spread(class_ref[...], device * share)
        for j, ref in enumerate(vectors):
            tab_ref[0, CLASSES + j : CLASSES + j + 1] = spread(ref[...], device * share)
        per_row = full // b_inner_ref.shape[1]
        inner_bias = spread(b_inner_ref[...], lax.rem(device, per_row) * b_inner_ref.shape[1])
        for j in range(4):
            tab_ref[0, 12 + j : 13 + j] = jnp.where(device // per_row == j, inner_bias, 0.0)
        for g in range(groups):
            for j, ref in enumerate((wq_ref, wk_ref, wv_ref)):
                qkv_shard[g, :, j * width : (j + 1) * width] = ref[:, g * width : (g + 1) * width].astype(BF)
        for target, ref in zip(own, shards):
            target[...] = ref[...].astype(BF)
        meet(all_partners(z, y, x, c))
        for level in (1, 0, 2):
            table_copy(level).start()
        for k in (3, 2, 1):
            row_copy(k).start()
        row_own().start()
        take_up(-1)
        row_own().wait()
        for k in (1, 2, 3):
            row_copy(k).wait_recv()
        rows_out().start()

    tokens = x_ref[...].reshape(length, x_ref.shape[2])
    weights = qkv_ref[group].astype(F32).reshape(x_ref.shape[2], 3 * width).astype(BF)
    w_ref[...] = weights
    bias = tab_ref[4, B_QUERY : B_QUERY + 2, pl.ds(pl.multiple_of(group * width, width), width)]
    q_ref[...] = (nn(tokens, weights[:, :width]) + bias[0:1]).astype(BF)
    keys = nn(tokens, weights[:, width : 2 * width]).astype(BF)
    k_ref[...] = keys
    values = (nn(tokens, weights[:, 2 * width :]) + bias[1:2]).astype(BF)
    v_ref[...] = values
    vt_ref[...] = values.astype(F32).T.astype(BF)
    ends = doc_ends(lens_ref)
    marks = key_marks(length, ends)
    for pair in range(width // 128):
        marked_ref[pair] = jnp.concatenate([keys[:, pair * 128 : (pair + 1) * 128], marks], axis=1)
    lane_half = lax.broadcasted_iota(jnp.int32, (1, 128), 1) // HEAD_DIM

    def step(i, carry):
        for point in range(groups * points):
            if point in GATHER_PLAN:

                @pl.when((group == point // points) & (i == point % points))
                def _(point=point):
                    take_up(point)

        at = pl.multiple_of(i * chunk, chunk)
        ours = query_marks(at, chunk, ends)
        scaled = q_ref[pl.ds(at, chunk), :] * jnp.asarray(0.125, BF)
        mixed = []
        for h in range(heads):
            two = scaled[:, h // 2 * 128 : (h // 2 + 1) * 128]
            own_q = jnp.concatenate([jnp.where(lane_half == h % 2, two, jnp.zeros_like(two)), ours], axis=1)
            blocks = [nt(marked_ref[h // 2, s : s + chunk, :], own_q) for s in range(0, length, chunk)]
            peak = functools.reduce(jnp.maximum, [jnp.max(b, axis=0, keepdims=True) for b in blocks])
            exps = [jnp.exp(b - peak) for b in blocks]
            total = functools.reduce(jnp.add, [jnp.sum(e, axis=0, keepdims=True) for e in exps])
            scale = 1.0 / total
            probs = jnp.concatenate([(e * scale).astype(BF) for e in exps], axis=0)
            mixed.append(nn(vt_ref[h * HEAD_DIM : (h + 1) * HEAD_DIM, :], probs))
            lse_ref[0, h : h + 1, pl.ds(at, chunk)] = peak + jnp.log(total)
        att_ref[pl.ds(at, chunk), :] = jnp.concatenate(mixed, axis=0).T.astype(BF)
        return carry

    lax.fori_loop(0, points, step, 0)

    @pl.when(group == groups - 1)
    def _():
        take_up(groups * points)
        all_sent()
        for level in range(6):
            table_copy(level).wait_send()
        for k in range(1, 4):
            row_copy(k).wait_send()
        rows_out().wait()


def attend(lens, tokens, class_shard, vectors, b_inner, qkv_shards, shards):
    seqs, local_len, width = tokens.shape
    length = seqs * local_len
    group = 256
    groups = width // group
    share = qkv_shards[0].shape[0]
    hbm = pl.BlockSpec(memory_space=pl.ANY)
    part = pl.BlockSpec((length, group), lambda g: (0, g))
    once = pl.Buffered(buffer_count=1)
    items = groups + len(GATHER_PIECES)

    def fixed(shape):
        return pl.BlockSpec(shape, lambda g: (0,) * len(shape), pipeline_mode=once)

    lead = (ZS, 2, 2, 2)
    return pl.pallas_call(
        functools.partial(attend_kernel, groups),
        grid=(groups,),
        out_shape=[jax.ShapeDtypeStruct((length, width), BF)] * 4
        + [
            jax.ShapeDtypeStruct((groups, 8, length), F32),
            jax.ShapeDtypeStruct((width, 3 * width), BF),
            jax.ShapeDtypeStruct((VEC_ROWS, width), F32),
            jax.ShapeDtypeStruct(tokens.shape, BF),
        ]
        + [jax.ShapeDtypeStruct(lead + s.shape, BF) for s in shards],
        in_specs=[SMEM, hbm, fixed(class_shard.shape)]
        + [fixed(v.shape) for v in vectors]
        + [fixed(b_inner.shape)]
        + [fixed(s.shape) for s in qkv_shards]
        + [fixed(s.shape) for s in shards],
        out_specs=[part] * 4
        + [
            pl.BlockSpec((1, 8, length), lambda g: (g, 0, 0)),
            pl.BlockSpec((width, 3 * group), lambda g: (0, g)),
            pl.BlockSpec((VEC_ROWS, width), lambda g: (0, 0)),
            hbm,
        ]
        + [hbm] * DENSE_ARRAYS,
        scratch_shapes=[
            pltpu.VMEM(tokens.shape, BF),
            pltpu.VMEM((group, length), BF),
            pltpu.VMEM((group // 128, length, 256), BF),
            pltpu.VMEM((groups, share, 3 * group), BF),
            pltpu.VMEM((groups,) + lead + (share, 3 * group), BF),
            pltpu.VMEM((5, VEC_ROWS, width), F32),
            pltpu.VMEM((6, VEC_ROWS, width), F32),
            pltpu.SemaphoreType.DMA((2 + items,)),
            pltpu.SemaphoreType.DMA((3,)),
            pltpu.SemaphoreType.DMA((3,)),
            pltpu.SemaphoreType.DMA((6,)),
            pltpu.SemaphoreType.DMA((6,)),
            pltpu.SemaphoreType.DMA((items, 9)),
            pltpu.SemaphoreType.DMA((items, 9)),
        ]
        + [pltpu.VMEM(s.shape, BF) for s in shards],
        compiler_params=pltpu.CompilerParams(
            collective_id=1, has_side_effects=True, vmem_limit_bytes=60 * 2**20
        ),
        name="attend",
    )(lens, tokens, class_shard, *vectors, b_inner, *qkv_shards, *shards)


DENSE = 4
DENSE_ITEMS = (
    (0, 0, 2, "columns", "yx"), (1, 0, 2, "rows", "xy"), (0, 1, 2, "columns", "yx"), (1, 1, 2, "rows", "xy"),
    (2, 0, 1, "rows", "yx"), (3, 0, 1, "rows", "yx"),
)
GROUP_ORDERS = ("yx", "xy", "yx")
SCATTER_PLAN = {
    -1: ((KB, 0),),
    0: ((KB, 1),),
    1: ((K0, 0), (K0, 1), (KB, 2), (K1, 0), (KB, 3), (K1, 1)),
    2: ((KB, 4),),
    3: ((K0, 2), (K0, 3), (KB, 5), (K1, 2), (K1, 3)),
    4: ((KF, 0), (KF, 1), (KB, 6)),
    6: ((K0, 4), (K1, 4)),
    8: ((KF, 2), (KF, 3), (KS, 0), (KS, 1), (K0, 5), (KB, 7), (K1, 5)),
    9: ((KF, 4), (K0, 7), (K1, 7)),
    10: ((K0, 6), (K1, 6)),
    11: ((KS, 2),),
    12: (
        (KS, 4), (KT, 0), (KF, 7), (KS, 3), (KZ, 0), (KZ, 1), (KF, 5), (K0, 8), (K1, 8), (KT, 1), (KF, 6), (KZ, 2), (KS, 7), (KZ, 4),
        (KS, 5), (KF, 8), (KT, 2), (KS, 6), (KZ, 3), (KZ, 7), (KZ, 5), (KS, 8), (KZ, 6), (KT, 3), (KZ, 8),
    ),
}
PIECES = len(DENSE_ITEMS)


def order_of(a):
    return DENSE_ITEMS[a][4] if a < PIECES else GROUP_ORDERS[a - PIECES]


def cut_of(a, block):
    _, which, count, along, _ = DENSE_ITEMS[a]
    rows, columns = block
    if along == "rows":
        return (which * (rows // count), rows // count), (0, columns)
    return (0, rows), (which * (columns // count), columns // count)


TABLE_ROWS = 24


def attend_back_kernel(groups, *refs):
    items = PIECES + groups
    lens_ref, x_ref, w_ref, q_ref, k_ref, v_ref, att_ref, datt_ref, lse_ref, start_ref = refs[:10]
    small_a_ref, small_b_ref, bi_ref, logit_ref = refs[10:14]
    parts = refs[14 : 14 + DENSE]
    back_ref, logits_ref, small_ref = refs[18:21]
    dense_outs, group_outs = refs[21 : 21 + DENSE], refs[21 + DENSE : 24 + DENSE]
    rest = refs[24 + DENSE :]
    xt_ref, kt_ref, marked_ref, dot_ref, dq_ref, dk_ref, dv_ref, acc_ref, dx_ref, bias_ref, dw_ref, tab_ref, tab_in_ref = rest[:13]
    local_sem, row_send, row_recv, tab_send, tab_recv, send_sem, recv_sem = rest[13:20]
    rest = rest[20:]
    keeps, rest = rest[:PIECES], rest[PIECES:]
    firsts, seconds, thirds, fourths = (rest[j * items : (j + 1) * items] for j in range(4))

    length, width = q_ref.shape
    chunk = 256
    points = length // chunk
    heads = width // HEAD_DIM
    group = pl.program_id(0)
    z, y, x, c = my_place()
    mine = x * 2 + c

    def axes(a):
        return (y, x) if order_of(a)[0] == "y" else (x, y)

    def device_along(axis):
        return device_at(z, 1 - y, x, c) if axis == "y" else device_at(z, y, 1 - x, c)

    def half(a, ref, place):
        return ref.at[:, place] if order_of(a)[0] == "y" else ref.at[:, :, place]

    def whole_of(a, core):
        if a >= PIECES:
            return dw_ref.at[a - PIECES].at[:, :, :, core]
        array = DENSE_ITEMS[a][0]
        (r0, rows), (c0, columns) = cut_of(a, parts[array].shape[-2:])
        return parts[array].at[:, :, :, core, pl.ds(r0, rows), pl.ds(c0, columns)]

    def kept(a):
        return keeps[a] if a < PIECES else whole_of(a, c)

    def load(a, turn):
        place = 1 - axes(a)[0] if turn == 0 else axes(a)[0]
        return pltpu.make_async_copy(
            half(a, whole_of(a, c), place), half(a, keeps[a], place), local_sem.at[a, turn]
        )

    def copy_of(a, number):
        at, other = axes(a)
        if number < 2:
            place = 1 - at if number == 0 else at
            source, target = half(a, whole_of(a, 1 - c), place), half(a, firsts[a], place)
            device = device_at(z, y, x, 1 - c)
        elif number == 2:
            source, target = half(a, kept(a), 1 - at), seconds[a]
            device = device_along(order_of(a)[0])
        elif number == 3:
            source, target = half(a, kept(a), at).at[:, 1 - other], thirds[a]
            device = device_along(order_of(a)[1])
        else:
            there = lax.rem(z + number - 3, ZS)
            source, target = half(a, kept(a), at).at[:, other].at[there], fourths[a].at[number - 4]
            device = device_at(there, y, x, c)
        return pltpu.make_async_remote_copy(
            src_ref=source,
            dst_ref=target,
            send_sem=send_sem.at[a, number],
            recv_sem=recv_sem.at[a, number],
            device_id=device,
            device_id_type=MESH,
        )

    def add_into(target, source):
        lead = target.shape[:-2]
        total = functools.reduce(lambda p, q: p * q, lead, 1)

        def step(i, carry):
            where = []
            for size in reversed(lead):
                where.append(lax.rem(i, size))
                i = i // size
            where = tuple(reversed(where))
            target[where] = target[where] + source[where]
            return carry

        lax.fori_loop(0, total, step, 0)

    def begin(a):
        if a < PIECES:
            load(a, 0).start()
            load(a, 1).start()
        copy_of(a, 0).start()
        copy_of(a, 1).start()

    def after_core(a, turn):
        place = 1 - axes(a)[0] if turn == 0 else axes(a)[0]
        if a < PIECES:
            load(a, turn).wait()
        copy_of(a, turn).wait_recv()
        add_into(half(a, kept(a), place), half(a, firsts[a], place))
        if turn == 0:
            copy_of(a, 2).start()

    def after_first(a):
        at, other = axes(a)
        ours = half(a, kept(a), at)
        copy_of(a, 2).wait_recv()
        add_into(ours.at[:, 1 - other], seconds[a].at[:, 1 - other])
        copy_of(a, 3).start()
        add_into(ours.at[:, other], seconds[a].at[:, other])

    def after_second(a):
        at, other = axes(a)
        copy_of(a, 3).wait_recv()
        add_into(half(a, kept(a), at).at[:, other], thirds[a])
        for number in (5, 4, 6):
            copy_of(a, number).start()

    def finish(a):
        at, other = axes(a)
        for number in (4, 5, 6):
            copy_of(a, number).wait_recv()
        ours = half(a, kept(a), at).at[:, other]
        total = (
            ours[z].astype(F32)
            + fourths[a][0].astype(F32)
            + fourths[a][1].astype(F32)
            + fourths[a][2].astype(F32)
        )
        if a < PIECES:
            out = dense_outs[DENSE_ITEMS[a][0]]
            (r0, rows), (c0, columns) = cut_of(a, out.shape)
            out[r0 : r0 + rows, c0 : c0 + columns] = total
        else:
            s = (a - PIECES) * width
            for j, out in enumerate(group_outs):
                out[:, s : s + width] = total[:, j * width : (j + 1) * width]

    def row_copy(which, k):
        px, pc = group_partner(k, x, c)
        if which == 0:
            source, target = dx_ref.at[px * 2 + pc], back_ref.at[mine]
        else:
            source, target = logit_ref, logits_ref.at[mine]
        return pltpu.make_async_remote_copy(
            src_ref=source,
            dst_ref=target,
            send_sem=row_send.at[which, k - 1],
            recv_sem=row_recv.at[which, k - 1],
            device_id=device_at(z, y, px, pc),
            device_id_type=MESH,
        )

    def row_own(which):
        if which == 0:
            source, target = dx_ref.at[mine], back_ref.at[mine]
        else:
            source, target = logit_ref, logits_ref.at[mine]
        return pltpu.make_async_copy(source, target, local_sem.at[PIECES, which])

    def table_copy(level):
        if level < 3:
            source, target = tab_ref.at[level], tab_in_ref.at[level]
            device = (
                device_at(z, y, x, 1 - c), device_at(z, 1 - y, x, c), device_at(z, y, 1 - x, c)
            )[level]
        else:
            source, target = tab_ref.at[3], tab_in_ref.at[3 + z]
            device = device_at(lax.rem(z + level - 2, ZS), y, x, c)
        return pltpu.make_async_remote_copy(
            src_ref=source,
            dst_ref=target,
            send_sem=tab_send.at[level],
            recv_sem=tab_recv.at[level],
            device_id=device,
            device_id_type=MESH,
        )

    def table_wait(level):
        if level < 3:
            table_copy(level).wait_recv()
        else:
            slot = tab_in_ref.at[3 + lax.rem(z + ZS - (level - 2), ZS)]
            pltpu.make_async_remote_copy(
                src_ref=slot,
                dst_ref=slot,
                send_sem=tab_send.at[level],
                recv_sem=tab_recv.at[level],
                device_id=device_at(lax.rem(z + level - 2, ZS), y, x, c),
                device_id_type=MESH,
            ).wait_recv()

    def table_level(level):
        if level == 3:
            for last in (3, 4, 5):
                table_wait(last)
            table = (tab_in_ref[3] + tab_in_ref[4]) + (tab_in_ref[5] + tab_in_ref[6])
            device = ((z * 2 + y) * 2 + x) * 2 + c
            full = table.shape[1]
            row = lax.broadcasted_iota(jnp.int32, (full, 128), 0)
            lane = lax.broadcasted_iota(jnp.int32, (full, 128), 1)

            def own_lanes(values, size, at):
                chosen = jnp.where((row == at + lane) & (lane < size), 1.0, 0.0)
                return lax.dot_general(
                    values, chosen, (((1,), (0,)), ((), ())), preferred_element_type=F32, precision=lax.Precision.HIGHEST
                )

            per_row = full * 4 // (8 * ZS)
            small_ref[0:TABLE_ROWS] = own_lanes(table, full // (8 * ZS), device * (full // (8 * ZS)))
            inner_bias = own_lanes(table, per_row, lax.rem(device, full // per_row) * per_row)
            for j in range(4):

                @pl.when(device // (full // per_row) == j)
                def _(j=j):
                    small_ref[TABLE_ROWS : TABLE_ROWS + 1] = inner_bias[12 + j : 13 + j]

            small_ref[TABLE_ROWS + 1 : TABLE_ROWS + 2] = table[16:17, 0:128]
            return
        table_wait(level)
        tab_ref[level + 1] = tab_ref[level] + tab_in_ref[level]
        if level < 2:
            table_copy(level + 1).start()
        else:
            tab_in_ref[3 + z] = tab_ref[3]
            for nxt in (4, 3, 5):
                table_copy(nxt).start()

    def take_up(point):
        for kind, a in SCATTER_PLAN.get(point, ()):
            if kind == KB:
                begin(a)
            elif kind == K0 or kind == K1:
                after_core(a, 0 if kind == K0 else 1)
            elif kind == KF:
                after_first(a)
            elif kind == KS:
                after_second(a)
            elif kind == KZ:
                finish(a)
            else:
                table_level(a)

    @pl.when(group == 0)
    def _():
        meet(all_partners(z, y, x, c))
        take_up(-1)
        for k in range(1, 4):
            row_copy(1, k).start()
        row_own(1).start()
        xt_ref[...] = x_ref[...].astype(F32).T.astype(BF)
        acc_ref[...] = start_ref[...]

    kt_ref[...] = k_ref[...].astype(F32).T.astype(BF)
    dot_ref[...] = (datt_ref[...].astype(F32) * att_ref[...].astype(F32)).T
    dk_ref[...] = jnp.zeros_like(dk_ref)
    dv_ref[...] = jnp.zeros_like(dv_ref)
    ends = doc_ends(lens_ref)
    marks = key_marks(length, ends)
    for pair in range(width // 128):
        marked_ref[pair] = jnp.concatenate([k_ref[:, pair * 128 : (pair + 1) * 128], marks], axis=1)
    lane_half = lax.broadcasted_iota(jnp.int32, (1, 128), 1) // HEAD_DIM
    lane_head = lax.broadcasted_iota(jnp.int32, (1, width), 1) // HEAD_DIM

    def step(i, carry):
        for point in range(groups * points):

            @pl.when((group == point // points) & (i == point % points))
            def _(point=point):
                take_up(point)

        at = pl.multiple_of(i * chunk, chunk)
        ours = query_marks(at, chunk, ends)
        scaled = q_ref[pl.ds(at, chunk), :] * jnp.asarray(0.125, BF)
        given = datt_ref[pl.ds(at, chunk), :]
        own_q = [jnp.where(lane_head == h, scaled, jnp.zeros_like(scaled)) for h in range(heads)]
        own_d = [jnp.where(lane_head == h, given, jnp.zeros_like(given)) for h in range(heads)]
        all_probs = [[] for _ in range(length // chunk)]
        all_grads = [[] for _ in range(length // chunk)]
        for h in range(heads):
            lse = lse_ref[0, h : h + 1, pl.ds(at, chunk)]
            dots = jnp.sum(
                dot_ref[h * HEAD_DIM : (h + 1) * HEAD_DIM, pl.ds(at, chunk)], axis=0, keepdims=True
            )
            two = scaled[:, h // 2 * 128 : (h // 2 + 1) * 128]
            marked_q = jnp.concatenate([jnp.where(lane_half == h % 2, two, jnp.zeros_like(two)), ours], axis=1)
            for j in range(length // chunk):
                s = j * chunk
                scores = nt(marked_ref[h // 2, s : s + chunk, :], marked_q)
                probs = jnp.exp(scores - lse)
                grad_probs = nt(v_ref[s : s + chunk, :], own_d[h])
                all_grads[j].append((probs * (grad_probs - dots)).astype(BF))
                all_probs[j].append(probs.astype(BF))
        stacked_q = jnp.concatenate(own_q, axis=0)
        stacked_d = jnp.concatenate(own_d, axis=0)
        for j in range(length // chunk):
            s = j * chunk
            dk_ref[s : s + chunk, :] += nn(jnp.concatenate(all_grads[j], axis=1), stacked_q)
            dv_ref[s : s + chunk, :] += nn(jnp.concatenate(all_probs[j], axis=1), stacked_d)
        mixed = []
        for h in range(heads):
            column = jnp.concatenate([all_grads[j][h] for j in range(length // chunk)], axis=0)
            mixed.append(nn(kt_ref[h * HEAD_DIM : (h + 1) * HEAD_DIM, :], column))
        dq_ref[pl.ds(at, chunk), :] = (jnp.concatenate(mixed, axis=0).T * 0.125).astype(BF)
        return carry

    lax.fori_loop(0, points, step, 0)
    xt = xt_ref[...]
    grads = (dq_ref[...], dk_ref[...].astype(BF), dv_ref[...].astype(BF))
    block = dw_ref.shape[1:6]
    for j, grad in enumerate(grads):
        dw_ref[group, :, :, :, :, :, j * width : (j + 1) * width] = nn(xt, grad).reshape(block + (width,)).astype(BF)
    bias_ref[group, 0:1, :] = jnp.sum(grads[0].astype(F32), axis=0, keepdims=True)
    bias_ref[group, 1:2, :] = jnp.sum(grads[2].astype(F32), axis=0, keepdims=True)

    @pl.when(group < groups - 1)
    def _():
        total = acc_ref[...]
        for j, grad in enumerate(grads):
            total = total + nt(grad, w_ref[:, j * width : (j + 1) * width])
        acc_ref[...] = total

    @pl.when(group == groups - 1)
    def _():
        begin(items - 1)
        size = dx_ref.shape[1]
        for k in (3, 2, 1, 0):
            px, pc = group_partner(k, x, c)
            block = px * 2 + pc
            here = pl.ds(pl.multiple_of(block * size, size), size)
            total = acc_ref[here, :]
            for j, ref in enumerate((dq_ref, dk_ref, dv_ref)):
                total = total + nt(ref[here, :].astype(BF), w_ref[:, j * width : (j + 1) * width])
            dx_ref[block] = total.astype(BF)
            if k == 0:
                row_own(0).start()
            else:
                row_copy(0, k).start()
        tab_ref[0, 0:CLASSES] = small_a_ref[0:CLASSES]
        for g in range(groups):
            tab_ref[0, B_QUERY : B_QUERY + 2, g * width : (g + 1) * width] = bias_ref[g, 0:2, :]
        for row, (ref, at) in {
            B_OUT: (small_b_ref, 3), GAIN1: (small_b_ref, 4), SHIFT1: (small_b_ref, 5), B_OUTER: (small_b_ref, 0),
            GAIN2: (small_b_ref, 1), SHIFT2: (small_b_ref, 2), B_POOL: (small_a_ref, 16), 16: (small_a_ref, 17),
        }.items():
            tab_ref[0, row : row + 1] = ref[at : at + 1, :]
        full = small_a_ref.shape[1]
        for j in range(4):
            tab_ref[0, 12 + j : 13 + j] = bi_ref[:, j * full : (j + 1) * full]
        tab_ref[0, 17:TABLE_ROWS] = jnp.zeros((TABLE_ROWS - 17, full), F32)
        table_copy(0).start()
        take_up(groups * points)
        for a in range(items):
            for number in range(7):
                copy_of(a, number).wait_send()
        for level in range(6):
            table_copy(level).wait_send()
        for which in (0, 1):
            for k in range(1, 4):
                row_copy(which, k).wait_recv()
                row_copy(which, k).wait_send()
            row_own(which).wait()


def attend_back(lens, rows, w_groups, q, k, v, att, datt, lse, grad_pre, small_a, small_b, grad_b_inner, logit_block, parts):
    length, width = rows.shape
    group = 256
    groups = width // group
    local_len = length // 4
    share = width // (8 * ZS)
    once = pl.Buffered(buffer_count=1)
    whole = pl.BlockSpec((length, width), lambda g: (0, 0), pipeline_mode=once)
    part = pl.BlockSpec((length, group), lambda g: (0, g))
    blocks = [p.shape[1:] for p in parts]
    split = [p.reshape((ZS, 2, 2, 2) + b) for p, b in zip(parts, blocks)]
    shapes = [r for r in blocks]
    cuts = [cut_of(a, blocks[DENSE_ITEMS[a][0]]) for a in range(PIECES)]
    blocks = [(r[1], q[1]) for r, q in cuts] + [(share, 3 * group)] * groups
    hbm = pl.BlockSpec(memory_space=pl.ANY)

    def fixed(shape):
        return pl.BlockSpec(shape, lambda g: (0,) * len(shape))

    results = [(TABLE_ROWS + 8, 128)] + shapes + [(share, width)] * 3
    arriving = []
    for lead in ((ZS, 2, 2), (ZS, 2), (ZS,), (ZS - 1,)):
        arriving += [pltpu.VMEM(lead + b, BF) for b in blocks]
    items = len(blocks)
    return pl.pallas_call(
        functools.partial(attend_back_kernel, groups),
        grid=(groups,),
        out_shape=[
            jax.ShapeDtypeStruct((4, local_len, width), BF),
            jax.ShapeDtypeStruct((4,) + logit_block.shape, F32),
        ]
        + [jax.ShapeDtypeStruct(r, F32) for r in results],
        in_specs=[
            SMEM,
            whole,
            pl.BlockSpec((width, 3 * group), lambda g: (0, g)),
            part, part, part, part, part,
            pl.BlockSpec((1, 8, length), lambda g: (g, 0, 0)),
            whole,
            fixed(small_a.shape), fixed(small_b.shape), fixed(grad_b_inner.shape), hbm,
        ]
        + [hbm] * DENSE,
        out_specs=[hbm, hbm] + [fixed(r) for r in results],
        scratch_shapes=[
            pltpu.VMEM((width, length), BF),
            pltpu.VMEM((group, length), BF),
            pltpu.VMEM((group // 128, length, 256), BF),
            pltpu.VMEM((group, length), F32),
            pltpu.VMEM((length, group), BF),
            pltpu.VMEM((length, group), F32),
            pltpu.VMEM((length, group), F32),
            pltpu.VMEM((length, width), F32),
            pltpu.VMEM((4, local_len, width), BF),
            pltpu.VMEM((groups, 8, group), F32),
            pltpu.VMEM((groups, ZS, 2, 2, 2, share, 3 * group), BF),
            pltpu.VMEM((4, TABLE_ROWS, width), F32),
            pltpu.VMEM((3 + ZS, TABLE_ROWS, width), F32),
            pltpu.SemaphoreType.DMA((PIECES + 1, 2)),
            pltpu.SemaphoreType.DMA((2, 3)),
            pltpu.SemaphoreType.DMA((2, 3)),
            pltpu.SemaphoreType.DMA((6,)),
            pltpu.SemaphoreType.DMA((6,)),
            pltpu.SemaphoreType.DMA((items, 7)),
            pltpu.SemaphoreType.DMA((items, 7)),
        ]
        + [pltpu.VMEM((ZS, 2, 2) + b, BF) for b in blocks[:PIECES]]
        + arriving,
        compiler_params=pltpu.CompilerParams(
            collective_id=2, has_side_effects=True, vmem_limit_bytes=60 * 2**20
        ),
        name="attend_back",
    )(lens, rows, w_groups, q, k, v, att, datt, lse, grad_pre, small_a, small_b, grad_b_inner, logit_block, *split)


def row_copies(source_ref, target_ref, send_sem, recv_sem):
    z, y, x, c = my_place()
    copies = []
    for k in (3, 2, 1):
        px, pc = group_partner(k, x, c)
        copies.append(
            pltpu.make_async_remote_copy(
                src_ref=source_ref.at[px * 2 + pc],
                dst_ref=target_ref.at[x * 2 + c],
                send_sem=send_sem.at[k - 1],
                recv_sem=recv_sem.at[k - 1],
                device_id=device_at(z, y, px, pc),
                device_id_type=MESH,
            )
        )
    return copies, pltpu.make_async_copy(source_ref.at[x * 2 + c], target_ref.at[x * 2 + c], send_sem.at[3])


ROW_SEMAPHORES = [pltpu.SemaphoreType.DMA((4,)), pltpu.SemaphoreType.DMA((3,))]


def normal_parts(v):
    bell = jnp.exp(v * v * -0.5)
    t = 1.0 / (1.0 + jnp.abs(v) * 0.23164189)
    tail = t * (0.127414796 + t * (-0.142248368 + t * (0.710706870 + t * (-0.726576013 + t * 0.530702714)))) * bell
    return jnp.where(v >= 0.0, 1.0 - tail, tail), bell


def centered_parts(values):
    average = jnp.mean(values, axis=-1, keepdims=True)
    centered = values - average
    variance = jnp.mean(centered * centered, axis=-1, keepdims=True)
    inverse = lax.rsqrt(variance + 1e-06)
    return centered * inverse, inverse


def norm_back(grad, values, gain):
    hat, inverse = centered_parts(values)
    scaled = grad * gain
    mean_scaled = jnp.mean(scaled, axis=-1, keepdims=True)
    mean_cross = jnp.mean(scaled * hat, axis=-1, keepdims=True)
    back = (scaled - mean_scaled - hat * mean_cross) * inverse
    return back, jnp.sum(grad * hat, axis=0, keepdims=True), jnp.sum(grad, axis=0, keepdims=True)


MIDDLE_ORDERS = ("xy",)
MIDDLE_PLAN = {
    0: ((KB, 0),),
    2: ((KZ, 0),),
    5: ((KF, 0),),
    8: ((KS, 0),),
    14: ((KE, 0),),
}
COTANGENT_POINT = 3


def middle_kernel(tiles, *refs):
    (
        lens_ref, labels_ref, b_class_ref, cot_ref, x_ref, att_ref, w_inner_ref, w_out_ref, outer_hbm_ref, pool_shard_ref,
        vec_ref,
    ) = refs[:11]
    (
        low_ref, act_out_ref, outer_ref, inner_ref, dout_ref, datt_ref, gpre_ref, dpool_ref, small_a_ref, small_b_ref, bi_ref,
        logits_ref, layer_out_ref,
    ) = refs[11:24]
    (
        act_ref, dact_ref, pre_ref, summed_ref, dout_acc_ref, result_ref, cot_rows_ref, first_ref, picked_ref, own_pool, w_outer_ref, pool_ref,
        outer_sem, act_sem, keep_sem, send_sem, recv_sem, cot_send, cot_recv, lo_send, lo_recv,
    ) = refs[24:]
    step = pl.program_id(0)
    rows, full = x_ref.shape
    chunks = act_ref.shape[1] // full

    def view(a, where):
        return pool_ref.at[where]

    def own_block(a):
        return own_pool

    gather_up, all_sent = gather_tools(MIDDLE_PLAN, MIDDLE_ORDERS, view, own_block, keep_sem, send_sem, recv_sem)

    def take_up(point):
        if point in MIDDLE_PLAN or point == COTANGENT_POINT:

            @pl.when(step == point // 2)
            def _():
                gather_up(point)
                if point == COTANGENT_POINT:
                    copies, own = row_copies(cot_ref, cot_rows_ref, cot_send, cot_recv)
                    for copy in copies:
                        copy.start()
                    own.start()

    def outer_copy():
        return pltpu.make_async_copy(outer_hbm_ref, w_outer_ref, outer_sem.at[0])

    def act_copy(tile):
        where = pl.ds(tile * rows, rows)
        return pltpu.make_async_copy(act_ref.at[where], act_out_ref.at[where], act_sem.at[tile])

    def vec(row):
        return vec_ref[row : row + 1, :]

    @pl.when(step == 0)
    def _():
        outer_copy().start()
        own_pool[...] = pool_shard_ref[...].astype(BF)
        z, y, x, c = my_place()
        meet(all_partners(z, y, x, c))

    tile = lax.rem(step, tiles)
    here = pl.ds(pl.multiple_of(tile * rows, rows), rows)
    for point in range(0, 2 * tiles, 2):
        take_up(point)

    @pl.when(step < tiles)
    def _():
        pre = x_ref[...].astype(F32) + (nn(att_ref[...], w_out_ref[...]) + vec(B_OUT))
        pre_ref[here, :] = pre
        low = (centered_parts(pre)[0] * vec(GAIN1) + vec(SHIFT1)).astype(BF)
        low_ref[...] = low
        for j in range(chunks):
            if j == chunks // 2:
                for point in range(1, 2 * tiles, 2):
                    take_up(point)
            s = j * full
            hidden = nn(low, w_inner_ref[:, s : s + full]) + vec(12 + j)
            phi, bell = normal_parts(hidden)
            act_ref[here, s : s + full] = (hidden * phi).astype(BF)
            dact_ref[here, s : s + full] = (phi + hidden * bell * 0.3989422804014327).astype(BF)
        for t in range(tiles):

            @pl.when(step == t)
            def _(t=t):
                act_copy(t).start()

    for point in range(2 * tiles, 4 * tiles, 2):
        take_up(point)

    def outer_part(j):
        return w_outer_ref[j].reshape(full, full)

    @pl.when(step == tiles)
    def _():
        outer_copy().wait()

    @pl.when((step >= tiles) & (step < 2 * tiles))
    def _():
        total = centered_parts(pre_ref[here, :])[0] * vec(GAIN1) + vec(SHIFT1) + vec(B_OUTER)
        for j in range(chunks):
            total = total + nn(act_ref[here, j * full : (j + 1) * full], outer_part(j))
        summed_ref[here, :] = total
        result = (centered_parts(total)[0] * vec(GAIN2) + vec(SHIFT2)).astype(BF)
        result_ref[tile] = result
        starts = doc_starts(lens_ref)
        places = lax.broadcasted_iota(jnp.int32, (VEC_ROWS, rows), 1) + tile * rows
        row_doc = lax.broadcasted_iota(jnp.int32, (VEC_ROWS, rows), 0)
        hit = jnp.zeros((VEC_ROWS, rows), jnp.bool_)
        for d, start in enumerate(starts):
            hit = hit | ((row_doc == d) & (places == start))
        found = nn(jnp.where(hit, 1.0, 0.0).astype(BF), result)

        @pl.when(tile == 0)
        def _():
            picked_ref[...] = found

        @pl.when(tile > 0)
        def _():
            picked_ref[...] += found

    @pl.when(step == 2 * tiles - 1)
    def _():
        copies, own = row_copies(result_ref, layer_out_ref, lo_send, lo_recv)
        for copy in copies:
            copy.start()
        own.start()
        w_pool = pool_ref[...].astype(F32).reshape(full, full).astype(BF)
        docs = lens_ref.shape[1]
        picked = picked_ref[...].astype(BF)
        pooled = jnp.tanh(nn(picked, w_pool) + vec(B_POOL))
        pooled_low = pooled.astype(BF)
        table = vec_ref[...].astype(BF)
        column = lax.broadcasted_iota(jnp.int32, (VEC_ROWS, VEC_ROWS), 1)
        row = lax.broadcasted_iota(jnp.int32, (VEC_ROWS, VEC_ROWS), 0)
        class_bias = jnp.zeros((VEC_ROWS, VEC_ROWS), F32)
        for j in range(CLASSES):
            class_bias = jnp.where(column == j, b_class_ref[j], class_bias)
        logits = nt(pooled_low, table) + class_bias
        logits_ref[...] = jnp.concatenate([logits[0:8], jnp.zeros((8, 128 - VEC_ROWS), F32)], axis=1)
        live = column < CLASSES
        shown = jnp.where(live, logits, -jnp.inf)
        exps = jnp.where(live, jnp.exp(shown - jnp.max(shown, axis=-1, keepdims=True)), 0.0)
        probs = exps / jnp.sum(exps, axis=-1, keepdims=True)
        label = jnp.zeros((VEC_ROWS, VEC_ROWS), jnp.int32)
        for d in range(docs):
            label = jnp.where(row == d, labels_ref[lax.axis_index("fsdp"), d], label)
        grad = jnp.where(live & (row < docs), probs - jnp.where(label == column, 1.0, 0.0), 0.0)
        grad_low = grad.astype(BF)
        grad_pool = (nn(grad_low, table) * (1.0 - pooled * pooled)).astype(BF)
        dpool_ref[...] = tn(picked, grad_pool).astype(BF)
        first_ref[...] = nt(grad_pool, w_pool)
        small_a_ref[0:16, :] = tn(grad_low, pooled_low)
        small_a_ref[16:17, :] = jnp.sum(grad_pool.astype(F32), axis=0, keepdims=True)
        class_sum = jnp.sum(grad_low.astype(F32), axis=0, keepdims=True)
        small_a_ref[17:18, :] = jnp.concatenate([class_sum, jnp.zeros((1, full - VEC_ROWS), F32)], axis=1)
        small_b_ref[...] = jnp.zeros_like(small_b_ref)
        bi_ref[...] = jnp.zeros_like(bi_ref)
        copies, own = row_copies(cot_ref, cot_rows_ref, cot_send, cot_recv)
        for copy in copies:
            copy.wait()
        own.wait()

    @pl.when(step >= 2 * tiles)
    def _():
        grad = cot_rows_ref[tile].astype(F32)
        places = lax.broadcasted_iota(jnp.int32, (rows, 1), 0) + tile * rows
        placed = jnp.zeros(grad.shape, F32)
        for d, start in enumerate(doc_starts(lens_ref)):
            placed = jnp.where(places == start, first_ref[d : d + 1, :], placed)
        grad = grad + placed
        grad_summed, gain2, shift2 = norm_back(grad, summed_ref[here, :], vec(GAIN2))
        outer = grad_summed.astype(BF)
        outer_ref[...] = outer
        grad_normed = grad_summed
        for j in range(chunks):
            s = j * full
            back = nt(outer, outer_part(j))
            inner = (back * dact_ref[here, s : s + full].astype(F32)).astype(BF)
            inner_ref[:, s : s + full] = inner
            bi_ref[:, s : s + full] += jnp.sum(inner.astype(F32), axis=0, keepdims=True)
            grad_normed = grad_normed + nt(inner, w_inner_ref[:, s : s + full])
        grad_pre, gain1, shift1 = norm_back(grad_normed, pre_ref[here, :], vec(GAIN1))
        gpre_ref[...] = grad_pre
        branch = grad_pre.astype(BF)
        dout = tn(att_ref[...], branch)

        @pl.when(tile == 0)
        def _():
            dout_acc_ref[...] = dout

        @pl.when(tile > 0)
        def _():
            dout_acc_ref[...] += dout

        datt_ref[...] = nt(branch, w_out_ref[...]).astype(BF)
        small_b_ref[0:1, :] += jnp.sum(outer.astype(F32), axis=0, keepdims=True)
        small_b_ref[1:2, :] += gain2
        small_b_ref[2:3, :] += shift2
        small_b_ref[3:4, :] += jnp.sum(branch.astype(F32), axis=0, keepdims=True)
        small_b_ref[4:5, :] += gain1
        small_b_ref[5:6, :] += shift1

    @pl.when(step == 3 * tiles - 1)
    def _():
        dout_ref[...] = dout_acc_ref[...].astype(BF)
        all_sent()
        for t in range(tiles):
            act_copy(t).wait()
        copies, own = row_copies(result_ref, layer_out_ref, lo_send, lo_recv)
        for copy in copies:
            copy.wait()
        own.wait()


def middle(lens, labels, b_class, cot, rows, att, w_inner, w_out, w_outer, pool_shard, vectors):
    length, width = rows.shape
    hidden = w_inner.shape[1]
    tile = 256
    tiles = length // tile
    items = len(MIDDLE_ORDERS)
    once = pl.Buffered(buffer_count=1)
    early = pl.BlockSpec((tile, width), lambda i: (jnp.minimum(i, tiles - 1), 0))

    twice = pl.BlockSpec((tile, width), lambda i: (jnp.where(i < 2 * tiles, jnp.minimum(i, tiles - 1), i - 2 * tiles), 0))

    def late(size):
        return pl.BlockSpec((tile, size), lambda i: (jnp.maximum(i - 2 * tiles, 0), 0))

    def fixed(shape):
        return pl.BlockSpec(shape, lambda i: (0,) * len(shape), pipeline_mode=once)

    lead = (ZS, 2, 2, 2)
    return pl.pallas_call(
        functools.partial(middle_kernel, tiles),
        grid=(3 * tiles,),
        out_shape=[
            jax.ShapeDtypeStruct((length, width), BF),
            jax.ShapeDtypeStruct((length, hidden), BF),
            jax.ShapeDtypeStruct((length, width), BF),
            jax.ShapeDtypeStruct((length, hidden), BF),
            jax.ShapeDtypeStruct((width, width), BF),
            jax.ShapeDtypeStruct((length, width), BF),
            jax.ShapeDtypeStruct((length, width), F32),
            jax.ShapeDtypeStruct((width, width), BF),
            jax.ShapeDtypeStruct((24, width), F32),
            jax.ShapeDtypeStruct((8, width), F32),
            jax.ShapeDtypeStruct((1, hidden), F32),
            jax.ShapeDtypeStruct((8, 128), F32),
            jax.ShapeDtypeStruct(cot.shape, BF),
        ],
        in_specs=[
            SMEM, SMEM, SMEM, ANY, early, twice, fixed((width, hidden)), fixed((width, width)), ANY,
            fixed(pool_shard.shape), fixed((VEC_ROWS, width)),
        ],
        out_specs=[
            early, ANY, late(width), late(hidden), fixed((width, width)), late(width), late(width), fixed((width, width)),
            fixed((24, width)), fixed((8, width)), fixed((1, hidden)), fixed((8, 128)), ANY,
        ],
        scratch_shapes=[
            pltpu.VMEM((length, hidden), BF),
            pltpu.VMEM((length, hidden), BF),
            pltpu.VMEM((length, width), F32),
            pltpu.VMEM((length, width), F32),
            pltpu.VMEM((width, width), F32),
            pltpu.VMEM(cot.shape, BF),
            pltpu.VMEM(cot.shape, BF),
            pltpu.VMEM((VEC_ROWS, width), F32),
            pltpu.VMEM((VEC_ROWS, width), F32),
            pltpu.VMEM(pool_shard.shape, BF),
            pltpu.VMEM(w_outer.shape, BF),
            pltpu.VMEM(lead + pool_shard.shape, BF),
            pltpu.SemaphoreType.DMA((1,)),
            pltpu.SemaphoreType.DMA((tiles,)),
            pltpu.SemaphoreType.DMA((items,)),
            pltpu.SemaphoreType.DMA((items, 9)),
            pltpu.SemaphoreType.DMA((items, 9)),
        ]
        + ROW_SEMAPHORES * 2,
        compiler_params=pltpu.CompilerParams(collective_id=3, has_side_effects=True, vmem_limit_bytes=60 * 2**20),
        name="middle",
    )(lens, labels, b_class, cot, rows, att, w_inner, w_out, w_outer, pool_shard, vectors)


def results_kernel(large, small_ref, *refs):
    sources, refs = refs[:large], refs[large:]
    targets, columns, inner_ref, class_ref, sem, *held = refs[:large], refs[large : large + VECTORS], *refs[large + VECTORS :]
    arriving = [pltpu.make_async_copy(s, h, sem.at[0, j]) for j, (s, h) in enumerate(zip(sources, held))]
    leaving = [pltpu.make_async_copy(h, t, sem.at[1, j]) for j, (h, t) in enumerate(zip(held, targets))]
    for copy in arriving:
        copy.start()
    for j, ref in enumerate(columns):
        ref[...] = small_ref[B_QUERY + j : B_QUERY + j + 1, 0 : ref.shape[1]]
    inner_ref[...] = small_ref[TABLE_ROWS : TABLE_ROWS + 1, 0 : inner_ref.shape[1]]
    class_ref[...] = small_ref[TABLE_ROWS + 1 : TABLE_ROWS + 2, 0 : class_ref.shape[1]]
    for came, goes in zip(arriving, leaving):
        came.wait()
        goes.start()
    for goes in leaving:
        goes.wait()


def write_results(small, arrays, share, hidden_share):
    shapes = [jax.ShapeDtypeStruct(a.shape, a.dtype) for a in arrays]
    vectors = [(1, share)] * VECTORS + [(1, hidden_share), (1, CLASSES)]
    inside = pl.BlockSpec(memory_space=pltpu.VMEM)
    return pl.pallas_call(
        functools.partial(results_kernel, len(arrays)),
        out_shape=shapes + [jax.ShapeDtypeStruct(v, F32) for v in vectors],
        in_specs=[inside] + [ANY] * len(arrays),
        out_specs=[ANY] * len(arrays) + [inside] * len(vectors),
        scratch_shapes=[pltpu.SemaphoreType.DMA((2, len(arrays)))] + [pltpu.VMEM(a.shape, a.dtype) for a in arrays],
        compiler_params=pltpu.CompilerParams(vmem_limit_bytes=60 * 2**20),
        name="results",
    )(small, *arrays)


def fast_body(
    inputs, cotangent, doc_lengths, labels, w_query, b_query, w_key, w_value, b_value, w_out, b_out, first_gain, first_shift,
    w_inner, b_inner, w_outer, b_outer, second_gain, second_shift, w_pool, b_pool, w_class, b_class,
):
    seqs, local_len, width = inputs.shape
    length = seqs * local_len
    devices = 8 * ZS
    docs = doc_lengths.shape[1]
    share = width // devices
    hidden_share = b_inner.shape[0]
    hidden = hidden_share * devices
    vector_shards = [b_query, b_value, b_out, first_gain, first_shift, b_outer, second_gain, second_shift, b_pool]
    q, k, v, att, lse, w_qkv, vectors, rows, full_inner, full_out, full_outer = attend(
        doc_lengths, inputs, w_class.T, [member.reshape(1, share) for member in vector_shards], b_inner.reshape(1, hidden_share),
        [w_query, w_key, w_value], [w_inner, w_out, w_outer],
    )
    rows = rows.reshape(length, width)
    full_inner = full_inner.reshape(width, hidden)
    full_out = full_out.reshape(width, width)
    low, act, outer, inner, grad_out_w, datt, grad_pre, grad_pool, small_a, small_b, grad_b_inner, logit_block, layer_out = middle(
        doc_lengths, labels, b_class, cotangent, rows, att, full_inner, full_out, full_outer, w_pool, vectors
    )
    grad_outer_w = tn(act, outer).astype(BF)
    grad_inner_w = tn(low, inner).astype(BF)
    grad_inputs, all_logits, small, *sums = attend_back(
        doc_lengths, rows, w_qkv, q, k, v, att, datt, lse, grad_pre, small_a, small_b, grad_b_inner, logit_block,
        [
            grad_inner_w.reshape(devices, share, hidden),
            grad_outer_w.reshape(devices, hidden_share, width),
            grad_out_w.reshape(devices, share, width),
            grad_pool.reshape(devices, share, width),
        ],
    )

    done = write_results(small, [grad_inputs, layer_out, *sums], share, hidden_share)
    grad_inputs, layer_out, o_inner, o_outer, o_out, o_pool, o_query, o_key, o_value = done[:9]
    (
        o_b_query, o_b_value, o_b_out, o_gain1, o_shift1, o_b_outer, o_gain2, o_shift2, o_b_pool, o_b_inner, o_b_class,
    ) = (vector.reshape(-1) for vector in done[9:])
    return (
        layer_out,
        all_logits[:, :docs, :CLASSES],
        grad_inputs,
        o_query,
        o_b_query,
        o_key,
        o_value,
        o_b_value,
        o_out,
        o_b_out,
        o_gain1,
        o_shift1,
        o_inner,
        o_b_inner,
        o_outer,
        o_b_outer,
        o_gain2,
        o_shift2,
        o_pool,
        o_b_pool,
        small[:CLASSES, :share].T,
        o_b_class,
    )


def solution(mesh):
    placed = (
        P("dp", "fsdp", None),
        P("dp", "fsdp", None),
        P("dp", None),
        P("dp", None),
        P(("dp", "fsdp"), None),
        P(("dp", "fsdp")),
        P(("dp", "fsdp"), None),
        P(("dp", "fsdp"), None),
        P(("dp", "fsdp")),
        P(("dp", "fsdp"), None),
        P(("dp", "fsdp")),
        P(("dp", "fsdp")),
        P(("dp", "fsdp")),
        P(("dp", "fsdp"), None),
        P(("dp", "fsdp")),
        P(("dp", "fsdp"), None),
        P(("dp", "fsdp")),
        P(("dp", "fsdp")),
        P(("dp", "fsdp")),
        P(("dp", "fsdp"), None),
        P(("dp", "fsdp")),
        P(("dp", "fsdp"), None),
        P(),
    )
    sizes = (mesh.shape["dp"], mesh.shape["fsdp"])
    chosen = fast_body if sizes == (8, 4) else general_body
    return jax.shard_map(
        chosen,
        mesh=mesh,
        in_specs=placed,
        out_specs=(
            P("dp", "fsdp", None),
            P("dp", None, None),
            P("dp", "fsdp", None),
            P(("dp", "fsdp"), None),
            P(("dp", "fsdp")),
            P(("dp", "fsdp"), None),
            P(("dp", "fsdp"), None),
            P(("dp", "fsdp")),
            P(("dp", "fsdp"), None),
            P(("dp", "fsdp")),
            P(("dp", "fsdp")),
            P(("dp", "fsdp")),
            P(("dp", "fsdp"), None),
            P(("dp", "fsdp")),
            P(("dp", "fsdp"), None),
            P(("dp", "fsdp")),
            P(("dp", "fsdp")),
            P(("dp", "fsdp")),
            P(("dp", "fsdp"), None),
            P(("dp", "fsdp")),
            P(("dp", "fsdp"), None),
            P(),
        ),
        check_vma=False,
    )
```

```python
import functools

import jax
import jax.numpy as jnp
from jax import lax
from jax.experimental import pallas as pl
from jax.experimental.pallas import tpu as pltpu
from jax.sharding import PartitionSpec as P

HEAD_DIM = 64
CLASSES = 3
MICRO = 4


def product(left_side, right_side):
    return jnp.dot(left_side, right_side, preferred_element_type=jnp.float32)


def contract_rows(left_side, right_side):
    return lax.dot_general(
        left_side, right_side, (((0,), (0,)), ((), ())), preferred_element_type=jnp.float32
    )


def times_transposed(left_side, right_side):
    return lax.dot_general(
        left_side, right_side, (((1,), (1,)), ((), ())), preferred_element_type=jnp.float32
    )


def layer_norm(values, norm_gain, norm_shift):
    average = jnp.mean(values, axis=-1, keepdims=True)
    centered = values - average
    variance = jnp.mean(centered * centered, axis=-1, keepdims=True)
    return centered * lax.rsqrt(variance + 1e-06) * norm_gain + norm_shift


def gelu_exact(values):
    return jax.nn.gelu(values, approximate=False)


def running_sum(lengths_rows):
    count = lengths_rows.shape[1]
    upper = jnp.arange(count)[:, None] <= jnp.arange(count)[None, :]
    return jnp.sum(jnp.where(upper[None], lengths_rows[:, :, None], 0), axis=1)


def segment_numbers(lengths_rows, places):
    doc_ends = running_sum(lengths_rows)
    above = (places[None, :, None] >= doc_ends[:, None, :]).astype(jnp.int32)
    return jnp.sum(above, axis=2)


def pair_heads(values):
    return values.reshape(values.shape[0], values.shape[1], 2, HEAD_DIM)


def pair_scores(query_pair, key_pair, same_doc):
    raw_scores = jnp.einsum(
        "bqhd,bkhd->bhqk", query_pair, key_pair, preferred_element_type=jnp.float32
    ) * HEAD_DIM ** (-0.5)
    return jnp.where(same_doc[:, None], raw_scores, -1000000000.0)


def lowered_masters(masters):
    return [member.astype(jnp.bfloat16) for member in masters]


def forward(tokens, lengths_rows, weights, bias_class):
    (
        w_query,
        b_query,
        w_key,
        w_value,
        b_value,
        w_out,
        b_out,
        first_gain,
        first_shift,
        w_inner,
        b_inner,
        w_outer,
        b_outer,
        second_gain,
        second_shift,
        w_pool,
        b_pool,
        w_class,
    ) = weights
    seq_count, local_len, model_width = tokens.shape
    doc_count = lengths_rows.shape[1]
    flat_rows = tokens.reshape(seq_count * local_len, model_width)
    queries = (
        (product(flat_rows, w_query) + b_query)
        .astype(jnp.bfloat16)
        .reshape(seq_count, local_len, model_width)
    )
    key_rows = (
        product(flat_rows, w_key).astype(jnp.bfloat16).reshape(seq_count, local_len, model_width)
    )
    value_rows = (
        (product(flat_rows, w_value) + b_value)
        .astype(jnp.bfloat16)
        .reshape(seq_count, local_len, model_width)
    )
    all_keys, all_values = (
        lax.all_gather(key_rows, "fsdp", axis=1, tiled=True),
        lax.all_gather(value_rows, "fsdp", axis=1, tiled=True),
    )
    full_len = all_keys.shape[1]
    own_places = lax.axis_index("fsdp") * local_len + jnp.arange(local_len, dtype=jnp.int32)
    key_places = jnp.arange(full_len, dtype=jnp.int32)
    same_doc = (
        segment_numbers(lengths_rows, own_places)[:, :, None]
        == segment_numbers(lengths_rows, key_places)[:, None, :]
    )
    pair_width = 2 * HEAD_DIM
    mixed_list = []
    log_totals = []
    for pair_index in range(model_width // pair_width):
        col_start = pair_index * pair_width
        query_pair = pair_heads(queries[:, :, col_start : col_start + pair_width])
        key_pair = pair_heads(all_keys[:, :, col_start : col_start + pair_width])
        value_pair = pair_heads(all_values[:, :, col_start : col_start + pair_width])
        scores = pair_scores(query_pair, key_pair, same_doc)
        row_peak = jnp.max(scores, axis=-1, keepdims=True)
        exp_total = jnp.sum(jnp.exp(scores - row_peak), axis=-1, keepdims=True)
        log_total = row_peak + jnp.log(exp_total)
        attn_probs = jnp.exp(scores - log_total).astype(jnp.bfloat16)
        mixed_pair = jnp.einsum(
            "bhqk,bkhd->bqhd", attn_probs, value_pair, preferred_element_type=jnp.float32
        )
        mixed_list.append(mixed_pair.reshape(seq_count, local_len, pair_width))
        log_totals.append(log_total)
    attended = (
        jnp.concatenate(mixed_list, axis=2)
        .astype(jnp.bfloat16)
        .reshape(seq_count * local_len, model_width)
    )
    branch = product(attended, w_out) + b_out
    pre_first = flat_rows.astype(jnp.float32) + branch
    normed = layer_norm(pre_first, first_gain.astype(jnp.float32), first_shift.astype(jnp.float32))
    normed_low = normed.astype(jnp.bfloat16)
    inner_pre = product(normed_low, w_inner) + b_inner
    activated = gelu_exact(inner_pre).astype(jnp.bfloat16)
    summed = normed + (product(activated, w_outer) + b_outer)
    result = layer_norm(summed, second_gain.astype(jnp.float32), second_shift.astype(jnp.float32))
    result_low = result.astype(jnp.bfloat16).reshape(seq_count, local_len, model_width)
    starts = running_sum(lengths_rows) - lengths_rows
    picker = (own_places[None, None, :] == starts[:, :, None]).astype(jnp.bfloat16)
    local_firsts = jnp.einsum(
        "bdl,blc->bdc", picker, result_low, preferred_element_type=jnp.float32
    )
    firsts = lax.psum(local_firsts, "fsdp")
    firsts_low = firsts.astype(jnp.bfloat16).reshape(seq_count * doc_count, model_width)
    pooled = jnp.tanh(product(firsts_low, w_pool) + b_pool)
    pooled_low = pooled.astype(jnp.bfloat16)
    logits = product(pooled_low, w_class) + bias_class
    stored = (
        flat_rows,
        queries,
        all_keys,
        all_values,
        same_doc,
        log_totals,
        attended,
        pre_first,
        summed,
        normed_low,
        inner_pre,
        activated,
        picker,
        firsts_low,
        pooled,
        pooled_low,
        logits,
    )
    return (result_low, logits.reshape(seq_count, doc_count, CLASSES), stored)


def backward(stored, weights, cot_rows, label_rows):
    (
        w_query,
        b_query,
        w_key,
        w_value,
        b_value,
        w_out,
        b_out,
        first_gain,
        first_shift,
        w_inner,
        b_inner,
        w_outer,
        b_outer,
        second_gain,
        second_shift,
        w_pool,
        b_pool,
        w_class,
    ) = weights
    (
        flat_rows,
        queries,
        all_keys,
        all_values,
        same_doc,
        log_totals,
        attended,
        pre_first,
        summed,
        normed_low,
        inner_pre,
        activated,
        picker,
        firsts_low,
        pooled,
        pooled_low,
        logits,
    ) = stored
    seq_count, local_len, model_width = queries.shape
    doc_count = picker.shape[1]
    owner_flag = (lax.axis_index("fsdp") == 0).astype(jnp.float32)
    row_peak = jnp.max(logits, axis=-1, keepdims=True)
    class_exp = jnp.exp(logits - row_peak)
    class_probs = class_exp / jnp.sum(class_exp, axis=-1, keepdims=True)
    onehot_labels = (
        label_rows.reshape(-1)[:, None] == jnp.arange(CLASSES, dtype=jnp.int32)[None, :]
    ).astype(jnp.float32)
    grad_logits = (class_probs - onehot_labels).astype(jnp.bfloat16)
    grad_b_class = owner_flag * jnp.sum(grad_logits.astype(jnp.float32), axis=0)
    grad_w_class = owner_flag * contract_rows(pooled_low, grad_logits)
    grad_pool_pre = (times_transposed(grad_logits, w_class) * (1.0 - pooled * pooled)).astype(
        jnp.bfloat16
    )
    grad_b_pool = owner_flag * jnp.sum(grad_pool_pre.astype(jnp.float32), axis=0)
    grad_w_pool = owner_flag * contract_rows(firsts_low, grad_pool_pre)
    grad_firsts = times_transposed(grad_pool_pre, w_pool).reshape(seq_count, doc_count, model_width)
    from_pool = jnp.einsum(
        "bdl,bdc->blc", picker.astype(jnp.float32), grad_firsts, precision=lax.Precision.HIGHEST
    )
    grad_result = cot_rows.astype(jnp.float32).reshape(-1, model_width) + from_pool.reshape(
        -1, model_width
    )
    second_back = jax.vjp(
        layer_norm, summed, second_gain.astype(jnp.float32), second_shift.astype(jnp.float32)
    )[1]
    grad_summed, grad_second_gain, grad_second_shift = second_back(grad_result)
    grad_outer = grad_summed.astype(jnp.bfloat16)
    grad_b_outer = jnp.sum(grad_outer.astype(jnp.float32), axis=0)
    grad_w_outer = contract_rows(activated, grad_outer)
    gelu_back = jax.vjp(gelu_exact, inner_pre)[1]
    grad_inner = gelu_back(times_transposed(grad_outer, w_outer))[0].astype(jnp.bfloat16)
    grad_b_inner = jnp.sum(grad_inner.astype(jnp.float32), axis=0)
    grad_w_inner = contract_rows(normed_low, grad_inner)
    grad_normed = grad_summed + times_transposed(grad_inner, w_inner)
    first_back = jax.vjp(
        layer_norm, pre_first, first_gain.astype(jnp.float32), first_shift.astype(jnp.float32)
    )[1]
    grad_pre_first, grad_first_gain, grad_first_shift = first_back(grad_normed)
    grad_branch = grad_pre_first.astype(jnp.bfloat16)
    grad_b_out = jnp.sum(grad_branch.astype(jnp.float32), axis=0)
    grad_w_out = contract_rows(attended, grad_branch)
    grad_attended = (
        times_transposed(grad_branch, w_out)
        .astype(jnp.bfloat16)
        .reshape(seq_count, local_len, model_width)
    )
    pair_width = 2 * HEAD_DIM
    query_list = []
    key_list = []
    value_list = []
    for pair_index in range(model_width // pair_width):
        col_start = pair_index * pair_width
        query_pair = pair_heads(queries[:, :, col_start : col_start + pair_width])
        key_pair = pair_heads(all_keys[:, :, col_start : col_start + pair_width])
        value_pair = pair_heads(all_values[:, :, col_start : col_start + pair_width])
        grad_pair = pair_heads(grad_attended[:, :, col_start : col_start + pair_width])
        scores = pair_scores(query_pair, key_pair, same_doc)
        attn_probs = jnp.exp(scores - log_totals[pair_index])
        grad_probs = jnp.einsum(
            "bqhd,bkhd->bhqk", grad_pair, value_pair, preferred_element_type=jnp.float32
        )
        row_dot = jnp.sum(attn_probs * grad_probs, axis=-1, keepdims=True)
        grad_scores = (attn_probs * (grad_probs - row_dot)).astype(jnp.bfloat16)
        query_part = jnp.einsum(
            "bhqk,bkhd->bqhd", grad_scores, key_pair, preferred_element_type=jnp.float32
        ) * HEAD_DIM ** (-0.5)
        query_list.append(query_part.reshape(seq_count, local_len, pair_width))
        probs_low = attn_probs.astype(jnp.bfloat16)
        key_part = jnp.einsum(
            "bhqk,bqhd->bkhd", grad_scores, query_pair, preferred_element_type=jnp.float32
        ) * HEAD_DIM ** (-0.5)
        value_part = jnp.einsum(
            "bhqk,bqhd->bkhd", probs_low, grad_pair, preferred_element_type=jnp.float32
        )
        key_list.append(key_part.reshape(seq_count, key_part.shape[1], pair_width))
        value_list.append(value_part.reshape(seq_count, value_part.shape[1], pair_width))
    key_partials = jnp.concatenate(key_list, axis=2)
    value_partials = jnp.concatenate(value_list, axis=2)
    own_keys, own_values = (
        lax.psum_scatter(
            key_partials.astype(jnp.bfloat16), "fsdp", scatter_dimension=1, tiled=True
        ).astype(jnp.float32),
        lax.psum_scatter(
            value_partials.astype(jnp.bfloat16), "fsdp", scatter_dimension=1, tiled=True
        ).astype(jnp.float32),
    )
    query_grad = jnp.concatenate(query_list, axis=2).astype(jnp.bfloat16).reshape(-1, model_width)
    key_grad = own_keys.astype(jnp.bfloat16).reshape(-1, model_width)
    value_grad = own_values.astype(jnp.bfloat16).reshape(-1, model_width)
    grad_w_query = contract_rows(flat_rows, query_grad)
    grad_b_query = jnp.sum(query_grad.astype(jnp.float32), axis=0)
    grad_w_key = contract_rows(flat_rows, key_grad)
    grad_w_value = contract_rows(flat_rows, value_grad)
    grad_b_value = jnp.sum(value_grad.astype(jnp.float32), axis=0)
    grad_tokens = (
        grad_pre_first
        + times_transposed(query_grad, w_query)
        + times_transposed(key_grad, w_key)
        + times_transposed(value_grad, w_value)
    )
    new_grads = (
        grad_w_query,
        grad_b_query,
        grad_w_key,
        grad_w_value,
        grad_b_value,
        grad_w_out,
        grad_b_out,
        grad_first_gain,
        grad_first_shift,
        grad_w_inner,
        grad_b_inner,
        grad_w_outer,
        grad_b_outer,
        grad_second_gain,
        grad_second_shift,
        grad_w_pool,
        grad_b_pool,
        grad_w_class,
    )
    return (
        new_grads,
        grad_b_class,
        grad_tokens.astype(jnp.bfloat16).reshape(seq_count, local_len, model_width),
    )


def general_body(
    inputs,
    cotangent,
    doc_lengths,
    labels,
    w_query,
    b_query,
    w_key,
    w_value,
    b_value,
    w_out,
    b_out,
    first_gain,
    first_shift,
    w_inner,
    b_inner,
    w_outer,
    b_outer,
    second_gain,
    second_shift,
    w_pool,
    b_pool,
    w_class,
    b_class,
):
    masters = (
        w_query,
        b_query,
        w_key,
        w_value,
        b_value,
        w_out,
        b_out,
        first_gain,
        first_shift,
        w_inner,
        b_inner,
        w_outer,
        b_outer,
        second_gain,
        second_shift,
        w_pool,
        b_pool,
        w_class,
    )
    group_size = lax.axis_size("dp") * lax.axis_size("fsdp")
    grad_sums = [
        jnp.zeros((member.shape[0] * group_size,) + member.shape[1:], jnp.float32)
        for member in masters
    ]
    class_sum = jnp.zeros((CLASSES,), jnp.float32)
    micro_seqs = inputs.shape[0] // MICRO
    out_list = []
    logit_list = []
    grad_list = []
    for micro_step in range(MICRO):
        first_seq = micro_step * micro_seqs
        after_seq = first_seq + micro_seqs
        tokens = inputs[first_seq:after_seq]
        lengths_rows = doc_lengths[first_seq:after_seq]
        pieces = lowered_masters(masters)
        front_weights = (
            lax.all_gather(pieces[0], ("dp", "fsdp"), axis=0, tiled=True),
            lax.all_gather(pieces[1], ("dp", "fsdp"), axis=0, tiled=True),
            lax.all_gather(pieces[2], ("dp", "fsdp"), axis=0, tiled=True),
            lax.all_gather(pieces[3], ("dp", "fsdp"), axis=0, tiled=True),
            lax.all_gather(pieces[4], ("dp", "fsdp"), axis=0, tiled=True),
            lax.all_gather(pieces[5], ("dp", "fsdp"), axis=0, tiled=True),
            lax.all_gather(pieces[6], ("dp", "fsdp"), axis=0, tiled=True),
            lax.all_gather(pieces[7], ("dp", "fsdp"), axis=0, tiled=True),
            lax.all_gather(pieces[8], ("dp", "fsdp"), axis=0, tiled=True),
            lax.all_gather(pieces[9], ("dp", "fsdp"), axis=0, tiled=True),
            lax.all_gather(pieces[10], ("dp", "fsdp"), axis=0, tiled=True),
            lax.all_gather(pieces[11], ("dp", "fsdp"), axis=0, tiled=True),
            lax.all_gather(pieces[12], ("dp", "fsdp"), axis=0, tiled=True),
            lax.all_gather(pieces[13], ("dp", "fsdp"), axis=0, tiled=True),
            lax.all_gather(pieces[14], ("dp", "fsdp"), axis=0, tiled=True),
            lax.all_gather(pieces[15], ("dp", "fsdp"), axis=0, tiled=True),
            lax.all_gather(pieces[16], ("dp", "fsdp"), axis=0, tiled=True),
            lax.all_gather(pieces[17], ("dp", "fsdp"), axis=0, tiled=True),
        )
        result_low, logits, stored = forward(tokens, lengths_rows, front_weights, b_class)
        out_list.append(result_low)
        logit_list.append(logits)
        back_weights = (
            lax.all_gather(pieces[0], ("dp", "fsdp"), axis=0, tiled=True),
            lax.all_gather(pieces[1], ("dp", "fsdp"), axis=0, tiled=True),
            lax.all_gather(pieces[2], ("dp", "fsdp"), axis=0, tiled=True),
            lax.all_gather(pieces[3], ("dp", "fsdp"), axis=0, tiled=True),
            lax.all_gather(pieces[4], ("dp", "fsdp"), axis=0, tiled=True),
            lax.all_gather(pieces[5], ("dp", "fsdp"), axis=0, tiled=True),
            lax.all_gather(pieces[6], ("dp", "fsdp"), axis=0, tiled=True),
            lax.all_gather(pieces[7], ("dp", "fsdp"), axis=0, tiled=True),
            lax.all_gather(pieces[8], ("dp", "fsdp"), axis=0, tiled=True),
            lax.all_gather(pieces[9], ("dp", "fsdp"), axis=0, tiled=True),
            lax.all_gather(pieces[10], ("dp", "fsdp"), axis=0, tiled=True),
            lax.all_gather(pieces[11], ("dp", "fsdp"), axis=0, tiled=True),
            lax.all_gather(pieces[12], ("dp", "fsdp"), axis=0, tiled=True),
            lax.all_gather(pieces[13], ("dp", "fsdp"), axis=0, tiled=True),
            lax.all_gather(pieces[14], ("dp", "fsdp"), axis=0, tiled=True),
            lax.all_gather(pieces[15], ("dp", "fsdp"), axis=0, tiled=True),
            lax.all_gather(pieces[16], ("dp", "fsdp"), axis=0, tiled=True),
            lax.all_gather(pieces[17], ("dp", "fsdp"), axis=0, tiled=True),
        )
        stored = forward(tokens, lengths_rows, back_weights, b_class)[2]
        new_grads, class_grad, grad_tokens = backward(
            stored, back_weights, cotangent[first_seq:after_seq], labels[first_seq:after_seq]
        )
        grad_sums = [running + fresh_grad for running, fresh_grad in zip(grad_sums, new_grads)]
        class_sum = class_sum + class_grad
        grad_list.append(grad_tokens)
    owned = (
        lax.psum_scatter(grad_sums[0], ("dp", "fsdp"), scatter_dimension=0, tiled=True),
        lax.psum_scatter(grad_sums[1], ("dp", "fsdp"), scatter_dimension=0, tiled=True),
        lax.psum_scatter(grad_sums[2], ("dp", "fsdp"), scatter_dimension=0, tiled=True),
        lax.psum_scatter(grad_sums[3], ("dp", "fsdp"), scatter_dimension=0, tiled=True),
        lax.psum_scatter(grad_sums[4], ("dp", "fsdp"), scatter_dimension=0, tiled=True),
        lax.psum_scatter(grad_sums[5], ("dp", "fsdp"), scatter_dimension=0, tiled=True),
        lax.psum_scatter(grad_sums[6], ("dp", "fsdp"), scatter_dimension=0, tiled=True),
        lax.psum_scatter(grad_sums[7], ("dp", "fsdp"), scatter_dimension=0, tiled=True),
        lax.psum_scatter(grad_sums[8], ("dp", "fsdp"), scatter_dimension=0, tiled=True),
        lax.psum_scatter(grad_sums[9], ("dp", "fsdp"), scatter_dimension=0, tiled=True),
        lax.psum_scatter(grad_sums[10], ("dp", "fsdp"), scatter_dimension=0, tiled=True),
        lax.psum_scatter(grad_sums[11], ("dp", "fsdp"), scatter_dimension=0, tiled=True),
        lax.psum_scatter(grad_sums[12], ("dp", "fsdp"), scatter_dimension=0, tiled=True),
        lax.psum_scatter(grad_sums[13], ("dp", "fsdp"), scatter_dimension=0, tiled=True),
        lax.psum_scatter(grad_sums[14], ("dp", "fsdp"), scatter_dimension=0, tiled=True),
        lax.psum_scatter(grad_sums[15], ("dp", "fsdp"), scatter_dimension=0, tiled=True),
        lax.psum_scatter(grad_sums[16], ("dp", "fsdp"), scatter_dimension=0, tiled=True),
        lax.psum_scatter(grad_sums[17], ("dp", "fsdp"), scatter_dimension=0, tiled=True),
    )
    class_total = lax.psum(class_sum, ("dp", "fsdp"))
    return (
        jnp.concatenate(out_list, axis=0),
        jnp.concatenate(logit_list, axis=0),
        jnp.concatenate(grad_list, axis=0),
        owned[0],
        owned[1],
        owned[2],
        owned[3],
        owned[4],
        owned[5],
        owned[6],
        owned[7],
        owned[8],
        owned[9],
        owned[10],
        owned[11],
        owned[12],
        owned[13],
        owned[14],
        owned[15],
        owned[16],
        owned[17],
        class_total,
    )


BF = jnp.bfloat16
F32 = jnp.float32
MESH = pl.DeviceIdType.MESH
ANY = pl.BlockSpec(memory_space=pl.ANY)
SMEM = pl.BlockSpec(memory_space=pltpu.SMEM)
ZS = 4
CLASS_ROWS, B_QUERY, B_VALUE, B_OUT, GAIN1, SHIFT1, B_OUTER, GAIN2, SHIFT2, B_POOL = (0, 3, 4, 5, 6, 7, 8, 9, 10, 11)
VEC_ROWS = 16
KB, K0, K1, KF, KS, KZ, KE, KT = range(8)


def nn(a, b):
    return lax.dot_general(a, b, (((1,), (0,)), ((), ())), preferred_element_type=F32)


def nt(a, b):
    return lax.dot_general(a, b, (((1,), (1,)), ((), ())), preferred_element_type=F32)


def tn(a, b):
    return lax.dot_general(a, b, (((0,), (0,)), ((), ())), preferred_element_type=F32)


def my_place():
    dp, fs = lax.axis_index("dp"), lax.axis_index("fsdp")
    return dp // 2, lax.rem(dp, 2), fs // 2, lax.rem(fs, 2)


def device_at(z, y, x, c):
    return (z * 2 + y, x * 2 + c)


def meet(partners):
    barrier = pltpu.get_barrier_semaphore()
    for partner in partners:
        pl.semaphore_signal(barrier, inc=1, device_id=partner, device_id_type=MESH)
    pl.semaphore_wait(barrier, len(partners))


def all_partners(z, y, x, c):
    found = [device_at(lax.rem(z + k, ZS), y, x, c) for k in range(1, ZS)]
    found.append(device_at(z, 1 - y, x, c))
    found.append(device_at(z, y, 1 - x, c))
    found.append(device_at(z, y, x, 1 - c))
    found.append(device_at(z, y, 1 - x, 1 - c))
    return found


def group_partner(k, x, c):
    return (1 - x if k >= 2 else x, 1 - c if k % 2 == 1 else c)


def doc_ends(lens_ref):
    ends = []
    total = 0
    for d in range(lens_ref.shape[1]):
        total = total + lens_ref[lax.axis_index("fsdp"), d]
        ends.append(total)
    return ends


def doc_starts(lens_ref):
    return [0] + doc_ends(lens_ref)[:-1]


def doc_numbers(places, ends):
    number = jnp.zeros(places.shape, jnp.int32)
    for end in ends:
        number = number + (places >= end).astype(jnp.int32)
    return number


def gather_tools(plan, orders, view, own_block, keep_sem, send_sem, recv_sem, other=None):
    z, y, x, c = my_place()
    everything = slice(None)

    def along(a, axis):
        return device_at(z, 1 - y, x, c) if orders[a][axis] == "y" else device_at(z, y, 1 - x, c)

    def copy_of(a, number):
        core = device_at(z, y, x, 1 - c)
        first_other = (1 - y, x) if orders[a][0] == "y" else (y, 1 - x)
        if number < 3:
            source, target = own_block(a), view(a, (z, y, x, c))
            device = device_at(lax.rem(z + number + 1, ZS), y, x, c)
        elif number < 6:
            source = target = view(a, (everything, y, x, c))
            device = (along(a, 0), along(a, 1), core)[number - 3]
        elif number < 8:
            source = target = view(a, (everything, first_other[0], first_other[1], c))
            device = along(a, 1) if number == 6 else core
        else:
            if orders[a][1] == "y":
                source = target = view(a, (everything, 1 - y, everything, c))
            else:
                source = target = view(a, (everything, everything, 1 - x, c))
            device = core
        return pltpu.make_async_remote_copy(
            src_ref=source,
            dst_ref=target,
            send_sem=send_sem.at[a, number],
            recv_sem=recv_sem.at[a, number],
            device_id=device,
            device_id_type=MESH,
        )

    def keep(a):
        return pltpu.make_async_copy(own_block(a), view(a, (z, y, x, c)), keep_sem.at[a])

    def take_up(point):
        for kind, a in plan.get(point, ()):
            if kind == KB:
                for number in (1, 0, 2):
                    copy_of(a, number).start()
                keep(a).start()
            elif kind == KZ:
                for number in (0, 1, 2):
                    copy_of(a, number).wait_recv()
                keep(a).wait()
                for number in (3, 4, 5):
                    copy_of(a, number).start()
            elif kind == KF:
                copy_of(a, 3).wait_recv()
                for number in (6, 7):
                    copy_of(a, number).start()
            elif kind == KS:
                copy_of(a, 4).wait_recv()
                copy_of(a, 6).wait_recv()
                copy_of(a, 8).start()
            elif kind == KT:
                other(a)
            else:
                for number in (5, 7, 8):
                    copy_of(a, number).wait_recv()

    def all_sent():
        for a in range(len(orders)):
            for number in range(9):
                copy_of(a, number).wait_send()

    return take_up, all_sent


GATHER_PIECES = ((1, 0, 1, "rows"), (0, 0, 2, "columns"), (0, 1, 2, "columns"), (2, 0, 2, "rows"), (2, 1, 2, "rows"))
GATHER_ORDERS = ("xy", "xy", "yx", "xy", "yx", "xy", "yx", "xy")
GATHER_PLAN = {
    -1: (
        (KB, 0), (KT, 0), (KZ, 0), (KB, 1), (KB, 2), (KT, 1), (KB, 3), (KB, 4), (KB, 5), (KF, 0), (KT, 2), (KS, 0), (KB, 6), (KZ, 1),
        (KT, 3), (KZ, 2), (KZ, 3), (KE, 0),
    ),
    0: ((KB, 7),),
    1: ((KF, 1), (KF, 2), (KF, 3), (KZ, 4)),
    3: ((KS, 1), (KS, 2), (KZ, 5), (KS, 3), (KE, 1)),
    4: ((KZ, 6), (KE, 2), (KE, 3), (KF, 4)),
    5: ((KF, 5),),
    7: ((KZ, 7),),
    8: ((KS, 4), (KF, 6)),
    9: ((KS, 5), (KE, 4), (KF, 7), (KE, 5)),
    10: ((KS, 6),),
    11: ((KS, 7), (KE, 6)),
    12: ((KE, 7),),
}
DENSE_ARRAYS = 3
VECTORS = 9


def part_of(piece, block):
    _, which, count, along = piece
    rows, columns = block
    if along == "rows":
        return (which * (rows // count), rows // count), (0, columns)
    return (0, rows), (which * (columns // count), columns // count)


def key_marks(length, ends):
    number = doc_numbers(lax.broadcasted_iota(jnp.int32, (length, 1), 0), ends)
    lane = lax.broadcasted_iota(jnp.int32, (length, 128), 1)
    return jnp.where(lane == number, 1.0, 0.0).astype(BF)


def query_marks(at, count, ends):
    number = doc_numbers(lax.broadcasted_iota(jnp.int32, (count, 1), 0) + at, ends)
    lane = lax.broadcasted_iota(jnp.int32, (count, 128), 1)
    return jnp.where(lane == number, 0.0, -1000000000.0).astype(BF)


def attend_kernel(groups, *refs):
    lens_ref, tokens_ref, class_ref = refs[:3]
    vectors, b_inner_ref, (wq_ref, wk_ref, wv_ref) = refs[3 : 3 + VECTORS], refs[3 + VECTORS], refs[4 + VECTORS : 7 + VECTORS]
    refs = refs[7 + VECTORS :]
    shards, refs = refs[:DENSE_ARRAYS], refs[DENSE_ARRAYS:]
    q_ref, k_ref, v_ref, att_ref, lse_ref, w_ref, vec_ref, rows_ref = refs[:8]
    wholes = refs[8 : 8 + DENSE_ARRAYS]
    refs = refs[8 + DENSE_ARRAYS :]
    x_ref, vt_ref, marked_ref, qkv_shard, qkv_ref, tab_ref, tab_in_ref = refs[:7]
    local_sem, row_send, row_recv, tab_send, tab_recv, send_sem, recv_sem = refs[7:14]
    own = refs[14 : 14 + DENSE_ARRAYS]
    length, width = q_ref.shape
    chunk = 256
    points = length // chunk
    heads = width // HEAD_DIM
    items = groups + len(GATHER_PIECES)
    group = pl.program_id(0)
    z, y, x, c = my_place()
    mine = x * 2 + c

    def row_copy(k):
        px, pc = group_partner(k, x, c)
        return pltpu.make_async_remote_copy(
            src_ref=tokens_ref.at[px * 2 + pc],
            dst_ref=x_ref.at[mine],
            send_sem=row_send.at[k - 1],
            recv_sem=row_recv.at[k - 1],
            device_id=device_at(z, y, px, pc),
            device_id_type=MESH,
        )

    def row_own():
        return pltpu.make_async_copy(tokens_ref.at[mine], x_ref.at[mine], local_sem.at[0])

    def rows_out():
        return pltpu.make_async_copy(x_ref, rows_ref, local_sem.at[1])

    def table_copy(level):
        if level < 3:
            source, device = tab_ref.at[0], device_at(lax.rem(z + level + 1, ZS), y, x, c)
        else:
            source = tab_ref.at[level - 2]
            device = (device_at(z, y, 1 - x, c), device_at(z, 1 - y, x, c), device_at(z, y, x, 1 - c))[level - 3]
        return pltpu.make_async_remote_copy(
            src_ref=source,
            dst_ref=tab_in_ref.at[level],
            send_sem=tab_send.at[level],
            recv_sem=tab_recv.at[level],
            device_id=device,
            device_id_type=MESH,
        )

    def array_of(a):
        if a < groups:
            return qkv_ref.at[a], qkv_shard.at[a], None
        piece = GATHER_PIECES[a - groups]
        return wholes[piece[0]], own[piece[0]], part_of(piece, own[piece[0]].shape)

    def view(a, where):
        ref, _, part = array_of(a)
        if part is None:
            return ref.at[where]
        (r0, rows), (c0, columns) = part
        return ref.at[where + (pl.ds(r0, rows), pl.ds(c0, columns))]

    def own_block(a):
        _, ref, part = array_of(a)
        if part is None:
            return ref
        (r0, rows), (c0, columns) = part
        return ref.at[pl.ds(r0, rows), pl.ds(c0, columns)]

    def table_level(level):
        if level == 0:
            for k in (0, 1, 2):
                table_copy(k).wait_recv()
            tab_ref[1] = (tab_ref[0] + tab_in_ref[0]) + (tab_in_ref[1] + tab_in_ref[2])
        else:
            table_copy(level + 2).wait_recv()
            tab_ref[level + 1] = tab_ref[level] + tab_in_ref[level + 2]
        if level < 3:
            table_copy(level + 3).start()
        else:
            vec_ref[...] = tab_ref[4]

    take_up, all_sent = gather_tools(
        GATHER_PLAN, GATHER_ORDERS, view, own_block, local_sem.at[pl.ds(2, items)], send_sem, recv_sem, table_level
    )

    @pl.when(group == 0)
    def _():
        device = ((z * 2 + y) * 2 + x) * 2 + c
        full = tab_ref.shape[2]

        def spread(values, at):
            n = values.shape[1]
            here = lax.broadcasted_iota(jnp.int32, (n, full), 1) - at == lax.broadcasted_iota(jnp.int32, (n, full), 0)
            return nn(values.astype(BF), jnp.where(here, 1.0, 0.0).astype(BF))

        share = class_ref.shape[1]
        tab_ref[0, 0:CLASSES] = spread(class_ref[...], device * share)
        for j, ref in enumerate(vectors):
            tab_ref[0, CLASSES + j : CLASSES + j + 1] = spread(ref[...], device * share)
        per_row = full // b_inner_ref.shape[1]
        inner_bias = spread(b_inner_ref[...], lax.rem(device, per_row) * b_inner_ref.shape[1])
        for j in range(4):
            tab_ref[0, 12 + j : 13 + j] = jnp.where(device // per_row == j, inner_bias, 0.0)
        for g in range(groups):
            for j, ref in enumerate((wq_ref, wk_ref, wv_ref)):
                qkv_shard[g, :, j * width : (j + 1) * width] = ref[:, g * width : (g + 1) * width].astype(BF)
        for target, ref in zip(own, shards):
            target[...] = ref[...].astype(BF)
        meet(all_partners(z, y, x, c))
        for level in (1, 0, 2):
            table_copy(level).start()
        for k in (3, 2, 1):
            row_copy(k).start()
        row_own().start()
        take_up(-1)
        row_own().wait()
        for k in (1, 2, 3):
            row_copy(k).wait_recv()
        rows_out().start()

    tokens = x_ref[...].reshape(length, x_ref.shape[2])
    weights = qkv_ref[group].astype(F32).reshape(x_ref.shape[2], 3 * width).astype(BF)
    w_ref[...] = weights
    bias = tab_ref[4, B_QUERY : B_QUERY + 2, pl.ds(pl.multiple_of(group * width, width), width)]
    q_ref[...] = (nn(tokens, weights[:, :width]) + bias[0:1]).astype(BF)
    keys = nn(tokens, weights[:, width : 2 * width]).astype(BF)
    k_ref[...] = keys
    values = (nn(tokens, weights[:, 2 * width :]) + bias[1:2]).astype(BF)
    v_ref[...] = values
    vt_ref[...] = values.astype(F32).T.astype(BF)
    ends = doc_ends(lens_ref)
    marks = key_marks(length, ends)
    for pair in range(width // 128):
        marked_ref[pair] = jnp.concatenate([keys[:, pair * 128 : (pair + 1) * 128], marks], axis=1)
    lane_half = lax.broadcasted_iota(jnp.int32, (1, 128), 1) // HEAD_DIM

    def step(i, carry):
        for point in range(groups * points):
            if point in GATHER_PLAN:

                @pl.when((group == point // points) & (i == point % points))
                def _(point=point):
                    take_up(point)

        at = pl.multiple_of(i * chunk, chunk)
        ours = query_marks(at, chunk, ends)
        scaled = q_ref[pl.ds(at, chunk), :] * jnp.asarray(0.125, BF)
        mixed = []
        for h in range(heads):
            two = scaled[:, h // 2 * 128 : (h // 2 + 1) * 128]
            own_q = jnp.concatenate([jnp.where(lane_half == h % 2, two, jnp.zeros_like(two)), ours], axis=1)
            blocks = [nt(marked_ref[h // 2, s : s + chunk, :], own_q) for s in range(0, length, chunk)]
            peak = functools.reduce(jnp.maximum, [jnp.max(b, axis=0, keepdims=True) for b in blocks])
            exps = [jnp.exp(b - peak) for b in blocks]
            total = functools.reduce(jnp.add, [jnp.sum(e, axis=0, keepdims=True) for e in exps])
            scale = 1.0 / total
            probs = jnp.concatenate([(e * scale).astype(BF) for e in exps], axis=0)
            mixed.append(nn(vt_ref[h * HEAD_DIM : (h + 1) * HEAD_DIM, :], probs))
            lse_ref[0, h : h + 1, pl.ds(at, chunk)] = peak + jnp.log(total)
        att_ref[pl.ds(at, chunk), :] = jnp.concatenate(mixed, axis=0).T.astype(BF)
        return carry

    lax.fori_loop(0, points, step, 0)

    @pl.when(group == groups - 1)
    def _():
        take_up(groups * points)
        all_sent()
        for level in range(6):
            table_copy(level).wait_send()
        for k in range(1, 4):
            row_copy(k).wait_send()
        rows_out().wait()


def attend(lens, tokens, class_shard, vectors, b_inner, qkv_shards, shards):
    seqs, local_len, width = tokens.shape
    length = seqs * local_len
    group = 256
    groups = width // group
    share = qkv_shards[0].shape[0]
    hbm = pl.BlockSpec(memory_space=pl.ANY)
    part = pl.BlockSpec((length, group), lambda g: (0, g))
    once = pl.Buffered(buffer_count=1)
    items = groups + len(GATHER_PIECES)

    def fixed(shape):
        return pl.BlockSpec(shape, lambda g: (0,) * len(shape), pipeline_mode=once)

    lead = (ZS, 2, 2, 2)
    return pl.pallas_call(
        functools.partial(attend_kernel, groups),
        grid=(groups,),
        out_shape=[jax.ShapeDtypeStruct((length, width), BF)] * 4
        + [
            jax.ShapeDtypeStruct((groups, 8, length), F32),
            jax.ShapeDtypeStruct((width, 3 * width), BF),
            jax.ShapeDtypeStruct((VEC_ROWS, width), F32),
            jax.ShapeDtypeStruct(tokens.shape, BF),
        ]
        + [jax.ShapeDtypeStruct(lead + s.shape, BF) for s in shards],
        in_specs=[SMEM, hbm, fixed(class_shard.shape)]
        + [fixed(v.shape) for v in vectors]
        + [fixed(b_inner.shape)]
        + [fixed(s.shape) for s in qkv_shards]
        + [fixed(s.shape) for s in shards],
        out_specs=[part] * 4
        + [
            pl.BlockSpec((1, 8, length), lambda g: (g, 0, 0)),
            pl.BlockSpec((width, 3 * group), lambda g: (0, g)),
            pl.BlockSpec((VEC_ROWS, width), lambda g: (0, 0)),
            hbm,
        ]
        + [hbm] * DENSE_ARRAYS,
        scratch_shapes=[
            pltpu.VMEM(tokens.shape, BF),
            pltpu.VMEM((group, length), BF),
            pltpu.VMEM((group // 128, length, 256), BF),
            pltpu.VMEM((groups, share, 3 * group), BF),
            pltpu.VMEM((groups,) + lead + (share, 3 * group), BF),
            pltpu.VMEM((5, VEC_ROWS, width), F32),
            pltpu.VMEM((6, VEC_ROWS, width), F32),
            pltpu.SemaphoreType.DMA((2 + items,)),
            pltpu.SemaphoreType.DMA((3,)),
            pltpu.SemaphoreType.DMA((3,)),
            pltpu.SemaphoreType.DMA((6,)),
            pltpu.SemaphoreType.DMA((6,)),
            pltpu.SemaphoreType.DMA((items, 9)),
            pltpu.SemaphoreType.DMA((items, 9)),
        ]
        + [pltpu.VMEM(s.shape, BF) for s in shards],
        compiler_params=pltpu.CompilerParams(
            collective_id=1, has_side_effects=True, vmem_limit_bytes=60 * 2**20
        ),
        name="attend",
    )(lens, tokens, class_shard, *vectors, b_inner, *qkv_shards, *shards)


DENSE = 4
DENSE_ITEMS = (
    (0, 0, 2, "columns", "yx"), (1, 0, 2, "rows", "xy"), (0, 1, 2, "columns", "yx"), (1, 1, 2, "rows", "xy"),
    (2, 0, 1, "rows", "yx"), (3, 0, 1, "rows", "yx"),
)
GROUP_ORDERS = ("yx", "xy", "yx")
SCATTER_PLAN = {
    -1: ((KB, 0),),
    0: ((KB, 1),),
    1: ((K0, 0), (K0, 1), (KB, 2), (K1, 0), (KB, 3), (K1, 1)),
    2: ((KB, 4),),
    3: ((K0, 2), (K0, 3), (KB, 5), (K1, 2), (K1, 3)),
    4: ((KF, 0), (KF, 1), (KB, 6)),
    6: ((K0, 4), (K1, 4)),
    8: ((KF, 2), (KF, 3), (KS, 0), (KS, 1), (K0, 5), (KB, 7), (K1, 5)),
    9: ((KF, 4), (K0, 7), (K1, 7)),
    10: ((K0, 6), (K1, 6)),
    11: ((KS, 2),),
    12: (
        (KS, 4), (KT, 0), (KF, 7), (KS, 3), (KZ, 0), (KZ, 1), (KF, 5), (K0, 8), (K1, 8), (KT, 1), (KF, 6), (KZ, 2), (KS, 7), (KZ, 4),
        (KS, 5), (KF, 8), (KT, 2), (KS, 6), (KZ, 3), (KZ, 7), (KZ, 5), (KS, 8), (KZ, 6), (KT, 3), (KZ, 8),
    ),
}
PIECES = len(DENSE_ITEMS)


def order_of(a):
    return DENSE_ITEMS[a][4] if a < PIECES else GROUP_ORDERS[a - PIECES]


def cut_of(a, block):
    _, which, count, along, _ = DENSE_ITEMS[a]
    rows, columns = block
    if along == "rows":
        return (which * (rows // count), rows // count), (0, columns)
    return (0, rows), (which * (columns // count), columns // count)


TABLE_ROWS = 24


def attend_back_kernel(groups, *refs):
    items = PIECES + groups
    lens_ref, x_ref, w_ref, q_ref, k_ref, v_ref, att_ref, datt_ref, lse_ref, start_ref = refs[:10]
    small_a_ref, small_b_ref, bi_ref, logit_ref = refs[10:14]
    parts = refs[14 : 14 + DENSE]
    back_ref, logits_ref, small_ref = refs[18:21]
    dense_outs, group_outs = refs[21 : 21 + DENSE], refs[21 + DENSE : 24 + DENSE]
    rest = refs[24 + DENSE :]
    xt_ref, kt_ref, marked_ref, dot_ref, dq_ref, dk_ref, dv_ref, acc_ref, dx_ref, bias_ref, dw_ref, tab_ref, tab_in_ref = rest[:13]
    local_sem, row_send, row_recv, tab_send, tab_recv, send_sem, recv_sem = rest[13:20]
    rest = rest[20:]
    keeps, rest = rest[:PIECES], rest[PIECES:]
    firsts, seconds, thirds, fourths = (rest[j * items : (j + 1) * items] for j in range(4))

    length, width = q_ref.shape
    chunk = 256
    points = length // chunk
    heads = width // HEAD_DIM
    group = pl.program_id(0)
    z, y, x, c = my_place()
    mine = x * 2 + c

    def axes(a):
        return (y, x) if order_of(a)[0] == "y" else (x, y)

    def device_along(axis):
        return device_at(z, 1 - y, x, c) if axis == "y" else device_at(z, y, 1 - x, c)

    def half(a, ref, place):
        return ref.at[:, place] if order_of(a)[0] == "y" else ref.at[:, :, place]

    def whole_of(a, core):
        if a >= PIECES:
            return dw_ref.at[a - PIECES].at[:, :, :, core]
        array = DENSE_ITEMS[a][0]
        (r0, rows), (c0, columns) = cut_of(a, parts[array].shape[-2:])
        return parts[array].at[:, :, :, core, pl.ds(r0, rows), pl.ds(c0, columns)]

    def kept(a):
        return keeps[a] if a < PIECES else whole_of(a, c)

    def load(a, turn):
        place = 1 - axes(a)[0] if turn == 0 else axes(a)[0]
        return pltpu.make_async_copy(
            half(a, whole_of(a, c), place), half(a, keeps[a], place), local_sem.at[a, turn]
        )

    def copy_of(a, number):
        at, other = axes(a)
        if number < 2:
            place = 1 - at if number == 0 else at
            source, target = half(a, whole_of(a, 1 - c), place), half(a, firsts[a], place)
            device = device_at(z, y, x, 1 - c)
        elif number == 2:
            source, target = half(a, kept(a), 1 - at), seconds[a]
            device = device_along(order_of(a)[0])
        elif number == 3:
            source, target = half(a, kept(a), at).at[:, 1 - other], thirds[a]
            device = device_along(order_of(a)[1])
        else:
            there = lax.rem(z + number - 3, ZS)
            source, target = half(a, kept(a), at).at[:, other].at[there], fourths[a].at[number - 4]
            device = device_at(there, y, x, c)
        return pltpu.make_async_remote_copy(
            src_ref=source,
            dst_ref=target,
            send_sem=send_sem.at[a, number],
            recv_sem=recv_sem.at[a, number],
            device_id=device,
            device_id_type=MESH,
        )

    def add_into(target, source):
        lead = target.shape[:-2]
        total = functools.reduce(lambda p, q: p * q, lead, 1)

        def step(i, carry):
            where = []
            for size in reversed(lead):
                where.append(lax.rem(i, size))
                i = i // size
            where = tuple(reversed(where))
            target[where] = target[where] + source[where]
            return carry

        lax.fori_loop(0, total, step, 0, unroll=True)

    def begin(a):
        if a < PIECES:
            load(a, 0).start()
            load(a, 1).start()
        copy_of(a, 0).start()
        copy_of(a, 1).start()

    def after_core(a, turn):
        place = 1 - axes(a)[0] if turn == 0 else axes(a)[0]
        if a < PIECES:
            load(a, turn).wait()
        copy_of(a, turn).wait_recv()
        add_into(half(a, kept(a), place), half(a, firsts[a], place))
        if turn == 0:
            copy_of(a, 2).start()

    def after_first(a):
        at, other = axes(a)
        ours = half(a, kept(a), at)
        copy_of(a, 2).wait_recv()
        add_into(ours.at[:, 1 - other], seconds[a].at[:, 1 - other])
        copy_of(a, 3).start()
        add_into(ours.at[:, other], seconds[a].at[:, other])

    def after_second(a):
        at, other = axes(a)
        copy_of(a, 3).wait_recv()
        add_into(half(a, kept(a), at).at[:, other], thirds[a])
        for number in (5, 4, 6):
            copy_of(a, number).start()

    def finish(a):
        at, other = axes(a)
        for number in (4, 5, 6):
            copy_of(a, number).wait_recv()
        ours = half(a, kept(a), at).at[:, other]
        total = (
            ours[z].astype(F32)
            + fourths[a][0].astype(F32)
            + fourths[a][1].astype(F32)
            + fourths[a][2].astype(F32)
        )
        if a < PIECES:
            out = dense_outs[DENSE_ITEMS[a][0]]
            (r0, rows), (c0, columns) = cut_of(a, out.shape)
            out[r0 : r0 + rows, c0 : c0 + columns] = total
        else:
            s = (a - PIECES) * width
            for j, out in enumerate(group_outs):
                out[:, s : s + width] = total[:, j * width : (j + 1) * width]

    def row_copy(which, k):
        px, pc = group_partner(k, x, c)
        if which == 0:
            source, target = dx_ref.at[px * 2 + pc], back_ref.at[mine]
        else:
            source, target = logit_ref, logits_ref.at[mine]
        return pltpu.make_async_remote_copy(
            src_ref=source,
            dst_ref=target,
            send_sem=row_send.at[which, k - 1],
            recv_sem=row_recv.at[which, k - 1],
            device_id=device_at(z, y, px, pc),
            device_id_type=MESH,
        )

    def row_own(which):
        if which == 0:
            source, target = dx_ref.at[mine], back_ref.at[mine]
        else:
            source, target = logit_ref, logits_ref.at[mine]
        return pltpu.make_async_copy(source, target, local_sem.at[PIECES, which])

    def table_copy(level):
        if level < 3:
            source, target = tab_ref.at[level], tab_in_ref.at[level]
            device = (
                device_at(z, y, x, 1 - c), device_at(z, 1 - y, x, c), device_at(z, y, 1 - x, c)
            )[level]
        else:
            source, target = tab_ref.at[3], tab_in_ref.at[3 + z]
            device = device_at(lax.rem(z + level - 2, ZS), y, x, c)
        return pltpu.make_async_remote_copy(
            src_ref=source,
            dst_ref=target,
            send_sem=tab_send.at[level],
            recv_sem=tab_recv.at[level],
            device_id=device,
            device_id_type=MESH,
        )

    def table_wait(level):
        if level < 3:
            table_copy(level).wait_recv()
        else:
            slot = tab_in_ref.at[3 + lax.rem(z + ZS - (level - 2), ZS)]
            pltpu.make_async_remote_copy(
                src_ref=slot,
                dst_ref=slot,
                send_sem=tab_send.at[level],
                recv_sem=tab_recv.at[level],
                device_id=device_at(lax.rem(z + level - 2, ZS), y, x, c),
                device_id_type=MESH,
            ).wait_recv()

    def table_level(level):
        if level == 3:
            for last in (3, 4, 5):
                table_wait(last)
            table = (tab_in_ref[3] + tab_in_ref[4]) + (tab_in_ref[5] + tab_in_ref[6])
            device = ((z * 2 + y) * 2 + x) * 2 + c
            full = table.shape[1]
            row = lax.broadcasted_iota(jnp.int32, (full, 128), 0)
            lane = lax.broadcasted_iota(jnp.int32, (full, 128), 1)

            def own_lanes(values, size, at):
                chosen = jnp.where((row == at + lane) & (lane < size), 1.0, 0.0)
                return lax.dot_general(
                    values, chosen, (((1,), (0,)), ((), ())), preferred_element_type=F32, precision=lax.Precision.HIGHEST
                )

            per_row = full * 4 // (8 * ZS)
            small_ref[0:TABLE_ROWS] = own_lanes(table, full // (8 * ZS), device * (full // (8 * ZS)))
            inner_bias = own_lanes(table, per_row, lax.rem(device, full // per_row) * per_row)
            for j in range(4):

                @pl.when(device // (full // per_row) == j)
                def _(j=j):
                    small_ref[TABLE_ROWS : TABLE_ROWS + 1] = inner_bias[12 + j : 13 + j]

            small_ref[TABLE_ROWS + 1 : TABLE_ROWS + 2] = table[16:17, 0:128]
            return
        table_wait(level)
        tab_ref[level + 1] = tab_ref[level] + tab_in_ref[level]
        if level < 2:
            table_copy(level + 1).start()
        else:
            tab_in_ref[3 + z] = tab_ref[3]
            for nxt in (4, 3, 5):
                table_copy(nxt).start()

    def take_up(point):
        for kind, a in SCATTER_PLAN.get(point, ()):
            if kind == KB:
                begin(a)
            elif kind == K0 or kind == K1:
                after_core(a, 0 if kind == K0 else 1)
            elif kind == KF:
                after_first(a)
            elif kind == KS:
                after_second(a)
            elif kind == KZ:
                finish(a)
            else:
                table_level(a)

    @pl.when(group == 0)
    def _():
        meet(all_partners(z, y, x, c))
        take_up(-1)
        for k in range(1, 4):
            row_copy(1, k).start()
        row_own(1).start()
        xt_ref[...] = x_ref[...].astype(F32).T.astype(BF)
        acc_ref[...] = start_ref[...]

    kt_ref[...] = k_ref[...].astype(F32).T.astype(BF)
    dot_ref[...] = (datt_ref[...].astype(F32) * att_ref[...].astype(F32)).T
    dk_ref[...] = jnp.zeros_like(dk_ref)
    dv_ref[...] = jnp.zeros_like(dv_ref)
    ends = doc_ends(lens_ref)
    marks = key_marks(length, ends)
    for pair in range(width // 128):
        marked_ref[pair] = jnp.concatenate([k_ref[:, pair * 128 : (pair + 1) * 128], marks], axis=1)
    lane_half = lax.broadcasted_iota(jnp.int32, (1, 128), 1) // HEAD_DIM
    lane_head = lax.broadcasted_iota(jnp.int32, (1, width), 1) // HEAD_DIM

    def step(i, carry):
        for point in range(groups * points):

            @pl.when((group == point // points) & (i == point % points))
            def _(point=point):
                take_up(point)

        at = pl.multiple_of(i * chunk, chunk)
        ours = query_marks(at, chunk, ends)
        scaled = q_ref[pl.ds(at, chunk), :] * jnp.asarray(0.125, BF)
        given = datt_ref[pl.ds(at, chunk), :]
        own_q = [jnp.where(lane_head == h, scaled, jnp.zeros_like(scaled)) for h in range(heads)]
        own_d = [jnp.where(lane_head == h, given, jnp.zeros_like(given)) for h in range(heads)]
        all_probs = [[] for _ in range(length // chunk)]
        all_grads = [[] for _ in range(length // chunk)]
        for h in range(heads):
            lse = lse_ref[0, h : h + 1, pl.ds(at, chunk)]
            dots = jnp.sum(
                dot_ref[h * HEAD_DIM : (h + 1) * HEAD_DIM, pl.ds(at, chunk)], axis=0, keepdims=True
            )
            two = scaled[:, h // 2 * 128 : (h // 2 + 1) * 128]
            marked_q = jnp.concatenate([jnp.where(lane_half == h % 2, two, jnp.zeros_like(two)), ours], axis=1)
            for j in range(length // chunk):
                s = j * chunk
                scores = nt(marked_ref[h // 2, s : s + chunk, :], marked_q)
                probs = jnp.exp(scores - lse)
                grad_probs = nt(v_ref[s : s + chunk, :], own_d[h])
                all_grads[j].append((probs * (grad_probs - dots)).astype(BF))
                all_probs[j].append(probs.astype(BF))
        stacked_q = jnp.concatenate(own_q, axis=0)
        stacked_d = jnp.concatenate(own_d, axis=0)
        for j in range(length // chunk):
            s = j * chunk
            dk_ref[s : s + chunk, :] += nn(jnp.concatenate(all_grads[j], axis=1), stacked_q)
            dv_ref[s : s + chunk, :] += nn(jnp.concatenate(all_probs[j], axis=1), stacked_d)
        mixed = []
        for h in range(heads):
            column = jnp.concatenate([all_grads[j][h] for j in range(length // chunk)], axis=0)
            mixed.append(nn(kt_ref[h * HEAD_DIM : (h + 1) * HEAD_DIM, :], column))
        dq_ref[pl.ds(at, chunk), :] = (jnp.concatenate(mixed, axis=0).T * 0.125).astype(BF)
        return carry

    lax.fori_loop(0, points, step, 0)
    xt = xt_ref[...]
    grads = (dq_ref[...], dk_ref[...].astype(BF), dv_ref[...].astype(BF))
    block = dw_ref.shape[1:6]
    for j, grad in enumerate(grads):
        dw_ref[group, :, :, :, :, :, j * width : (j + 1) * width] = nn(xt, grad).reshape(block + (width,)).astype(BF)
    bias_ref[group, 0:1, :] = jnp.sum(grads[0].astype(F32), axis=0, keepdims=True)
    bias_ref[group, 1:2, :] = jnp.sum(grads[2].astype(F32), axis=0, keepdims=True)

    @pl.when(group < groups - 1)
    def _():
        total = acc_ref[...]
        for j, grad in enumerate(grads):
            total = total + nt(grad, w_ref[:, j * width : (j + 1) * width])
        acc_ref[...] = total

    @pl.when(group == groups - 1)
    def _():
        begin(items - 1)
        size = dx_ref.shape[1]
        for k in (3, 2, 1, 0):
            px, pc = group_partner(k, x, c)
            block = px * 2 + pc
            here = pl.ds(pl.multiple_of(block * size, size), size)
            total = acc_ref[here, :]
            for j, ref in enumerate((dq_ref, dk_ref, dv_ref)):
                total = total + nt(ref[here, :].astype(BF), w_ref[:, j * width : (j + 1) * width])
            dx_ref[block] = total.astype(BF)
            if k == 0:
                row_own(0).start()
            else:
                row_copy(0, k).start()
        tab_ref[0, 0:CLASSES] = small_a_ref[0:CLASSES]
        for g in range(groups):
            tab_ref[0, B_QUERY : B_QUERY + 2, g * width : (g + 1) * width] = bias_ref[g, 0:2, :]
        for row, (ref, at) in {
            B_OUT: (small_b_ref, 3), GAIN1: (small_b_ref, 4), SHIFT1: (small_b_ref, 5), B_OUTER: (small_b_ref, 0),
            GAIN2: (small_b_ref, 1), SHIFT2: (small_b_ref, 2), B_POOL: (small_a_ref, 16), 16: (small_a_ref, 17),
        }.items():
            tab_ref[0, row : row + 1] = ref[at : at + 1, :]
        full = small_a_ref.shape[1]
        for j in range(4):
            tab_ref[0, 12 + j : 13 + j] = bi_ref[:, j * full : (j + 1) * full]
        tab_ref[0, 17:TABLE_ROWS] = jnp.zeros((TABLE_ROWS - 17, full), F32)
        table_copy(0).start()
        take_up(groups * points)
        for a in range(items):
            for number in range(7):
                copy_of(a, number).wait_send()
        for level in range(6):
            table_copy(level).wait_send()
        for which in (0, 1):
            for k in range(1, 4):
                row_copy(which, k).wait_recv()
                row_copy(which, k).wait_send()
            row_own(which).wait()


def attend_back(lens, rows, w_groups, q, k, v, att, datt, lse, grad_pre, small_a, small_b, grad_b_inner, logit_block, parts):
    length, width = rows.shape
    group = 256
    groups = width // group
    local_len = length // 4
    share = width // (8 * ZS)
    once = pl.Buffered(buffer_count=1)
    whole = pl.BlockSpec((length, width), lambda g: (0, 0), pipeline_mode=once)
    part = pl.BlockSpec((length, group), lambda g: (0, g))
    blocks = [p.shape[1:] for p in parts]
    split = [p.reshape((ZS, 2, 2, 2) + b) for p, b in zip(parts, blocks)]
    shapes = [r for r in blocks]
    cuts = [cut_of(a, blocks[DENSE_ITEMS[a][0]]) for a in range(PIECES)]
    blocks = [(r[1], q[1]) for r, q in cuts] + [(share, 3 * group)] * groups
    hbm = pl.BlockSpec(memory_space=pl.ANY)

    def fixed(shape):
        return pl.BlockSpec(shape, lambda g: (0,) * len(shape))

    results = [(TABLE_ROWS + 8, 128)] + shapes + [(share, width)] * 3
    arriving = []
    for lead in ((ZS, 2, 2), (ZS, 2), (ZS,), (ZS - 1,)):
        arriving += [pltpu.VMEM(lead + b, BF) for b in blocks]
    items = len(blocks)
    return pl.pallas_call(
        functools.partial(attend_back_kernel, groups),
        grid=(groups,),
        out_shape=[
            jax.ShapeDtypeStruct((4, local_len, width), BF),
            jax.ShapeDtypeStruct((4,) + logit_block.shape, F32),
        ]
        + [jax.ShapeDtypeStruct(r, F32) for r in results],
        in_specs=[
            SMEM,
            whole,
            pl.BlockSpec((width, 3 * group), lambda g: (0, g)),
            part, part, part, part, part,
            pl.BlockSpec((1, 8, length), lambda g: (g, 0, 0)),
            whole,
            fixed(small_a.shape), fixed(small_b.shape), fixed(grad_b_inner.shape), hbm,
        ]
        + [hbm] * DENSE,
        out_specs=[hbm, hbm] + [fixed(r) for r in results],
        scratch_shapes=[
            pltpu.VMEM((width, length), BF),
            pltpu.VMEM((group, length), BF),
            pltpu.VMEM((group // 128, length, 256), BF),
            pltpu.VMEM((group, length), F32),
            pltpu.VMEM((length, group), BF),
            pltpu.VMEM((length, group), F32),
            pltpu.VMEM((length, group), F32),
            pltpu.VMEM((length, width), F32),
            pltpu.VMEM((4, local_len, width), BF),
            pltpu.VMEM((groups, 8, group), F32),
            pltpu.VMEM((groups, ZS, 2, 2, 2, share, 3 * group), BF),
            pltpu.VMEM((4, TABLE_ROWS, width), F32),
            pltpu.VMEM((3 + ZS, TABLE_ROWS, width), F32),
            pltpu.SemaphoreType.DMA((PIECES + 1, 2)),
            pltpu.SemaphoreType.DMA((2, 3)),
            pltpu.SemaphoreType.DMA((2, 3)),
            pltpu.SemaphoreType.DMA((6,)),
            pltpu.SemaphoreType.DMA((6,)),
            pltpu.SemaphoreType.DMA((items, 7)),
            pltpu.SemaphoreType.DMA((items, 7)),
        ]
        + [pltpu.VMEM((ZS, 2, 2) + b, BF) for b in blocks[:PIECES]]
        + arriving,
        compiler_params=pltpu.CompilerParams(
            collective_id=2, has_side_effects=True, vmem_limit_bytes=60 * 2**20
        ),
        name="attend_back",
    )(lens, rows, w_groups, q, k, v, att, datt, lse, grad_pre, small_a, small_b, grad_b_inner, logit_block, *split)


def row_copies(source_ref, target_ref, send_sem, recv_sem):
    z, y, x, c = my_place()
    copies = []
    for k in (3, 2, 1):
        px, pc = group_partner(k, x, c)
        copies.append(
            pltpu.make_async_remote_copy(
                src_ref=source_ref.at[px * 2 + pc],
                dst_ref=target_ref.at[x * 2 + c],
                send_sem=send_sem.at[k - 1],
                recv_sem=recv_sem.at[k - 1],
                device_id=device_at(z, y, px, pc),
                device_id_type=MESH,
            )
        )
    return copies, pltpu.make_async_copy(source_ref.at[x * 2 + c], target_ref.at[x * 2 + c], send_sem.at[3])


ROW_SEMAPHORES = [pltpu.SemaphoreType.DMA((4,)), pltpu.SemaphoreType.DMA((3,))]


def normal_parts(v):
    bell = jnp.exp(v * v * -0.5)
    t = 1.0 / (1.0 + jnp.abs(v) * 0.23164189)
    tail = t * (0.127414796 + t * (-0.142248368 + t * (0.710706870 + t * (-0.726576013 + t * 0.530702714)))) * bell
    return jnp.where(v >= 0.0, 1.0 - tail, tail), bell


def centered_parts(values):
    average = jnp.mean(values, axis=-1, keepdims=True)
    centered = values - average
    variance = jnp.mean(centered * centered, axis=-1, keepdims=True)
    inverse = lax.rsqrt(variance + 1e-06)
    return centered * inverse, inverse


def norm_back(grad, values, gain):
    hat, inverse = centered_parts(values)
    scaled = grad * gain
    mean_scaled = jnp.mean(scaled, axis=-1, keepdims=True)
    mean_cross = jnp.mean(scaled * hat, axis=-1, keepdims=True)
    back = (scaled - mean_scaled - hat * mean_cross) * inverse
    return back, jnp.sum(grad * hat, axis=0, keepdims=True), jnp.sum(grad, axis=0, keepdims=True)


MIDDLE_ORDERS = ("xy",)
MIDDLE_PLAN = {
    0: ((KB, 0),),
    2: ((KZ, 0),),
    5: ((KF, 0),),
    8: ((KS, 0),),
    14: ((KE, 0),),
}
COTANGENT_POINT = 3


def middle_kernel(tiles, *refs):
    (
        lens_ref, labels_ref, b_class_ref, cot_ref, x_ref, att_ref, w_inner_ref, w_out_ref, outer_hbm_ref, pool_shard_ref,
        vec_ref,
    ) = refs[:11]
    (
        low_ref, act_out_ref, outer_ref, inner_ref, dout_ref, datt_ref, gpre_ref, dpool_ref, small_a_ref, small_b_ref, bi_ref,
        logits_ref, layer_out_ref,
    ) = refs[11:24]
    (
        act_ref, dact_ref, pre_ref, summed_ref, dout_acc_ref, result_ref, cot_rows_ref, first_ref, picked_ref, own_pool, w_outer_ref, pool_ref,
        outer_sem, act_sem, keep_sem, send_sem, recv_sem, cot_send, cot_recv, lo_send, lo_recv,
    ) = refs[24:]
    step = pl.program_id(0)
    rows, full = x_ref.shape
    chunks = act_ref.shape[1] // full

    def view(a, where):
        return pool_ref.at[where]

    def own_block(a):
        return own_pool

    gather_up, all_sent = gather_tools(MIDDLE_PLAN, MIDDLE_ORDERS, view, own_block, keep_sem, send_sem, recv_sem)

    def take_up(point):
        if point in MIDDLE_PLAN or point == COTANGENT_POINT:

            @pl.when(step == point // 2)
            def _():
                gather_up(point)
                if point == COTANGENT_POINT:
                    copies, own = row_copies(cot_ref, cot_rows_ref, cot_send, cot_recv)
                    for copy in copies:
                        copy.start()
                    own.start()

    def outer_copy():
        return pltpu.make_async_copy(outer_hbm_ref, w_outer_ref, outer_sem.at[0])

    def act_copy(tile):
        where = pl.ds(tile * rows, rows)
        return pltpu.make_async_copy(act_ref.at[where], act_out_ref.at[where], act_sem.at[tile])

    def vec(row):
        return vec_ref[row : row + 1, :]

    @pl.when(step == 0)
    def _():
        outer_copy().start()
        own_pool[...] = pool_shard_ref[...].astype(BF)
        z, y, x, c = my_place()
        meet(all_partners(z, y, x, c))

    tile = lax.rem(step, tiles)
    here = pl.ds(pl.multiple_of(tile * rows, rows), rows)
    for point in range(0, 2 * tiles, 2):
        take_up(point)

    @pl.when(step < tiles)
    def _():
        pre = x_ref[...].astype(F32) + (nn(att_ref[...], w_out_ref[...]) + vec(B_OUT))
        pre_ref[here, :] = pre
        low = (centered_parts(pre)[0] * vec(GAIN1) + vec(SHIFT1)).astype(BF)
        low_ref[...] = low
        for j in range(chunks):
            if j == chunks // 2:
                for point in range(1, 2 * tiles, 2):
                    take_up(point)
            s = j * full
            hidden = nn(low, w_inner_ref[:, s : s + full]) + vec(12 + j)
            phi, bell = normal_parts(hidden)
            act_ref[here, s : s + full] = (hidden * phi).astype(BF)
            dact_ref[here, s : s + full] = (phi + hidden * bell * 0.3989422804014327).astype(BF)
        for t in range(tiles):

            @pl.when(step == t)
            def _(t=t):
                act_copy(t).start()

    for point in range(2 * tiles, 4 * tiles, 2):
        take_up(point)

    def outer_part(j):
        return w_outer_ref[j].reshape(full, full)

    @pl.when(step == tiles)
    def _():
        outer_copy().wait()

    @pl.when((step >= tiles) & (step < 2 * tiles))
    def _():
        total = centered_parts(pre_ref[here, :])[0] * vec(GAIN1) + vec(SHIFT1) + vec(B_OUTER)
        for j in range(chunks):
            total = total + nn(act_ref[here, j * full : (j + 1) * full], outer_part(j))
        summed_ref[here, :] = total
        result = (centered_parts(total)[0] * vec(GAIN2) + vec(SHIFT2)).astype(BF)
        result_ref[tile] = result
        starts = doc_starts(lens_ref)
        places = lax.broadcasted_iota(jnp.int32, (VEC_ROWS, rows), 1) + tile * rows
        row_doc = lax.broadcasted_iota(jnp.int32, (VEC_ROWS, rows), 0)
        hit = jnp.zeros((VEC_ROWS, rows), jnp.bool_)
        for d, start in enumerate(starts):
            hit = hit | ((row_doc == d) & (places == start))
        found = nn(jnp.where(hit, 1.0, 0.0).astype(BF), result)

        @pl.when(tile == 0)
        def _():
            picked_ref[...] = found

        @pl.when(tile > 0)
        def _():
            picked_ref[...] += found

    @pl.when(step == 2 * tiles - 1)
    def _():
        copies, own = row_copies(result_ref, layer_out_ref, lo_send, lo_recv)
        for copy in copies:
            copy.start()
        own.start()
        w_pool = pool_ref[...].astype(F32).reshape(full, full).astype(BF)
        docs = lens_ref.shape[1]
        picked = picked_ref[...].astype(BF)
        pooled = jnp.tanh(nn(picked, w_pool) + vec(B_POOL))
        pooled_low = pooled.astype(BF)
        table = vec_ref[...].astype(BF)
        column = lax.broadcasted_iota(jnp.int32, (VEC_ROWS, VEC_ROWS), 1)
        row = lax.broadcasted_iota(jnp.int32, (VEC_ROWS, VEC_ROWS), 0)
        class_bias = jnp.zeros((VEC_ROWS, VEC_ROWS), F32)
        for j in range(CLASSES):
            class_bias = jnp.where(column == j, b_class_ref[j], class_bias)
        logits = nt(pooled_low, table) + class_bias
        logits_ref[...] = jnp.concatenate([logits[0:8], jnp.zeros((8, 128 - VEC_ROWS), F32)], axis=1)
        live = column < CLASSES
        shown = jnp.where(live, logits, -jnp.inf)
        exps = jnp.where(live, jnp.exp(shown - jnp.max(shown, axis=-1, keepdims=True)), 0.0)
        probs = exps / jnp.sum(exps, axis=-1, keepdims=True)
        label = jnp.zeros((VEC_ROWS, VEC_ROWS), jnp.int32)
        for d in range(docs):
            label = jnp.where(row == d, labels_ref[lax.axis_index("fsdp"), d], label)
        grad = jnp.where(live & (row < docs), probs - jnp.where(label == column, 1.0, 0.0), 0.0)
        grad_low = grad.astype(BF)
        grad_pool = (nn(grad_low, table) * (1.0 - pooled * pooled)).astype(BF)
        dpool_ref[...] = tn(picked, grad_pool).astype(BF)
        first_ref[...] = nt(grad_pool, w_pool)
        small_a_ref[0:16, :] = tn(grad_low, pooled_low)
        small_a_ref[16:17, :] = jnp.sum(grad_pool.astype(F32), axis=0, keepdims=True)
        class_sum = jnp.sum(grad_low.astype(F32), axis=0, keepdims=True)
        small_a_ref[17:18, :] = jnp.concatenate([class_sum, jnp.zeros((1, full - VEC_ROWS), F32)], axis=1)
        small_b_ref[...] = jnp.zeros_like(small_b_ref)
        bi_ref[...] = jnp.zeros_like(bi_ref)
        copies, own = row_copies(cot_ref, cot_rows_ref, cot_send, cot_recv)
        for copy in copies:
            copy.wait()
        own.wait()

    @pl.when(step >= 2 * tiles)
    def _():
        grad = cot_rows_ref[tile].astype(F32)
        places = lax.broadcasted_iota(jnp.int32, (rows, 1), 0) + tile * rows
        placed = jnp.zeros(grad.shape, F32)
        for d, start in enumerate(doc_starts(lens_ref)):
            placed = jnp.where(places == start, first_ref[d : d + 1, :], placed)
        grad = grad + placed
        grad_summed, gain2, shift2 = norm_back(grad, summed_ref[here, :], vec(GAIN2))
        outer = grad_summed.astype(BF)
        outer_ref[...] = outer
        grad_normed = grad_summed
        for j in range(chunks):
            s = j * full
            back = nt(outer, outer_part(j))
            inner = (back * dact_ref[here, s : s + full].astype(F32)).astype(BF)
            inner_ref[:, s : s + full] = inner
            bi_ref[:, s : s + full] += jnp.sum(inner.astype(F32), axis=0, keepdims=True)
            grad_normed = grad_normed + nt(inner, w_inner_ref[:, s : s + full])
        grad_pre, gain1, shift1 = norm_back(grad_normed, pre_ref[here, :], vec(GAIN1))
        gpre_ref[...] = grad_pre
        branch = grad_pre.astype(BF)
        dout = tn(att_ref[...], branch)

        @pl.when(tile == 0)
        def _():
            dout_acc_ref[...] = dout

        @pl.when(tile > 0)
        def _():
            dout_acc_ref[...] += dout

        datt_ref[...] = nt(branch, w_out_ref[...]).astype(BF)
        small_b_ref[0:1, :] += jnp.sum(outer.astype(F32), axis=0, keepdims=True)
        small_b_ref[1:2, :] += gain2
        small_b_ref[2:3, :] += shift2
        small_b_ref[3:4, :] += jnp.sum(branch.astype(F32), axis=0, keepdims=True)
        small_b_ref[4:5, :] += gain1
        small_b_ref[5:6, :] += shift1

    @pl.when(step == 3 * tiles - 1)
    def _():
        dout_ref[...] = dout_acc_ref[...].astype(BF)
        all_sent()
        for t in range(tiles):
            act_copy(t).wait()
        copies, own = row_copies(result_ref, layer_out_ref, lo_send, lo_recv)
        for copy in copies:
            copy.wait()
        own.wait()


def middle(lens, labels, b_class, cot, rows, att, w_inner, w_out, w_outer, pool_shard, vectors):
    length, width = rows.shape
    hidden = w_inner.shape[1]
    tile = 256
    tiles = length // tile
    items = len(MIDDLE_ORDERS)
    once = pl.Buffered(buffer_count=1)
    early = pl.BlockSpec((tile, width), lambda i: (jnp.minimum(i, tiles - 1), 0))

    twice = pl.BlockSpec((tile, width), lambda i: (jnp.where(i < 2 * tiles, jnp.minimum(i, tiles - 1), i - 2 * tiles), 0))

    def late(size):
        return pl.BlockSpec((tile, size), lambda i: (jnp.maximum(i - 2 * tiles, 0), 0))

    def fixed(shape):
        return pl.BlockSpec(shape, lambda i: (0,) * len(shape), pipeline_mode=once)

    lead = (ZS, 2, 2, 2)
    return pl.pallas_call(
        functools.partial(middle_kernel, tiles),
        grid=(3 * tiles,),
        out_shape=[
            jax.ShapeDtypeStruct((length, width), BF),
            jax.ShapeDtypeStruct((length, hidden), BF),
            jax.ShapeDtypeStruct((length, width), BF),
            jax.ShapeDtypeStruct((length, hidden), BF),
            jax.ShapeDtypeStruct((width, width), BF),
            jax.ShapeDtypeStruct((length, width), BF),
            jax.ShapeDtypeStruct((length, width), F32),
            jax.ShapeDtypeStruct((width, width), BF),
            jax.ShapeDtypeStruct((24, width), F32),
            jax.ShapeDtypeStruct((8, width), F32),
            jax.ShapeDtypeStruct((1, hidden), F32),
            jax.ShapeDtypeStruct((8, 128), F32),
            jax.ShapeDtypeStruct(cot.shape, BF),
        ],
        in_specs=[
            SMEM, SMEM, SMEM, ANY, early, twice, fixed((width, hidden)), fixed((width, width)), ANY,
            fixed(pool_shard.shape), fixed((VEC_ROWS, width)),
        ],
        out_specs=[
            early, ANY, late(width), late(hidden), fixed((width, width)), late(width), late(width), fixed((width, width)),
            fixed((24, width)), fixed((8, width)), fixed((1, hidden)), fixed((8, 128)), ANY,
        ],
        scratch_shapes=[
            pltpu.VMEM((length, hidden), BF),
            pltpu.VMEM((length, hidden), BF),
            pltpu.VMEM((length, width), F32),
            pltpu.VMEM((length, width), F32),
            pltpu.VMEM((width, width), F32),
            pltpu.VMEM(cot.shape, BF),
            pltpu.VMEM(cot.shape, BF),
            pltpu.VMEM((VEC_ROWS, width), F32),
            pltpu.VMEM((VEC_ROWS, width), F32),
            pltpu.VMEM(pool_shard.shape, BF),
            pltpu.VMEM(w_outer.shape, BF),
            pltpu.VMEM(lead + pool_shard.shape, BF),
            pltpu.SemaphoreType.DMA((1,)),
            pltpu.SemaphoreType.DMA((tiles,)),
            pltpu.SemaphoreType.DMA((items,)),
            pltpu.SemaphoreType.DMA((items, 9)),
            pltpu.SemaphoreType.DMA((items, 9)),
        ]
        + ROW_SEMAPHORES * 2,
        compiler_params=pltpu.CompilerParams(collective_id=3, has_side_effects=True, vmem_limit_bytes=60 * 2**20),
        name="middle",
    )(lens, labels, b_class, cot, rows, att, w_inner, w_out, w_outer, pool_shard, vectors)


def results_kernel(large, small_ref, *refs):
    sources, refs = refs[:large], refs[large:]
    targets, columns, inner_ref, class_ref, sem, *held = refs[:large], refs[large : large + VECTORS], *refs[large + VECTORS :]
    arriving = [pltpu.make_async_copy(s, h, sem.at[0, j]) for j, (s, h) in enumerate(zip(sources, held))]
    leaving = [pltpu.make_async_copy(h, t, sem.at[1, j]) for j, (h, t) in enumerate(zip(held, targets))]
    for copy in arriving:
        copy.start()
    for j, ref in enumerate(columns):
        ref[...] = small_ref[B_QUERY + j : B_QUERY + j + 1, 0 : ref.shape[1]]
    inner_ref[...] = small_ref[TABLE_ROWS : TABLE_ROWS + 1, 0 : inner_ref.shape[1]]
    class_ref[...] = small_ref[TABLE_ROWS + 1 : TABLE_ROWS + 2, 0 : class_ref.shape[1]]
    for came, goes in zip(arriving, leaving):
        came.wait()
        goes.start()
    for goes in leaving:
        goes.wait()


def write_results(small, arrays, share, hidden_share):
    shapes = [jax.ShapeDtypeStruct(a.shape, a.dtype) for a in arrays]
    vectors = [(1, share)] * VECTORS + [(1, hidden_share), (1, CLASSES)]
    inside = pl.BlockSpec(memory_space=pltpu.VMEM)
    return pl.pallas_call(
        functools.partial(results_kernel, len(arrays)),
        out_shape=shapes + [jax.ShapeDtypeStruct(v, F32) for v in vectors],
        in_specs=[inside] + [ANY] * len(arrays),
        out_specs=[ANY] * len(arrays) + [inside] * len(vectors),
        scratch_shapes=[pltpu.SemaphoreType.DMA((2, len(arrays)))] + [pltpu.VMEM(a.shape, a.dtype) for a in arrays],
        compiler_params=pltpu.CompilerParams(vmem_limit_bytes=60 * 2**20),
        name="results",
    )(small, *arrays)


def fast_body(
    inputs, cotangent, doc_lengths, labels, w_query, b_query, w_key, w_value, b_value, w_out, b_out, first_gain, first_shift,
    w_inner, b_inner, w_outer, b_outer, second_gain, second_shift, w_pool, b_pool, w_class, b_class,
):
    seqs, local_len, width = inputs.shape
    length = seqs * local_len
    devices = 8 * ZS
    docs = doc_lengths.shape[1]
    share = width // devices
    hidden_share = b_inner.shape[0]
    hidden = hidden_share * devices
    vector_shards = [b_query, b_value, b_out, first_gain, first_shift, b_outer, second_gain, second_shift, b_pool]
    q, k, v, att, lse, w_qkv, vectors, rows, full_inner, full_out, full_outer = attend(
        doc_lengths, inputs, w_class.T, [member.reshape(1, share) for member in vector_shards], b_inner.reshape(1, hidden_share),
        [w_query, w_key, w_value], [w_inner, w_out, w_outer],
    )
    rows = rows.reshape(length, width)
    full_inner = full_inner.reshape(width, hidden)
    full_out = full_out.reshape(width, width)
    low, act, outer, inner, grad_out_w, datt, grad_pre, grad_pool, small_a, small_b, grad_b_inner, logit_block, layer_out = middle(
        doc_lengths, labels, b_class, cotangent, rows, att, full_inner, full_out, full_outer, w_pool, vectors
    )
    grad_outer_w = tn(act, outer).astype(BF)
    grad_inner_w = tn(low, inner).astype(BF)
    grad_inputs, all_logits, small, *sums = attend_back(
        doc_lengths, rows, w_qkv, q, k, v, att, datt, lse, grad_pre, small_a, small_b, grad_b_inner, logit_block,
        [
            grad_inner_w.reshape(devices, share, hidden),
            grad_outer_w.reshape(devices, hidden_share, width),
            grad_out_w.reshape(devices, share, width),
            grad_pool.reshape(devices, share, width),
        ],
    )

    done = write_results(small, [grad_inputs, layer_out, *sums], share, hidden_share)
    grad_inputs, layer_out, o_inner, o_outer, o_out, o_pool, o_query, o_key, o_value = done[:9]
    (
        o_b_query, o_b_value, o_b_out, o_gain1, o_shift1, o_b_outer, o_gain2, o_shift2, o_b_pool, o_b_inner, o_b_class,
    ) = (vector.reshape(-1) for vector in done[9:])
    return (
        layer_out,
        all_logits[:, :docs, :CLASSES],
        grad_inputs,
        o_query,
        o_b_query,
        o_key,
        o_value,
        o_b_value,
        o_out,
        o_b_out,
        o_gain1,
        o_shift1,
        o_inner,
        o_b_inner,
        o_outer,
        o_b_outer,
        o_gain2,
        o_shift2,
        o_pool,
        o_b_pool,
        small[:CLASSES, :share].T,
        o_b_class,
    )


def solution(mesh):
    placed = (
        P("dp", "fsdp", None),
        P("dp", "fsdp", None),
        P("dp", None),
        P("dp", None),
        P(("dp", "fsdp"), None),
        P(("dp", "fsdp")),
        P(("dp", "fsdp"), None),
        P(("dp", "fsdp"), None),
        P(("dp", "fsdp")),
        P(("dp", "fsdp"), None),
        P(("dp", "fsdp")),
        P(("dp", "fsdp")),
        P(("dp", "fsdp")),
        P(("dp", "fsdp"), None),
        P(("dp", "fsdp")),
        P(("dp", "fsdp"), None),
        P(("dp", "fsdp")),
        P(("dp", "fsdp")),
        P(("dp", "fsdp")),
        P(("dp", "fsdp"), None),
        P(("dp", "fsdp")),
        P(("dp", "fsdp"), None),
        P(),
    )
    sizes = (mesh.shape["dp"], mesh.shape["fsdp"])
    chosen = fast_body if sizes == (8, 4) else general_body
    return jax.shard_map(
        chosen,
        mesh=mesh,
        in_specs=placed,
        out_specs=(
            P("dp", "fsdp", None),
            P("dp", None, None),
            P("dp", "fsdp", None),
            P(("dp", "fsdp"), None),
            P(("dp", "fsdp")),
            P(("dp", "fsdp"), None),
            P(("dp", "fsdp"), None),
            P(("dp", "fsdp")),
            P(("dp", "fsdp"), None),
            P(("dp", "fsdp")),
            P(("dp", "fsdp")),
            P(("dp", "fsdp")),
            P(("dp", "fsdp"), None),
            P(("dp", "fsdp")),
            P(("dp", "fsdp"), None),
            P(("dp", "fsdp")),
            P(("dp", "fsdp")),
            P(("dp", "fsdp")),
            P(("dp", "fsdp"), None),
            P(("dp", "fsdp")),
            P(("dp", "fsdp"), None),
            P(),
        ),
        check_vma=False,
    )
```
